32 devices in a mesh: dp: 8 (over z, x), head: 4 (over y, core).
Axes of the slice: x: 2, y: 2, z: 4, core: 2. Of those that a mesh axis runs over, the one named last changes fastest.
Arguments:
- series: bfloat16 [16384, 96], P(('dp', 'head')), may hold values from -6 to 6
- cotangent: float32 [16384, 512], P(('dp', 'head')), may hold values from -6 to 6
- window_lengths: int32 [16, 16], P('dp'), may hold values from 0 to 862, as said below
- owner_list: int32 [4, 96], P('head'), may hold values from 0 to 95, as said below
- master: float32 [4, 96, 128, 128], P('head', 'dp'), may hold values from -0.70710678 to 0.70710678
- first_moment: float32 [4, 96, 128, 128], P('head', 'dp'), may hold values from -320 to 320
- second_moment: float32 [4, 96, 128, 128], P('head', 'dp'), may hold values from 2621.44 to 10485.76
- left_stats: float32 [4, 96, 128, 128], P('head', 'dp'), may hold values from -2097.152 to 1342177.3, as said below
- right_stats: float32 [4, 96, 128, 128], P('head', 'dp'), may hold values from -2097.152 to 1342177.3, as said below
- left_basis: float32 [4, 96, 128, 128], P('head', 'dp'), may hold values from -1 to 1, as said below
- right_basis: float32 [4, 96, 128, 128], P('head', 'dp'), may hold values from -1 to 1, as said below
- vec_values: float32 [121, 512], replicated, may hold values from -1.2 to 1.4
- vec_first: float32 [121, 512], replicated, may hold values from -448 to 448
- vec_second: float32 [121, 512], replicated, may hold values from 5898.24 to 23592.96
Outputs:
- activations: float32 [16384, 512], P(('dp', 'head'))
- input_grad: float32 [16384, 96], P(('dp', 'head'))
- new_master: float32 [4, 96, 128, 128], P('head', 'dp')
- new_copy: bfloat16 [4, 96, 128, 128], P('head', 'dp')
- new_first: float32 [4, 96, 128, 128], P('head', 'dp')
- new_second: float32 [4, 96, 128, 128], P('head', 'dp')
- new_left_stats: float32 [4, 96, 128, 128], P('head', 'dp')
- new_right_stats: float32 [4, 96, 128, 128], P('head', 'dp')
- new_left_basis: float32 [4, 96, 128, 128], P('head', 'dp')
- new_right_basis: float32 [4, 96, 128, 128], P('head', 'dp')
- vec_new_values: float32 [121, 512], replicated
- vec_new_first: float32 [121, 512], replicated
- vec_new_second: float32 [121, 512], replicated
- branch_bias_grads: float32 [4, 512], replicated
The draws below stay inside these ranges and needn't reach their ends.
Inputs may be any that keep to these rules, and one draw needn't show every extreme that they name: `window_lengths`: each row lists the variate counts of the windows packed into one bucket of 1024 rows, in order: nonzero entries come first, each 8 or more, and they sum to at most 1024; zeros mark unused slots. Some entry equals 862. `owner_list`: the entries of a row are distinct; slot s belongs to the device of index s // 12 along dp, and in each row some device owns 12 blocks. `left_stats`: each block is symmetric and positive definite. `right_stats`: each block is symmetric and positive definite. `left_basis`: each block is orthogonal. `right_basis`: each block is orthogonal.
All inputs are finite; a program needn't handle non-finite values.
Results may differ from the reference program's by a relative error of at most 0.03.
Values may be sent and summed in bfloat16 or wider, within the bound.
No kernel may reach another device: no remote copies, remote signals or barrier semaphores. Data moves between devices by JAX's collectives and lax.ppermute only.
A program may use at most 192 MiB of HBM per device.

```python
import math
import jax
import jax.numpy as jnp
from jax import lax

D = 512
HEADS = 8
HD = 64
FF = 2048
LOOK = 96
LAYERS = 2
ROWS = 1024
WIN = 16
LMIN = 8
LMAX = 862
BLK = 128
STEP = 10
BUCKETS = 16
TOKENS = 16384
NBLK = 96
SLOTS = 96
VROWS = 121
N_HEAD = 4


def owners_from(key):
    row_keys = jax.random.split(jax.random.fold_in(key, 101), N_HEAD)

    def one_row(row_key):
        shuffled = jax.random.permutation(row_key, SLOTS)[:NBLK]
        return (shuffled - shuffled[0] + SLOTS - 1) % SLOTS
    return jax.vmap(one_row)(row_keys).astype(jnp.int32)


def stats_from(diagonal, offdiag, unit_size):
    symmetric = 0.4 * unit_size * (offdiag + jnp.swapaxes(offdiag, -1, -2))
    identity = jnp.eye(BLK, dtype=jnp.float32)
    return symmetric * (1.0 - identity) + identity * (diagonal * BLK * unit_size)[..., None]


def basis_from(key):
    total = N_HEAD * SLOTS
    first_key, second_key, third_key = jax.random.split(key, 3)
    row_perm = jax.vmap(lambda one_key: jax.random.permutation(one_key, BLK))(jax.random.split(first_key, total))
    col_perm = jax.vmap(lambda one_key: jax.random.permutation(one_key, BLK))(jax.random.split(second_key, total))
    signs = (2 * jax.random.randint(third_key, (total, BLK), 0, 2) - 1).astype(jnp.float32)
    freq = jnp.arange(BLK, dtype=jnp.float32)[:, None]
    place = jnp.arange(BLK, dtype=jnp.float32)[None, :]
    table = math.sqrt(2.0 / BLK) * jnp.cos(math.pi * (place + 0.5) * freq / BLK)
    table = jnp.where(freq == 0.0, table * math.sqrt(0.5), table).astype(jnp.float32)

    def one_block(rows_at, cols_at, sign_row):
        return jnp.take(jnp.take(table, rows_at, axis=0), cols_at, axis=1) * sign_row[:, None]
    blocks = jax.vmap(one_block)(row_perm, col_perm, signs)
    return blocks.reshape(N_HEAD, SLOTS, BLK, BLK).astype(jnp.float32)


def draw_window_lengths(key, part):
    key = jax.random.fold_in(key, 5)
    first_key, second_key, third_key = jax.random.split(key, 3)
    spread = jax.random.randint(first_key, (BUCKETS, WIN), 1, 65)
    levels = 64 // spread - 1
    jitter = jax.random.randint(second_key, (BUCKETS, WIN), 0, LMIN)
    lengths = jnp.minimum(LMIN + (LMAX - LMIN) * levels // 63 + jitter, LMAX)
    chosen = jax.random.randint(third_key, (), 0, BUCKETS)
    lengths = lengths.at[chosen, 0].set(LMAX)
    running = jnp.cumsum(lengths, axis=1)
    return jnp.where(running <= ROWS, lengths, 0).astype(jnp.int32)


def draw_owner_list(key, part):
    chosen = owners_from(key)
    return chosen


def draw_master(key, part):
    chosen = owners_from(key)
    key = jax.random.fold_in(key, 3)
    width_head = HD * HEADS // N_HEAD
    ff_head = FF // N_HEAD
    per_layer = NBLK // LAYERS
    count_qkv = D // BLK * (3 * width_head // BLK)
    count_out = width_head // BLK * (D // BLK)
    count_up = D // BLK * (ff_head // BLK)
    local_index = jnp.arange(NBLK) % per_layer
    block_scale = jnp.where(local_index < count_qkv, D ** (-0.5), jnp.where(local_index < count_qkv + count_out, 4.0 * D ** (-0.5), jnp.where(local_index < count_qkv + count_out + count_up, D ** (-0.5), 2.0 * FF ** (-0.5))))
    slot_scale = jnp.full((N_HEAD, SLOTS), D ** (-0.5), jnp.float32)
    slot_scale = slot_scale.at[jnp.arange(N_HEAD)[:, None], chosen].set(jnp.broadcast_to(block_scale, (N_HEAD, NBLK)).astype(jnp.float32))
    shape_all = (N_HEAD, SLOTS, BLK, BLK)
    noise_draw = jnp.clip(jax.random.normal(key, shape_all, jnp.float32), -4.0, 4.0)
    return noise_draw * slot_scale[:, :, None, None]


def draw_left_stats(key, part):
    key = jax.random.fold_in(key, 7)
    first_key, second_key = jax.random.split(key)
    shape_all = (N_HEAD, SLOTS, BLK, BLK)
    diagonal = jnp.exp(jax.random.uniform(first_key, shape_all[:3], jnp.float32, 0.0, math.log(4.0)))
    offdiag = jax.random.uniform(second_key, shape_all, jnp.float32, -1.0, 1.0)
    return stats_from(diagonal, offdiag, 0.16 * TOKENS)


def draw_right_stats(key, part):
    key = jax.random.fold_in(key, 8)
    first_key, second_key = jax.random.split(key)
    shape_all = (N_HEAD, SLOTS, BLK, BLK)
    diagonal = jnp.exp(jax.random.uniform(first_key, shape_all[:3], jnp.float32, 0.0, math.log(4.0)))
    offdiag = jax.random.uniform(second_key, shape_all, jnp.float32, -1.0, 1.0)
    return stats_from(diagonal, offdiag, 0.16 * TOKENS)


def draw_left_basis(key, part):
    key = jax.random.fold_in(key, 9)
    return basis_from(key)


def draw_right_basis(key, part):
    key = jax.random.fold_in(key, 10)
    return basis_from(key)


def draw_vec_values(key, part):
    key = jax.random.fold_in(key, 13)
    row_index = jnp.arange(VROWS)[:, None]
    ff_ratio = FF // D
    offset = row_index - (LOOK + 1)
    within = offset % (8 + ff_ratio)
    is_gain = (offset >= 0) & ((within == 3) | (within == 6 + ff_ratio))
    row_scale = jnp.where(row_index < LOOK, LOOK ** (-0.5), 0.3)
    noise_draw = jnp.clip(jax.random.normal(key, (VROWS, D), jnp.float32), -4.0, 4.0)
    return jnp.where(is_gain, 1.0 + 0.1 * noise_draw, row_scale * noise_draw).astype(jnp.float32)


def shard_levels(stream_key, dims, cuts, low, top_value):
    def one(axis_at, shards_of):
        heights = jax.random.uniform(jax.random.fold_in(jax.random.fold_in(stream_key, 6), axis_at), (shards_of,), jnp.float32, low / len(cuts), top_value / len(cuts))
        return jnp.repeat(jnp.exp(heights), dims[axis_at] // shards_of).reshape((-1,) + (1,) * (len(dims) - axis_at - 1))

    loudness = one(*cuts[0])
    for cut in cuts[1:]:
        loudness = loudness * one(*cut)
    return loudness


def gaussian(rng, shape, width, most, shards=(), kind=jnp.bfloat16):
    values = width * jax.random.normal(rng, shape, jnp.float32)
    if shards:
        values = values * shard_levels(rng, shape, shards, -0.22, 0.18)
    return jnp.clip(values, -most, most).astype(kind)


def setup_inputs(seed: int = 0) -> dict:
    streams_of = jax.random.split(jax.random.key(seed), 15)
    series = gaussian(streams_of[0], (TOKENS, LOOK), 1.0, 6.0, ((0, 32),))
    cotangent = gaussian(streams_of[1], (TOKENS, D), 1.0, 6.0, ((0, 32),), jnp.float32)
    window_lengths = draw_window_lengths(jax.random.fold_in(streams_of[14], 71), 0)
    owner_list = draw_owner_list(jax.random.fold_in(streams_of[14], 71), 0)
    master = draw_master(jax.random.fold_in(streams_of[14], 71), 0)
    first_moment = gaussian(streams_of[5], (N_HEAD, SLOTS, BLK, BLK), (0.4 * TOKENS ** 0.5), 320.0, ((0, 4), (1, 8)), jnp.float32)
    second_moment = jnp.clip(jnp.exp(math.log(10485.76) - 1.3862944 * jax.random.uniform(streams_of[6], (N_HEAD, SLOTS, BLK, BLK), jnp.float32) ** shard_levels(streams_of[6], (N_HEAD, SLOTS, BLK, BLK), ((0, 4), (1, 8)), -0.2, 0.2)), 2621.44, 10485.76)
    left_stats = draw_left_stats(jax.random.fold_in(streams_of[14], 71), 0)
    right_stats = draw_right_stats(jax.random.fold_in(streams_of[14], 71), 0)
    left_basis = draw_left_basis(jax.random.fold_in(streams_of[14], 71), 0)
    right_basis = draw_right_basis(jax.random.fold_in(streams_of[14], 71), 0)
    vec_values = draw_vec_values(jax.random.fold_in(streams_of[14], 71), 0)
    vec_first = gaussian(streams_of[12], (VROWS, D), (0.6 * TOKENS ** 0.5), 448.0, (), jnp.float32)
    vec_second = jnp.clip(jnp.exp(jax.random.uniform(streams_of[13], (VROWS, D), jnp.float32, math.log(5898.24), math.log(23592.96))), 5898.24, 23592.96)
    return dict(series=series, cotangent=cotangent, window_lengths=window_lengths, owner_list=owner_list, master=master, first_moment=first_moment, second_moment=second_moment, left_stats=left_stats, right_stats=right_stats, left_basis=left_basis, right_basis=right_basis, vec_values=vec_values, vec_first=vec_first, vec_second=vec_second)


@jax.custom_vjp
def low(v):
    return lax.optimization_barrier(v.astype(jnp.bfloat16)).astype(jnp.float32)

@jax.custom_vjp
def low_back(v):
    return v

def low_keep(v):
    return (low(v), None)

def low_pass(kept, grad):
    return (grad,)

def back_keep(v):
    return (v, None)

def back_low(kept, grad):
    return (low(grad),)
low.defvjp(low_keep, low_pass)
low_back.defvjp(back_keep, back_low)
top_precision = lax.Precision.HIGHEST
norm_eps = 1e-05
beta_first = 0.5
beta_second = 0.5
beta_stats = 0.5
adam_eps = 1e-08
rate_matrix = 0.02
rate_vector = 0.15
weight_decay = 0.01
mask_fill = -1e+30

def product(left_mat, right_mat):
    return jnp.dot(left_mat.astype(jnp.float32), right_mat.astype(jnp.float32), precision=top_precision, preferred_element_type=jnp.float32)

def assemble(pieces, row_count, col_count):
    return pieces.reshape(row_count, col_count, BLK, BLK).transpose(0, 2, 1, 3).reshape(row_count * BLK, col_count * BLK)

def window_ids(lengths):
    bounds = jnp.cumsum(lengths, axis=1, dtype=jnp.int32)
    places = jnp.arange(ROWS, dtype=jnp.int32)
    return lax.optimization_barrier(jnp.sum((places[None, :, None] >= bounds[:, None, :]).astype(jnp.int32), axis=2, dtype=jnp.int32))

def normalize(resid, gain_vec, shift_vec):
    center = resid - lax.optimization_barrier(jnp.mean(resid, axis=-1, keepdims=True))
    spread = lax.optimization_barrier(jnp.mean(center * center, axis=-1, keepdims=True))
    return center * lax.rsqrt(spread + norm_eps) * gain_vec + shift_vec

def head_matrices(blocks_all, layer_at):
    width_head = HD * HEADS // N_HEAD
    ff_head = FF // N_HEAD
    per_layer = NBLK // LAYERS
    count_qkv = D // BLK * (3 * width_head // BLK)
    count_out = width_head // BLK * (D // BLK)
    count_up = D // BLK * (ff_head // BLK)
    query_cols, key_cols, value_cols, out_rows, up_cols, down_rows = ([], [], [], [], [], [])
    for head_group in range(N_HEAD):
        pieces = blocks_all[head_group, layer_at * per_layer:(layer_at + 1) * per_layer]
        joint_mat = assemble(pieces[:count_qkv], D // BLK, 3 * width_head // BLK)
        query_cols.append(joint_mat[:, :width_head])
        key_cols.append(joint_mat[:, width_head:2 * width_head])
        value_cols.append(joint_mat[:, 2 * width_head:])
        out_rows.append(assemble(pieces[count_qkv:count_qkv + count_out], width_head // BLK, D // BLK))
        up_cols.append(assemble(pieces[count_qkv + count_out:count_qkv + count_out + count_up], D // BLK, ff_head // BLK))
        down_rows.append(assemble(pieces[count_qkv + count_out + count_up:], ff_head // BLK, D // BLK))
    return (jnp.concatenate(query_cols, axis=1), jnp.concatenate(key_cols, axis=1), jnp.concatenate(value_cols, axis=1), jnp.concatenate(out_rows, axis=0), jnp.concatenate(up_cols, axis=1), jnp.concatenate(down_rows, axis=0))

def depth_vectors(vec_table, layer_at):
    ff_ratio = FF // D
    base_row = LOOK + 1 + layer_at * (8 + ff_ratio)
    return (vec_table[base_row], vec_table[base_row + 1], vec_table[base_row + 2], vec_table[base_row + 3], vec_table[base_row + 4], vec_table[base_row + 5:base_row + 5 + ff_ratio].reshape(FF), vec_table[base_row + 5 + ff_ratio], vec_table[base_row + 6 + ff_ratio], vec_table[base_row + 7 + ff_ratio])

def attend(operands):
    queries, keys_in, values, windows = operands
    scores = low_back(jnp.einsum('qhd,khd->hqk', queries, keys_in, precision=top_precision) * HD ** (-0.5))
    joined = windows[:, None] == windows[None, :]
    scores = jnp.where(joined[None], scores, mask_fill)
    weights = jax.nn.softmax(scores, axis=-1)
    mixed = jnp.einsum('hqk,khd->qhd', low(weights), values, precision=top_precision)
    return mixed.reshape(ROWS, HEADS * HD)

def encoder_layer(residual, matrices, vectors, windows):
    query_w, key_w, value_w, out_w, up_w, down_w = matrices
    query_b, value_b, out_b, gain_one, shift_one, up_b, down_b, gain_two, shift_two = vectors
    inputs = low(residual)
    queries = low(low_back(product(inputs, query_w) + query_b))
    keys_in = low(low_back(product(inputs, key_w)))
    values = low(low_back(product(inputs, value_w) + value_b))
    group_count = windows.shape[0]
    shape_four = (group_count, ROWS, HEADS, HD)
    mixed = lax.map(jax.checkpoint(attend), (queries.reshape(shape_four), keys_in.reshape(shape_four), values.reshape(shape_four), windows))
    mixed = low(low_back(mixed.reshape(group_count * ROWS, HEADS * HD)))
    attended = low_back(product(mixed, out_w)) + out_b
    normed = normalize(residual + attended, gain_one, shift_one)
    hidden_pre = low_back(product(low(normed), up_w) + up_b)
    hidden = low(jax.nn.gelu(hidden_pre, approximate=False))
    fed_out = low_back(product(hidden, down_w)) + down_b
    return normalize(normed + fed_out, gain_two, shift_two)

def forward(blocks_all, vec_table, series_rows, windows):
    residual = product(series_rows, vec_table[:LOOK]) + vec_table[LOOK]
    for layer_at in range(LAYERS):
        residual = encoder_layer(residual, head_matrices(blocks_all, layer_at), depth_vectors(vec_table, layer_at), windows)
    return residual

def rotate(left_mat, mid_mat, right_mat):
    inner_prod = jnp.einsum('...ji,...jk->...ik', left_mat, mid_mat, precision=top_precision)
    return jnp.einsum('...ik,...kl->...il', inner_prod, right_mat, precision=top_precision)

def rotate_back(left_mat, mid_mat, right_mat):
    inner_prod = jnp.einsum('...ij,...jk->...ik', left_mat, mid_mat, precision=top_precision)
    return jnp.einsum('...ik,...lk->...il', inner_prod, right_mat, precision=top_precision)

def orthonormal(matrix):
    gram_mat = jnp.einsum('...ji,...jk->...ik', matrix, matrix, precision=top_precision)
    factor = jnp.linalg.cholesky(gram_mat)
    flat_factor = factor.reshape(-1, BLK, BLK)
    flat_matrix = matrix.reshape(-1, BLK, BLK)
    solved = jax.vmap(lambda lower_part, full_part: jax.scipy.linalg.solve_triangular(lower_part, full_part.T, lower=True))(flat_factor, flat_matrix)
    return jnp.swapaxes(solved, 1, 2).reshape(matrix.shape)

def soap_update(gradient, master, moment_one, moment_two, left_stats, right_stats, left_basis, right_basis):
    turned = rotate(left_basis, gradient, right_basis)
    new_first = beta_first * moment_one + (1.0 - beta_first) * turned
    new_second = beta_second * moment_two + (1.0 - beta_second) * turned * turned
    step_ratio = new_first / (1.0 - beta_first ** STEP) / (jnp.sqrt(new_second / (1.0 - beta_second ** STEP)) + adam_eps)
    update = rotate_back(left_basis, step_ratio, right_basis)
    new_master = master - rate_matrix * (update + weight_decay * master)
    new_left = beta_stats * left_stats + (1.0 - beta_stats) * jnp.einsum('...ik,...jk->...ij', gradient, gradient, precision=top_precision)
    new_right = beta_stats * right_stats + (1.0 - beta_stats) * jnp.einsum('...ki,...kj->...ij', gradient, gradient, precision=top_precision)
    left_next = orthonormal(jnp.einsum('...ij,...jk->...ik', new_left, left_basis, precision=top_precision))
    right_next = orthonormal(jnp.einsum('...ij,...jk->...ik', new_right, right_basis, precision=top_precision))
    return (new_master, new_master.astype(jnp.bfloat16), new_first, new_second, new_left, new_right, left_next, right_next)

def adamw_update(gradient, values, moment_one, moment_two):
    new_first = beta_first * moment_one + (1.0 - beta_first) * gradient
    new_second = beta_second * moment_two + (1.0 - beta_second) * gradient * gradient
    step_ratio = new_first / (1.0 - beta_first ** STEP) / (jnp.sqrt(new_second / (1.0 - beta_second ** STEP)) + adam_eps)
    new_values = values - rate_vector * (step_ratio + weight_decay * values)
    return (new_values, new_first, new_second)

def branch_biases(grad_table):
    ff_ratio = FF // D
    bias_rows = []
    for layer_at in range(LAYERS):
        base_row = LOOK + 1 + layer_at * (8 + ff_ratio)
        bias_rows.append(grad_table[base_row + 2])
        bias_rows.append(grad_table[base_row + 5 + ff_ratio])
    return jnp.stack(bias_rows, axis=0)

def reference(series, cotangent, window_lengths, owner_list, master, first_moment, second_moment, left_stats, right_stats, left_basis, right_basis, vec_values, vec_first, vec_second):
    copies = master.astype(jnp.bfloat16)
    blocks_all = jax.vmap(lambda slot_stack, owner_row: slot_stack[owner_row])(copies, owner_list).astype(jnp.float32)
    windows = window_ids(window_lengths)
    valid_rows = (windows < WIN).astype(jnp.float32).reshape(BUCKETS // 4, 4 * ROWS, 1)
    series_groups = series.astype(jnp.float32).reshape(BUCKETS // 4, 4 * ROWS, LOOK)
    cot_groups = cotangent.astype(jnp.float32).reshape(BUCKETS // 4, 4 * ROWS, D)
    window_groups = windows.reshape(BUCKETS // 4, 4, ROWS)

    def group_step(totals, operands):
        rows_in, rows_cot, rows_valid, rows_win = operands

        def masked(blocks_in, table_in, series_in):
            return forward(blocks_in, table_in, series_in, rows_win) * rows_valid
        outputs, pullback = jax.vjp(masked, blocks_all, vec_values, rows_in)
        grad_blocks, grad_table, grad_series = pullback(rows_cot)
        return ((totals[0] + grad_blocks, totals[1] + grad_table), (outputs, grad_series))
    initial = (jnp.zeros(blocks_all.shape, jnp.float32), jnp.zeros(vec_values.shape, jnp.float32))
    (grad_blocks, grad_table), (outputs, grad_series) = lax.scan(group_step, initial, (series_groups, cot_groups, valid_rows, window_groups))
    activations = outputs.reshape(TOKENS, D)
    input_grad = grad_series.reshape(TOKENS, LOOK)
    grad_slots = jax.vmap(lambda owner_row, pieces: jnp.zeros((SLOTS, BLK, BLK), jnp.float32).at[owner_row].set(pieces))(owner_list, grad_blocks)
    new_master, new_copy, new_first, new_second, new_left, new_right, left_next, right_next = soap_update(grad_slots, master, first_moment, second_moment, left_stats, right_stats, left_basis, right_basis)
    vec_new_values, vec_new_first, vec_new_second = adamw_update(grad_table, vec_values, vec_first, vec_second)
    branch_bias_grads = branch_biases(grad_table)
    return (activations, input_grad, new_master, new_copy, new_first, new_second, new_left, new_right, left_next, right_next, vec_new_values, vec_new_first, vec_new_second, branch_bias_grads)
```

```python
import functools

import jax
import jax.numpy as jnp
from jax import lax
from jax.experimental import pallas as pl
from jax.experimental.pallas import tpu as pltpu
from jax.sharding import PartitionSpec as P

D = 512
HEADS = 8
HD = 64
FF = 2048
LOOK = 96
LAYERS = 2
BLK = 128
STEP = 10

f32 = jnp.float32
HI = lax.Precision.HIGHEST
norm_eps = 1e-05
beta_first = 0.5
beta_second = 0.5
beta_stats = 0.5
adam_eps = 1e-08
rate_matrix = 0.02
rate_vector = 0.15
weight_decay = 0.01


def window_ids(lengths, bucket_rows):
    bounds = jnp.cumsum(lengths, axis=1, dtype=jnp.int32)
    places = jnp.arange(bucket_rows, dtype=jnp.int32)
    return jnp.sum(
        (places[None, :, None] >= bounds[:, None, :]).astype(jnp.int32), axis=2, dtype=jnp.int32
    )


def depth_vectors(vec_table, layer_at):
    ff_ratio = FF // D
    base_row = LOOK + 1 + layer_at * (8 + ff_ratio)
    return (
        vec_table[base_row],
        vec_table[base_row + 1],
        vec_table[base_row + 2],
        vec_table[base_row + 3],
        vec_table[base_row + 4],
        vec_table[base_row + 5 : base_row + 5 + ff_ratio].reshape(FF),
        vec_table[base_row + 5 + ff_ratio],
        vec_table[base_row + 6 + ff_ratio],
        vec_table[base_row + 7 + ff_ratio],
    )


def adamw_update(gradient, values, moment_one, moment_two):
    new_first = beta_first * moment_one + (1.0 - beta_first) * gradient
    new_second = beta_second * moment_two + (1.0 - beta_second) * gradient * gradient
    step_ratio = (
        new_first
        / (1.0 - beta_first**STEP)
        / (jnp.sqrt(new_second / (1.0 - beta_second**STEP)) + adam_eps)
    )
    new_values = values - rate_vector * (step_ratio + weight_decay * values)
    return (new_values, new_first, new_second)


def branch_biases(grad_table):
    ff_ratio = FF // D
    bias_rows = []
    for layer_at in range(LAYERS):
        base_row = LOOK + 1 + layer_at * (8 + ff_ratio)
        bias_rows.append(grad_table[base_row + 2])
        bias_rows.append(grad_table[base_row + 5 + ff_ratio])
    return jnp.stack(bias_rows, axis=0)


def dot_hi(a,b,ca,cb):
    return lax.dot_general(a,b,(((ca,),(cb,)),((),())),precision=HI,preferred_element_type=f32)
PANEL=32
def qr_batch(a_ref, count):
    lane = lax.broadcasted_iota(jnp.int32,(1,1,BLK),2)
    sub8 = lax.broadcasted_iota(jnp.int32,(1,8,1),1)
    sub32 = lax.broadcasted_iota(jnp.int32,(1,PANEL,1),1)
    def panel(sp, carry):
        r0 = pl.multiple_of(sp*PANEL, PANEL)
        block = a_ref[:, pl.ds(r0,PANEL), :]
        block = pltpu.roll(block.reshape(count*PANEL,BLK), lax.rem(BLK - r0, BLK), 1).reshape(count,PANEL,BLK)
        tiles = [block[:, 8*t:8*t+8, :] for t in range(PANEL//8)]
        for k in range(PANEL):
            t0, s = divmod(k,8)
            row = tiles[t0][:, s:s+1, :]
            inv = 1.0/row[:, :, k:k+1]
            pn = (row + (lane==k).astype(f32))*inv
            for t in range(t0,PANEL//8):
                c = tiles[t][:, :, k:k+1]
                if t==t0:
                    if s==7: continue
                    c = jnp.where(sub8 > s, c, 0.0)
                tiles[t] = tiles[t] - c*pn
        done = jnp.concatenate(tiles, axis=1)
        diag = lane==sub32
        piv = jnp.sum(jnp.where(diag, done, 0.0), axis=2, keepdims=True)
        done = jnp.where(diag, 1.0, jnp.where((lane > sub32) & (lane < PANEL), 0.0, done))
        done = pltpu.roll(done.reshape(count*PANEL,BLK), r0, 1).reshape(count,PANEL,BLK)
        scale = lax.rsqrt(piv)
        done = done*scale
        a_ref[:, pl.ds(r0,PANEL), :] = done
        @pl.when(sp < BLK//PANEL-1)
        def _():
            lane2 = lax.broadcasted_iota(jnp.int32,(BLK,BLK),1)
            row2 = lax.broadcasted_iota(jnp.int32,(BLK,BLK),0)
            clear = (row2 >= r0+PANEL) & (lane2 >= r0) & (lane2 < r0+PANEL)
            lanep = lax.broadcasted_iota(jnp.int32,(PANEL,BLK),1)
            for b in range(count):
                z = a_ref[b, pl.ds(r0,PANEL), :]
                zm = jnp.where(lanep >= r0+PANEL, z, 0.0)
                upd = dot_hi(zm, z, 0, 0)
                a_ref[b] = jnp.where(clear, 0.0, a_ref[b]) - upd
        return carry
    lax.fori_loop(0, BLK//PANEL, panel, 0)

def soap_kernel(count, *refs):
    g = sum(ref[0].astype(f32) for ref in refs[:count])
    soap_body(g, *refs[count:])


def soap_body(g, mas_ref, m1_ref, m2_ref, ls_ref, rs_ref, lb_ref, rb_ref,
                nm_ref, nc_ref, n1_ref, n2_ref, nl_ref, nr_ref, ql_ref, qr_ref, mat_ref, a_ref):
    n = pl.num_programs(0); i = pl.program_id(0)
    lb = lb_ref[0]; rb = rb_ref[0]
    rot = dot_hi(dot_hi(lb,g,0,0), rb, 1, 0)
    n1 = 0.5*m1_ref[0]+0.5*rot
    n2 = 0.5*m2_ref[0]+0.5*rot*rot
    n1_ref[0]=n1; n2_ref[0]=n2
    corr = 1.0-0.5**STEP
    ratio = n1/corr/(jnp.sqrt(n2/corr)+1e-8)
    upd = dot_hi(dot_hi(lb,ratio,1,0), rb, 1, 1)
    mas = mas_ref[0]
    nm = mas - 0.02*(upd+0.01*mas)
    nm_ref[0]=nm; nc_ref[0]=nm.astype(jnp.bfloat16)
    nl = 0.5*ls_ref[0]+0.5*dot_hi(g,g,1,1)
    nr = 0.5*rs_ref[0]+0.5*dot_hi(g,g,0,0)
    nl_ref[0]=nl; nr_ref[0]=nr
    for side,(st,ba) in enumerate(((nl,lb),(nr,rb))):
        m = dot_hi(st,ba,1,0)
        m = m*lax.rsqrt(jnp.sum(m*m,axis=0,keepdims=True))
        mat_ref[2*i+side] = m
        a_ref[2*i+side] = dot_hi(m,m,0,0)
    @pl.when(i==n-1)
    def _():
        count = a_ref.shape[0]
        qr_batch(a_ref, count)
        keep = lax.broadcasted_iota(jnp.int32,(BLK,BLK),1) <= lax.broadcasted_iota(jnp.int32,(BLK,BLK),0)
        def fin(j, c):
            for side,ref in enumerate((ql_ref,qr_ref)):
                x = jnp.where(keep, a_ref[2*j+side], 0.0)
                ref[j] = dot_hi(mat_ref[2*j+side], x, 1, 1)
            return c
        lax.fori_loop(0, n, fin, 0)

def soap(gs, master, m1, m2, ls, rs, lb, rb):
    n = master.shape[0]
    one = pl.BlockSpec((1,BLK,BLK), lambda i:(i,0,0))
    whole = pl.BlockSpec((n,BLK,BLK), lambda i:(0,0,0))
    sh = jax.ShapeDtypeStruct((n,BLK,BLK), f32)
    shb = jax.ShapeDtypeStruct((n,BLK,BLK), jnp.bfloat16)
    return pl.pallas_call(functools.partial(soap_kernel, len(gs)), grid=(n,), in_specs=[one]*(len(gs)+7),
        out_specs=[one]*6+[whole]*2, out_shape=[sh,shb,sh,sh,sh,sh,sh,sh],
        scratch_shapes=[pltpu.VMEM((2*n,BLK,BLK),f32)]*2,
        compiler_params=pltpu.CompilerParams(vmem_limit_bytes=50*2**20), name="soap")(*gs,master,m1,m2,ls,rs,lb,rb)


bf16 = jnp.bfloat16
LANES = 128
ROW_TILE = 256
BIG = 1e30
CORR = 1.0 - 0.5**STEP


def params(mib=48):
    return pltpu.CompilerParams(vmem_limit_bytes=mib * 2**20)


def shape(dims, kind=f32):
    return jax.ShapeDtypeStruct(dims, kind)


def dot(a, b, ca=1, cb=0):
    return lax.dot_general(a, b, (((ca,), (cb,)), ((), ())), preferred_element_type=f32)


def place_blocks(dst, refs, first, rows, cols, row_step, col_step, col_base=0):
    for r, ref in enumerate(refs):
        for j in range(rows * cols):
            row, col = divmod(j, cols)
            r0 = r * row_step + row * BLK
            c0 = col_base + r * col_step + col * BLK
            dst[r0 : r0 + BLK, c0 : c0 + BLK] = ref[first + j]


def place_qkv(dst, refs):
    for r, ref in enumerate(refs):
        for j in range(12):
            row, col = divmod(j, 3)
            c0 = col * D + r * BLK
            dst[row * BLK : (row + 1) * BLK, c0 : c0 + BLK] = ref[j]


def layer_norm(resid):
    center = resid - jnp.mean(resid, axis=1, keepdims=True)
    inv = lax.rsqrt(jnp.mean(center * center, axis=1, keepdims=True) + norm_eps)
    return center * inv, inv


def layer_norm_grad(grad, unit, inv, gain):
    dn = grad * gain
    return inv * (
        dn
        - jnp.mean(dn, axis=1, keepdims=True)
        - unit * jnp.mean(dn * unit, axis=1, keepdims=True)
    )


def col_sum(values):
    return jnp.sum(values, axis=0, keepdims=True)


def embed_kernel(series_ref, we_ref, be_ref, x_ref):
    x_ref[...] = dot_hi(series_ref[...].astype(f32), we_ref[...], 1, 0) + be_ref[...]


def embed(series, table):
    rows = series.shape[0]
    return pl.pallas_call(
        embed_kernel, out_shape=shape((rows, D)), compiler_params=params(), name="embed"
    )(series, table[:LOOK], table[LOOK : LOOK + 1])


def proj_kernel(x_ref, bq_ref, bv_ref, w0, w1, w2, w3, xs_ref, q_ref, k_ref, v_ref, w_s):
    place_qkv(w_s, (w0, w1, w2, w3))

    def tile(t, c):
        at = pl.ds(t * ROW_TILE, ROW_TILE)
        xs = x_ref[at].astype(bf16)
        xs_ref[at] = xs
        q_ref[at] = (dot(xs, w_s[:, :D]) + bq_ref[...]).astype(bf16)
        k_ref[at] = dot(xs, w_s[:, D : 2 * D]).astype(bf16)
        v_ref[at] = (dot(xs, w_s[:, 2 * D :]) + bv_ref[...]).astype(bf16)
        return c

    lax.fori_loop(0, x_ref.shape[0] // ROW_TILE, tile, 0)


def project(x, bq, bv, wqkv):
    rows = x.shape[0]
    return pl.pallas_call(
        proj_kernel,
        out_shape=[shape((rows, D), bf16)] * 4,
        scratch_shapes=[pltpu.VMEM((D, 3 * D), bf16)],
        compiler_params=params(),
        name="project",
    )(x, bq, bv, *wqkv)


def half_mask(i, kind=bf16):
    lane = lax.broadcasted_iota(jnp.int32, (1, LANES), 1)
    return ((lane >= HD * i) & (lane < HD * (i + 1))).astype(f32).astype(kind)


def three_terms(col):
    first = col.astype(bf16).astype(f32)
    second = (col - first).astype(bf16).astype(f32)
    return first, second, col - first - second


def lanes_with(base, at, cols):
    lane = lax.broadcasted_iota(jnp.int32, base.shape, 1)
    for i, col in enumerate(cols):
        base = jnp.where(lane == at + i, col, base)
    return base.astype(bf16)


def attend_kernel(q_ref, k_ref, kp_ref, v_ref, vp_ref, ohq_ref, ohk_ref, o_ref, lse_ref, ka, va):
    rows = q_ref.shape[0]
    ka[:rows, :LANES] = k_ref[...]
    ka[rows:, :LANES] = kp_ref[...]
    ka[:, LANES:] = ohk_ref[...]
    lane = lax.broadcasted_iota(jnp.int32, (ROW_TILE, LANES), 1)
    for i in range(2):
        m = half_mask(i)
        va[i, :rows, :LANES] = v_ref[...] * m
        va[i, rows:, :LANES] = vp_ref[...] * m
        va[i, :, LANES:] = jnp.ones((2 * rows, LANES), bf16)

    def tile(t, c):
        at = pl.ds(t * ROW_TILE, ROW_TILE)
        total = jnp.zeros((ROW_TILE, LANES), f32)
        stat = jnp.zeros((ROW_TILE, LANES), f32)
        for i in range(2):
            qa = jnp.concatenate([q_ref[at] * (half_mask(i) * bf16(0.125)), ohq_ref[at]], axis=1)
            s = dot(qa, ka[...], 1, 1)
            high = jnp.max(s, axis=1, keepdims=True)
            e = jnp.exp(s - high).astype(bf16)
            out = dot(e, va[i])
            norm = out[:, LANES:]
            total = total + out[:, :LANES] / norm
            stat = jnp.where(lane == i, high + jnp.log(norm), stat)
        o_ref[at] = total.astype(bf16)
        lse_ref[at] = stat
        return c

    lax.fori_loop(0, rows // ROW_TILE, tile, 0)


def attend(q, k, kp, v, vp, ohq, ohk):
    rows = q.shape[0]
    pair = pl.BlockSpec((rows, LANES), lambda h: (0, h))
    other = pl.BlockSpec((rows, LANES), lambda h: (0, h + 1 - 2 * lax.rem(h, 2)))
    return pl.pallas_call(
        attend_kernel,
        grid=(D // LANES,),
        in_specs=[pair, pair, other, pair, other]
        + [
            pl.BlockSpec((rows, LANES), lambda h: (0, 0)),
            pl.BlockSpec((2 * rows, LANES), lambda h: (0, 0)),
        ],
        out_specs=[pair, pair],
        out_shape=[shape((rows, D), bf16), shape((rows, D))],
        scratch_shapes=[
            pltpu.VMEM((2 * rows, 2 * LANES), bf16),
            pltpu.VMEM((2, 2 * rows, 2 * LANES), bf16),
        ],
        compiler_params=params(),
        name="attend",
    )(q, k, kp, v, vp, ohq, ohk)


def post_kernel(
    o_ref, x_ref, vec_ref, b1_ref, a0, a1, a2, a3, f0, f1, f2, f3,
    n1_ref, i1_ref, y_ref, hid_ref, slope_ref, n2_ref, i2_ref, x2_ref,
    wo_s, w1_s, w2_s,
):
    place_blocks(wo_s, (a0, a1, a2, a3), 0, 1, 4, BLK, 0)
    place_blocks(w1_s, (f0, f1, f2, f3), 0, 4, 4, 0, D)
    place_blocks(w2_s, (f0, f1, f2, f3), 16, 4, 4, D, 0)

    def tile(t, c):
        at = pl.ds(t * ROW_TILE, ROW_TILE)
        vec = [vec_ref[i : i + 1, :] for i in range(6)]
        unit, inv = layer_norm(x_ref[at] + dot(o_ref[at], wo_s[...]) + vec[0])
        n1_ref[at] = unit
        i1_ref[at] = jnp.broadcast_to(inv, (ROW_TILE, LANES))
        y = unit * vec[1] + vec[2]
        yb = y.astype(bf16)
        y_ref[at] = yb
        fed = jnp.zeros((ROW_TILE, D), f32)
        for r in range(FF // D):
            cols = slice(r * D, (r + 1) * D)
            pre = dot(yb, w1_s[:, cols]) + b1_ref[:, cols]
            phi = 0.5 * (1.0 + lax.erf(pre * (0.5**0.5)))
            hid = (pre * phi).astype(bf16)
            hid_ref[at, cols] = hid
            slope_ref[at, cols] = (
                phi + pre * (jnp.exp(-0.5 * pre * pre) * 0.3989422804014327)
            ).astype(bf16)
            fed = fed + dot(hid, w2_s[cols, :])
        unit, inv = layer_norm(y + fed + vec[3])
        n2_ref[at] = unit
        i2_ref[at] = jnp.broadcast_to(inv, (ROW_TILE, LANES))
        x2_ref[at] = unit * vec[4] + vec[5]
        return c

    lax.fori_loop(0, x_ref.shape[0] // ROW_TILE, tile, 0)


def post(o, x, vec, b1, wout, wffn):
    rows = x.shape[0]
    return pl.pallas_call(
        post_kernel,
        out_shape=[
            shape((rows, D)),
            shape((rows, LANES)),
            shape((rows, D), bf16),
            shape((rows, FF), bf16),
            shape((rows, FF), bf16),
            shape((rows, D)),
            shape((rows, LANES)),
            shape((rows, D)),
        ],
        scratch_shapes=[
            pltpu.VMEM((D, D), bf16),
            pltpu.VMEM((D, FF), bf16),
            pltpu.VMEM((FF, D), bf16),
        ],
        compiler_params=params(),
        name="post",
    )(o, x, vec, b1, *wout, *wffn)


def store_blocks(refs, r, first, rows, cols, value):
    keep_ref, send_ref = refs
    ref = send_ref if r % 2 else keep_ref
    for j in range(rows * cols):
        row, col = divmod(j, cols)
        ref[r // 2, first + j] = value[row * BLK : (row + 1) * BLK, col * BLK : (col + 1) * BLK]


def ffn_grad_kernel(
    e_ref, n2_ref, i2_ref, n1_ref, i1_ref, y_ref, hid_ref, slope_ref, o_ref, vec_ref,
    a0, a1, a2, a3, f0, f1, f2, f3,
    gk_ref, gs_ref, ok_ref, os_ref, dr1_ref, do_ref, db1_ref, sums_ref,
    wo_s, w1_s, w2_s, dr2_s, dfr_s, dpre_s, dar_s,
):
    rows = e_ref.shape[0]
    place_blocks(wo_s, (a0, a1, a2, a3), 0, 1, 4, BLK, 0)
    place_blocks(w1_s, (f0, f1, f2, f3), 0, 4, 4, 0, D)
    place_blocks(w2_s, (f0, f1, f2, f3), 16, 4, 4, D, 0)
    tiles = rows // ROW_TILE
    gain_two = vec_ref[4:5, :]
    gain_one = vec_ref[1:2, :]
    zero = jnp.zeros((1, D), f32)

    def tile_two(t, c):
        at = pl.ds(t * ROW_TILE, ROW_TILE)
        grad = e_ref[at]
        unit = n2_ref[at]
        dr2 = layer_norm_grad(grad, unit, i2_ref[at, 0:1], gain_two)
        dr2_s[at] = dr2
        dfr_s[at] = dr2.astype(bf16)
        return (c[0] + col_sum(dr2), c[1] + col_sum(grad * unit), c[2] + col_sum(grad))

    db2, dg2, dc2 = lax.fori_loop(0, tiles, tile_two, (zero, zero, zero))

    for r in range(FF // D):
        cols = slice(r * D, (r + 1) * D)

        def tile_up(t, c):
            at = pl.ds(t * ROW_TILE, ROW_TILE)
            dh = dot(dfr_s[at], w2_s[cols, :], 1, 1)
            dpre = (dh * slope_ref[at, cols].astype(f32)).astype(bf16)
            dpre_s[at, cols] = dpre
            dr2_s[at] = dr2_s[at] + dot(dpre, w1_s[:, cols], 1, 1)
            return c + col_sum(dpre.astype(f32))

        db1_ref[r : r + 1, :] = lax.fori_loop(0, tiles, tile_up, zero)
        store_blocks((gk_ref, gs_ref), r, 16, 4, 4, dot(hid_ref[:, cols], dfr_s[...], 0, 0).astype(bf16))
        store_blocks((gk_ref, gs_ref), r, 0, 4, 4, dot(y_ref[...], dpre_s[:, cols], 0, 0).astype(bf16))

    def tile_one(t, c):
        at = pl.ds(t * ROW_TILE, ROW_TILE)
        grad = dr2_s[at]
        unit = n1_ref[at]
        dr1 = layer_norm_grad(grad, unit, i1_ref[at, 0:1], gain_one)
        dr1_ref[at] = dr1
        dar = dr1.astype(bf16)
        dar_s[at] = dar
        do_ref[at] = dot(dar, wo_s[...], 1, 1).astype(bf16)
        return (c[0] + col_sum(dr1), c[1] + col_sum(grad * unit), c[2] + col_sum(grad))

    dbo, dg1, dc1 = lax.fori_loop(0, tiles, tile_one, (zero, zero, zero))
    dwo = dot(o_ref[...], dar_s[...], 0, 0).astype(bf16)
    for r in range(4):
        store_blocks((ok_ref, os_ref), r, 0, 1, 4, dwo[r * BLK : (r + 1) * BLK])
    for i, value in enumerate((dbo, dg1, dc1, db2, dg2, dc2, zero, zero)):
        sums_ref[i : i + 1, :] = value


def ffn_grad(e, n2, i2, n1, i1, y, hid, slope, o, vec, wout, wffn):
    rows = e.shape[0]
    return pl.pallas_call(
        ffn_grad_kernel,
        out_shape=[
            shape((2, 32, BLK, BLK), bf16),
            shape((2, 32, BLK, BLK), bf16),
            shape((2, 4, BLK, BLK), bf16),
            shape((2, 4, BLK, BLK), bf16),
            shape((rows, D)),
            shape((rows, D), bf16),
            shape((FF // D, D)),
            shape((8, D)),
        ],
        scratch_shapes=[
            pltpu.VMEM((D, D), bf16),
            pltpu.VMEM((D, FF), bf16),
            pltpu.VMEM((FF, D), bf16),
            pltpu.VMEM((rows, D), f32),
            pltpu.VMEM((rows, D), bf16),
            pltpu.VMEM((rows, FF), bf16),
            pltpu.VMEM((rows, D), bf16),
        ],
        compiler_params=params(),
        name="ffn_grad",
    )(e, n2, i2, n1, i1, y, hid, slope, o, vec, *wout, *wffn)


def attend_grad_kernel(
    q_ref, k_ref, kp_ref, v_ref, vp_ref, do_ref, o_ref, lse_ref, ohq_ref, ohk_ref,
    dq_ref, dk_ref, dkp_ref, dv_ref, dvp_ref,
    ka, va, qa, da, kt,
):
    rows = q_ref.shape[0]
    ka[:rows, :LANES] = k_ref[...]
    ka[rows:, :LANES] = kp_ref[...]
    ka[:, LANES:] = ohk_ref[...]
    va[:rows, :LANES] = v_ref[...]
    va[rows:, :LANES] = vp_ref[...]
    va[:, LANES:] = jnp.ones((2 * rows, LANES), bf16)
    kt[...] = ka[:, :LANES].T
    product = do_ref[...].astype(f32) * o_ref[...].astype(f32)
    for i in range(2):
        m = half_mask(i)
        qa[i, :, :LANES] = q_ref[...] * (m * bf16(0.125))
        qa[i, :, LANES:] = lanes_with(
            ohq_ref[...].astype(f32), 120, three_terms(-lse_ref[:, i : i + 1])
        )
        da[i, :, :LANES] = do_ref[...] * m
        delta = jnp.sum(product * half_mask(i, f32), axis=1, keepdims=True)
        da[i, :, LANES:] = lanes_with(jnp.zeros((rows, LANES), f32), 0, three_terms(-delta))

    def tile(t, sums):
        at = pl.ds(pl.multiple_of(t * ROW_TILE, ROW_TILE), ROW_TILE)
        dk = jnp.zeros((ROW_TILE, LANES), f32)
        dv = jnp.zeros((ROW_TILE, LANES), f32)
        new = []
        for i in range(2):
            p = jnp.exp(dot(ka[at], qa[i], 1, 1))
            ds = (p * dot(va[at], da[i], 1, 1)).astype(bf16)
            dv = dv + dot(p.astype(bf16), da[i, :, :LANES])
            dk = dk + dot(ds, qa[i, :, :LANES])
            new.append(sums[i] + dot(kt[:, at], ds))
        return tuple(new), dk.astype(bf16), dv.astype(bf16)

    sums = (jnp.zeros((LANES, rows), f32),) * 2
    half = rows // ROW_TILE

    def own(t, sums):
        sums, dk, dv = tile(t, sums)
        at = pl.ds(t * ROW_TILE, ROW_TILE)
        dk_ref[at] = dk
        dv_ref[at] = dv
        return sums

    def other(t, sums):
        sums, dk, dv = tile(t + half, sums)
        at = pl.ds(t * ROW_TILE, ROW_TILE)
        dkp_ref[at] = dk
        dvp_ref[at] = dv
        return sums

    sums = lax.fori_loop(0, half, own, sums)
    sums = lax.fori_loop(0, half, other, sums)
    row = lax.broadcasted_iota(jnp.int32, (LANES, rows), 0)
    dq_ref[...] = (jnp.where(row < HD, sums[0], sums[1]) * 0.125).T.astype(bf16)


def attend_grad(q, k, kp, v, vp, do, o, lse, ohq, ohk):
    rows = q.shape[0]
    pair = pl.BlockSpec((rows, LANES), lambda h: (0, h))
    other = pl.BlockSpec((rows, LANES), lambda h: (0, h + 1 - 2 * lax.rem(h, 2)))
    return pl.pallas_call(
        attend_grad_kernel,
        grid=(D // LANES,),
        in_specs=[pair, pair, other, pair, other, pair, pair, pair]
        + [
            pl.BlockSpec((rows, LANES), lambda h: (0, 0)),
            pl.BlockSpec((2 * rows, LANES), lambda h: (0, 0)),
        ],
        out_specs=[pair, pair, other, pair, other],
        out_shape=[shape((rows, D), bf16)] * 5,
        scratch_shapes=[
            pltpu.VMEM((2 * rows, 2 * LANES), bf16),
            pltpu.VMEM((2 * rows, 2 * LANES), bf16),
            pltpu.VMEM((2, rows, 2 * LANES), bf16),
            pltpu.VMEM((2, rows, 2 * LANES), bf16),
            pltpu.VMEM((LANES, 2 * rows), bf16),
        ],
        compiler_params=params(),
        name="attend_grad",
    )(q, k, kp, v, vp, do, o, lse, ohq, ohk)


def proj_grad_kernel(
    dq_ref, dk_ref, dv_ref, dkr_ref, dvr_ref, xs_ref, dr1_ref, w0, w1, w2, w3,
    gk_ref, gs_ref, dx_ref, sums_ref, w_s, dk_s, dv_s,
):
    place_qkv(w_s, (w0, w1, w2, w3))
    zero = jnp.zeros((1, D), f32)

    def tile(t, c):
        at = pl.ds(t * ROW_TILE, ROW_TILE)
        dq = dq_ref[at]
        dk = (dk_ref[at].astype(f32) + dkr_ref[at].astype(f32)).astype(bf16)
        dv = (dv_ref[at].astype(f32) + dvr_ref[at].astype(f32)).astype(bf16)
        dk_s[at] = dk
        dv_s[at] = dv
        dx_ref[at] = (
            dr1_ref[at]
            + dot(dq, w_s[:, :D], 1, 1)
            + dot(dk, w_s[:, D : 2 * D], 1, 1)
            + dot(dv, w_s[:, 2 * D :], 1, 1)
        )
        return (c[0] + col_sum(dq.astype(f32)), c[1] + col_sum(dv.astype(f32)))

    dbq, dbv = lax.fori_loop(0, xs_ref.shape[0] // ROW_TILE, tile, (zero, zero))
    sums_ref[0:1, :] = dbq
    sums_ref[1:2, :] = dbv
    sums_ref[2:8, :] = jnp.zeros((6, D), f32)
    for part, ref in enumerate((dq_ref, dk_s, dv_s)):
        grad = dot(xs_ref[...], ref[...], 0, 0).astype(bf16)
        for r in range(4):
            out = gs_ref if r % 2 else gk_ref
            for row in range(4):
                out[r // 2, row * 3 + part] = grad[row * BLK : (row + 1) * BLK, r * BLK : (r + 1) * BLK]


def proj_grad(dq, dk, dv, dkr, dvr, xs, dr1, wqkv):
    rows = xs.shape[0]
    return pl.pallas_call(
        proj_grad_kernel,
        out_shape=[
            shape((2, 12, BLK, BLK), bf16),
            shape((2, 12, BLK, BLK), bf16),
            shape((rows, D)),
            shape((8, D)),
        ],
        scratch_shapes=[
            pltpu.VMEM((D, 3 * D), bf16),
            pltpu.VMEM((rows, D), bf16),
            pltpu.VMEM((rows, D), bf16),
        ],
        compiler_params=params(),
        name="proj_grad",
    )(dq, dk, dv, dkr, dvr, xs, dr1, *wqkv)


def embed_grad_kernel(series_ref, g_ref, we_ref, in_ref, dwe_ref, dbe_ref):
    g = g_ref[...]
    in_ref[...] = dot_hi(g, we_ref[...], 1, 1)
    dwe_ref[...] = dot_hi(series_ref[...].astype(f32), g, 0, 0)
    dbe_ref[...] = col_sum(g)


def embed_grad(series, g, table):
    rows = series.shape[0]
    return pl.pallas_call(
        embed_grad_kernel,
        out_shape=[shape((rows, LOOK)), shape((LOOK, D)), shape((1, D))],
        compiler_params=params(),
        name="embed_grad",
    )(series, g, table[:LOOK])


PARTS = ((0, 12), (12, 4), (16, 32))


def natural_kernel(at_ref, *refs):
    count = len(refs) - 7
    slots, outs, held = refs[:count], refs[count : count + 6], refs[-1]
    step = slots[0].shape[0]
    for i in range(count):
        held[i * step : (i + 1) * step] = slots[i][...]
    for i, out in enumerate(outs):
        layer, part = divmod(i, 3)
        first, n = PARTS[part]
        for j in range(n):
            out[j] = held[at_ref[layer * 48 + first + j]]


def natural_order(at, slots):
    total = sum(s.shape[0] for s in slots)
    spec = pl.BlockSpec(memory_space=pltpu.VMEM)
    return pl.pallas_call(
        natural_kernel,
        in_specs=[pl.BlockSpec(memory_space=pltpu.SMEM)] + [spec] * len(slots),
        out_shape=[shape((n, BLK, BLK), bf16) for _ in range(LAYERS) for _, n in PARTS],
        scratch_shapes=[pltpu.VMEM((total, BLK, BLK), bf16)],
        compiler_params=params(),
        name="natural",
    )(at, *slots)


def routed_kernel(at_ref, tab_ref, tabr_ref, *refs):
    own, got, out = refs[:6], refs[6:12], refs[12]
    count, span = out.shape[0], out.shape[1]
    share = BLK // count
    out[...] = jnp.zeros(out.shape, bf16)
    for i in range(6):
        layer, part = divmod(i, 3)
        first, n = PARTS[part]
        for j in range(n):
            place = at_ref[layer * 48 + first + j]
            who = at_ref[96 + layer * 48 + first + j]
            value = own[i][j].astype(f32) + got[i][j].astype(f32)
            out[who, pl.ds(pl.multiple_of(place * BLK, BLK), BLK), :] = value.astype(bf16)
    table = (tab_ref[...].astype(f32) + tabr_ref[...].astype(f32)).astype(bf16)
    for d in range(count):
        who = at_ref[192 + d]
        out[who, span - share : span, :] = table[d * share : (d + 1) * share]


def routed(at, table, table_got, own, got, count, slots_each):
    spec = pl.BlockSpec(memory_space=pltpu.VMEM)
    return pl.pallas_call(
        routed_kernel,
        in_specs=[pl.BlockSpec(memory_space=pltpu.SMEM)] + [spec] * 14,
        out_shape=shape((count, slots_each * BLK + BLK // count, BLK), bf16),
        compiler_params=params(),
        name="routed",
    )(at, table, table_got, *own, *got)


def routed_plain_kernel(at_ref, *refs):
    own, got, out = refs[:6], refs[6:12], refs[12]
    out[...] = jnp.zeros(out.shape, bf16)
    for i in range(6):
        layer, part = divmod(i, 3)
        first, n = PARTS[part]
        for j in range(n):
            place = at_ref[layer * 48 + first + j]
            who = at_ref[96 + layer * 48 + first + j]
            value = own[i][j].astype(f32) + got[i][j].astype(f32)
            out[who, pl.ds(pl.multiple_of(place * BLK, BLK), BLK), :] = value.astype(bf16)


def routed_plain(at, own, got, count, slots_each):
    spec = pl.BlockSpec(memory_space=pltpu.VMEM)
    return pl.pallas_call(
        routed_plain_kernel,
        in_specs=[pl.BlockSpec(memory_space=pltpu.SMEM)] + [spec] * 12,
        out_shape=shape((count, slots_each * BLK, BLK), bf16),
        compiler_params=params(),
        name="routed",
    )(at, *own, *got)


def ring_of(count):
    half = count // 2
    return [2 * i for i in range(half)] + [2 * (half - 1 - i) + 1 for i in range(half)]


def ring_shift(value, order, by):
    n = len(order)
    return lax.ppermute(value, "dp", [(order[i], order[(i + by) % n]) for i in range(n)])


def ring_gather(value, order):
    n = len(order)
    held = [value] + [None] * (n - 1)
    ahead = behind = value
    for step in range(1, n // 2 + 1):
        behind = ring_shift(behind, order, 1)
        held[n - step] = behind
        if step < n // 2:
            ahead = ring_shift(ahead, order, -1)
            held[step] = ahead
    return held


def ring_reduce(pieces, order):
    n = len(order)
    up = pieces[n // 2]
    down = pieces[n // 2 + 1]
    for step in range(1, n // 2 + 1):
        up = ring_shift(up, order, 1)
        if step < n // 2:
            up = add_low(up, pieces[n // 2 - step])
            down = ring_shift(down, order, -1)
            if step < n // 2 - 1:
                down = add_low(down, pieces[n // 2 + 1 + step])
    return pieces[0], up, down


def add_low(a, b):
    return (a.astype(f32) + b.astype(f32)).astype(bf16)


def core_swap(value):
    return lax.ppermute(value, "head", [(i, i ^ 1) for i in range(4)])


def far_swap(value):
    return lax.ppermute(value, "head", [(i, i ^ 2) for i in range(4)])


def one_hots(ids):
    lane = jnp.arange(LANES, dtype=jnp.int32)[None, :]
    same = ids[:, None] == lane
    return jnp.where(same, -BIG, 0.0).astype(bf16), jnp.where(same, 0.0, 1.0).astype(bf16)


def relative(row, place):
    pieces = row.reshape(4, -1)
    return jnp.take(pieces, jnp.arange(4) ^ place, axis=0).reshape(1, -1)


def on_device(
    series,
    cotangent,
    window_lengths,
    owner_list,
    master,
    first_moment,
    second_moment,
    left_stats,
    right_stats,
    left_basis,
    right_basis,
    vec_values,
    vec_first,
    vec_second,
):
    place = lax.axis_index("head")
    spot = lax.axis_index("dp")
    dp = lax.axis_size("dp")
    ringed = dp == 8
    rows = series.shape[0]
    own_slots = master.shape[1]
    buckets, win = window_lengths.shape
    bucket_rows = rows * 4 // buckets
    owner_row = owner_list[0]
    who = owner_row // own_slots
    if ringed:
        order = ring_of(dp)
        ring_at = jnp.asarray([order.index(d) for d in range(dp)], jnp.int32)
        who = (ring_at[who] - ring_at[spot]) % dp
    inner = owner_row % own_slots
    gather_at = who * own_slots + inner

    copies = master[0].astype(bf16)
    if ringed:
        slots = ring_gather(copies, order)
    else:
        slots = [lax.all_gather(copies, "dp", axis=0, tiled=True)]
    mine = natural_order(gather_at, slots)
    weights = []
    for own in mine:
        far = far_swap(own)
        weights.append([own, core_swap(own), far, core_swap(far)])

    windows = window_ids(window_lengths, bucket_rows)
    ids = windows.reshape(4, rows)
    own_ids = lax.dynamic_index_in_dim(ids, place, 0, False)
    pair_ids = lax.dynamic_index_in_dim(ids, place ^ 1, 0, False)
    ohq, ohk_own = one_hots(own_ids)
    ohk = jnp.concatenate([ohk_own, one_hots(pair_ids)[1]], axis=0)
    valid = (own_ids < win).astype(f32)[:, None]

    x = embed(series, vec_values)
    saved = []
    for layer in range(LAYERS):
        bq, bv, bo, g1, c1, b1, b2, g2, c2 = depth_vectors(vec_values, layer)
        wqkv, wout, wffn = weights[3 * layer : 3 * layer + 3]
        xs, q, k, v = project(x, relative(bq, place), relative(bv, place), wqkv)
        kp, vp = core_swap(k), core_swap(v)
        o, lse = attend(q, k, kp, v, vp, ohq, ohk)
        vec = jnp.stack([bo, g1, c1, b2, g2, c2, g2, c2])
        n1, i1, y, hid, slope, n2, i2, x = post(o, x, vec, relative(b1, place), wout, wffn)
        saved.append((xs, q, k, v, kp, vp, o, lse, vec, n1, i1, y, hid, slope, n2, i2))
    activations = x * valid
    grad = cotangent * valid

    own_sums = [None] * (3 * LAYERS)
    far_sums = [None] * (3 * LAYERS)
    table_rows = [None] * LAYERS

    def reduce_head(at, keep, send):
        got = core_swap(send)
        own_sums[at] = add_low(keep[0], got[0])
        far_sums[at] = far_swap(add_low(keep[1], got[1]))

    for layer in reversed(range(LAYERS)):
        xs, q, k, v, kp, vp, o, lse, vec, n1, i1, y, hid, slope, n2, i2 = saved[layer]
        wqkv, wout, wffn = weights[3 * layer : 3 * layer + 3]
        gk, gs, ok, os, dr1, do, db1, sums = ffn_grad(
            grad, n2, i2, n1, i1, y, hid, slope, o, vec, wout, wffn
        )
        reduce_head(3 * layer + 2, gk, gs)
        reduce_head(3 * layer + 1, ok, os)
        dq, dk, dkp, dv, dvp = attend_grad(q, k, kp, v, vp, do, o, lse, ohq, ohk)
        dkr, dvr = core_swap(dkp), core_swap(dvp)
        pk, ps, grad, qsums = proj_grad(dq, dk, dv, dkr, dvr, xs, dr1, wqkv)
        reduce_head(3 * layer, pk, ps)
        table_rows[layer] = jnp.concatenate(
            [
                relative(qsums[0], place),
                relative(qsums[1], place),
                sums[0:3],
                relative(db1, place).reshape(FF // D, D),
                sums[3:6],
            ],
            axis=0,
        )
    input_grad, dwe, dbe = embed_grad(series, grad, vec_values)
    local_table = jnp.concatenate([dwe, dbe] + table_rows, axis=0)
    vrows = local_table.shape[0]
    padded = jnp.pad(local_table, ((0, BLK - vrows), (0, 0)))
    parts = jnp.take(padded.reshape(4, BLK, BLK), jnp.arange(4) ^ place, axis=0).astype(bf16)
    got = core_swap(parts[1::2])
    tab_own = add_low(parts[0], got[0])
    tab_far = far_swap(add_low(parts[2], got[1]))
    share = BLK // dp
    if ringed:
        dist = (jnp.asarray(ring_at) - ring_at[spot]) % dp
        at = jnp.concatenate([inner, who, dist]).astype(jnp.int32)
        pieces = routed(at, tab_own, tab_far, own_sums, far_sums, dp, own_slots)
        terms = ring_reduce([pieces[i] for i in range(dp)], order)
        grads = [t[: own_slots * BLK].reshape(own_slots, BLK, BLK) for t in terms]
        part = sum(t[own_slots * BLK :].astype(f32) for t in terms)
    else:
        at = jnp.concatenate([inner, who, jnp.arange(dp)]).astype(jnp.int32)
        pieces = routed_plain(at, own_sums, far_sums, dp, own_slots)
        whole = lax.psum_scatter(pieces, "dp", scatter_dimension=0, tiled=True)
        grads = [whole.reshape(own_slots, BLK, BLK)]
        part = lax.psum_scatter(
            tab_own.astype(f32) + tab_far.astype(f32), "dp", scatter_dimension=0, tiled=True
        )
    shares = lax.all_gather(part, ("head", "dp"), axis=0, tiled=True)
    grad_table = shares.reshape(4, BLK, BLK).reshape(BLK, D)[:vrows]
    new_master, new_copy, new_first, new_second, new_left, new_right, left_next, right_next = soap(
        grads,
        master[0],
        first_moment[0],
        second_moment[0],
        left_stats[0],
        right_stats[0],
        left_basis[0],
        right_basis[0],
    )
    vec_new_values, vec_new_first, vec_new_second = adamw_update(
        grad_table, vec_values, vec_first, vec_second
    )
    branch_bias_grads = branch_biases(grad_table)
    return (
        activations,
        input_grad,
        new_master[None],
        new_copy[None],
        new_first[None],
        new_second[None],
        new_left[None],
        new_right[None],
        left_next[None],
        right_next[None],
        vec_new_values,
        vec_new_first,
        vec_new_second,
        branch_bias_grads,
    )


def solution(mesh):
    placed = (
        P(("dp", "head"), None),
        P(("dp", "head"), None),
        P("dp", None),
        P("head", None),
        P("head", "dp", None, None),
        P("head", "dp", None, None),
        P("head", "dp", None, None),
        P("head", "dp", None, None),
        P("head", "dp", None, None),
        P("head", "dp", None, None),
        P("head", "dp", None, None),
        P(),
        P(),
        P(),
    )
    return jax.shard_map(
        on_device,
        mesh=mesh,
        in_specs=placed,
        out_specs=(
            P(("dp", "head"), None),
            P(("dp", "head"), None),
            P("head", "dp", None, None),
            P("head", "dp", None, None),
            P("head", "dp", None, None),
            P("head", "dp", None, None),
            P("head", "dp", None, None),
            P("head", "dp", None, None),
            P("head", "dp", None, None),
            P("head", "dp", None, None),
            P(),
            P(),
            P(),
            P(),
        ),
        check_vma=False,
    )
```

```python
import functools

import jax
import jax.numpy as jnp
from jax import lax
from jax.experimental import pallas as pl
from jax.experimental.pallas import tpu as pltpu
from jax.sharding import PartitionSpec as P

D = 512
HEADS = 8
HD = 64
FF = 2048
LOOK = 96
LAYERS = 2
BLK = 128
STEP = 10

f32 = jnp.float32
HI = lax.Precision.HIGHEST
norm_eps = 1e-05
beta_first = 0.5
beta_second = 0.5
beta_stats = 0.5
adam_eps = 1e-08
rate_matrix = 0.02
rate_vector = 0.15
weight_decay = 0.01


def window_ids(lengths, bucket_rows):
    bounds = jnp.cumsum(lengths, axis=1, dtype=jnp.int32)
    places = jnp.arange(bucket_rows, dtype=jnp.int32)
    return jnp.sum(
        (places[None, :, None] >= bounds[:, None, :]).astype(jnp.int32), axis=2, dtype=jnp.int32
    )


def depth_vectors(vec_table, layer_at):
    ff_ratio = FF // D
    base_row = LOOK + 1 + layer_at * (8 + ff_ratio)
    return (
        vec_table[base_row],
        vec_table[base_row + 1],
        vec_table[base_row + 2],
        vec_table[base_row + 3],
        vec_table[base_row + 4],
        vec_table[base_row + 5 : base_row + 5 + ff_ratio].reshape(FF),
        vec_table[base_row + 5 + ff_ratio],
        vec_table[base_row + 6 + ff_ratio],
        vec_table[base_row + 7 + ff_ratio],
    )


def adamw_update(gradient, values, moment_one, moment_two):
    new_first = beta_first * moment_one + (1.0 - beta_first) * gradient
    new_second = beta_second * moment_two + (1.0 - beta_second) * gradient * gradient
    step_ratio = (
        new_first
        / (1.0 - beta_first**STEP)
        / (jnp.sqrt(new_second / (1.0 - beta_second**STEP)) + adam_eps)
    )
    new_values = values - rate_vector * (step_ratio + weight_decay * values)
    return (new_values, new_first, new_second)


def branch_biases(grad_table):
    ff_ratio = FF // D
    bias_rows = []
    for layer_at in range(LAYERS):
        base_row = LOOK + 1 + layer_at * (8 + ff_ratio)
        bias_rows.append(grad_table[base_row + 2])
        bias_rows.append(grad_table[base_row + 5 + ff_ratio])
    return jnp.stack(bias_rows, axis=0)


def dot_hi(a,b,ca,cb):
    return lax.dot_general(a,b,(((ca,),(cb,)),((),())),precision=HI,preferred_element_type=f32)
PANEL=32
def qr_batch(a_ref, count):
    lane = lax.broadcasted_iota(jnp.int32,(1,1,BLK),2)
    sub8 = lax.broadcasted_iota(jnp.int32,(1,8,1),1)
    sub32 = lax.broadcasted_iota(jnp.int32,(1,PANEL,1),1)
    def panel(sp, carry):
        r0 = pl.multiple_of(sp*PANEL, PANEL)
        block = a_ref[:, pl.ds(r0,PANEL), :]
        block = pltpu.roll(block.reshape(count*PANEL,BLK), lax.rem(BLK - r0, BLK), 1).reshape(count,PANEL,BLK)
        tiles = [block[:, 8*t:8*t+8, :] for t in range(PANEL//8)]
        for k in range(PANEL):
            t0, s = divmod(k,8)
            row = tiles[t0][:, s:s+1, :]
            inv = 1.0/row[:, :, k:k+1]
            pn = (row + (lane==k).astype(f32))*inv
            for t in range(t0,PANEL//8):
                c = tiles[t][:, :, k:k+1]
                if t==t0:
                    if s==7: continue
                    c = jnp.where(sub8 > s, c, 0.0)
                tiles[t] = tiles[t] - c*pn
        done = jnp.concatenate(tiles, axis=1)
        diag = lane==sub32
        piv = jnp.sum(jnp.where(diag, done, 0.0), axis=2, keepdims=True)
        done = jnp.where(diag, 1.0, jnp.where((lane > sub32) & (lane < PANEL), 0.0, done))
        done = pltpu.roll(done.reshape(count*PANEL,BLK), r0, 1).reshape(count,PANEL,BLK)
        scale = lax.rsqrt(piv)
        done = done*scale
        a_ref[:, pl.ds(r0,PANEL), :] = done
        @pl.when(sp < BLK//PANEL-1)
        def _():
            lane2 = lax.broadcasted_iota(jnp.int32,(BLK,BLK),1)
            row2 = lax.broadcasted_iota(jnp.int32,(BLK,BLK),0)
            clear = (row2 >= r0+PANEL) & (lane2 >= r0) & (lane2 < r0+PANEL)
            lanep = lax.broadcasted_iota(jnp.int32,(PANEL,BLK),1)
            for b in range(count):
                z = a_ref[b, pl.ds(r0,PANEL), :]
                zm = jnp.where(lanep >= r0+PANEL, z, 0.0)
                upd = dot_hi(zm, z, 0, 0)
                a_ref[b] = jnp.where(clear, 0.0, a_ref[b]) - upd
        return carry
    lax.fori_loop(0, BLK//PANEL, panel, 0)

def soap_kernel(count, *refs):
    g = sum(ref[0].astype(f32) for ref in refs[:count])
    soap_body(g, *refs[count:])


def soap_body(g, mas_ref, m1_ref, m2_ref, ls_ref, rs_ref, lb_ref, rb_ref,
                nm_ref, nc_ref, n1_ref, n2_ref, nl_ref, nr_ref, ql_ref, qr_ref, mat_ref, a_ref):
    n = pl.num_programs(0); i = pl.program_id(0)
    lb = lb_ref[0]; rb = rb_ref[0]
    rot = dot_hi(dot_hi(lb,g,0,0), rb, 1, 0)
    n1 = 0.5*m1_ref[0]+0.5*rot
    n2 = 0.5*m2_ref[0]+0.5*rot*rot
    n1_ref[0]=n1; n2_ref[0]=n2
    corr = 1.0-0.5**STEP
    ratio = n1/corr/(jnp.sqrt(n2/corr)+1e-8)
    upd = dot_hi(dot_hi(lb,ratio,1,0), rb, 1, 1)
    mas = mas_ref[0]
    nm = mas - 0.02*(upd+0.01*mas)
    nm_ref[0]=nm; nc_ref[0]=nm.astype(jnp.bfloat16)
    nl = 0.5*ls_ref[0]+0.5*dot_hi(g,g,1,1)
    nr = 0.5*rs_ref[0]+0.5*dot_hi(g,g,0,0)
    nl_ref[0]=nl; nr_ref[0]=nr
    for side,(st,ba) in enumerate(((nl,lb),(nr,rb))):
        m = dot_hi(st,ba,1,0)
        m = m*lax.rsqrt(jnp.sum(m*m,axis=0,keepdims=True))
        mat_ref[2*i+side] = m
        a_ref[2*i+side] = dot_hi(m,m,0,0)
    @pl.when(i==n-1)
    def _():
        count = a_ref.shape[0]
        qr_batch(a_ref, count)
        keep = lax.broadcasted_iota(jnp.int32,(BLK,BLK),1) <= lax.broadcasted_iota(jnp.int32,(BLK,BLK),0)
        def fin(j, c):
            for side,ref in enumerate((ql_ref,qr_ref)):
                x = jnp.where(keep, a_ref[2*j+side], 0.0)
                ref[j] = dot_hi(mat_ref[2*j+side], x, 1, 1)
            return c
        lax.fori_loop(0, n, fin, 0)

def soap(gs, master, m1, m2, ls, rs, lb, rb):
    n = master.shape[0]
    one = pl.BlockSpec((1,BLK,BLK), lambda i:(i,0,0))
    whole = pl.BlockSpec((n,BLK,BLK), lambda i:(0,0,0))
    sh = jax.ShapeDtypeStruct((n,BLK,BLK), f32)
    shb = jax.ShapeDtypeStruct((n,BLK,BLK), jnp.bfloat16)
    return pl.pallas_call(functools.partial(soap_kernel, len(gs)), grid=(n,), in_specs=[one]*(len(gs)+7),
        out_specs=[one]*6+[whole]*2, out_shape=[sh,shb,sh,sh,sh,sh,sh,sh],
        scratch_shapes=[pltpu.VMEM((2*n,BLK,BLK),f32)]*2,
        compiler_params=pltpu.CompilerParams(vmem_limit_bytes=50*2**20), name="soap", cost_estimate=pl.CostEstimate(flops=60*10**9, bytes_accessed=0, transcendentals=0))(*gs,master,m1,m2,ls,rs,lb,rb)


bf16 = jnp.bfloat16
LANES = 128
ROW_TILE = 256
BIG = 1e30
CORR = 1.0 - 0.5**STEP


def params(mib=48):
    return pltpu.CompilerParams(vmem_limit_bytes=mib * 2**20)


def cost(micros):
    return pl.CostEstimate(flops=int(micros * 1e9), bytes_accessed=0, transcendentals=0)


def shape(dims, kind=f32):
    return jax.ShapeDtypeStruct(dims, kind)


def dot(a, b, ca=1, cb=0):
    return lax.dot_general(a, b, (((ca,), (cb,)), ((), ())), preferred_element_type=f32)


def place_blocks(dst, refs, first, rows, cols, row_step, col_step, col_base=0):
    for r, ref in enumerate(refs):
        for j in range(rows * cols):
            row, col = divmod(j, cols)
            r0 = r * row_step + row * BLK
            c0 = col_base + r * col_step + col * BLK
            dst[r0 : r0 + BLK, c0 : c0 + BLK] = ref[first + j]


def place_qkv(dst, refs):
    for r, ref in enumerate(refs):
        for j in range(12):
            row, col = divmod(j, 3)
            c0 = col * D + r * BLK
            dst[row * BLK : (row + 1) * BLK, c0 : c0 + BLK] = ref[j]


def layer_norm(resid):
    center = resid - jnp.mean(resid, axis=1, keepdims=True)
    inv = lax.rsqrt(jnp.mean(center * center, axis=1, keepdims=True) + norm_eps)
    return center * inv, inv


def layer_norm_grad(grad, unit, inv, gain):
    dn = grad * gain
    return inv * (
        dn
        - jnp.mean(dn, axis=1, keepdims=True)
        - unit * jnp.mean(dn * unit, axis=1, keepdims=True)
    )


def col_sum(values):
    return jnp.sum(values, axis=0, keepdims=True)


def embed_kernel(series_ref, we_ref, be_ref, x_ref):
    x_ref[...] = dot_hi(series_ref[...].astype(f32), we_ref[...], 1, 0) + be_ref[...]


def embed(series, table):
    rows = series.shape[0]
    return pl.pallas_call(
        embed_kernel, out_shape=shape((rows, D)), compiler_params=params(), name="embed"
    )(series, table[:LOOK], table[LOOK : LOOK + 1])


def proj_kernel(x_ref, bq_ref, bv_ref, w0, w1, w2, w3, xs_ref, q_ref, k_ref, v_ref, w_s):
    place_qkv(w_s, (w0, w1, w2, w3))

    def tile(t, c):
        at = pl.ds(t * ROW_TILE, ROW_TILE)
        xs = x_ref[at].astype(bf16)
        xs_ref[at] = xs
        q_ref[at] = (dot(xs, w_s[:, :D]) + bq_ref[...]).astype(bf16)
        k_ref[at] = dot(xs, w_s[:, D : 2 * D]).astype(bf16)
        v_ref[at] = (dot(xs, w_s[:, 2 * D :]) + bv_ref[...]).astype(bf16)
        return c

    lax.fori_loop(0, x_ref.shape[0] // ROW_TILE, tile, 0)


def project(x, bq, bv, wqkv):
    rows = x.shape[0]
    return pl.pallas_call(
        proj_kernel,
        out_shape=[shape((rows, D), bf16)] * 4,
        scratch_shapes=[pltpu.VMEM((D, 3 * D), bf16)],
        compiler_params=params(),
        name="project",
        cost_estimate=cost(3),
    )(x, bq, bv, *wqkv)


def half_mask(i, kind=bf16):
    lane = lax.broadcasted_iota(jnp.int32, (1, LANES), 1)
    return ((lane >= HD * i) & (lane < HD * (i + 1))).astype(f32).astype(kind)


def three_terms(col):
    first = col.astype(bf16).astype(f32)
    second = (col - first).astype(bf16).astype(f32)
    return first, second, col - first - second


def lanes_with(base, at, cols):
    lane = lax.broadcasted_iota(jnp.int32, base.shape, 1)
    for i, col in enumerate(cols):
        base = jnp.where(lane == at + i, col, base)
    return base.astype(bf16)


def attend_kernel(q_ref, k_ref, kp_ref, v_ref, vp_ref, ohq_ref, ohk_ref, o_ref, lse_ref, ka, va):
    rows = q_ref.shape[0]
    ka[:rows, :LANES] = k_ref[...]
    ka[rows:, :LANES] = kp_ref[...]
    ka[:, LANES:] = ohk_ref[...]
    lane = lax.broadcasted_iota(jnp.int32, (ROW_TILE, LANES), 1)
    for i in range(2):
        m = half_mask(i)
        va[i, :rows, :LANES] = v_ref[...] * m
        va[i, rows:, :LANES] = vp_ref[...] * m
        va[i, :, LANES:] = jnp.ones((2 * rows, LANES), bf16)

    def tile(t, c):
        at = pl.ds(t * ROW_TILE, ROW_TILE)
        total = jnp.zeros((ROW_TILE, LANES), f32)
        stat = jnp.zeros((ROW_TILE, LANES), f32)
        for i in range(2):
            qa = jnp.concatenate([q_ref[at] * (half_mask(i) * bf16(0.125)), ohq_ref[at]], axis=1)
            s = dot(qa, ka[...], 1, 1)
            high = jnp.max(s, axis=1, keepdims=True)
            e = jnp.exp(s - high).astype(bf16)
            out = dot(e, va[i])
            norm = out[:, LANES:]
            total = total + out[:, :LANES] / norm
            stat = jnp.where(lane == i, high + jnp.log(norm), stat)
        o_ref[at] = total.astype(bf16)
        lse_ref[at] = stat
        return c

    lax.fori_loop(0, rows // ROW_TILE, tile, 0)


def attend(q, k, kp, v, vp, ohq, ohk):
    rows = q.shape[0]
    pair = pl.BlockSpec((rows, LANES), lambda h: (0, h))
    other = pl.BlockSpec((rows, LANES), lambda h: (0, h + 1 - 2 * lax.rem(h, 2)))
    return pl.pallas_call(
        attend_kernel,
        grid=(D // LANES,),
        in_specs=[pair, pair, other, pair, other]
        + [
            pl.BlockSpec((rows, LANES), lambda h: (0, 0)),
            pl.BlockSpec((2 * rows, LANES), lambda h: (0, 0)),
        ],
        out_specs=[pair, pair],
        out_shape=[shape((rows, D), bf16), shape((rows, D))],
        scratch_shapes=[
            pltpu.VMEM((2 * rows, 2 * LANES), bf16),
            pltpu.VMEM((2, 2 * rows, 2 * LANES), bf16),
        ],
        compiler_params=params(),
        name="attend",
        cost_estimate=cost(11),
    )(q, k, kp, v, vp, ohq, ohk)


def post_kernel(
    o_ref, x_ref, vec_ref, b1_ref, a0, a1, a2, a3, f0, f1, f2, f3,
    n1_ref, i1_ref, y_ref, hid_ref, slope_ref, n2_ref, i2_ref, x2_ref,
    wo_s, w1_s, w2_s,
):
    place_blocks(wo_s, (a0, a1, a2, a3), 0, 1, 4, BLK, 0)
    place_blocks(w1_s, (f0, f1, f2, f3), 0, 4, 4, 0, D)
    place_blocks(w2_s, (f0, f1, f2, f3), 16, 4, 4, D, 0)

    def tile(t, c):
        at = pl.ds(t * ROW_TILE, ROW_TILE)
        vec = [vec_ref[i : i + 1, :] for i in range(6)]
        unit, inv = layer_norm(x_ref[at] + dot(o_ref[at], wo_s[...]) + vec[0])
        n1_ref[at] = unit
        i1_ref[at] = jnp.broadcast_to(inv, (ROW_TILE, LANES))
        y = unit * vec[1] + vec[2]
        yb = y.astype(bf16)
        y_ref[at] = yb
        fed = jnp.zeros((ROW_TILE, D), f32)
        for r in range(FF // D):
            cols = slice(r * D, (r + 1) * D)
            pre = dot(yb, w1_s[:, cols]) + b1_ref[:, cols]
            phi = 0.5 * (1.0 + lax.erf(pre * (0.5**0.5)))
            hid = (pre * phi).astype(bf16)
            hid_ref[at, cols] = hid
            slope_ref[at, cols] = (
                phi + pre * (jnp.exp(-0.5 * pre * pre) * 0.3989422804014327)
            ).astype(bf16)
            fed = fed + dot(hid, w2_s[cols, :])
        unit, inv = layer_norm(y + fed + vec[3])
        n2_ref[at] = unit
        i2_ref[at] = jnp.broadcast_to(inv, (ROW_TILE, LANES))
        x2_ref[at] = unit * vec[4] + vec[5]
        return c

    lax.fori_loop(0, x_ref.shape[0] // ROW_TILE, tile, 0)


def post(o, x, vec, b1, wout, wffn):
    rows = x.shape[0]
    return pl.pallas_call(
        post_kernel,
        out_shape=[
            shape((rows, D)),
            shape((rows, LANES)),
            shape((rows, D), bf16),
            shape((rows, FF), bf16),
            shape((rows, FF), bf16),
            shape((rows, D)),
            shape((rows, LANES)),
            shape((rows, D)),
        ],
        scratch_shapes=[
            pltpu.VMEM((D, D), bf16),
            pltpu.VMEM((D, FF), bf16),
            pltpu.VMEM((FF, D), bf16),
        ],
        compiler_params=params(),
        name="post",
        cost_estimate=cost(11),
    )(o, x, vec, b1, *wout, *wffn)


def store_blocks(refs, r, first, rows, cols, value):
    keep_ref, send_ref = refs
    ref = send_ref if r % 2 else keep_ref
    for j in range(rows * cols):
        row, col = divmod(j, cols)
        ref[r // 2, first + j] = value[row * BLK : (row + 1) * BLK, col * BLK : (col + 1) * BLK]


def ffn_grad_kernel(
    e_ref, n2_ref, i2_ref, n1_ref, i1_ref, y_ref, hid_ref, slope_ref, o_ref, vec_ref,
    a0, a1, a2, a3, f0, f1, f2, f3,
    gk_ref, gs_ref, ok_ref, os_ref, dr1_ref, do_ref, db1_ref, sums_ref,
    wo_s, w1_s, w2_s, dr2_s, dfr_s, dpre_s, dar_s,
):
    rows = e_ref.shape[0]
    place_blocks(wo_s, (a0, a1, a2, a3), 0, 1, 4, BLK, 0)
    place_blocks(w1_s, (f0, f1, f2, f3), 0, 4, 4, 0, D)
    place_blocks(w2_s, (f0, f1, f2, f3), 16, 4, 4, D, 0)
    tiles = rows // ROW_TILE
    gain_two = vec_ref[4:5, :]
    gain_one = vec_ref[1:2, :]
    zero = jnp.zeros((1, D), f32)

    def tile_two(t, c):
        at = pl.ds(t * ROW_TILE, ROW_TILE)
        grad = e_ref[at]
        unit = n2_ref[at]
        dr2 = layer_norm_grad(grad, unit, i2_ref[at, 0:1], gain_two)
        dr2_s[at] = dr2
        dfr_s[at] = dr2.astype(bf16)
        return (c[0] + col_sum(dr2), c[1] + col_sum(grad * unit), c[2] + col_sum(grad))

    db2, dg2, dc2 = lax.fori_loop(0, tiles, tile_two, (zero, zero, zero))

    for r in range(FF // D):
        cols = slice(r * D, (r + 1) * D)

        def tile_up(t, c):
            at = pl.ds(t * ROW_TILE, ROW_TILE)
            dh = dot(dfr_s[at], w2_s[cols, :], 1, 1)
            dpre = (dh * slope_ref[at, cols].astype(f32)).astype(bf16)
            dpre_s[at, cols] = dpre
            dr2_s[at] = dr2_s[at] + dot(dpre, w1_s[:, cols], 1, 1)
            return c + col_sum(dpre.astype(f32))

        db1_ref[r : r + 1, :] = lax.fori_loop(0, tiles, tile_up, zero)
        store_blocks((gk_ref, gs_ref), r, 16, 4, 4, dot(hid_ref[:, cols], dfr_s[...], 0, 0).astype(bf16))
        store_blocks((gk_ref, gs_ref), r, 0, 4, 4, dot(y_ref[...], dpre_s[:, cols], 0, 0).astype(bf16))

    def tile_one(t, c):
        at = pl.ds(t * ROW_TILE, ROW_TILE)
        grad = dr2_s[at]
        unit = n1_ref[at]
        dr1 = layer_norm_grad(grad, unit, i1_ref[at, 0:1], gain_one)
        dr1_ref[at] = dr1
        dar = dr1.astype(bf16)
        dar_s[at] = dar
        do_ref[at] = dot(dar, wo_s[...], 1, 1).astype(bf16)
        return (c[0] + col_sum(dr1), c[1] + col_sum(grad * unit), c[2] + col_sum(grad))

    dbo, dg1, dc1 = lax.fori_loop(0, tiles, tile_one, (zero, zero, zero))
    dwo = dot(o_ref[...], dar_s[...], 0, 0).astype(bf16)
    for r in range(4):
        store_blocks((ok_ref, os_ref), r, 0, 1, 4, dwo[r * BLK : (r + 1) * BLK])
    for i, value in enumerate((dbo, dg1, dc1, db2, dg2, dc2, zero, zero)):
        sums_ref[i : i + 1, :] = value


def ffn_grad(e, n2, i2, n1, i1, y, hid, slope, o, vec, wout, wffn):
    rows = e.shape[0]
    return pl.pallas_call(
        ffn_grad_kernel,
        out_shape=[
            shape((2, 32, BLK, BLK), bf16),
            shape((2, 32, BLK, BLK), bf16),
            shape((2, 4, BLK, BLK), bf16),
            shape((2, 4, BLK, BLK), bf16),
            shape((rows, D)),
            shape((rows, D), bf16),
            shape((FF // D, D)),
            shape((8, D)),
        ],
        scratch_shapes=[
            pltpu.VMEM((D, D), bf16),
            pltpu.VMEM((D, FF), bf16),
            pltpu.VMEM((FF, D), bf16),
            pltpu.VMEM((rows, D), f32),
            pltpu.VMEM((rows, D), bf16),
            pltpu.VMEM((rows, FF), bf16),
            pltpu.VMEM((rows, D), bf16),
        ],
        compiler_params=params(),
        name="ffn_grad",
        cost_estimate=cost(16),
    )(e, n2, i2, n1, i1, y, hid, slope, o, vec, *wout, *wffn)


def attend_grad_kernel(
    q_ref, k_ref, kp_ref, v_ref, vp_ref, do_ref, o_ref, lse_ref, ohq_ref, ohk_ref,
    dq_ref, dk_ref, dkp_ref, dv_ref, dvp_ref,
    ka, va, qa, da, kt,
):
    rows = q_ref.shape[0]
    ka[:rows, :LANES] = k_ref[...]
    ka[rows:, :LANES] = kp_ref[...]
    ka[:, LANES:] = ohk_ref[...]
    va[:rows, :LANES] = v_ref[...]
    va[rows:, :LANES] = vp_ref[...]
    va[:, LANES:] = jnp.ones((2 * rows, LANES), bf16)
    kt[...] = ka[:, :LANES].T
    product = do_ref[...].astype(f32) * o_ref[...].astype(f32)
    for i in range(2):
        m = half_mask(i)
        qa[i, :, :LANES] = q_ref[...] * (m * bf16(0.125))
        qa[i, :, LANES:] = lanes_with(
            ohq_ref[...].astype(f32), 120, three_terms(-lse_ref[:, i : i + 1])
        )
        da[i, :, :LANES] = do_ref[...] * m
        delta = jnp.sum(product * half_mask(i, f32), axis=1, keepdims=True)
        da[i, :, LANES:] = lanes_with(jnp.zeros((rows, LANES), f32), 0, three_terms(-delta))

    def tile(t, sums):
        at = pl.ds(pl.multiple_of(t * ROW_TILE, ROW_TILE), ROW_TILE)
        dk = jnp.zeros((ROW_TILE, LANES), f32)
        dv = jnp.zeros((ROW_TILE, LANES), f32)
        new = []
        for i in range(2):
            p = jnp.exp(dot(ka[at], qa[i], 1, 1))
            ds = (p * dot(va[at], da[i], 1, 1)).astype(bf16)
            dv = dv + dot(p.astype(bf16), da[i, :, :LANES])
            dk = dk + dot(ds, qa[i, :, :LANES])
            new.append(sums[i] + dot(kt[:, at], ds))
        return tuple(new), dk.astype(bf16), dv.astype(bf16)

    sums = (jnp.zeros((LANES, rows), f32),) * 2
    half = rows // ROW_TILE

    def own(t, sums):
        sums, dk, dv = tile(t, sums)
        at = pl.ds(t * ROW_TILE, ROW_TILE)
        dk_ref[at] = dk
        dv_ref[at] = dv
        return sums

    def other(t, sums):
        sums, dk, dv = tile(t + half, sums)
        at = pl.ds(t * ROW_TILE, ROW_TILE)
        dkp_ref[at] = dk
        dvp_ref[at] = dv
        return sums

    sums = lax.fori_loop(0, half, own, sums)
    sums = lax.fori_loop(0, half, other, sums)
    row = lax.broadcasted_iota(jnp.int32, (LANES, rows), 0)
    dq_ref[...] = (jnp.where(row < HD, sums[0], sums[1]) * 0.125).T.astype(bf16)


def attend_grad(q, k, kp, v, vp, do, o, lse, ohq, ohk):
    rows = q.shape[0]
    pair = pl.BlockSpec((rows, LANES), lambda h: (0, h))
    other = pl.BlockSpec((rows, LANES), lambda h: (0, h + 1 - 2 * lax.rem(h, 2)))
    return pl.pallas_call(
        attend_grad_kernel,
        grid=(D // LANES,),
        in_specs=[pair, pair, other, pair, other, pair, pair, pair]
        + [
            pl.BlockSpec((rows, LANES), lambda h: (0, 0)),
            pl.BlockSpec((2 * rows, LANES), lambda h: (0, 0)),
        ],
        out_specs=[pair, pair, other, pair, other],
        out_shape=[shape((rows, D), bf16)] * 5,
        scratch_shapes=[
            pltpu.VMEM((2 * rows, 2 * LANES), bf16),
            pltpu.VMEM((2 * rows, 2 * LANES), bf16),
            pltpu.VMEM((2, rows, 2 * LANES), bf16),
            pltpu.VMEM((2, rows, 2 * LANES), bf16),
            pltpu.VMEM((LANES, 2 * rows), bf16),
        ],
        compiler_params=params(),
        name="attend_grad",
        cost_estimate=cost(23),
    )(q, k, kp, v, vp, do, o, lse, ohq, ohk)


def proj_grad_kernel(
    dq_ref, dk_ref, dv_ref, dkr_ref, dvr_ref, xs_ref, dr1_ref, w0, w1, w2, w3,
    gk_ref, gs_ref, dx_ref, sums_ref, w_s, dk_s, dv_s,
):
    place_qkv(w_s, (w0, w1, w2, w3))
    zero = jnp.zeros((1, D), f32)

    def tile(t, c):
        at = pl.ds(t * ROW_TILE, ROW_TILE)
        dq = dq_ref[at]
        dk = (dk_ref[at].astype(f32) + dkr_ref[at].astype(f32)).astype(bf16)
        dv = (dv_ref[at].astype(f32) + dvr_ref[at].astype(f32)).astype(bf16)
        dk_s[at] = dk
        dv_s[at] = dv
        dx_ref[at] = (
            dr1_ref[at]
            + dot(dq, w_s[:, :D], 1, 1)
            + dot(dk, w_s[:, D : 2 * D], 1, 1)
            + dot(dv, w_s[:, 2 * D :], 1, 1)
        )
        return (c[0] + col_sum(dq.astype(f32)), c[1] + col_sum(dv.astype(f32)))

    dbq, dbv = lax.fori_loop(0, xs_ref.shape[0] // ROW_TILE, tile, (zero, zero))
    sums_ref[0:1, :] = dbq
    sums_ref[1:2, :] = dbv
    sums_ref[2:8, :] = jnp.zeros((6, D), f32)
    for part, ref in enumerate((dq_ref, dk_s, dv_s)):
        grad = dot(xs_ref[...], ref[...], 0, 0).astype(bf16)
        for r in range(4):
            out = gs_ref if r % 2 else gk_ref
            for row in range(4):
                out[r // 2, row * 3 + part] = grad[row * BLK : (row + 1) * BLK, r * BLK : (r + 1) * BLK]


def proj_grad(dq, dk, dv, dkr, dvr, xs, dr1, wqkv):
    rows = xs.shape[0]
    return pl.pallas_call(
        proj_grad_kernel,
        out_shape=[
            shape((2, 12, BLK, BLK), bf16),
            shape((2, 12, BLK, BLK), bf16),
            shape((rows, D)),
            shape((8, D)),
        ],
        scratch_shapes=[
            pltpu.VMEM((D, 3 * D), bf16),
            pltpu.VMEM((rows, D), bf16),
            pltpu.VMEM((rows, D), bf16),
        ],
        compiler_params=params(),
        name="proj_grad",
        cost_estimate=cost(5),
    )(dq, dk, dv, dkr, dvr, xs, dr1, *wqkv)


def embed_grad_kernel(
    place_ref, series_ref, g_ref, we_ref, s0, q0, b0, s1, q1, b1, in_ref, keep_ref, send_ref, tab
):
    place = place_ref[0]
    g = g_ref[...]
    in_ref[...] = dot_hi(g, we_ref[...], 1, 1)
    tab[:LOOK] = dot_hi(series_ref[...].astype(f32), g, 0, 0)
    tab[LOOK : LOOK + 1] = col_sum(g)
    per_layer = 8 + FF // D
    for layer, (sums, qsums, db1) in enumerate(((s0, q0, b0), (s1, q1, b1))):
        base = LOOK + 1 + layer * per_layer
        for r in range(4):
            h = place ^ r
            lanes = pl.ds(pl.multiple_of(h * BLK, BLK), BLK)
            tab[base : base + 2, lanes] = qsums[0:2, r * BLK : (r + 1) * BLK]
            tab[pl.ds(base + 5 + h, 1), :] = db1[r : r + 1, :]
        tab[base + 2 : base + 5] = sums[0:3]
        tab[base + 5 + FF // D : base + per_layer] = sums[3:6]
    used = LOOK + 1 + LAYERS * per_layer
    tab[used:] = jnp.zeros((BLK - used, D), f32)
    for r in range(4):
        rows = tab[pl.ds(pl.multiple_of((place ^ r) * 32, 32), 32), :].astype(bf16)
        out = send_ref if r % 2 else keep_ref
        for c in range(4):
            out[r // 2, c * 32 : (c + 1) * 32] = rows[:, c * BLK : (c + 1) * BLK]


def embed_grad(place, series, g, table, sums):
    rows = series.shape[0]
    spec = pl.BlockSpec(memory_space=pltpu.VMEM)
    return pl.pallas_call(
        embed_grad_kernel,
        in_specs=[pl.BlockSpec(memory_space=pltpu.SMEM)] + [spec] * 9,
        out_shape=[
            shape((rows, LOOK)),
            shape((2, BLK, BLK), bf16),
            shape((2, BLK, BLK), bf16),
        ],
        scratch_shapes=[pltpu.VMEM((BLK, D), f32)],
        compiler_params=params(),
        name="embed_grad",
        cost_estimate=cost(2),
    )(place, series, g, table[:LOOK], *sums)


def vector_kernel(at_ref, val_ref, first_ref, second_ref, *refs):
    count = len(refs) - 6
    parts = refs[:count]
    nv_ref, n1_ref, n2_ref, bias_ref, held, tab = refs[count:]
    share = BLK // count
    for k in range(count):
        held[k] = parts[k][...]
    for d in range(count):
        for h in range(4):
            c, i = divmod(d * share, 32)
            tab[h * 32 + i : h * 32 + i + share, c * BLK : (c + 1) * BLK] = held[
                at_ref[d], at_ref[count] ^ h
            ]
    used = val_ref.shape[0]
    grad = tab[:used]
    val = val_ref[...]
    first = 0.5 * first_ref[...] + 0.5 * grad
    second = 0.5 * second_ref[...] + 0.5 * grad * grad
    n1_ref[...] = first
    n2_ref[...] = second
    nv_ref[...] = val - rate_vector * (
        first / CORR / (jnp.sqrt(second / CORR) + adam_eps) + weight_decay * val
    )
    per_layer = 8 + FF // D
    for layer in range(LAYERS):
        base = LOOK + 1 + layer * per_layer
        bias_ref[2 * layer : 2 * layer + 1] = tab[base + 2 : base + 3]
        bias_ref[2 * layer + 1 : 2 * layer + 2] = tab[base + 5 + FF // D : base + 6 + FF // D]


def vector_update(at, values, first, second, parts):
    spec = pl.BlockSpec(memory_space=pltpu.VMEM)
    return pl.pallas_call(
        vector_kernel,
        in_specs=[pl.BlockSpec(memory_space=pltpu.SMEM)] + [spec] * (3 + len(parts)),
        out_shape=[shape(values.shape)] * 3 + [shape((2 * LAYERS, D))],
        scratch_shapes=[
            pltpu.VMEM((len(parts), 4, BLK // len(parts), BLK), f32),
            pltpu.VMEM((BLK, D), f32),
        ],
        compiler_params=params(),
        name="vector",
        cost_estimate=cost(2),
    )(at, values, first, second, *parts)


PARTS = ((0, 12), (12, 4), (16, 32))


def natural_kernel(at_ref, *refs):
    count = len(refs) - 7
    slots, outs, held = refs[:count], refs[count : count + 6], refs[-1]
    step = slots[0].shape[0]
    for i in range(count):
        held[i * step : (i + 1) * step] = slots[i][...]
    for i, out in enumerate(outs):
        layer, part = divmod(i, 3)
        first, n = PARTS[part]
        for j in range(n):
            out[j] = held[at_ref[layer * 48 + first + j]]


def natural_order(at, slots):
    total = sum(s.shape[0] for s in slots)
    spec = pl.BlockSpec(memory_space=pltpu.VMEM)
    return pl.pallas_call(
        natural_kernel,
        in_specs=[pl.BlockSpec(memory_space=pltpu.SMEM)] + [spec] * len(slots),
        out_shape=[shape((n, BLK, BLK), bf16) for _ in range(LAYERS) for _, n in PARTS],
        scratch_shapes=[pltpu.VMEM((total, BLK, BLK), bf16)],
        compiler_params=params(),
        name="natural",
        cost_estimate=cost(3),
    )(at, *slots)


def routed_kernel(at_ref, tab_ref, tabr_ref, *refs):
    own, got, out = refs[:6], refs[6:12], refs[12]
    count, span = out.shape[0], out.shape[1]
    share = BLK // count
    out[...] = jnp.zeros(out.shape, bf16)
    for i in range(6):
        layer, part = divmod(i, 3)
        first, n = PARTS[part]
        for j in range(n):
            place = at_ref[layer * 48 + first + j]
            who = at_ref[96 + layer * 48 + first + j]
            value = own[i][j].astype(f32) + got[i][j].astype(f32)
            out[who, pl.ds(pl.multiple_of(place * BLK, BLK), BLK), :] = value.astype(bf16)
    table = (tab_ref[...].astype(f32) + tabr_ref[...].astype(f32)).astype(bf16)
    for d in range(count):
        who = at_ref[192 + d]
        out[who, span - share : span, :] = table[d * share : (d + 1) * share]


def routed(at, table, table_got, own, got, count, slots_each):
    spec = pl.BlockSpec(memory_space=pltpu.VMEM)
    return pl.pallas_call(
        routed_kernel,
        in_specs=[pl.BlockSpec(memory_space=pltpu.SMEM)] + [spec] * 14,
        out_shape=shape((count, slots_each * BLK + BLK // count, BLK), bf16),
        compiler_params=params(),
        name="routed",
        cost_estimate=cost(4),
    )(at, table, table_got, *own, *got)


def routed_plain_kernel(at_ref, *refs):
    own, got, out = refs[:6], refs[6:12], refs[12]
    out[...] = jnp.zeros(out.shape, bf16)
    for i in range(6):
        layer, part = divmod(i, 3)
        first, n = PARTS[part]
        for j in range(n):
            place = at_ref[layer * 48 + first + j]
            who = at_ref[96 + layer * 48 + first + j]
            value = own[i][j].astype(f32) + got[i][j].astype(f32)
            out[who, pl.ds(pl.multiple_of(place * BLK, BLK), BLK), :] = value.astype(bf16)


def routed_plain(at, own, got, count, slots_each):
    spec = pl.BlockSpec(memory_space=pltpu.VMEM)
    return pl.pallas_call(
        routed_plain_kernel,
        in_specs=[pl.BlockSpec(memory_space=pltpu.SMEM)] + [spec] * 12,
        out_shape=shape((count, slots_each * BLK, BLK), bf16),
        compiler_params=params(),
        name="routed",
        cost_estimate=cost(4),
    )(at, *own, *got)


def ring_of(count):
    half = count // 2
    return [2 * i for i in range(half)] + [2 * (half - 1 - i) + 1 for i in range(half)]


def ring_shift(value, order, by):
    n = len(order)
    return lax.ppermute(value, "dp", [(order[i], order[(i + by) % n]) for i in range(n)])


def ring_gather(value, order):
    n = len(order)
    held = [value] + [None] * (n - 1)
    ahead = behind = value
    for step in range(1, n // 2 + 1):
        behind = ring_shift(behind, order, 1)
        held[n - step] = behind
        if step < n // 2:
            ahead = ring_shift(ahead, order, -1)
            held[step] = ahead
    return held


def ring_reduce(pieces, order):
    n = len(order)
    up = pieces[n // 2]
    down = pieces[n // 2 + 1]
    for step in range(1, n // 2 + 1):
        up = ring_shift(up, order, 1)
        if step < n // 2:
            up = add_low(up, pieces[n // 2 - step])
            down = ring_shift(down, order, -1)
            if step < n // 2 - 1:
                down = add_low(down, pieces[n // 2 + 1 + step])
    return pieces[0], up, down


def add_low(a, b):
    return (a.astype(f32) + b.astype(f32)).astype(bf16)


def core_swap(value):
    return lax.ppermute(value, "head", [(i, i ^ 1) for i in range(4)])


def far_swap(value):
    return lax.ppermute(value, "head", [(i, i ^ 2) for i in range(4)])


def tied(values, after):
    return lax.optimization_barrier((values, after))[0]


def one_hots(ids):
    lane = jnp.arange(LANES, dtype=jnp.int32)[None, :]
    same = ids[:, None] == lane
    return jnp.where(same, -BIG, 0.0).astype(bf16), jnp.where(same, 0.0, 1.0).astype(bf16)


def relative(row, place):
    pieces = row.reshape(4, -1)
    return jnp.take(pieces, jnp.arange(4) ^ place, axis=0).reshape(1, -1)


def on_device(
    series,
    cotangent,
    window_lengths,
    owner_list,
    master,
    first_moment,
    second_moment,
    left_stats,
    right_stats,
    left_basis,
    right_basis,
    vec_values,
    vec_first,
    vec_second,
):
    place = lax.axis_index("head")
    spot = lax.axis_index("dp")
    dp = lax.axis_size("dp")
    ringed = dp == 8
    rows = series.shape[0]
    own_slots = master.shape[1]
    buckets, win = window_lengths.shape
    bucket_rows = rows * 4 // buckets
    owner_row = owner_list[0]
    who = owner_row // own_slots
    if ringed:
        order = ring_of(dp)
        ring_at = jnp.asarray([order.index(d) for d in range(dp)], jnp.int32)
        who = (ring_at[who] - ring_at[spot]) % dp
    inner = owner_row % own_slots
    gather_at = who * own_slots + inner

    copies = master[0].astype(bf16)
    if ringed:
        slots = ring_gather(copies, order)
    else:
        slots = [lax.all_gather(copies, "dp", axis=0, tiled=True)]
    mine = natural_order(gather_at, slots)
    weights = []
    far = None
    for at in range(LAYERS):
        for group in ((0,), (1, 2)):
            group_own = [mine[3 * at + i] for i in group]
            ready = group_own if far is None else tied(group_own, far)
            far = [far_swap(one) for one in ready]
            for own, there in zip(group_own, far):
                weights.append([own, core_swap(own), there, core_swap(there)])

    windows = window_ids(window_lengths, bucket_rows)
    ids = windows.reshape(4, rows)
    own_ids = lax.dynamic_index_in_dim(ids, place, 0, False)
    pair_ids = lax.dynamic_index_in_dim(ids, place ^ 1, 0, False)
    ohq, ohk_own = one_hots(own_ids)
    ohk = jnp.concatenate([ohk_own, one_hots(pair_ids)[1]], axis=0)
    valid = (own_ids < win).astype(f32)[:, None]

    x = embed(series, vec_values)
    saved = []
    for layer in range(LAYERS):
        bq, bv, bo, g1, c1, b1, b2, g2, c2 = depth_vectors(vec_values, layer)
        wqkv, wout, wffn = weights[3 * layer : 3 * layer + 3]
        xs, q, k, v = project(x, relative(bq, place), relative(bv, place), wqkv)
        kp, vp = core_swap(k), core_swap(v)
        o, lse = attend(q, k, kp, v, vp, ohq, ohk)
        vec = jnp.stack([bo, g1, c1, b2, g2, c2, g2, c2])
        n1, i1, y, hid, slope, n2, i2, x = post(o, x, vec, relative(b1, place), wout, wffn)
        saved.append((xs, q, k, v, kp, vp, o, lse, vec, n1, i1, y, hid, slope, n2, i2))
    activations = x * valid
    grad = cotangent * valid

    own_sums = [None] * (3 * LAYERS)
    far_sums = [None] * (3 * LAYERS)
    table_rows = [None] * LAYERS

    def chip_sum(at, keep, got):
        own_sums[at] = add_low(keep[0], got[0])
        return add_low(keep[1], got[1])

    moving = []
    for layer in reversed(range(LAYERS)):
        xs, q, k, v, kp, vp, o, lse, vec, n1, i1, y, hid, slope, n2, i2 = saved[layer]
        wqkv, wout, wffn = weights[3 * layer : 3 * layer + 3]
        gk, gs, ok, os, dr1, do, db1, sums = ffn_grad(
            grad, n2, i2, n1, i1, y, hid, slope, o, vec, wout, wffn
        )
        got = [core_swap(gs), core_swap(os)]
        do, far = tied(
            (do, [chip_sum(3 * layer + 2, gk, got[0]), chip_sum(3 * layer + 1, ok, got[1])]), moving
        )
        far_sums[3 * layer + 2] = far_swap(far[0])
        far_sums[3 * layer + 1] = far_swap(far[1])
        do = tied(do, far)
        dq, dk, dkp, dv, dvp = attend_grad(q, k, kp, v, vp, do, o, lse, ohq, ohk)
        dkr, dvr = core_swap(dkp), core_swap(dvp)
        dkr, dvr = tied((dkr, dvr), far_sums[3 * layer + 1 : 3 * layer + 3])
        pk, ps, grad, qsums = proj_grad(dq, dk, dv, dkr, dvr, xs, dr1, wqkv)
        table_rows[layer] = (sums, qsums, db1)
        got = core_swap(ps)
        if layer:
            far = chip_sum(3 * layer, pk, got)
            grad = tied(grad, far)
            far_sums[3 * layer] = far_swap(far)
            moving = [far_sums[3 * layer]]
    input_grad, tab_keep, tab_send = embed_grad(
        place.astype(jnp.int32)[None], series, grad, vec_values, table_rows[0] + table_rows[1]
    )
    tab_got = core_swap(tab_send)
    far_sums[0] = far_swap(chip_sum(0, pk, got))
    tab_own = add_low(tab_keep[0], tab_got[0])
    tab_far = far_swap(add_low(tab_keep[1], tab_got[1]))
    if ringed:
        dist = (ring_at - ring_at[spot]) % dp
        at = jnp.concatenate([inner, who, dist]).astype(jnp.int32)
        pieces = routed(at, tab_own, tab_far, own_sums, far_sums, dp, own_slots)
        terms = ring_reduce([pieces[i] for i in range(dp)], order)
        grads = [t[: own_slots * BLK].reshape(own_slots, BLK, BLK) for t in terms]
        part = sum(t[own_slots * BLK :].astype(f32) for t in terms)
        group = jnp.stack(
            [part] + [lax.ppermute(part, "head", [(i, i ^ r) for i in range(4)]) for r in (1, 2, 3)]
        )
        grads = tied(grads, group)
        parts = [group] + [ring_shift(group, order, -k) for k in range(1, dp)]
        vec_at = jnp.concatenate([dist, place[None]]).astype(jnp.int32)
        vec_new_values, vec_new_first, vec_new_second, branch_bias_grads = vector_update(
            vec_at, vec_values, vec_first, vec_second, parts
        )
    else:
        at = jnp.concatenate([inner, who]).astype(jnp.int32)
        pieces = routed_plain(at, own_sums, far_sums, dp, own_slots)
        whole = lax.psum_scatter(pieces, "dp", scatter_dimension=0, tiled=True)
        grads = [whole.reshape(own_slots, BLK, BLK)]
        total = lax.psum(tab_own.astype(f32) + tab_far.astype(f32), "dp")
        shares = lax.all_gather(total, "head", axis=0)
        grad_table = shares.reshape(4, 4, 32, BLK).transpose(0, 2, 1, 3).reshape(BLK, D)
        grad_table = grad_table[: vec_values.shape[0]]
        vec_new_values, vec_new_first, vec_new_second = adamw_update(
            grad_table, vec_values, vec_first, vec_second
        )
        branch_bias_grads = branch_biases(grad_table)
    new_master, new_copy, new_first, new_second, new_left, new_right, left_next, right_next = soap(
        grads,
        master[0],
        first_moment[0],
        second_moment[0],
        left_stats[0],
        right_stats[0],
        left_basis[0],
        right_basis[0],
    )
    return (
        activations,
        input_grad,
        new_master[None],
        new_copy[None],
        new_first[None],
        new_second[None],
        new_left[None],
        new_right[None],
        left_next[None],
        right_next[None],
        vec_new_values,
        vec_new_first,
        vec_new_second,
        branch_bias_grads,
    )


def solution(mesh):
    placed = (
        P(("dp", "head"), None),
        P(("dp", "head"), None),
        P("dp", None),
        P("head", None),
        P("head", "dp", None, None),
        P("head", "dp", None, None),
        P("head", "dp", None, None),
        P("head", "dp", None, None),
        P("head", "dp", None, None),
        P("head", "dp", None, None),
        P("head", "dp", None, None),
        P(),
        P(),
        P(),
    )
    return jax.shard_map(
        on_device,
        mesh=mesh,
        in_specs=placed,
        out_specs=(
            P(("dp", "head"), None),
            P(("dp", "head"), None),
            P("head", "dp", None, None),
            P("head", "dp", None, None),
            P("head", "dp", None, None),
            P("head", "dp", None, None),
            P("head", "dp", None, None),
            P("head", "dp", None, None),
            P("head", "dp", None, None),
            P("head", "dp", None, None),
            P(),
            P(),
            P(),
            P(),
        ),
        check_vma=False,
    )
```

```python
import functools

import jax
import jax.numpy as jnp
from jax import lax
from jax.experimental import pallas as pl
from jax.experimental.pallas import tpu as pltpu
from jax.sharding import PartitionSpec as P

D = 512
HEADS = 8
HD = 64
FF = 2048
LOOK = 96
LAYERS = 2
BLK = 128
STEP = 10

f32 = jnp.float32
HI = lax.Precision.HIGHEST
norm_eps = 1e-05
beta_first = 0.5
beta_second = 0.5
beta_stats = 0.5
adam_eps = 1e-08
rate_matrix = 0.02
rate_vector = 0.15
weight_decay = 0.01


def window_ids(lengths, bucket_rows):
    bounds = jnp.cumsum(lengths, axis=1, dtype=jnp.int32)
    places = jnp.arange(bucket_rows, dtype=jnp.int32)
    return jnp.sum(
        (places[None, :, None] >= bounds[:, None, :]).astype(jnp.int32), axis=2, dtype=jnp.int32
    )


def depth_vectors(vec_table, layer_at):
    ff_ratio = FF // D
    base_row = LOOK + 1 + layer_at * (8 + ff_ratio)
    return (
        vec_table[base_row],
        vec_table[base_row + 1],
        vec_table[base_row + 2],
        vec_table[base_row + 3],
        vec_table[base_row + 4],
        vec_table[base_row + 5 : base_row + 5 + ff_ratio].reshape(FF),
        vec_table[base_row + 5 + ff_ratio],
        vec_table[base_row + 6 + ff_ratio],
        vec_table[base_row + 7 + ff_ratio],
    )


def adamw_update(gradient, values, moment_one, moment_two):
    new_first = beta_first * moment_one + (1.0 - beta_first) * gradient
    new_second = beta_second * moment_two + (1.0 - beta_second) * gradient * gradient
    step_ratio = (
        new_first
        / (1.0 - beta_first**STEP)
        / (jnp.sqrt(new_second / (1.0 - beta_second**STEP)) + adam_eps)
    )
    new_values = values - rate_vector * (step_ratio + weight_decay * values)
    return (new_values, new_first, new_second)


def branch_biases(grad_table):
    ff_ratio = FF // D
    bias_rows = []
    for layer_at in range(LAYERS):
        base_row = LOOK + 1 + layer_at * (8 + ff_ratio)
        bias_rows.append(grad_table[base_row + 2])
        bias_rows.append(grad_table[base_row + 5 + ff_ratio])
    return jnp.stack(bias_rows, axis=0)


def dot_hi(a, b, ca, cb):
    return lax.dot_general(
        a, b, (((ca,), (cb,)), ((), ())), precision=HI, preferred_element_type=f32
    )


def terms(x, count):
    out = []
    for i in range(count):
        part = x.astype(jnp.bfloat16)
        out.append(part)
        if i < count - 1:
            x = x - part.astype(f32)
    return out


def dot_terms(a, b, ca, cb, full=False):
    a = terms(a, 3 if full else 2)
    b = terms(b, 3 if full else 2)
    dims = (((ca,), (cb,)), ((), ()))
    left = jnp.concatenate(a[:2], axis=ca)
    right = jnp.concatenate(
        [jnp.concatenate([b[0], b[1]], axis=cb), jnp.concatenate([b[1], b[0]], axis=cb)], axis=1 - cb
    )
    out = lax.dot_general(left, right, dims, preferred_element_type=f32)
    out = out[:, :BLK] + out[:, BLK:]
    if full:
        out = out + lax.dot_general(
            jnp.concatenate([a[0], a[2]], axis=ca),
            jnp.concatenate([b[2], b[0]], axis=cb),
            dims,
            preferred_element_type=f32,
        )
    return out


PANEL = 32


def qr_batch(a_ref, count):
    lane = lax.broadcasted_iota(jnp.int32, (1, 1, BLK), 2)
    sub8 = lax.broadcasted_iota(jnp.int32, (1, 8, 1), 1)
    sub = lax.broadcasted_iota(jnp.int32, (1, PANEL, 1), 1)
    for r0 in range(0, BLK, PANEL):
        tiles = [a_ref[:, r0 + 8 * t : r0 + 8 * t + 8, :] for t in range(PANEL // 8)]
        for k in range(PANEL):
            t0, s = divmod(k, 8)
            row = tiles[t0][:, s : s + 1, :]
            pn = (row + (lane == r0 + k).astype(f32)) * (1.0 / row[:, :, r0 + k : r0 + k + 1])
            for t in range(t0, PANEL // 8):
                c = tiles[t][:, :, r0 + k : r0 + k + 1]
                if t == t0:
                    if s == 7:
                        continue
                    c = jnp.where(sub8 > s, c, 0.0)
                tiles[t] = tiles[t] - c * pn
        done = jnp.concatenate(tiles, axis=1)
        diag = lane == sub + r0
        pivot = jnp.sum(jnp.where(diag, done, 0.0), axis=2, keepdims=True)
        done = jnp.where(diag, 1.0, jnp.where((lane > sub + r0) & (lane < r0 + PANEL), 0.0, done))
        done = done * lax.rsqrt(pivot)
        a_ref[:, r0 : r0 + PANEL, :] = done
        r1 = r0 + PANEL
        if r1 < BLK:
            lane2 = lax.broadcasted_iota(jnp.int32, (BLK - r1, BLK), 1)
            clear = (lane2 >= r0) & (lane2 < r1)
            z0, z1, z2 = terms(done, 3)
            left = jnp.concatenate([z0, z0, z0, z1, z1, z2], axis=1)
            right = jnp.concatenate([z0, z1, z2, z0, z1, z0], axis=1)
            for b in range(count):
                update = lax.dot_general(
                    left[b], right[b], (((0,), (0,)), ((), ())), preferred_element_type=f32
                )
                a_ref[b, r1:, :] = jnp.where(clear, 0.0, a_ref[b, r1:, :]) - update[r1:]


def soap_kernel(count, *refs):
    for s in range(refs[0].shape[0]):
        soap_slot(s, sum(ref[s].astype(f32) for ref in refs[:count]), *refs[count:])
    soap_finish(*refs[-4:])


def soap_slot(
    s, g, mas_ref, m1_ref, m2_ref, ls_ref, rs_ref, lb_ref, rb_ref,
    nm_ref, nc_ref, n1_ref, n2_ref, nl_ref, nr_ref, ql_ref, qr_ref, mat_ref, a_ref,
):
    group = mas_ref.shape[0]
    lb = lb_ref[s]
    rb = rb_ref[s]
    rot = dot_terms(dot_terms(lb, g, 0, 0), rb, 1, 0)
    n1 = 0.5 * m1_ref[s] + 0.5 * rot
    n2 = 0.5 * m2_ref[s] + 0.5 * rot * rot
    n1_ref[s] = n1
    n2_ref[s] = n2
    corr = 1.0 - 0.5**STEP
    ratio = n1 / corr / (jnp.sqrt(n2 / corr) + adam_eps)
    upd = dot_terms(dot_terms(lb, ratio, 1, 0), rb, 1, 1)
    mas = mas_ref[s]
    nm = mas - rate_matrix * (upd + weight_decay * mas)
    nm_ref[s] = nm
    nc_ref[s] = nm.astype(jnp.bfloat16)
    nl = 0.5 * ls_ref[s] + 0.5 * dot_terms(g, g, 1, 1)
    nr = 0.5 * rs_ref[s] + 0.5 * dot_terms(g, g, 0, 0)
    nl_ref[s] = nl
    nr_ref[s] = nr
    for side, (st, ba) in enumerate(((nl, lb), (nr, rb))):
        m = dot_terms(st, ba, 1, 0, True)
        m = m * lax.rsqrt(jnp.sum(m * m, axis=0, keepdims=True))
        at = 2 * (pl.program_id(0) * group + s) + side
        mat_ref[at] = m
        a_ref[at] = dot_terms(m, m, 0, 0, True)


def soap_finish(ql_ref, qr_ref, mat_ref, a_ref):
    @pl.when(pl.program_id(0) == pl.num_programs(0) - 1)
    def _():
        count = a_ref.shape[0]
        qr_batch(a_ref, count)
        keep = lax.broadcasted_iota(jnp.int32, (BLK, BLK), 1) <= lax.broadcasted_iota(
            jnp.int32, (BLK, BLK), 0
        )
        for j in range(count // 2):
            for side, ref in enumerate((ql_ref, qr_ref)):
                x = jnp.where(keep, a_ref[2 * j + side], 0.0)
                ref[j] = dot_terms(mat_ref[2 * j + side], x, 1, 1, True)


def soap(gs, master, m1, m2, ls, rs, lb, rb):
    n = master.shape[0]
    group = SOAP_GROUP if n % SOAP_GROUP == 0 else n
    one = pl.BlockSpec((group, BLK, BLK), lambda i: (i, 0, 0))
    whole = pl.BlockSpec((n, BLK, BLK), lambda i: (0, 0, 0))
    sh = jax.ShapeDtypeStruct((n, BLK, BLK), f32)
    shb = jax.ShapeDtypeStruct((n, BLK, BLK), jnp.bfloat16)
    return pl.pallas_call(
        functools.partial(soap_kernel, len(gs)),
        grid=(n // group,),
        in_specs=[one] * (len(gs) + 7),
        out_specs=[one] * 6 + [whole] * 2,
        out_shape=[sh, shb, sh, sh, sh, sh, sh, sh],
        scratch_shapes=[pltpu.VMEM((2 * n, BLK, BLK), f32)] * 2,
        compiler_params=pltpu.CompilerParams(vmem_limit_bytes=50 * 2**20),
        cost_estimate=pl.CostEstimate(flops=40 * 10**9, bytes_accessed=0, transcendentals=0),
        name="soap",
    )(*gs, master, m1, m2, ls, rs, lb, rb)


SOAP_GROUP = 2


bf16 = jnp.bfloat16
LANES = 128
ROW_TILE = 512
BIG = 1e30
CORR = 1.0 - 0.5**STEP


def params(mib=48):
    return pltpu.CompilerParams(vmem_limit_bytes=mib * 2**20)


def cost(micros):
    return pl.CostEstimate(flops=int(micros * 1e9), bytes_accessed=0, transcendentals=0)


def shape(dims, kind=f32):
    return jax.ShapeDtypeStruct(dims, kind)


def dot(a, b, ca=1, cb=0):
    return lax.dot_general(a, b, (((ca,), (cb,)), ((), ())), preferred_element_type=f32)


def place_blocks(dst, refs, first, rows, cols, row_step, col_step, col_base=0):
    for r, ref in enumerate(refs):
        for j in range(rows * cols):
            row, col = divmod(j, cols)
            r0 = r * row_step + row * BLK
            c0 = col_base + r * col_step + col * BLK
            dst[r0 : r0 + BLK, c0 : c0 + BLK] = ref[first + j]


def place_qkv(dst, refs):
    for r, ref in enumerate(refs):
        for j in range(12):
            row, col = divmod(j, 3)
            c0 = col * D + r * BLK
            dst[row * BLK : (row + 1) * BLK, c0 : c0 + BLK] = ref[j]


def layer_norm(resid):
    center = resid - jnp.mean(resid, axis=1, keepdims=True)
    inv = lax.rsqrt(jnp.mean(center * center, axis=1, keepdims=True) + norm_eps)
    return center * inv, inv


def layer_norm_grad(grad, unit, inv, gain):
    dn = grad * gain
    return inv * (
        dn
        - jnp.mean(dn, axis=1, keepdims=True)
        - unit * jnp.mean(dn * unit, axis=1, keepdims=True)
    )


def col_sum(values):
    return jnp.sum(values, axis=0, keepdims=True)


def embed_kernel(series_ref, we_ref, be_ref, x_ref):
    x_ref[...] = dot_hi(series_ref[...].astype(f32), we_ref[...], 1, 0) + be_ref[...]


def embed(series, table):
    rows = series.shape[0]
    return pl.pallas_call(
        embed_kernel, out_shape=shape((rows, D)), compiler_params=params(), name="embed"
    )(series, table[:LOOK], table[LOOK : LOOK + 1])


def proj_kernel(x_ref, bq_ref, bv_ref, w0, w1, w2, w3, xs_ref, q_ref, k_ref, v_ref, w_s):
    place_qkv(w_s, (w0, w1, w2, w3))

    def tile(t, c):
        at = pl.ds(t * ROW_TILE, ROW_TILE)
        xs = x_ref[at].astype(bf16)
        xs_ref[at] = xs
        q_ref[at] = (dot(xs, w_s[:, :D]) + bq_ref[...]).astype(bf16)
        k_ref[at] = dot(xs, w_s[:, D : 2 * D]).astype(bf16)
        v_ref[at] = (dot(xs, w_s[:, 2 * D :]) + bv_ref[...]).astype(bf16)
        return c

    lax.fori_loop(0, x_ref.shape[0] // ROW_TILE, tile, 0)


def project(x, bq, bv, wqkv):
    rows = x.shape[0]
    return pl.pallas_call(
        proj_kernel,
        out_shape=[shape((rows, D), bf16)] * 4,
        scratch_shapes=[pltpu.VMEM((D, 3 * D), bf16)],
        compiler_params=params(),
        name="project",
        cost_estimate=cost(3),
    )(x, bq, bv, *wqkv)


def half_mask(i, kind=bf16):
    lane = lax.broadcasted_iota(jnp.int32, (1, LANES), 1)
    return ((lane >= HD * i) & (lane < HD * (i + 1))).astype(f32).astype(kind)


def three_terms(col):
    first = col.astype(bf16).astype(f32)
    second = (col - first).astype(bf16).astype(f32)
    return first, second, col - first - second


def lanes_with(base, at, cols):
    lane = lax.broadcasted_iota(jnp.int32, base.shape, 1)
    for i, col in enumerate(cols):
        base = jnp.where(lane == at + i, col, base)
    return base.astype(bf16)


def attend_kernel(q_ref, k_ref, kp_ref, v_ref, vp_ref, ohq_ref, ohk_ref, o_ref, lse_ref, ka, va):
    rows = q_ref.shape[0]
    ka[:rows, :LANES] = k_ref[...]
    ka[rows:, :LANES] = kp_ref[...]
    ka[:, LANES:] = ohk_ref[...]
    lane = lax.broadcasted_iota(jnp.int32, (ROW_TILE, LANES), 1)
    for i in range(2):
        m = half_mask(i)
        va[i, :rows, :LANES] = v_ref[...] * m
        va[i, rows:, :LANES] = vp_ref[...] * m
        va[i, :, LANES:] = jnp.ones((2 * rows, LANES), bf16)

    def tile(t, c):
        at = pl.ds(t * ROW_TILE, ROW_TILE)
        total = jnp.zeros((ROW_TILE, LANES), f32)
        stat = jnp.zeros((ROW_TILE, LANES), f32)
        for i in range(2):
            qa = jnp.concatenate([q_ref[at] * (half_mask(i) * bf16(0.125)), ohq_ref[at]], axis=1)
            s = dot(qa, ka[...], 1, 1)
            high = jnp.max(s, axis=1, keepdims=True)
            e = jnp.exp(s - high).astype(bf16)
            out = dot(e, va[i])
            norm = out[:, LANES:]
            total = total + out[:, :LANES] / norm
            stat = jnp.where(lane == i, high + jnp.log(norm), stat)
        o_ref[at] = total.astype(bf16)
        lse_ref[at] = stat
        return c

    lax.fori_loop(0, rows // ROW_TILE, tile, 0)


def attend(q, k, kp, v, vp, ohq, ohk):
    rows = q.shape[0]
    pair = pl.BlockSpec((rows, LANES), lambda h: (0, h))
    other = pl.BlockSpec((rows, LANES), lambda h: (0, h + 1 - 2 * lax.rem(h, 2)))
    return pl.pallas_call(
        attend_kernel,
        grid=(D // LANES,),
        in_specs=[pair, pair, other, pair, other]
        + [
            pl.BlockSpec((rows, LANES), lambda h: (0, 0)),
            pl.BlockSpec((2 * rows, LANES), lambda h: (0, 0)),
        ],
        out_specs=[pair, pair],
        out_shape=[shape((rows, D), bf16), shape((rows, D))],
        scratch_shapes=[
            pltpu.VMEM((2 * rows, 2 * LANES), bf16),
            pltpu.VMEM((2, 2 * rows, 2 * LANES), bf16),
        ],
        compiler_params=params(),
        name="attend",
        cost_estimate=cost(11),
    )(q, k, kp, v, vp, ohq, ohk)


def post_kernel(
    o_ref, x_ref, vec_ref, b1_ref, a0, a1, a2, a3, f0, f1, f2, f3,
    n1_ref, i1_ref, y_ref, hid_ref, slope_ref, n2_ref, i2_ref, x2_ref,
    wo_s, w1_s, w2_s,
):
    place_blocks(wo_s, (a0, a1, a2, a3), 0, 1, 4, BLK, 0)
    place_blocks(w1_s, (f0, f1, f2, f3), 0, 4, 4, 0, D)
    place_blocks(w2_s, (f0, f1, f2, f3), 16, 4, 4, D, 0)

    def tile(t, c):
        at = pl.ds(t * ROW_TILE, ROW_TILE)
        vec = [vec_ref[i : i + 1, :] for i in range(6)]
        unit, inv = layer_norm(x_ref[at] + dot(o_ref[at], wo_s[...]) + vec[0])
        n1_ref[at] = unit
        i1_ref[at] = jnp.broadcast_to(inv, (ROW_TILE, LANES))
        y = unit * vec[1] + vec[2]
        yb = y.astype(bf16)
        y_ref[at] = yb
        fed = jnp.zeros((ROW_TILE, D), f32)
        for r in range(FF // D):
            cols = slice(r * D, (r + 1) * D)
            pre = dot(yb, w1_s[:, cols]) + b1_ref[:, cols]
            phi = 0.5 * (1.0 + lax.erf(pre * (0.5**0.5)))
            hid = (pre * phi).astype(bf16)
            hid_ref[at, cols] = hid
            slope_ref[at, cols] = (
                phi + pre * (jnp.exp(-0.5 * pre * pre) * 0.3989422804014327)
            ).astype(bf16)
            fed = fed + dot(hid, w2_s[cols, :])
        unit, inv = layer_norm(y + fed + vec[3])
        n2_ref[at] = unit
        i2_ref[at] = jnp.broadcast_to(inv, (ROW_TILE, LANES))
        x2_ref[at] = unit * vec[4] + vec[5]
        return c

    lax.fori_loop(0, x_ref.shape[0] // ROW_TILE, tile, 0)


def post(o, x, vec, b1, wout, wffn):
    rows = x.shape[0]
    return pl.pallas_call(
        post_kernel,
        out_shape=[
            shape((rows, D)),
            shape((rows, LANES)),
            shape((rows, D), bf16),
            shape((rows, FF), bf16),
            shape((rows, FF), bf16),
            shape((rows, D)),
            shape((rows, LANES)),
            shape((rows, D)),
        ],
        scratch_shapes=[
            pltpu.VMEM((D, D), bf16),
            pltpu.VMEM((D, FF), bf16),
            pltpu.VMEM((FF, D), bf16),
        ],
        compiler_params=params(),
        name="post",
        cost_estimate=cost(11),
    )(o, x, vec, b1, *wout, *wffn)


def store_blocks(refs, r, first, rows, cols, value):
    keep_ref, send_ref = refs
    ref = send_ref if r % 2 else keep_ref
    for j in range(rows * cols):
        row, col = divmod(j, cols)
        ref[r // 2, first + j] = value[row * BLK : (row + 1) * BLK, col * BLK : (col + 1) * BLK]


def ffn_grad_kernel(
    e_ref, n2_ref, i2_ref, n1_ref, i1_ref, y_ref, hid_ref, slope_ref, o_ref, vec_ref,
    a0, a1, a2, a3, f0, f1, f2, f3,
    gk_ref, gs_ref, ok_ref, os_ref, dr1_ref, do_ref, db1_ref, sums_ref,
    wo_s, w1_s, w2_s, dr2_s, dfr_s, dpre_s, dar_s,
):
    rows = e_ref.shape[0]
    place_blocks(wo_s, (a0, a1, a2, a3), 0, 1, 4, BLK, 0)
    place_blocks(w1_s, (f0, f1, f2, f3), 0, 4, 4, 0, D)
    place_blocks(w2_s, (f0, f1, f2, f3), 16, 4, 4, D, 0)
    tiles = rows // ROW_TILE
    gain_two = vec_ref[4:5, :]
    gain_one = vec_ref[1:2, :]
    zero = jnp.zeros((1, D), f32)

    def tile_two(t, c):
        at = pl.ds(t * ROW_TILE, ROW_TILE)
        grad = e_ref[at]
        unit = n2_ref[at]
        dr2 = layer_norm_grad(grad, unit, i2_ref[at, 0:1], gain_two)
        dr2_s[at] = dr2
        dfr_s[at] = dr2.astype(bf16)
        return (c[0] + col_sum(dr2), c[1] + col_sum(grad * unit), c[2] + col_sum(grad))

    db2, dg2, dc2 = lax.fori_loop(0, tiles, tile_two, (zero, zero, zero))

    for r in range(FF // D):
        cols = slice(r * D, (r + 1) * D)

        def tile_up(t, c):
            at = pl.ds(t * ROW_TILE, ROW_TILE)
            dh = dot(dfr_s[at], w2_s[cols, :], 1, 1)
            dpre = (dh * slope_ref[at, cols].astype(f32)).astype(bf16)
            dpre_s[at, cols] = dpre
            dr2_s[at] = dr2_s[at] + dot(dpre, w1_s[:, cols], 1, 1)
            return c + col_sum(dpre.astype(f32))

        db1_ref[r : r + 1, :] = lax.fori_loop(0, tiles, tile_up, zero)
        store_blocks((gk_ref, gs_ref), r, 16, 4, 4, dot(hid_ref[:, cols], dfr_s[...], 0, 0).astype(bf16))
        store_blocks((gk_ref, gs_ref), r, 0, 4, 4, dot(y_ref[...], dpre_s[:, cols], 0, 0).astype(bf16))

    def tile_one(t, c):
        at = pl.ds(t * ROW_TILE, ROW_TILE)
        grad = dr2_s[at]
        unit = n1_ref[at]
        dr1 = layer_norm_grad(grad, unit, i1_ref[at, 0:1], gain_one)
        dr1_ref[at] = dr1
        dar = dr1.astype(bf16)
        dar_s[at] = dar
        do_ref[at] = dot(dar, wo_s[...], 1, 1).astype(bf16)
        return (c[0] + col_sum(dr1), c[1] + col_sum(grad * unit), c[2] + col_sum(grad))

    dbo, dg1, dc1 = lax.fori_loop(0, tiles, tile_one, (zero, zero, zero))
    dwo = dot(o_ref[...], dar_s[...], 0, 0).astype(bf16)
    for r in range(4):
        store_blocks((ok_ref, os_ref), r, 0, 1, 4, dwo[r * BLK : (r + 1) * BLK])
    for i, value in enumerate((dbo, dg1, dc1, db2, dg2, dc2, zero, zero)):
        sums_ref[i : i + 1, :] = value


def ffn_grad(e, n2, i2, n1, i1, y, hid, slope, o, vec, wout, wffn):
    rows = e.shape[0]
    return pl.pallas_call(
        ffn_grad_kernel,
        out_shape=[
            shape((2, 32, BLK, BLK), bf16),
            shape((2, 32, BLK, BLK), bf16),
            shape((2, 4, BLK, BLK), bf16),
            shape((2, 4, BLK, BLK), bf16),
            shape((rows, D)),
            shape((rows, D), bf16),
            shape((FF // D, D)),
            shape((8, D)),
        ],
        scratch_shapes=[
            pltpu.VMEM((D, D), bf16),
            pltpu.VMEM((D, FF), bf16),
            pltpu.VMEM((FF, D), bf16),
            pltpu.VMEM((rows, D), f32),
            pltpu.VMEM((rows, D), bf16),
            pltpu.VMEM((rows, FF), bf16),
            pltpu.VMEM((rows, D), bf16),
        ],
        compiler_params=params(),
        name="ffn_grad",
        cost_estimate=cost(16),
    )(e, n2, i2, n1, i1, y, hid, slope, o, vec, *wout, *wffn)


def attend_grad_kernel(
    q_ref, k_ref, kp_ref, v_ref, vp_ref, do_ref, o_ref, lse_ref, ohq_ref, ohk_ref,
    dq_ref, dk_ref, dkp_ref, dv_ref, dvp_ref,
    ka, va, qa, da, kt,
):
    rows = q_ref.shape[0]
    ka[:rows, :LANES] = k_ref[...]
    ka[rows:, :LANES] = kp_ref[...]
    ka[:, LANES:] = ohk_ref[...]
    va[:rows, :LANES] = v_ref[...]
    va[rows:, :LANES] = vp_ref[...]
    va[:, LANES:] = jnp.ones((2 * rows, LANES), bf16)
    kt[...] = ka[:, :LANES].T
    product = do_ref[...].astype(f32) * o_ref[...].astype(f32)
    for i in range(2):
        m = half_mask(i)
        qa[i, :, :LANES] = q_ref[...] * (m * bf16(0.125))
        qa[i, :, LANES:] = lanes_with(
            ohq_ref[...].astype(f32), 120, three_terms(-lse_ref[:, i : i + 1])
        )
        da[i, :, :LANES] = do_ref[...] * m
        delta = jnp.sum(product * half_mask(i, f32), axis=1, keepdims=True)
        da[i, :, LANES:] = lanes_with(jnp.zeros((rows, LANES), f32), 0, three_terms(-delta))

    def tile(t, sums):
        at = pl.ds(pl.multiple_of(t * ROW_TILE, ROW_TILE), ROW_TILE)
        dk = jnp.zeros((ROW_TILE, LANES), f32)
        dv = jnp.zeros((ROW_TILE, LANES), f32)
        new = []
        for i in range(2):
            p = jnp.exp(dot(ka[at], qa[i], 1, 1))
            ds = (p * dot(va[at], da[i], 1, 1)).astype(bf16)
            dv = dv + dot(p.astype(bf16), da[i, :, :LANES])
            dk = dk + dot(ds, qa[i, :, :LANES])
            new.append(sums[i] + dot(kt[:, at], ds))
        return tuple(new), dk.astype(bf16), dv.astype(bf16)

    sums = (jnp.zeros((LANES, rows), f32),) * 2
    half = rows // ROW_TILE

    def own(t, sums):
        sums, dk, dv = tile(t, sums)
        at = pl.ds(t * ROW_TILE, ROW_TILE)
        dk_ref[at] = dk
        dv_ref[at] = dv
        return sums

    def other(t, sums):
        sums, dk, dv = tile(t + half, sums)
        at = pl.ds(t * ROW_TILE, ROW_TILE)
        dkp_ref[at] = dk
        dvp_ref[at] = dv
        return sums

    sums = lax.fori_loop(0, half, own, sums)
    sums = lax.fori_loop(0, half, other, sums)
    row = lax.broadcasted_iota(jnp.int32, (LANES, rows), 0)
    dq_ref[...] = (jnp.where(row < HD, sums[0], sums[1]) * 0.125).T.astype(bf16)


def attend_grad(q, k, kp, v, vp, do, o, lse, ohq, ohk):
    rows = q.shape[0]
    pair = pl.BlockSpec((rows, LANES), lambda h: (0, h))
    other = pl.BlockSpec((rows, LANES), lambda h: (0, h + 1 - 2 * lax.rem(h, 2)))
    return pl.pallas_call(
        attend_grad_kernel,
        grid=(D // LANES,),
        in_specs=[pair, pair, other, pair, other, pair, pair, pair]
        + [
            pl.BlockSpec((rows, LANES), lambda h: (0, 0)),
            pl.BlockSpec((2 * rows, LANES), lambda h: (0, 0)),
        ],
        out_specs=[pair, pair, other, pair, other],
        out_shape=[shape((rows, D), bf16)] * 5,
        scratch_shapes=[
            pltpu.VMEM((2 * rows, 2 * LANES), bf16),
            pltpu.VMEM((2 * rows, 2 * LANES), bf16),
            pltpu.VMEM((2, rows, 2 * LANES), bf16),
            pltpu.VMEM((2, rows, 2 * LANES), bf16),
            pltpu.VMEM((LANES, 2 * rows), bf16),
        ],
        compiler_params=params(),
        name="attend_grad",
        cost_estimate=cost(23),
    )(q, k, kp, v, vp, do, o, lse, ohq, ohk)


def proj_grad_kernel(
    dq_ref, dk_ref, dv_ref, dkr_ref, dvr_ref, xs_ref, dr1_ref, w0, w1, w2, w3,
    gk_ref, gs_ref, dx_ref, sums_ref, w_s, dk_s, dv_s,
):
    place_qkv(w_s, (w0, w1, w2, w3))
    zero = jnp.zeros((1, D), f32)

    def tile(t, c):
        at = pl.ds(t * ROW_TILE, ROW_TILE)
        dq = dq_ref[at]
        dk = (dk_ref[at].astype(f32) + dkr_ref[at].astype(f32)).astype(bf16)
        dv = (dv_ref[at].astype(f32) + dvr_ref[at].astype(f32)).astype(bf16)
        dk_s[at] = dk
        dv_s[at] = dv
        dx_ref[at] = (
            dr1_ref[at]
            + dot(dq, w_s[:, :D], 1, 1)
            + dot(dk, w_s[:, D : 2 * D], 1, 1)
            + dot(dv, w_s[:, 2 * D :], 1, 1)
        )
        return (c[0] + col_sum(dq.astype(f32)), c[1] + col_sum(dv.astype(f32)))

    dbq, dbv = lax.fori_loop(0, xs_ref.shape[0] // ROW_TILE, tile, (zero, zero))
    sums_ref[0:1, :] = dbq
    sums_ref[1:2, :] = dbv
    sums_ref[2:8, :] = jnp.zeros((6, D), f32)
    for part, ref in enumerate((dq_ref, dk_s, dv_s)):
        grad = dot(xs_ref[...], ref[...], 0, 0).astype(bf16)
        for r in range(4):
            out = gs_ref if r % 2 else gk_ref
            for row in range(4):
                out[r // 2, row * 3 + part] = grad[row * BLK : (row + 1) * BLK, r * BLK : (r + 1) * BLK]


def proj_grad(dq, dk, dv, dkr, dvr, xs, dr1, wqkv):
    rows = xs.shape[0]
    return pl.pallas_call(
        proj_grad_kernel,
        out_shape=[
            shape((2, 12, BLK, BLK), bf16),
            shape((2, 12, BLK, BLK), bf16),
            shape((rows, D)),
            shape((8, D)),
        ],
        scratch_shapes=[
            pltpu.VMEM((D, 3 * D), bf16),
            pltpu.VMEM((rows, D), bf16),
            pltpu.VMEM((rows, D), bf16),
        ],
        compiler_params=params(),
        name="proj_grad",
        cost_estimate=cost(5),
    )(dq, dk, dv, dkr, dvr, xs, dr1, *wqkv)


def embed_grad_kernel(
    place_ref, series_ref, g_ref, we_ref, s0, q0, b0, s1, q1, b1, in_ref, keep_ref, send_ref, tab
):
    place = place_ref[0]
    g = g_ref[...]
    in_ref[...] = dot_hi(g, we_ref[...], 1, 1)
    tab[:LOOK] = dot_hi(series_ref[...].astype(f32), g, 0, 0)
    tab[LOOK : LOOK + 1] = col_sum(g)
    per_layer = 8 + FF // D
    for layer, (sums, qsums, db1) in enumerate(((s0, q0, b0), (s1, q1, b1))):
        base = LOOK + 1 + layer * per_layer
        for r in range(4):
            h = place ^ r
            lanes = pl.ds(pl.multiple_of(h * BLK, BLK), BLK)
            tab[base : base + 2, lanes] = qsums[0:2, r * BLK : (r + 1) * BLK]
            tab[pl.ds(base + 5 + h, 1), :] = db1[r : r + 1, :]
        tab[base + 2 : base + 5] = sums[0:3]
        tab[base + 5 + FF // D : base + per_layer] = sums[3:6]
    used = LOOK + 1 + LAYERS * per_layer
    tab[used:] = jnp.zeros((BLK - used, D), f32)
    for r in range(4):
        rows = tab[pl.ds(pl.multiple_of((place ^ r) * 32, 32), 32), :].astype(bf16)
        out = send_ref if r % 2 else keep_ref
        for c in range(4):
            out[r // 2, c * 32 : (c + 1) * 32] = rows[:, c * BLK : (c + 1) * BLK]


def embed_grad(place, series, g, table, sums):
    rows = series.shape[0]
    spec = pl.BlockSpec(memory_space=pltpu.VMEM)
    return pl.pallas_call(
        embed_grad_kernel,
        in_specs=[pl.BlockSpec(memory_space=pltpu.SMEM)] + [spec] * 9,
        out_shape=[
            shape((rows, LOOK)),
            shape((2, BLK, BLK), bf16),
            shape((2, BLK, BLK), bf16),
        ],
        scratch_shapes=[pltpu.VMEM((BLK, D), f32)],
        compiler_params=params(),
        name="embed_grad",
        cost_estimate=cost(2),
    )(place, series, g, table[:LOOK], *sums)


def vector_kernel(at_ref, val_ref, first_ref, second_ref, *refs):
    count = len(refs) - 6
    parts = refs[:count]
    nv_ref, n1_ref, n2_ref, bias_ref, held, tab = refs[count:]
    share = BLK // count
    for k in range(count):
        held[k] = parts[k][...]
    for d in range(count):
        for h in range(4):
            c, i = divmod(d * share, 32)
            tab[h * 32 + i : h * 32 + i + share, c * BLK : (c + 1) * BLK] = held[
                at_ref[d], at_ref[count] ^ h
            ]
    used = val_ref.shape[0]
    grad = tab[:used]
    val = val_ref[...]
    first = 0.5 * first_ref[...] + 0.5 * grad
    second = 0.5 * second_ref[...] + 0.5 * grad * grad
    n1_ref[...] = first
    n2_ref[...] = second
    nv_ref[...] = val - rate_vector * (
        first / CORR / (jnp.sqrt(second / CORR) + adam_eps) + weight_decay * val
    )
    per_layer = 8 + FF // D
    for layer in range(LAYERS):
        base = LOOK + 1 + layer * per_layer
        bias_ref[2 * layer : 2 * layer + 1] = tab[base + 2 : base + 3]
        bias_ref[2 * layer + 1 : 2 * layer + 2] = tab[base + 5 + FF // D : base + 6 + FF // D]


def vector_update(at, values, first, second, parts):
    spec = pl.BlockSpec(memory_space=pltpu.VMEM)
    return pl.pallas_call(
        vector_kernel,
        in_specs=[pl.BlockSpec(memory_space=pltpu.SMEM)] + [spec] * (3 + len(parts)),
        out_shape=[shape(values.shape)] * 3 + [shape((2 * LAYERS, D))],
        scratch_shapes=[
            pltpu.VMEM((len(parts), 4, BLK // len(parts), BLK), f32),
            pltpu.VMEM((BLK, D), f32),
        ],
        compiler_params=params(),
        name="vector",
        cost_estimate=cost(2),
    )(at, values, first, second, *parts)


PARTS = ((0, 12), (12, 4), (16, 32))


def natural_kernel(at_ref, *refs):
    count = len(refs) - 7
    slots, outs, held = refs[:count], refs[count : count + 6], refs[-1]
    step = slots[0].shape[0]
    for i in range(count):
        held[i * step : (i + 1) * step] = slots[i][...]
    for i, out in enumerate(outs):
        layer, part = divmod(i, 3)
        first, n = PARTS[part]
        for j in range(n):
            out[j] = held[at_ref[layer * 48 + first + j]]


def natural_order(at, slots):
    total = sum(s.shape[0] for s in slots)
    spec = pl.BlockSpec(memory_space=pltpu.VMEM)
    return pl.pallas_call(
        natural_kernel,
        in_specs=[pl.BlockSpec(memory_space=pltpu.SMEM)] + [spec] * len(slots),
        out_shape=[shape((n, BLK, BLK), bf16) for _ in range(LAYERS) for _, n in PARTS],
        scratch_shapes=[pltpu.VMEM((total, BLK, BLK), bf16)],
        compiler_params=params(),
        name="natural",
        cost_estimate=cost(3),
    )(at, *slots)


def routed_kernel(at_ref, tab_ref, tabr_ref, *refs):
    own, got, out = refs[:6], refs[6:12], refs[12]
    count, span = out.shape[0], out.shape[1]
    share = BLK // count
    out[...] = jnp.zeros(out.shape, bf16)
    for i in range(6):
        layer, part = divmod(i, 3)
        first, n = PARTS[part]
        for j in range(n):
            place = at_ref[layer * 48 + first + j]
            who = at_ref[96 + layer * 48 + first + j]
            value = own[i][j].astype(f32) + got[i][j].astype(f32)
            out[who, pl.ds(pl.multiple_of(place * BLK, BLK), BLK), :] = value.astype(bf16)
    table = (tab_ref[...].astype(f32) + tabr_ref[...].astype(f32)).astype(bf16)
    for d in range(count):
        who = at_ref[192 + d]
        out[who, span - share : span, :] = table[d * share : (d + 1) * share]


def routed(at, table, table_got, own, got, count, slots_each):
    spec = pl.BlockSpec(memory_space=pltpu.VMEM)
    return pl.pallas_call(
        routed_kernel,
        in_specs=[pl.BlockSpec(memory_space=pltpu.SMEM)] + [spec] * 14,
        out_shape=shape((count, slots_each * BLK + BLK // count, BLK), bf16),
        compiler_params=params(),
        name="routed",
        cost_estimate=cost(4),
    )(at, table, table_got, *own, *got)


def routed_plain_kernel(at_ref, *refs):
    own, got, out = refs[:6], refs[6:12], refs[12]
    out[...] = jnp.zeros(out.shape, bf16)
    for i in range(6):
        layer, part = divmod(i, 3)
        first, n = PARTS[part]
        for j in range(n):
            place = at_ref[layer * 48 + first + j]
            who = at_ref[96 + layer * 48 + first + j]
            value = own[i][j].astype(f32) + got[i][j].astype(f32)
            out[who, pl.ds(pl.multiple_of(place * BLK, BLK), BLK), :] = value.astype(bf16)


def routed_plain(at, own, got, count, slots_each):
    spec = pl.BlockSpec(memory_space=pltpu.VMEM)
    return pl.pallas_call(
        routed_plain_kernel,
        in_specs=[pl.BlockSpec(memory_space=pltpu.SMEM)] + [spec] * 12,
        out_shape=shape((count, slots_each * BLK, BLK), bf16),
        compiler_params=params(),
        name="routed",
        cost_estimate=cost(4),
    )(at, *own, *got)


def ring_of(count):
    half = count // 2
    return [2 * i for i in range(half)] + [2 * (half - 1 - i) + 1 for i in range(half)]


def ring_shift(value, order, by):
    n = len(order)
    return lax.ppermute(value, "dp", [(order[i], order[(i + by) % n]) for i in range(n)])


def ring_gather(value, order):
    n = len(order)
    held = [value] + [None] * (n - 1)
    ahead = behind = value
    for step in range(1, n // 2 + 1):
        behind = ring_shift(behind, order, 1)
        held[n - step] = behind
        if step < n // 2:
            ahead = ring_shift(ahead, order, -1)
            held[step] = ahead
    return held


def ring_reduce(pieces, order):
    n = len(order)
    up = pieces[n // 2]
    down = pieces[n // 2 + 1]
    for step in range(1, n // 2 + 1):
        up = ring_shift(up, order, 1)
        if step < n // 2:
            up = add_low(up, pieces[n // 2 - step])
            down = ring_shift(down, order, -1)
            if step < n // 2 - 1:
                down = add_low(down, pieces[n // 2 + 1 + step])
    return pieces[0], up, down


def add_low(a, b):
    return (a.astype(f32) + b.astype(f32)).astype(bf16)


def core_swap(value):
    return lax.ppermute(value, "head", [(i, i ^ 1) for i in range(4)])


def far_swap(value):
    return lax.ppermute(value, "head", [(i, i ^ 2) for i in range(4)])


def tied(values, after):
    return lax.optimization_barrier((values, after))[0]


def one_hots(ids):
    lane = jnp.arange(LANES, dtype=jnp.int32)[None, :]
    same = ids[:, None] == lane
    return jnp.where(same, -BIG, 0.0).astype(bf16), jnp.where(same, 0.0, 1.0).astype(bf16)


def relative(row, place):
    pieces = row.reshape(4, -1)
    return jnp.take(pieces, jnp.arange(4) ^ place, axis=0).reshape(1, -1)


def on_device(
    series,
    cotangent,
    window_lengths,
    owner_list,
    master,
    first_moment,
    second_moment,
    left_stats,
    right_stats,
    left_basis,
    right_basis,
    vec_values,
    vec_first,
    vec_second,
):
    place = lax.axis_index("head")
    spot = lax.axis_index("dp")
    dp = lax.axis_size("dp")
    ringed = dp == 8
    rows = series.shape[0]
    own_slots = master.shape[1]
    buckets, win = window_lengths.shape
    bucket_rows = rows * 4 // buckets
    owner_row = owner_list[0]
    who = owner_row // own_slots
    if ringed:
        order = ring_of(dp)
        ring_at = jnp.asarray([order.index(d) for d in range(dp)], jnp.int32)
        who = (ring_at[who] - ring_at[spot]) % dp
    inner = owner_row % own_slots
    gather_at = who * own_slots + inner

    copies = master[0].astype(bf16)
    if ringed:
        slots = ring_gather(copies, order)
    else:
        slots = [lax.all_gather(copies, "dp", axis=0, tiled=True)]
    mine = natural_order(gather_at, slots)
    weights = []
    far = None
    for at in range(LAYERS):
        for group in ((0,), (1, 2)):
            group_own = [mine[3 * at + i] for i in group]
            ready = group_own if far is None else tied(group_own, far)
            far = [far_swap(one) for one in ready]
            for own, there in zip(group_own, far):
                weights.append([own, core_swap(own), there, core_swap(there)])

    windows = window_ids(window_lengths, bucket_rows)
    ids = windows.reshape(4, rows)
    own_ids = lax.dynamic_index_in_dim(ids, place, 0, False)
    pair_ids = lax.dynamic_index_in_dim(ids, place ^ 1, 0, False)
    ohq, ohk_own = one_hots(own_ids)
    ohk = jnp.concatenate([ohk_own, one_hots(pair_ids)[1]], axis=0)
    valid = (own_ids < win).astype(f32)[:, None]

    x = embed(series, vec_values)
    saved = []
    for layer in range(LAYERS):
        bq, bv, bo, g1, c1, b1, b2, g2, c2 = depth_vectors(vec_values, layer)
        wqkv, wout, wffn = weights[3 * layer : 3 * layer + 3]
        xs, q, k, v = project(x, relative(bq, place), relative(bv, place), wqkv)
        kp, vp = core_swap(k), core_swap(v)
        o, lse = attend(q, k, kp, v, vp, ohq, ohk)
        vec = jnp.stack([bo, g1, c1, b2, g2, c2, g2, c2])
        n1, i1, y, hid, slope, n2, i2, x = post(o, x, vec, relative(b1, place), wout, wffn)
        saved.append((xs, q, k, v, kp, vp, o, lse, vec, n1, i1, y, hid, slope, n2, i2))
    activations = x * valid
    grad = cotangent * valid

    own_sums = [None] * (3 * LAYERS)
    far_sums = [None] * (3 * LAYERS)
    table_rows = [None] * LAYERS

    def chip_sum(at, keep, got):
        own_sums[at] = add_low(keep[0], got[0])
        return add_low(keep[1], got[1])

    moving = []
    for layer in reversed(range(LAYERS)):
        xs, q, k, v, kp, vp, o, lse, vec, n1, i1, y, hid, slope, n2, i2 = saved[layer]
        wqkv, wout, wffn = weights[3 * layer : 3 * layer + 3]
        gk, gs, ok, os, dr1, do, db1, sums = ffn_grad(
            grad, n2, i2, n1, i1, y, hid, slope, o, vec, wout, wffn
        )
        got = [core_swap(gs), core_swap(os)]
        do, far = tied(
            (do, [chip_sum(3 * layer + 2, gk, got[0]), chip_sum(3 * layer + 1, ok, got[1])]), moving
        )
        far_sums[3 * layer + 2] = far_swap(far[0])
        far_sums[3 * layer + 1] = far_swap(far[1])
        do = tied(do, far)
        dq, dk, dkp, dv, dvp = attend_grad(q, k, kp, v, vp, do, o, lse, ohq, ohk)
        dkr, dvr = core_swap(dkp), core_swap(dvp)
        dkr, dvr = tied((dkr, dvr), far_sums[3 * layer + 1 : 3 * layer + 3])
        pk, ps, grad, qsums = proj_grad(dq, dk, dv, dkr, dvr, xs, dr1, wqkv)
        table_rows[layer] = (sums, qsums, db1)
        got = core_swap(ps)
        if layer:
            far = chip_sum(3 * layer, pk, got)
            grad = tied(grad, far)
            far_sums[3 * layer] = far_swap(far)
            moving = [far_sums[3 * layer]]
    input_grad, tab_keep, tab_send = embed_grad(
        place.astype(jnp.int32)[None], series, grad, vec_values, table_rows[0] + table_rows[1]
    )
    tab_got = core_swap(tab_send)
    far_sums[0] = far_swap(chip_sum(0, pk, got))
    tab_own = add_low(tab_keep[0], tab_got[0])
    tab_far = far_swap(add_low(tab_keep[1], tab_got[1]))
    if ringed:
        dist = (ring_at - ring_at[spot]) % dp
        at = jnp.concatenate([inner, who, dist]).astype(jnp.int32)
        pieces = routed(at, tab_own, tab_far, own_sums, far_sums, dp, own_slots)
        terms = ring_reduce([pieces[i] for i in range(dp)], order)
        grads = [t[: own_slots * BLK].reshape(own_slots, BLK, BLK) for t in terms]
        part = sum(t[own_slots * BLK :].astype(f32) for t in terms)
        group = jnp.stack(
            [part] + [lax.ppermute(part, "head", [(i, i ^ r) for i in range(4)]) for r in (1, 2, 3)]
        )
        grads = tied(grads, group)
        parts = [group] + [ring_shift(group, order, -k) for k in range(1, dp)]
        vec_at = jnp.concatenate([dist, place[None]]).astype(jnp.int32)
        vec_new_values, vec_new_first, vec_new_second, branch_bias_grads = vector_update(
            vec_at, vec_values, vec_first, vec_second, parts
        )
    else:
        at = jnp.concatenate([inner, who]).astype(jnp.int32)
        pieces = routed_plain(at, own_sums, far_sums, dp, own_slots)
        whole = lax.psum_scatter(pieces, "dp", scatter_dimension=0, tiled=True)
        grads = [whole.reshape(own_slots, BLK, BLK)]
        total = lax.psum(tab_own.astype(f32) + tab_far.astype(f32), "dp")
        shares = lax.all_gather(total, "head", axis=0)
        grad_table = shares.reshape(4, 4, 32, BLK).transpose(0, 2, 1, 3).reshape(BLK, D)
        grad_table = grad_table[: vec_values.shape[0]]
        vec_new_values, vec_new_first, vec_new_second = adamw_update(
            grad_table, vec_values, vec_first, vec_second
        )
        branch_bias_grads = branch_biases(grad_table)
    new_master, new_copy, new_first, new_second, new_left, new_right, left_next, right_next = soap(
        grads,
        master[0],
        first_moment[0],
        second_moment[0],
        left_stats[0],
        right_stats[0],
        left_basis[0],
        right_basis[0],
    )
    return (
        activations,
        input_grad,
        new_master[None],
        new_copy[None],
        new_first[None],
        new_second[None],
        new_left[None],
        new_right[None],
        left_next[None],
        right_next[None],
        vec_new_values,
        vec_new_first,
        vec_new_second,
        branch_bias_grads,
    )


def solution(mesh):
    placed = (
        P(("dp", "head"), None),
        P(("dp", "head"), None),
        P("dp", None),
        P("head", None),
        P("head", "dp", None, None),
        P("head", "dp", None, None),
        P("head", "dp", None, None),
        P("head", "dp", None, None),
        P("head", "dp", None, None),
        P("head", "dp", None, None),
        P("head", "dp", None, None),
        P(),
        P(),
        P(),
    )
    return jax.shard_map(
        on_device,
        mesh=mesh,
        in_specs=placed,
        out_specs=(
            P(("dp", "head"), None),
            P(("dp", "head"), None),
            P("head", "dp", None, None),
            P("head", "dp", None, None),
            P("head", "dp", None, None),
            P("head", "dp", None, None),
            P("head", "dp", None, None),
            P("head", "dp", None, None),
            P("head", "dp", None, None),
            P("head", "dp", None, None),
            P(),
            P(),
            P(),
            P(),
        ),
        check_vma=False,
    )
```

```python
import functools

import jax
import jax.numpy as jnp
from jax import lax
from jax.experimental import pallas as pl
from jax.experimental.pallas import tpu as pltpu
from jax.sharding import PartitionSpec as P

D = 512
HEADS = 8
HD = 64
FF = 2048
LOOK = 96
LAYERS = 2
BLK = 128
STEP = 10

f32 = jnp.float32
HI = lax.Precision.HIGHEST
norm_eps = 1e-05
beta_first = 0.5
beta_second = 0.5
beta_stats = 0.5
adam_eps = 1e-08
rate_matrix = 0.02
rate_vector = 0.15
weight_decay = 0.01


def window_ids(lengths, bucket_rows):
    bounds = jnp.cumsum(lengths, axis=1, dtype=jnp.int32)
    places = jnp.arange(bucket_rows, dtype=jnp.int32)
    return jnp.sum(
        (places[None, :, None] >= bounds[:, None, :]).astype(jnp.int32), axis=2, dtype=jnp.int32
    )


def depth_vectors(vec_table, layer_at):
    ff_ratio = FF // D
    base_row = LOOK + 1 + layer_at * (8 + ff_ratio)
    return (
        vec_table[base_row],
        vec_table[base_row + 1],
        vec_table[base_row + 2],
        vec_table[base_row + 3],
        vec_table[base_row + 4],
        vec_table[base_row + 5 : base_row + 5 + ff_ratio].reshape(FF),
        vec_table[base_row + 5 + ff_ratio],
        vec_table[base_row + 6 + ff_ratio],
        vec_table[base_row + 7 + ff_ratio],
    )


def dot_hi(a, b, ca, cb):
    return lax.dot_general(
        a, b, (((ca,), (cb,)), ((), ())), precision=HI, preferred_element_type=f32
    )


def terms(x, count):
    out = []
    for i in range(count):
        part = x.astype(jnp.bfloat16)
        out.append(part)
        if i < count - 1:
            x = x - part.astype(f32)
    return out


def dot_terms(a, b, ca, cb, full=False):
    a = terms(a, 3 if full else 2)
    b = terms(b, 3 if full else 2)
    dims = (((ca,), (cb,)), ((), ()))
    left = jnp.concatenate(a[:2], axis=ca)
    right = jnp.concatenate(
        [jnp.concatenate([b[0], b[1]], axis=cb), jnp.concatenate([b[1], b[0]], axis=cb)], axis=1 - cb
    )
    out = lax.dot_general(left, right, dims, preferred_element_type=f32)
    out = out[:, :BLK] + out[:, BLK:]
    if full:
        out = out + lax.dot_general(
            jnp.concatenate([a[0], a[2]], axis=ca),
            jnp.concatenate([b[2], b[0]], axis=cb),
            dims,
            preferred_element_type=f32,
        )
    return out


PANEL = 32


def qr_batch(a_ref, count):
    lane = lax.broadcasted_iota(jnp.int32, (1, 1, BLK), 2)
    sub8 = lax.broadcasted_iota(jnp.int32, (1, 8, 1), 1)
    sub = lax.broadcasted_iota(jnp.int32, (1, PANEL, 1), 1)
    for r0 in range(0, BLK, PANEL):
        tiles = [a_ref[:, r0 + 8 * t : r0 + 8 * t + 8, :] for t in range(PANEL // 8)]
        for k in range(PANEL):
            t0, s = divmod(k, 8)
            row = tiles[t0][:, s : s + 1, :]
            pn = (row + (lane == r0 + k).astype(f32)) * (1.0 / row[:, :, r0 + k : r0 + k + 1])
            for t in range(t0, PANEL // 8):
                c = tiles[t][:, :, r0 + k : r0 + k + 1]
                if t == t0:
                    if s == 7:
                        continue
                    c = jnp.where(sub8 > s, c, 0.0)
                tiles[t] = tiles[t] - c * pn
        done = jnp.concatenate(tiles, axis=1)
        diag = lane == sub + r0
        pivot = jnp.sum(jnp.where(diag, done, 0.0), axis=2, keepdims=True)
        done = jnp.where(diag, 1.0, jnp.where((lane > sub + r0) & (lane < r0 + PANEL), 0.0, done))
        done = done * lax.rsqrt(pivot)
        a_ref[:, r0 : r0 + PANEL, :] = done
        r1 = r0 + PANEL
        if r1 < BLK:
            lane2 = lax.broadcasted_iota(jnp.int32, (BLK - r1, BLK), 1)
            clear = (lane2 >= r0) & (lane2 < r1)
            z0, z1, z2 = terms(done, 3)
            left = jnp.concatenate([z0, z0, z0, z1, z1, z2], axis=1)
            right = jnp.concatenate([z0, z1, z2, z0, z1, z0], axis=1)
            for b in range(count):
                update = lax.dot_general(
                    left[b], right[b], (((0,), (0,)), ((), ())), preferred_element_type=f32
                )
                a_ref[b, r1:, :] = jnp.where(clear, 0.0, a_ref[b, r1:, :]) - update[r1:]


def soap_kernel(count, *refs):
    for s in range(refs[0].shape[0]):
        soap_slot(s, sum(ref[s].astype(f32) for ref in refs[:count]), *refs[count:])
    soap_finish(*refs[-4:])


def soap_slot(
    s, g, mas_ref, m1_ref, m2_ref, ls_ref, rs_ref, lb_ref, rb_ref,
    nm_ref, nc_ref, n1_ref, n2_ref, nl_ref, nr_ref, ql_ref, qr_ref, mat_ref, a_ref,
):
    group = mas_ref.shape[0]
    lb = lb_ref[s]
    rb = rb_ref[s]
    rot = dot_terms(dot_terms(lb, g, 0, 0), rb, 1, 0)
    n1 = 0.5 * m1_ref[s] + 0.5 * rot
    n2 = 0.5 * m2_ref[s] + 0.5 * rot * rot
    n1_ref[s] = n1
    n2_ref[s] = n2
    corr = 1.0 - 0.5**STEP
    ratio = n1 / corr / (jnp.sqrt(n2 / corr) + adam_eps)
    upd = dot_terms(dot_terms(lb, ratio, 1, 0), rb, 1, 1)
    mas = mas_ref[s]
    nm = mas - rate_matrix * (upd + weight_decay * mas)
    nm_ref[s] = nm
    nc_ref[s] = nm.astype(jnp.bfloat16)
    nl = 0.5 * ls_ref[s] + 0.5 * dot_terms(g, g, 1, 1)
    nr = 0.5 * rs_ref[s] + 0.5 * dot_terms(g, g, 0, 0)
    nl_ref[s] = nl
    nr_ref[s] = nr
    for side, (st, ba) in enumerate(((nl, lb), (nr, rb))):
        m = dot_terms(st, ba, 1, 0, True)
        m = m * lax.rsqrt(jnp.sum(m * m, axis=0, keepdims=True))
        at = 2 * (pl.program_id(0) * group + s) + side
        mat_ref[at] = m
        a_ref[at] = dot_terms(m, m, 0, 0, True)


def soap_finish(ql_ref, qr_ref, mat_ref, a_ref):
    @pl.when(pl.program_id(0) == pl.num_programs(0) - 1)
    def _():
        count = a_ref.shape[0]
        qr_batch(a_ref, count)
        keep = lax.broadcasted_iota(jnp.int32, (BLK, BLK), 1) <= lax.broadcasted_iota(
            jnp.int32, (BLK, BLK), 0
        )
        for j in range(count // 2):
            for side, ref in enumerate((ql_ref, qr_ref)):
                x = jnp.where(keep, a_ref[2 * j + side], 0.0)
                ref[j] = dot_terms(mat_ref[2 * j + side], x, 1, 1, True)


def soap(gs, master, m1, m2, ls, rs, lb, rb):
    n = master.shape[0]
    group = SOAP_GROUP if n % SOAP_GROUP == 0 else n
    one = pl.BlockSpec((group, BLK, BLK), lambda i: (i, 0, 0))
    whole = pl.BlockSpec((n, BLK, BLK), lambda i: (0, 0, 0))
    sh = jax.ShapeDtypeStruct((n, BLK, BLK), f32)
    shb = jax.ShapeDtypeStruct((n, BLK, BLK), jnp.bfloat16)
    return pl.pallas_call(
        functools.partial(soap_kernel, len(gs)),
        grid=(n // group,),
        in_specs=[one] * (len(gs) + 7),
        out_specs=[one] * 6 + [whole] * 2,
        out_shape=[sh, shb, sh, sh, sh, sh, sh, sh],
        scratch_shapes=[pltpu.VMEM((2 * n, BLK, BLK), f32)] * 2,
        compiler_params=pltpu.CompilerParams(vmem_limit_bytes=50 * 2**20),
        cost_estimate=pl.CostEstimate(flops=40 * 10**6, bytes_accessed=0, transcendentals=0),
        name="soap",
    )(*gs, master, m1, m2, ls, rs, lb, rb)


SOAP_GROUP = 2


bf16 = jnp.bfloat16
LANES = 128
ROW_TILE = 512
BIG = 1e30
CORR = 1.0 - 0.5**STEP


def params(mib=48):
    return pltpu.CompilerParams(vmem_limit_bytes=mib * 2**20)


def cost(micros):
    return pl.CostEstimate(flops=int(micros * 1e6), bytes_accessed=0, transcendentals=0)


def shape(dims, kind=f32):
    return jax.ShapeDtypeStruct(dims, kind)


def dot(a, b, ca=1, cb=0):
    return lax.dot_general(a, b, (((ca,), (cb,)), ((), ())), preferred_element_type=f32)


def place_blocks(dst, refs, first, rows, cols, row_step, col_step, col_base=0):
    for r, ref in enumerate(refs):
        for j in range(rows * cols):
            row, col = divmod(j, cols)
            r0 = r * row_step + row * BLK
            c0 = col_base + r * col_step + col * BLK
            dst[r0 : r0 + BLK, c0 : c0 + BLK] = ref[first + j]


def place_qkv(dst, refs):
    for r, ref in enumerate(refs):
        for j in range(12):
            row, col = divmod(j, 3)
            c0 = col * D + r * BLK
            dst[row * BLK : (row + 1) * BLK, c0 : c0 + BLK] = ref[j]


def layer_norm(resid):
    center = resid - jnp.mean(resid, axis=1, keepdims=True)
    inv = lax.rsqrt(jnp.mean(center * center, axis=1, keepdims=True) + norm_eps)
    return center * inv, inv


def layer_norm_grad(grad, unit, inv, gain):
    dn = grad * gain
    return inv * (
        dn
        - jnp.mean(dn, axis=1, keepdims=True)
        - unit * jnp.mean(dn * unit, axis=1, keepdims=True)
    )


def col_sum(values):
    return jnp.sum(values, axis=0, keepdims=True)


def embed_kernel(series_ref, we_ref, be_ref, x_ref):
    x_ref[...] = dot_hi(series_ref[...].astype(f32), we_ref[...], 1, 0) + be_ref[...]


def embed(series, table):
    rows = series.shape[0]
    return pl.pallas_call(
        embed_kernel, out_shape=shape((rows, D)), compiler_params=params(), name="embed"
    )(series, table[:LOOK], table[LOOK : LOOK + 1])


def proj_kernel(x_ref, bq_ref, bv_ref, w0, w1, w2, w3, xs_ref, q_ref, k_ref, v_ref, w_s):
    place_qkv(w_s, (w0, w1, w2, w3))

    def tile(t, c):
        at = pl.ds(t * ROW_TILE, ROW_TILE)
        xs = x_ref[at].astype(bf16)
        xs_ref[at] = xs
        q_ref[at] = (dot(xs, w_s[:, :D]) + bq_ref[...]).astype(bf16)
        k_ref[at] = dot(xs, w_s[:, D : 2 * D]).astype(bf16)
        v_ref[at] = (dot(xs, w_s[:, 2 * D :]) + bv_ref[...]).astype(bf16)
        return c

    lax.fori_loop(0, x_ref.shape[0] // ROW_TILE, tile, 0)


def project(x, bq, bv, wqkv):
    rows = x.shape[0]
    return pl.pallas_call(
        proj_kernel,
        out_shape=[shape((rows, D), bf16)] * 4,
        scratch_shapes=[pltpu.VMEM((D, 3 * D), bf16)],
        compiler_params=params(),
        name="project",
        cost_estimate=cost(3),
    )(x, bq, bv, *wqkv)


def half_mask(i, kind=bf16):
    lane = lax.broadcasted_iota(jnp.int32, (1, LANES), 1)
    return ((lane >= HD * i) & (lane < HD * (i + 1))).astype(f32).astype(kind)


def three_terms(col):
    first = col.astype(bf16).astype(f32)
    second = (col - first).astype(bf16).astype(f32)
    return first, second, col - first - second


def lanes_with(base, at, cols):
    lane = lax.broadcasted_iota(jnp.int32, base.shape, 1)
    for i, col in enumerate(cols):
        base = jnp.where(lane == at + i, col, base)
    return base.astype(bf16)


def attend_kernel(q_ref, k_ref, kp_ref, v_ref, vp_ref, ohq_ref, ohk_ref, o_ref, lse_ref, ka, va):
    rows = q_ref.shape[0]
    ka[:rows, :LANES] = k_ref[...]
    ka[rows:, :LANES] = kp_ref[...]
    ka[:, LANES:] = ohk_ref[...]
    lane = lax.broadcasted_iota(jnp.int32, (ROW_TILE, LANES), 1)
    for i in range(2):
        m = half_mask(i)
        va[i, :rows, :LANES] = v_ref[...] * m
        va[i, rows:, :LANES] = vp_ref[...] * m
        va[i, :, LANES:] = jnp.ones((2 * rows, LANES), bf16)

    def tile(t, c):
        at = pl.ds(t * ROW_TILE, ROW_TILE)
        total = jnp.zeros((ROW_TILE, LANES), f32)
        stat = jnp.zeros((ROW_TILE, LANES), f32)
        for i in range(2):
            qa = jnp.concatenate([q_ref[at] * (half_mask(i) * bf16(0.125)), ohq_ref[at]], axis=1)
            s = dot(qa, ka[...], 1, 1)
            high = jnp.max(s, axis=1, keepdims=True)
            e = jnp.exp(s - high).astype(bf16)
            out = dot(e, va[i])
            norm = out[:, LANES:]
            total = total + out[:, :LANES] / norm
            stat = jnp.where(lane == i, high + jnp.log(norm), stat)
        o_ref[at] = total.astype(bf16)
        lse_ref[at] = stat
        return c

    lax.fori_loop(0, rows // ROW_TILE, tile, 0)


def attend(q, k, kp, v, vp, ohq, ohk):
    rows = q.shape[0]
    pair = pl.BlockSpec((rows, LANES), lambda h: (0, h))
    other = pl.BlockSpec((rows, LANES), lambda h: (0, h + 1 - 2 * lax.rem(h, 2)))
    return pl.pallas_call(
        attend_kernel,
        grid=(D // LANES,),
        in_specs=[pair, pair, other, pair, other]
        + [
            pl.BlockSpec((rows, LANES), lambda h: (0, 0)),
            pl.BlockSpec((2 * rows, LANES), lambda h: (0, 0)),
        ],
        out_specs=[pair, pair],
        out_shape=[shape((rows, D), bf16), shape((rows, D))],
        scratch_shapes=[
            pltpu.VMEM((2 * rows, 2 * LANES), bf16),
            pltpu.VMEM((2, 2 * rows, 2 * LANES), bf16),
        ],
        compiler_params=params(),
        name="attend",
        cost_estimate=cost(11),
    )(q, k, kp, v, vp, ohq, ohk)


def post_kernel(
    o_ref, x_ref, vec_ref, b1_ref, a0, a1, a2, a3, f0, f1, f2, f3,
    n1_ref, i1_ref, y_ref, hid_ref, slope_ref, n2_ref, i2_ref, x2_ref,
    wo_s, w1_s, w2_s,
):
    place_blocks(wo_s, (a0, a1, a2, a3), 0, 1, 4, BLK, 0)
    place_blocks(w1_s, (a0, a1, a2, a3), 4, 4, 4, 0, D)
    place_blocks(w2_s, (f0, f1, f2, f3), 0, 4, 4, D, 0)

    def tile(t, c):
        at = pl.ds(t * ROW_TILE, ROW_TILE)
        vec = [vec_ref[i : i + 1, :] for i in range(6)]
        unit, inv = layer_norm(x_ref[at] + dot(o_ref[at], wo_s[...]) + vec[0])
        n1_ref[at] = unit
        i1_ref[at] = jnp.broadcast_to(inv, (ROW_TILE, LANES))
        y = unit * vec[1] + vec[2]
        yb = y.astype(bf16)
        y_ref[at] = yb
        fed = jnp.zeros((ROW_TILE, D), f32)
        for r in range(FF // D):
            cols = slice(r * D, (r + 1) * D)
            pre = dot(yb, w1_s[:, cols]) + b1_ref[:, cols]
            phi = 0.5 * (1.0 + lax.erf(pre * (0.5**0.5)))
            hid = (pre * phi).astype(bf16)
            hid_ref[at, cols] = hid
            slope_ref[at, cols] = (
                phi + pre * (jnp.exp(-0.5 * pre * pre) * 0.3989422804014327)
            ).astype(bf16)
            fed = fed + dot(hid, w2_s[cols, :])
        unit, inv = layer_norm(y + fed + vec[3])
        n2_ref[at] = unit
        i2_ref[at] = jnp.broadcast_to(inv, (ROW_TILE, LANES))
        x2_ref[at] = unit * vec[4] + vec[5]
        return c

    lax.fori_loop(0, x_ref.shape[0] // ROW_TILE, tile, 0)


def post(o, x, vec, b1, wmid, wdown):
    rows = x.shape[0]
    return pl.pallas_call(
        post_kernel,
        out_shape=[
            shape((rows, D)),
            shape((rows, LANES)),
            shape((rows, D), bf16),
            shape((rows, FF), bf16),
            shape((rows, FF), bf16),
            shape((rows, D)),
            shape((rows, LANES)),
            shape((rows, D)),
        ],
        scratch_shapes=[
            pltpu.VMEM((D, D), bf16),
            pltpu.VMEM((D, FF), bf16),
            pltpu.VMEM((FF, D), bf16),
        ],
        compiler_params=params(),
        name="post",
        cost_estimate=cost(11),
    )(o, x, vec, b1, *wmid, *wdown)


def store_blocks(refs, r, first, rows, cols, value):
    keep_ref, send_ref = refs
    ref = send_ref if r % 2 else keep_ref
    for j in range(rows * cols):
        row, col = divmod(j, cols)
        ref[r // 2, first + j] = value[row * BLK : (row + 1) * BLK, col * BLK : (col + 1) * BLK]


def ffn_grad_kernel(
    e_ref, n2_ref, i2_ref, n1_ref, i1_ref, y_ref, hid_ref, slope_ref, o_ref, vec_ref,
    a0, a1, a2, a3, f0, f1, f2, f3,
    gk_ref, gs_ref, ok_ref, os_ref, dr1_ref, do_ref, db1_ref, sums_ref,
    wo_s, w1_s, w2_s, dr2_s, dfr_s, dpre_s, dar_s,
):
    rows = e_ref.shape[0]
    place_blocks(wo_s, (a0, a1, a2, a3), 0, 1, 4, BLK, 0)
    place_blocks(w1_s, (a0, a1, a2, a3), 4, 4, 4, 0, D)
    place_blocks(w2_s, (f0, f1, f2, f3), 0, 4, 4, D, 0)
    tiles = rows // ROW_TILE
    gain_two = vec_ref[4:5, :]
    gain_one = vec_ref[1:2, :]
    zero = jnp.zeros((1, D), f32)

    def tile_two(t, c):
        at = pl.ds(t * ROW_TILE, ROW_TILE)
        grad = e_ref[at]
        unit = n2_ref[at]
        dr2 = layer_norm_grad(grad, unit, i2_ref[at, 0:1], gain_two)
        dr2_s[at] = dr2
        dfr_s[at] = dr2.astype(bf16)
        return (c[0] + col_sum(dr2), c[1] + col_sum(grad * unit), c[2] + col_sum(grad))

    db2, dg2, dc2 = lax.fori_loop(0, tiles, tile_two, (zero, zero, zero))

    for r in range(FF // D):
        cols = slice(r * D, (r + 1) * D)

        def tile_up(t, c):
            at = pl.ds(t * ROW_TILE, ROW_TILE)
            dh = dot(dfr_s[at], w2_s[cols, :], 1, 1)
            dpre = (dh * slope_ref[at, cols].astype(f32)).astype(bf16)
            dpre_s[at, cols] = dpre
            dr2_s[at] = dr2_s[at] + dot(dpre, w1_s[:, cols], 1, 1)
            return c + col_sum(dpre.astype(f32))

        db1_ref[r : r + 1, :] = lax.fori_loop(0, tiles, tile_up, zero)
        store_blocks((gk_ref, gs_ref), r, 0, 4, 4, dot(hid_ref[:, cols], dfr_s[...], 0, 0).astype(bf16))
        store_blocks((ok_ref, os_ref), r, 4, 4, 4, dot(y_ref[...], dpre_s[:, cols], 0, 0).astype(bf16))

    def tile_one(t, c):
        at = pl.ds(t * ROW_TILE, ROW_TILE)
        grad = dr2_s[at]
        unit = n1_ref[at]
        dr1 = layer_norm_grad(grad, unit, i1_ref[at, 0:1], gain_one)
        dr1_ref[at] = dr1
        dar = dr1.astype(bf16)
        dar_s[at] = dar
        do_ref[at] = dot(dar, wo_s[...], 1, 1).astype(bf16)
        return (c[0] + col_sum(dr1), c[1] + col_sum(grad * unit), c[2] + col_sum(grad))

    dbo, dg1, dc1 = lax.fori_loop(0, tiles, tile_one, (zero, zero, zero))
    dwo = dot(o_ref[...], dar_s[...], 0, 0).astype(bf16)
    for r in range(4):
        store_blocks((ok_ref, os_ref), r, 0, 1, 4, dwo[r * BLK : (r + 1) * BLK])
    for i, value in enumerate((dbo, dg1, dc1, db2, dg2, dc2, zero, zero)):
        sums_ref[i : i + 1, :] = value


def ffn_grad(e, n2, i2, n1, i1, y, hid, slope, o, vec, wmid, wdown):
    rows = e.shape[0]
    return pl.pallas_call(
        ffn_grad_kernel,
        out_shape=[
            shape((2, 16, BLK, BLK), bf16),
            shape((2, 16, BLK, BLK), bf16),
            shape((2, 20, BLK, BLK), bf16),
            shape((2, 20, BLK, BLK), bf16),
            shape((rows, D)),
            shape((rows, D), bf16),
            shape((FF // D, D)),
            shape((8, D)),
        ],
        scratch_shapes=[
            pltpu.VMEM((D, D), bf16),
            pltpu.VMEM((D, FF), bf16),
            pltpu.VMEM((FF, D), bf16),
            pltpu.VMEM((rows, D), f32),
            pltpu.VMEM((rows, D), bf16),
            pltpu.VMEM((rows, FF), bf16),
            pltpu.VMEM((rows, D), bf16),
        ],
        compiler_params=params(),
        name="ffn_grad",
        cost_estimate=cost(16),
    )(e, n2, i2, n1, i1, y, hid, slope, o, vec, *wmid, *wdown)


def attend_grad_kernel(
    q_ref, k_ref, kp_ref, v_ref, vp_ref, do_ref, o_ref, lse_ref, ohq_ref, ohk_ref,
    dq_ref, dk_ref, dkp_ref, dv_ref, dvp_ref,
    ka, va, qa, da, kt,
):
    rows = q_ref.shape[0]
    ka[:rows, :LANES] = k_ref[...]
    ka[rows:, :LANES] = kp_ref[...]
    ka[:, LANES:] = ohk_ref[...]
    va[:rows, :LANES] = v_ref[...]
    va[rows:, :LANES] = vp_ref[...]
    va[:, LANES:] = jnp.ones((2 * rows, LANES), bf16)
    kt[...] = ka[:, :LANES].T
    product = do_ref[...].astype(f32) * o_ref[...].astype(f32)
    for i in range(2):
        m = half_mask(i)
        qa[i, :, :LANES] = q_ref[...] * (m * bf16(0.125))
        qa[i, :, LANES:] = lanes_with(
            ohq_ref[...].astype(f32), 120, three_terms(-lse_ref[:, i : i + 1])
        )
        da[i, :, :LANES] = do_ref[...] * m
        delta = jnp.sum(product * half_mask(i, f32), axis=1, keepdims=True)
        da[i, :, LANES:] = lanes_with(jnp.zeros((rows, LANES), f32), 0, three_terms(-delta))

    def tile(t, sums):
        at = pl.ds(pl.multiple_of(t * ROW_TILE, ROW_TILE), ROW_TILE)
        dk = jnp.zeros((ROW_TILE, LANES), f32)
        dv = jnp.zeros((ROW_TILE, LANES), f32)
        new = []
        for i in range(2):
            p = jnp.exp(dot(ka[at], qa[i], 1, 1))
            ds = (p * dot(va[at], da[i], 1, 1)).astype(bf16)
            dv = dv + dot(p.astype(bf16), da[i, :, :LANES])
            dk = dk + dot(ds, qa[i, :, :LANES])
            new.append(sums[i] + dot(kt[:, at], ds))
        return tuple(new), dk.astype(bf16), dv.astype(bf16)

    sums = (jnp.zeros((LANES, rows), f32),) * 2
    half = rows // ROW_TILE

    def own(t, sums):
        sums, dk, dv = tile(t, sums)
        at = pl.ds(t * ROW_TILE, ROW_TILE)
        dk_ref[at] = dk
        dv_ref[at] = dv
        return sums

    def other(t, sums):
        sums, dk, dv = tile(t + half, sums)
        at = pl.ds(t * ROW_TILE, ROW_TILE)
        dkp_ref[at] = dk
        dvp_ref[at] = dv
        return sums

    sums = lax.fori_loop(0, half, own, sums)
    sums = lax.fori_loop(0, half, other, sums)
    row = lax.broadcasted_iota(jnp.int32, (LANES, rows), 0)
    dq_ref[...] = (jnp.where(row < HD, sums[0], sums[1]) * 0.125).T.astype(bf16)


def attend_grad(q, k, kp, v, vp, do, o, lse, ohq, ohk):
    rows = q.shape[0]
    pair = pl.BlockSpec((rows, LANES), lambda h: (0, h))
    other = pl.BlockSpec((rows, LANES), lambda h: (0, h + 1 - 2 * lax.rem(h, 2)))
    return pl.pallas_call(
        attend_grad_kernel,
        grid=(D // LANES,),
        in_specs=[pair, pair, other, pair, other, pair, pair, pair]
        + [
            pl.BlockSpec((rows, LANES), lambda h: (0, 0)),
            pl.BlockSpec((2 * rows, LANES), lambda h: (0, 0)),
        ],
        out_specs=[pair, pair, other, pair, other],
        out_shape=[shape((rows, D), bf16)] * 5,
        scratch_shapes=[
            pltpu.VMEM((2 * rows, 2 * LANES), bf16),
            pltpu.VMEM((2 * rows, 2 * LANES), bf16),
            pltpu.VMEM((2, rows, 2 * LANES), bf16),
            pltpu.VMEM((2, rows, 2 * LANES), bf16),
            pltpu.VMEM((LANES, 2 * rows), bf16),
        ],
        compiler_params=params(),
        name="attend_grad",
        cost_estimate=cost(23),
    )(q, k, kp, v, vp, do, o, lse, ohq, ohk)


def proj_grad_kernel(
    dq_ref, dk_ref, dv_ref, dkr_ref, dvr_ref, xs_ref, dr1_ref, w0, w1, w2, w3,
    gk_ref, gs_ref, dx_ref, sums_ref, w_s, dk_s, dv_s,
):
    place_qkv(w_s, (w0, w1, w2, w3))
    zero = jnp.zeros((1, D), f32)

    def tile(t, c):
        at = pl.ds(t * ROW_TILE, ROW_TILE)
        dq = dq_ref[at]
        dk = (dk_ref[at].astype(f32) + dkr_ref[at].astype(f32)).astype(bf16)
        dv = (dv_ref[at].astype(f32) + dvr_ref[at].astype(f32)).astype(bf16)
        dk_s[at] = dk
        dv_s[at] = dv
        dx_ref[at] = (
            dr1_ref[at]
            + dot(dq, w_s[:, :D], 1, 1)
            + dot(dk, w_s[:, D : 2 * D], 1, 1)
            + dot(dv, w_s[:, 2 * D :], 1, 1)
        )
        return (c[0] + col_sum(dq.astype(f32)), c[1] + col_sum(dv.astype(f32)))

    dbq, dbv = lax.fori_loop(0, xs_ref.shape[0] // ROW_TILE, tile, (zero, zero))
    sums_ref[0:1, :] = dbq
    sums_ref[1:2, :] = dbv
    sums_ref[2:8, :] = jnp.zeros((6, D), f32)
    for part, ref in enumerate((dq_ref, dk_s, dv_s)):
        grad = dot(xs_ref[...], ref[...], 0, 0).astype(bf16)
        for r in range(4):
            out = gs_ref if r % 2 else gk_ref
            for row in range(4):
                out[r // 2, row * 3 + part] = grad[row * BLK : (row + 1) * BLK, r * BLK : (r + 1) * BLK]


def proj_grad(dq, dk, dv, dkr, dvr, xs, dr1, wqkv):
    rows = xs.shape[0]
    return pl.pallas_call(
        proj_grad_kernel,
        out_shape=[
            shape((2, 12, BLK, BLK), bf16),
            shape((2, 12, BLK, BLK), bf16),
            shape((rows, D)),
            shape((8, D)),
        ],
        scratch_shapes=[
            pltpu.VMEM((D, 3 * D), bf16),
            pltpu.VMEM((rows, D), bf16),
            pltpu.VMEM((rows, D), bf16),
        ],
        compiler_params=params(),
        name="proj_grad",
        cost_estimate=cost(5),
    )(dq, dk, dv, dkr, dvr, xs, dr1, *wqkv)


def embed_grad_kernel(
    place_ref, series_ref, g_ref, we_ref, s0, q0, b0, s1, q1, b1, in_ref, keep_ref, send_ref, tab
):
    place = place_ref[0]
    g = g_ref[...]
    in_ref[...] = dot_hi(g, we_ref[...], 1, 1)
    tab[:LOOK] = dot_hi(series_ref[...].astype(f32), g, 0, 0)
    tab[LOOK : LOOK + 1] = col_sum(g)
    per_layer = 8 + FF // D
    for layer, (sums, qsums, db1) in enumerate(((s0, q0, b0), (s1, q1, b1))):
        base = LOOK + 1 + layer * per_layer
        for r in range(4):
            h = place ^ r
            lanes = pl.ds(pl.multiple_of(h * BLK, BLK), BLK)
            tab[base : base + 2, lanes] = qsums[0:2, r * BLK : (r + 1) * BLK]
            tab[pl.ds(base + 5 + h, 1), :] = db1[r : r + 1, :]
        tab[base + 2 : base + 5] = sums[0:3]
        tab[base + 5 + FF // D : base + per_layer] = sums[3:6]
    used = LOOK + 1 + LAYERS * per_layer
    tab[used:] = jnp.zeros((BLK - used, D), f32)
    for r in range(4):
        rows = tab[pl.ds(pl.multiple_of((place ^ r) * 32, 32), 32), :]
        out = send_ref if r % 2 else keep_ref
        for c in range(4):
            out[r // 2, c * 32 : (c + 1) * 32] = rows[:, c * BLK : (c + 1) * BLK]


def embed_grad(place, series, g, table, sums):
    rows = series.shape[0]
    spec = pl.BlockSpec(memory_space=pltpu.VMEM)
    return pl.pallas_call(
        embed_grad_kernel,
        in_specs=[pl.BlockSpec(memory_space=pltpu.SMEM)] + [spec] * 9,
        out_shape=[
            shape((rows, LOOK)),
            shape((2, BLK, BLK)),
            shape((2, BLK, BLK)),
        ],
        scratch_shapes=[pltpu.VMEM((BLK, D), f32)],
        compiler_params=params(),
        name="embed_grad",
        cost_estimate=cost(2),
    )(place, series, g, table[:LOOK], *sums)


def vector_kernel(
    place_ref, val_ref, first_ref, second_ref, p0, p1, p2, p3, nv_ref, n1_ref, n2_ref, bias_ref, tab
):
    for r, part in enumerate((p0, p1, p2, p3)):
        rows = pl.ds(pl.multiple_of((place_ref[0] ^ r) * 32, 32), 32)
        for c in range(4):
            tab[rows, c * BLK : (c + 1) * BLK] = part[c * 32 : (c + 1) * 32]
    grad = tab[: val_ref.shape[0]]
    val = val_ref[...]
    first = 0.5 * first_ref[...] + 0.5 * grad
    second = 0.5 * second_ref[...] + 0.5 * grad * grad
    n1_ref[...] = first
    n2_ref[...] = second
    nv_ref[...] = val - rate_vector * (
        first / CORR / (jnp.sqrt(second / CORR) + adam_eps) + weight_decay * val
    )
    per_layer = 8 + FF // D
    for layer in range(LAYERS):
        base = LOOK + 1 + layer * per_layer
        bias_ref[2 * layer : 2 * layer + 1] = tab[base + 2 : base + 3]
        bias_ref[2 * layer + 1 : 2 * layer + 2] = tab[base + 5 + FF // D : base + 6 + FF // D]


def vector_update(place, values, first, second, parts):
    spec = pl.BlockSpec(memory_space=pltpu.VMEM)
    return pl.pallas_call(
        vector_kernel,
        in_specs=[pl.BlockSpec(memory_space=pltpu.SMEM)] + [spec] * 7,
        out_shape=[shape(values.shape)] * 3 + [shape((2 * LAYERS, D))],
        scratch_shapes=[pltpu.VMEM((BLK, D), f32)],
        compiler_params=params(),
        name="vector",
        cost_estimate=cost(2),
    )(place, values, first, second, *parts)


PARTS = ((0, 12), (12, 20), (32, 16))


def natural_kernel(plan, at_ref, *refs):
    count = len(plan)
    slots, outs, held = refs[:count], refs[count:-1], refs[-1]
    for ref, start in zip(slots, plan):
        held[start : start + ref.shape[0]] = ref[...]
    for i, out in enumerate(outs):
        plane, rest = divmod(i, 3 * LAYERS)
        layer, part = divmod(rest, 3)
        first, n = PARTS[part]
        for j in range(n):
            out[j] = held[at_ref[plane * 96 + layer * 48 + first + j]]


def natural_order(at, slots, plan):
    total = sum(s.shape[0] for s in slots)
    spec = pl.BlockSpec(memory_space=pltpu.VMEM)
    return pl.pallas_call(
        functools.partial(natural_kernel, plan),
        in_specs=[pl.BlockSpec(memory_space=pltpu.SMEM)] + [spec] * len(slots),
        out_shape=[
            shape((n, BLK, BLK), bf16)
            for _ in range(at.shape[0] // 96 * LAYERS)
            for _, n in PARTS
        ],
        scratch_shapes=[pltpu.VMEM((total, BLK, BLK), bf16)],
        compiler_params=params(),
        name="natural",
        cost_estimate=cost(4),
    )(at, *slots)


def routed_kernel(at_ref, *refs):
    own, got, out = refs[:6], refs[6:12], refs[12]
    out[...] = jnp.zeros(out.shape, bf16)
    for i in range(6):
        layer, part = divmod(i, 3)
        first, n = PARTS[part]
        for j in range(n):
            place = at_ref[layer * 48 + first + j]
            who = at_ref[96 + layer * 48 + first + j]
            value = own[i][j].astype(f32) + got[i][j].astype(f32)
            out[who, pl.ds(pl.multiple_of(place * BLK, BLK), BLK), :] = value.astype(bf16)


def routed(at, own, got, count, slots_each):
    spec = pl.BlockSpec(memory_space=pltpu.VMEM)
    return pl.pallas_call(
        routed_kernel,
        in_specs=[pl.BlockSpec(memory_space=pltpu.SMEM)] + [spec] * 12,
        out_shape=shape((count, slots_each * BLK, BLK), bf16),
        compiler_params=params(),
        name="routed",
        cost_estimate=cost(4),
    )(at, *own, *got)


def ring_of(count):
    half = count // 2
    return [2 * i for i in range(half)] + [2 * (half - 1 - i) + 1 for i in range(half)]


def ring_shift(value, order, by):
    n = len(order)
    return lax.ppermute(value, "dp", [(order[i], order[(i + by) % n]) for i in range(n)])


def ring_gather(value, order):
    n = len(order)
    half = value.shape[0] // 2
    held = [(value, 0, 0)]
    ahead = behind = value
    for step in range(1, n // 2):
        behind = ring_shift(behind, order, 1)
        ahead = ring_shift(ahead, order, -1)
        held += [(behind, n - step, 0), (ahead, step, 0)]
    held.append((ring_shift(behind[:half], order, 1), n // 2, 0))
    held.append((ring_shift(ahead[half:], order, -1), n // 2, half))
    return held


def ring_reduce(pieces, order):
    n = len(order)
    half = pieces[0].shape[0] // 2
    up = ring_shift(pieces[n // 2][:half], order, 1)
    down = ring_shift(pieces[n // 2][half:], order, -1)
    for step in range(1, n // 2):
        near, far = pieces[n // 2 - step], pieces[n // 2 + step]
        if step == 1:
            up = jnp.concatenate([add_low(up, near[:half]), near[half:]], axis=0)
            down = jnp.concatenate([far[:half], add_low(down, far[half:])], axis=0)
        else:
            up, down = add_low(up, near), add_low(down, far)
        up, down = ring_shift(up, order, 1), ring_shift(down, order, -1)
    return pieces[0], up, down


def dp_sum(value, count):
    bit = 1
    while bit < count:
        value = value + lax.ppermute(value, "dp", [(i, i ^ bit) for i in range(count)])
        bit *= 2
    return value


def add_low(a, b):
    return (a.astype(f32) + b.astype(f32)).astype(bf16)


def core_swap(value):
    return lax.ppermute(value, "head", [(i, i ^ 1) for i in range(4)])


def far_swap(value):
    return lax.ppermute(value, "head", [(i, i ^ 2) for i in range(4)])


def tied(values, after):
    return lax.optimization_barrier((values, after))[0]


def one_hots(ids):
    lane = jnp.arange(LANES, dtype=jnp.int32)[None, :]
    same = ids[:, None] == lane
    return jnp.where(same, -BIG, 0.0).astype(bf16), jnp.where(same, 0.0, 1.0).astype(bf16)


def relative(row, place):
    pieces = row.reshape(4, -1)
    return jnp.take(pieces, jnp.arange(4) ^ place, axis=0).reshape(1, -1)


def on_device(
    series,
    cotangent,
    window_lengths,
    owner_list,
    master,
    first_moment,
    second_moment,
    left_stats,
    right_stats,
    left_basis,
    right_basis,
    vec_values,
    vec_first,
    vec_second,
):
    place = lax.axis_index("head")
    spot = lax.axis_index("dp")
    dp = lax.axis_size("dp")
    ringed = dp == 8
    rows = series.shape[0]
    own_slots = master.shape[1]
    buckets, win = window_lengths.shape
    bucket_rows = rows * 4 // buckets
    owner_row = owner_list[0]
    who = owner_row // own_slots
    if ringed:
        order = ring_of(dp)
        ring_at = jnp.asarray([order.index(d) for d in range(dp)], jnp.int32)
        who = (ring_at[who] - ring_at[spot]) % dp
    inner = owner_row % own_slots
    gather_at = who * own_slots + inner

    copies = master[0].astype(bf16)
    if ringed:
        held = ring_gather(copies, order)
        slots, plan = [x[0] for x in held], tuple(x[1] * own_slots + x[2] for x in held)
    else:
        slots, plan = [lax.all_gather(copies, "dp", axis=0, tiled=True)], (0,)
    windows = window_ids(window_lengths, bucket_rows)
    ids = windows.reshape(4, rows)
    own_ids = lax.dynamic_index_in_dim(ids, place, 0, False)
    pair_ids = lax.dynamic_index_in_dim(ids, place ^ 1, 0, False)
    ohq, ohk_own = one_hots(own_ids)
    ohk = jnp.concatenate([ohk_own, one_hots(pair_ids)[1]], axis=0)
    valid = (own_ids < win).astype(f32)[:, None]

    x = embed(series, vec_values)
    vectors = []
    for layer in range(LAYERS):
        bq, bv, bo, g1, c1, b1, b2, g2, c2 = depth_vectors(vec_values, layer)
        vec = jnp.stack([bo, g1, c1, b2, g2, c2, g2, c2])
        vectors.append([vec] + [relative(row, place) for row in (bq, bv, b1)])
    slots, (x, vectors, ohq, ohk, valid, gather_at) = lax.optimization_barrier(
        (slots, (x, vectors, ohq, ohk, valid, gather_at))
    )
    mine = natural_order(gather_at, slots, plan)
    moved = []

    def cross(i, after=None):
        own = mine[i] if after is None else tied(mine[i], after)
        moved.append(far_swap(own))
        return moved[-1]

    def four(i, after=None):
        there = moved[i] if after is None else tied(moved[i], after)
        return [mine[i], core_swap(mine[i]), there, core_swap(there)]

    weights = []
    saved = []
    for layer in range(LAYERS):
        vec, bq, bv, b1 = vectors[layer]
        if layer == 0:
            cross(0)
        wqkv = four(3 * layer, x if layer else None)
        x = tied(x, wqkv)
        if layer == 0:
            cross(1, moved[0])
            cross(2, moved[0])
        xs, q, k, v = project(x, bq, bv, wqkv)
        kp, vp = core_swap(k), core_swap(v)
        o, lse = attend(q, k, kp, v, vp, ohq, ohk)
        wmid, wdown = four(3 * layer + 1, o), four(3 * layer + 2, o)
        weights += [wqkv, wmid, wdown]
        if layer + 1 < LAYERS:
            done = moved[-1]
            for i in range(3):
                cross(3 * layer + 3 + i, done if i == 0 else (done, moved[3 * layer + 3]))
        n1, i1, y, hid, slope, n2, i2, x = post(o, x, vec, b1, wmid, wdown)
        saved.append((xs, q, k, v, kp, vp, o, lse, vec, n1, i1, y, hid, slope, n2, i2))
    activations = x * valid
    grad = cotangent * valid

    own_sums = [None] * (3 * LAYERS)
    far_sums = [None] * (3 * LAYERS)
    table_rows = [None] * LAYERS

    def chip_sum(at, keep, got):
        own_sums[at] = add_low(keep[0], got[0])
        return add_low(keep[1], got[1])

    moving = []
    for layer in reversed(range(LAYERS)):
        xs, q, k, v, kp, vp, o, lse, vec, n1, i1, y, hid, slope, n2, i2 = saved[layer]
        wqkv, wmid, wdown = weights[3 * layer : 3 * layer + 3]
        gk, gs, ok, os, dr1, do, db1, sums = ffn_grad(
            grad, n2, i2, n1, i1, y, hid, slope, o, vec, wmid, wdown
        )
        os, gs, ok, gk, do = tied((os, gs, ok, gk, do), moving)
        got = [core_swap(os), core_swap(gs)]
        mid = chip_sum(3 * layer + 1, ok, got[0])
        down = chip_sum(3 * layer + 2, gk, got[1])
        far_sums[3 * layer + 1] = far_swap(mid)
        do = tied(do, (mid, down))
        dq, dk, dkp, dv, dvp = attend_grad(q, k, kp, v, vp, do, o, lse, ohq, ohk)
        dkp, dvp = tied((dkp, dvp), far_sums[3 * layer + 1])
        far_sums[3 * layer + 2] = far_swap(tied(down, far_sums[3 * layer + 1]))
        dkr, dvr = core_swap(dkp), core_swap(dvp)
        pk, ps, grad, qsums = proj_grad(dq, dk, dv, dkr, dvr, xs, dr1, wqkv)
        table_rows[layer] = (sums, qsums, db1)
        got = core_swap(ps)
        if layer:
            far = chip_sum(3 * layer, pk, got)
            grad = tied(grad, far)
            far_sums[3 * layer] = far_swap(far)
            moving = far_sums[3 * layer : 3 * layer + 3]
    input_grad, tab_keep, tab_send = embed_grad(
        place.astype(jnp.int32)[None], series, grad, vec_values, table_rows[0] + table_rows[1]
    )
    far_sums[0] = far_swap(chip_sum(0, pk, got))
    tab = dp_sum(tab_keep + core_swap(tab_send), dp)
    own_sums[0] = tied(own_sums[0], tab)
    tab_part = tab[0] + far_swap(tab[1])
    tab_there = far_swap(tab_part)
    parts = [tab_part, core_swap(tab_part), tab_there, core_swap(tab_there)]
    at = jnp.concatenate([inner, who]).astype(jnp.int32)
    pieces = routed(at, own_sums, far_sums, dp, own_slots)
    if ringed:
        terms = ring_reduce([pieces[i] for i in range(dp)], order)
        grads = [t.reshape(own_slots, BLK, BLK) for t in terms]
    else:
        whole = lax.psum_scatter(pieces, "dp", scatter_dimension=0, tiled=True)
        grads = [whole.reshape(own_slots, BLK, BLK)]
    vec_new_values, vec_new_first, vec_new_second, branch_bias_grads = vector_update(
        place.astype(jnp.int32)[None], vec_values, vec_first, vec_second, parts
    )
    new_master, new_copy, new_first, new_second, new_left, new_right, left_next, right_next = soap(
        grads,
        master[0],
        first_moment[0],
        second_moment[0],
        left_stats[0],
        right_stats[0],
        left_basis[0],
        right_basis[0],
    )
    return (
        activations,
        input_grad,
        new_master[None],
        new_copy[None],
        new_first[None],
        new_second[None],
        new_left[None],
        new_right[None],
        left_next[None],
        right_next[None],
        vec_new_values,
        vec_new_first,
        vec_new_second,
        branch_bias_grads,
    )


def solution(mesh):
    placed = (
        P(("dp", "head"), None),
        P(("dp", "head"), None),
        P("dp", None),
        P("head", None),
        P("head", "dp", None, None),
        P("head", "dp", None, None),
        P("head", "dp", None, None),
        P("head", "dp", None, None),
        P("head", "dp", None, None),
        P("head", "dp", None, None),
        P("head", "dp", None, None),
        P(),
        P(),
        P(),
    )
    return jax.shard_map(
        on_device,
        mesh=mesh,
        in_specs=placed,
        out_specs=(
            P(("dp", "head"), None),
            P(("dp", "head"), None),
            P("head", "dp", None, None),
            P("head", "dp", None, None),
            P("head", "dp", None, None),
            P("head", "dp", None, None),
            P("head", "dp", None, None),
            P("head", "dp", None, None),
            P("head", "dp", None, None),
            P("head", "dp", None, None),
            P(),
            P(),
            P(),
            P(),
        ),
        check_vma=False,
    )
```

```python
import functools

import jax
import jax.numpy as jnp
from jax import lax
from jax.experimental import pallas as pl
from jax.experimental.pallas import tpu as pltpu
from jax.sharding import PartitionSpec as P

D = 512
HEADS = 8
HD = 64
FF = 2048
LOOK = 96
LAYERS = 2
BLK = 128
STEP = 10

f32 = jnp.float32
HI = lax.Precision.HIGHEST
norm_eps = 1e-05
beta_first = 0.5
beta_second = 0.5
beta_stats = 0.5
adam_eps = 1e-08
rate_matrix = 0.02
rate_vector = 0.15
weight_decay = 0.01


def window_ids(lengths, bucket_rows):
    bounds = jnp.cumsum(lengths, axis=1, dtype=jnp.int32)
    places = jnp.arange(bucket_rows, dtype=jnp.int32)
    return jnp.sum(
        (places[None, :, None] >= bounds[:, None, :]).astype(jnp.int32), axis=2, dtype=jnp.int32
    )


def depth_vectors(vec_table, layer_at):
    ff_ratio = FF // D
    base_row = LOOK + 1 + layer_at * (8 + ff_ratio)
    return (
        vec_table[base_row],
        vec_table[base_row + 1],
        vec_table[base_row + 2],
        vec_table[base_row + 3],
        vec_table[base_row + 4],
        vec_table[base_row + 5 : base_row + 5 + ff_ratio].reshape(FF),
        vec_table[base_row + 5 + ff_ratio],
        vec_table[base_row + 6 + ff_ratio],
        vec_table[base_row + 7 + ff_ratio],
    )


def dot_hi(a, b, ca, cb):
    return lax.dot_general(
        a, b, (((ca,), (cb,)), ((), ())), precision=HI, preferred_element_type=f32
    )


def terms(x, count):
    out = []
    for i in range(count):
        part = x.astype(jnp.bfloat16)
        out.append(part)
        if i < count - 1:
            x = x - part.astype(f32)
    return out


def dot_terms(a, b, ca, cb, full=False):
    a = terms(a, 3 if full else 2)
    b = terms(b, 3 if full else 2)
    dims = (((ca,), (cb,)), ((), ()))
    left = jnp.concatenate(a[:2], axis=ca)
    right = jnp.concatenate(
        [jnp.concatenate([b[0], b[1]], axis=cb), jnp.concatenate([b[1], b[0]], axis=cb)], axis=1 - cb
    )
    out = lax.dot_general(left, right, dims, preferred_element_type=f32)
    out = out[:, :BLK] + out[:, BLK:]
    if full:
        out = out + lax.dot_general(
            jnp.concatenate([a[0], a[2]], axis=ca),
            jnp.concatenate([b[2], b[0]], axis=cb),
            dims,
            preferred_element_type=f32,
        )
    return out


PANEL = 32
AHEAD = 2


def recip(x):
    guess = pl.reciprocal(x, approx=True)
    guess = guess * (2.0 - x * guess)
    return guess * (2.0 - x * guess)


def qr_batch(a_ref, count):
    lane = lax.broadcasted_iota(jnp.int32, (1, 1, BLK), 2)
    sub8 = lax.broadcasted_iota(jnp.int32, (1, 8, 1), 1)
    sub = lax.broadcasted_iota(jnp.int32, (1, PANEL, 1), 1)
    for r0 in range(0, BLK, PANEL):
        tiles = [a_ref[:, r0 + 8 * t : r0 + 8 * t + 8, :] for t in range(PANEL // 8)]
        for k0 in range(0, PANEL, AHEAD):
            t0, s0 = divmod(k0, 8)
            cols = [
                [
                    jnp.broadcast_to(tiles[t][:, :, r0 + k : r0 + k + 1], (count, 8, BLK))
                    for k in range(k0, k0 + AHEAD)
                ]
                for t in range(PANEL // 8)
            ]
            for i in range(AHEAD):
                s = s0 + i
                inv = recip(cols[t0][i][:, s : s + 1, :])
                pn = (tiles[t0][:, s : s + 1, :] + (lane == r0 + k0 + i).astype(f32)) * inv
                rest = [cols[t0][j][:, s : s + 1, :] * inv for j in range(i + 1, AHEAD)]
                for t in range(t0, PANEL // 8):
                    c = cols[t][i]
                    if t == t0:
                        if s == 7:
                            continue
                        c = jnp.where(sub8 > s, c, 0.0)
                    tiles[t] = tiles[t] - c * pn
                    for j, m in enumerate(rest):
                        cols[t][i + 1 + j] = cols[t][i + 1 + j] - c * m
        done = jnp.concatenate(tiles, axis=1)
        diag = lane == sub + r0
        pivot = jnp.sum(jnp.where(diag, done, 0.0), axis=2, keepdims=True)
        done = jnp.where(diag, 1.0, jnp.where((lane > sub + r0) & (lane < r0 + PANEL), 0.0, done))
        done = done * lax.rsqrt(pivot)
        a_ref[:, r0 : r0 + PANEL, :] = done
        r1 = r0 + PANEL
        if r1 < BLK:
            lane2 = lax.broadcasted_iota(jnp.int32, (BLK - r1, BLK), 1)
            clear = (lane2 >= r0) & (lane2 < r1)
            z0, z1, z2 = terms(done, 3)
            left = jnp.concatenate([z0, z0, z0, z1, z1, z2], axis=1)
            right = jnp.concatenate([z0, z1, z2, z0, z1, z0], axis=1)
            for b in range(count):
                update = lax.dot_general(
                    left[b], right[b], (((0,), (0,)), ((), ())), preferred_element_type=f32
                )
                a_ref[b, r1:, :] = jnp.where(clear, 0.0, a_ref[b, r1:, :]) - update[r1:]


def soap_kernel(count, *refs):
    for s in range(refs[0].shape[0]):
        soap_slot(s, sum(ref[s].astype(f32) for ref in refs[:count]), *refs[count:])
    soap_finish(*refs[-4:])


def soap_slot(
    s, g, mas_ref, m1_ref, m2_ref, ls_ref, rs_ref, lb_ref, rb_ref,
    nm_ref, nc_ref, n1_ref, n2_ref, nl_ref, nr_ref, ql_ref, qr_ref, mat_ref, a_ref,
):
    group = mas_ref.shape[0]
    lb = lb_ref[s]
    rb = rb_ref[s]
    rot = dot_terms(dot_terms(lb, g, 0, 0), rb, 1, 0)
    n1 = 0.5 * m1_ref[s] + 0.5 * rot
    n2 = 0.5 * m2_ref[s] + 0.5 * rot * rot
    n1_ref[s] = n1
    n2_ref[s] = n2
    corr = 1.0 - 0.5**STEP
    ratio = n1 / corr / (jnp.sqrt(n2 / corr) + adam_eps)
    upd = dot_terms(dot_terms(lb, ratio, 1, 0), rb, 1, 1)
    mas = mas_ref[s]
    nm = mas - rate_matrix * (upd + weight_decay * mas)
    nm_ref[s] = nm
    nc_ref[s] = nm.astype(jnp.bfloat16)
    nl = 0.5 * ls_ref[s] + 0.5 * dot_terms(g, g, 1, 1)
    nr = 0.5 * rs_ref[s] + 0.5 * dot_terms(g, g, 0, 0)
    nl_ref[s] = nl
    nr_ref[s] = nr
    for side, (st, ba) in enumerate(((nl, lb), (nr, rb))):
        m = dot_terms(st, ba, 1, 0, True)
        m = m * lax.rsqrt(jnp.sum(m * m, axis=0, keepdims=True))
        at = 2 * (pl.program_id(0) * group + s) + side
        mat_ref[at] = m
        a_ref[at] = dot_terms(m, m, 0, 0, True)


def soap_finish(ql_ref, qr_ref, mat_ref, a_ref):
    @pl.when(pl.program_id(0) == pl.num_programs(0) - 1)
    def _():
        count = a_ref.shape[0]
        qr_batch(a_ref, count)
        keep = lax.broadcasted_iota(jnp.int32, (BLK, BLK), 1) <= lax.broadcasted_iota(
            jnp.int32, (BLK, BLK), 0
        )
        for j in range(count // 2):
            for side, ref in enumerate((ql_ref, qr_ref)):
                x = jnp.where(keep, a_ref[2 * j + side], 0.0)
                ref[j] = dot_terms(mat_ref[2 * j + side], x, 1, 1, True)


def soap(gs, master, m1, m2, ls, rs, lb, rb):
    n = master.shape[0]
    group = SOAP_GROUP if n % SOAP_GROUP == 0 else n
    one = pl.BlockSpec((group, BLK, BLK), lambda i: (i, 0, 0))
    whole = pl.BlockSpec((n, BLK, BLK), lambda i: (0, 0, 0))
    sh = jax.ShapeDtypeStruct((n, BLK, BLK), f32)
    shb = jax.ShapeDtypeStruct((n, BLK, BLK), jnp.bfloat16)
    return pl.pallas_call(
        functools.partial(soap_kernel, len(gs)),
        grid=(n // group,),
        in_specs=[one] * (len(gs) + 7),
        out_specs=[one] * 6 + [whole] * 2,
        out_shape=[sh, shb, sh, sh, sh, sh, sh, sh],
        scratch_shapes=[pltpu.VMEM((2 * n, BLK, BLK), f32)] * 2,
        compiler_params=pltpu.CompilerParams(vmem_limit_bytes=50 * 2**20),
        cost_estimate=pl.CostEstimate(flops=40 * 10**6, bytes_accessed=0, transcendentals=0),
        name="soap",
    )(*gs, master, m1, m2, ls, rs, lb, rb)


SOAP_GROUP = 2


bf16 = jnp.bfloat16
LANES = 128
ROW_TILE = 512
BIG = 1e30
CORR = 1.0 - 0.5**STEP


def params(mib=48):
    return pltpu.CompilerParams(vmem_limit_bytes=mib * 2**20)


def cost(micros):
    return pl.CostEstimate(flops=int(micros * 1e6), bytes_accessed=0, transcendentals=0)


def shape(dims, kind=f32):
    return jax.ShapeDtypeStruct(dims, kind)


def dot(a, b, ca=1, cb=0):
    return lax.dot_general(a, b, (((ca,), (cb,)), ((), ())), preferred_element_type=f32)


def place_blocks(dst, refs, first, rows, cols, row_step, col_step, col_base=0):
    for r, ref in enumerate(refs):
        for j in range(rows * cols):
            row, col = divmod(j, cols)
            r0 = r * row_step + row * BLK
            c0 = col_base + r * col_step + col * BLK
            dst[r0 : r0 + BLK, c0 : c0 + BLK] = ref[first + j]


def place_qkv(dst, refs):
    for r, ref in enumerate(refs):
        for j in range(12):
            row, col = divmod(j, 3)
            c0 = col * D + r * BLK
            dst[row * BLK : (row + 1) * BLK, c0 : c0 + BLK] = ref[j]


def layer_norm(resid):
    center = resid - jnp.mean(resid, axis=1, keepdims=True)
    inv = lax.rsqrt(jnp.mean(center * center, axis=1, keepdims=True) + norm_eps)
    return center * inv, inv


def layer_norm_grad(grad, unit, inv, gain):
    dn = grad * gain
    return inv * (
        dn
        - jnp.mean(dn, axis=1, keepdims=True)
        - unit * jnp.mean(dn * unit, axis=1, keepdims=True)
    )


def col_sum(values):
    return jnp.sum(values, axis=0, keepdims=True)


def embed_kernel(series_ref, we_ref, be_ref, x_ref):
    x_ref[...] = dot_hi(series_ref[...].astype(f32), we_ref[...], 1, 0) + be_ref[...]


def embed(series, table):
    rows = series.shape[0]
    return pl.pallas_call(
        embed_kernel, out_shape=shape((rows, D)), compiler_params=params(), name="embed"
    )(series, table[:LOOK], table[LOOK : LOOK + 1])


def proj_kernel(x_ref, bq_ref, bv_ref, w0, w1, w2, w3, xs_ref, q_ref, k_ref, v_ref, w_s):
    place_qkv(w_s, (w0, w1, w2, w3))

    def tile(t, c):
        at = pl.ds(t * ROW_TILE, ROW_TILE)
        xs = x_ref[at].astype(bf16)
        xs_ref[at] = xs
        q_ref[at] = (dot(xs, w_s[:, :D]) + bq_ref[...]).astype(bf16)
        k_ref[at] = dot(xs, w_s[:, D : 2 * D]).astype(bf16)
        v_ref[at] = (dot(xs, w_s[:, 2 * D :]) + bv_ref[...]).astype(bf16)
        return c

    lax.fori_loop(0, x_ref.shape[0] // ROW_TILE, tile, 0)


def project(x, bq, bv, wqkv):
    rows = x.shape[0]
    return pl.pallas_call(
        proj_kernel,
        out_shape=[shape((rows, D), bf16)] * 4,
        scratch_shapes=[pltpu.VMEM((D, 3 * D), bf16)],
        compiler_params=params(),
        name="project",
        cost_estimate=cost(3),
    )(x, bq, bv, *wqkv)


def half_mask(i, kind=bf16):
    lane = lax.broadcasted_iota(jnp.int32, (1, LANES), 1)
    return ((lane >= HD * i) & (lane < HD * (i + 1))).astype(f32).astype(kind)


def three_terms(col):
    first = col.astype(bf16).astype(f32)
    second = (col - first).astype(bf16).astype(f32)
    return first, second, col - first - second


def lanes_with(base, at, cols):
    lane = lax.broadcasted_iota(jnp.int32, base.shape, 1)
    for i, col in enumerate(cols):
        base = jnp.where(lane == at + i, col, base)
    return base.astype(bf16)


def attend_kernel(q_ref, k_ref, kp_ref, v_ref, vp_ref, ohq_ref, ohk_ref, o_ref, lse_ref, ka, va):
    rows = q_ref.shape[0]
    ka[:rows, :LANES] = k_ref[...]
    ka[rows:, :LANES] = kp_ref[...]
    ka[:, LANES:] = ohk_ref[...]
    lane = lax.broadcasted_iota(jnp.int32, (ROW_TILE, LANES), 1)
    for i in range(2):
        m = half_mask(i)
        va[i, :rows, :LANES] = v_ref[...] * m
        va[i, rows:, :LANES] = vp_ref[...] * m
        va[i, :, LANES:] = jnp.ones((2 * rows, LANES), bf16)

    def tile(t, c):
        at = pl.ds(t * ROW_TILE, ROW_TILE)
        total = jnp.zeros((ROW_TILE, LANES), f32)
        stat = jnp.zeros((ROW_TILE, LANES), f32)
        for i in range(2):
            qa = jnp.concatenate([q_ref[at] * (half_mask(i) * bf16(0.125)), ohq_ref[at]], axis=1)
            s = dot(qa, ka[...], 1, 1)
            high = jnp.max(s, axis=1, keepdims=True)
            e = jnp.exp(s - high).astype(bf16)
            out = dot(e, va[i])
            norm = out[:, LANES:]
            total = total + out[:, :LANES] / norm
            stat = jnp.where(lane == i, high + jnp.log(norm), stat)
        o_ref[at] = total.astype(bf16)
        lse_ref[at] = stat
        return c

    lax.fori_loop(0, rows // ROW_TILE, tile, 0)


def attend(q, k, kp, v, vp, ohq, ohk):
    rows = q.shape[0]
    pair = pl.BlockSpec((rows, LANES), lambda h: (0, h))
    other = pl.BlockSpec((rows, LANES), lambda h: (0, h + 1 - 2 * lax.rem(h, 2)))
    return pl.pallas_call(
        attend_kernel,
        grid=(D // LANES,),
        in_specs=[pair, pair, other, pair, other]
        + [
            pl.BlockSpec((rows, LANES), lambda h: (0, 0)),
            pl.BlockSpec((2 * rows, LANES), lambda h: (0, 0)),
        ],
        out_specs=[pair, pair],
        out_shape=[shape((rows, D), bf16), shape((rows, D))],
        scratch_shapes=[
            pltpu.VMEM((2 * rows, 2 * LANES), bf16),
            pltpu.VMEM((2, 2 * rows, 2 * LANES), bf16),
        ],
        compiler_params=params(),
        name="attend",
        cost_estimate=cost(11),
    )(q, k, kp, v, vp, ohq, ohk)


def post_kernel(
    o_ref, x_ref, vec_ref, b1_ref, a0, a1, a2, a3, f0, f1, f2, f3,
    n1_ref, i1_ref, y_ref, hid_ref, slope_ref, n2_ref, i2_ref, x2_ref,
    wo_s, w1_s, w2_s,
):
    place_blocks(wo_s, (a0, a1, a2, a3), 0, 1, 4, BLK, 0)
    place_blocks(w1_s, (a0, a1, a2, a3), 4, 4, 4, 0, D)
    place_blocks(w2_s, (f0, f1, f2, f3), 0, 4, 4, D, 0)

    def tile(t, c):
        at = pl.ds(t * ROW_TILE, ROW_TILE)
        vec = [vec_ref[i : i + 1, :] for i in range(6)]
        unit, inv = layer_norm(x_ref[at] + dot(o_ref[at], wo_s[...]) + vec[0])
        n1_ref[at] = unit
        i1_ref[at] = jnp.broadcast_to(inv, (ROW_TILE, LANES))
        y = unit * vec[1] + vec[2]
        yb = y.astype(bf16)
        y_ref[at] = yb
        pre = dot(yb, w1_s[...]) + b1_ref[...]
        phi = 0.5 * (1.0 + lax.erf(pre * (0.5**0.5)))
        hid = (pre * phi).astype(bf16)
        hid_ref[at] = hid
        slope = phi + pre * (jnp.exp(-0.5 * pre * pre) * 0.3989422804014327)
        slope_ref[at] = slope.astype(bf16)
        fed = dot(hid, w2_s[...])
        unit, inv = layer_norm(y + fed + vec[3])
        n2_ref[at] = unit
        i2_ref[at] = jnp.broadcast_to(inv, (ROW_TILE, LANES))
        x2_ref[at] = unit * vec[4] + vec[5]
        return c

    lax.fori_loop(0, x_ref.shape[0] // ROW_TILE, tile, 0)


def post(o, x, vec, b1, wmid, wdown):
    rows = x.shape[0]
    return pl.pallas_call(
        post_kernel,
        out_shape=[
            shape((rows, D)),
            shape((rows, LANES)),
            shape((rows, D), bf16),
            shape((rows, FF), bf16),
            shape((rows, FF), bf16),
            shape((rows, D)),
            shape((rows, LANES)),
            shape((rows, D)),
        ],
        scratch_shapes=[
            pltpu.VMEM((D, D), bf16),
            pltpu.VMEM((D, FF), bf16),
            pltpu.VMEM((FF, D), bf16),
        ],
        compiler_params=params(),
        name="post",
        cost_estimate=cost(11),
    )(o, x, vec, b1, *wmid, *wdown)


def store_blocks(refs, r, first, rows, cols, value):
    keep_ref, send_ref = refs
    ref = send_ref if r % 2 else keep_ref
    for j in range(rows * cols):
        row, col = divmod(j, cols)
        ref[r // 2, first + j] = value[row * BLK : (row + 1) * BLK, col * BLK : (col + 1) * BLK]


def ffn_grad_kernel(
    e_ref, n2_ref, i2_ref, n1_ref, i1_ref, y_ref, hid_ref, slope_ref, o_ref, vec_ref,
    a0, a1, a2, a3, f0, f1, f2, f3,
    gk_ref, gs_ref, ok_ref, os_ref, dr1_ref, do_ref, db1_ref, sums_ref,
    wo_s, w1_s, w2_s, dr2_s, dfr_s, dpre_s, dar_s,
):
    rows = e_ref.shape[0]
    place_blocks(wo_s, (a0, a1, a2, a3), 0, 1, 4, BLK, 0)
    place_blocks(w1_s, (a0, a1, a2, a3), 4, 4, 4, 0, D)
    place_blocks(w2_s, (f0, f1, f2, f3), 0, 4, 4, D, 0)
    tiles = rows // ROW_TILE
    gain_two = vec_ref[4:5, :]
    gain_one = vec_ref[1:2, :]
    zero = jnp.zeros((1, D), f32)

    def tile_two(t, c):
        at = pl.ds(t * ROW_TILE, ROW_TILE)
        grad = e_ref[at]
        unit = n2_ref[at]
        dr2 = layer_norm_grad(grad, unit, i2_ref[at, 0:1], gain_two)
        dr2_s[at] = dr2
        dfr_s[at] = dr2.astype(bf16)
        return (c[0] + col_sum(dr2), c[1] + col_sum(grad * unit), c[2] + col_sum(grad))

    db2, dg2, dc2 = lax.fori_loop(0, tiles, tile_two, (zero, zero, zero))

    for r in range(FF // D):
        cols = slice(r * D, (r + 1) * D)

        def tile_up(t, c):
            at = pl.ds(t * ROW_TILE, ROW_TILE)
            dh = dot(dfr_s[at], w2_s[cols, :], 1, 1)
            dpre = (dh * slope_ref[at, cols].astype(f32)).astype(bf16)
            dpre_s[at, cols] = dpre
            dr2_s[at] = dr2_s[at] + dot(dpre, w1_s[:, cols], 1, 1)
            return c + col_sum(dpre.astype(f32))

        db1_ref[r : r + 1, :] = lax.fori_loop(0, tiles, tile_up, zero)
        store_blocks((gk_ref, gs_ref), r, 0, 4, 4, dot(hid_ref[:, cols], dfr_s[...], 0, 0).astype(bf16))
        store_blocks((ok_ref, os_ref), r, 4, 4, 4, dot(y_ref[...], dpre_s[:, cols], 0, 0).astype(bf16))

    def tile_one(t, c):
        at = pl.ds(t * ROW_TILE, ROW_TILE)
        grad = dr2_s[at]
        unit = n1_ref[at]
        dr1 = layer_norm_grad(grad, unit, i1_ref[at, 0:1], gain_one)
        dr1_ref[at] = dr1
        dar = dr1.astype(bf16)
        dar_s[at] = dar
        do_ref[at] = dot(dar, wo_s[...], 1, 1).astype(bf16)
        return (c[0] + col_sum(dr1), c[1] + col_sum(grad * unit), c[2] + col_sum(grad))

    dbo, dg1, dc1 = lax.fori_loop(0, tiles, tile_one, (zero, zero, zero))
    dwo = dot(o_ref[...], dar_s[...], 0, 0).astype(bf16)
    for r in range(4):
        store_blocks((ok_ref, os_ref), r, 0, 1, 4, dwo[r * BLK : (r + 1) * BLK])
    for i, value in enumerate((dbo, dg1, dc1, db2, dg2, dc2, zero, zero)):
        sums_ref[i : i + 1, :] = value


def ffn_grad(e, n2, i2, n1, i1, y, hid, slope, o, vec, wmid, wdown):
    rows = e.shape[0]
    return pl.pallas_call(
        ffn_grad_kernel,
        out_shape=[
            shape((2, 16, BLK, BLK), bf16),
            shape((2, 16, BLK, BLK), bf16),
            shape((2, 20, BLK, BLK), bf16),
            shape((2, 20, BLK, BLK), bf16),
            shape((rows, D)),
            shape((rows, D), bf16),
            shape((FF // D, D)),
            shape((8, D)),
        ],
        scratch_shapes=[
            pltpu.VMEM((D, D), bf16),
            pltpu.VMEM((D, FF), bf16),
            pltpu.VMEM((FF, D), bf16),
            pltpu.VMEM((rows, D), f32),
            pltpu.VMEM((rows, D), bf16),
            pltpu.VMEM((rows, FF), bf16),
            pltpu.VMEM((rows, D), bf16),
        ],
        compiler_params=params(),
        name="ffn_grad",
        cost_estimate=cost(16),
    )(e, n2, i2, n1, i1, y, hid, slope, o, vec, *wmid, *wdown)


def attend_grad_kernel(
    q_ref, k_ref, kp_ref, v_ref, vp_ref, do_ref, o_ref, lse_ref, ohq_ref, ohk_ref,
    dq_ref, dk_ref, dkp_ref, dv_ref, dvp_ref,
    ka, va, qa, da, kt,
):
    rows = q_ref.shape[0]
    ka[:rows, :LANES] = k_ref[...]
    ka[rows:, :LANES] = kp_ref[...]
    ka[:, LANES:] = ohk_ref[...]
    va[:rows, :LANES] = v_ref[...]
    va[rows:, :LANES] = vp_ref[...]
    va[:, LANES:] = jnp.ones((2 * rows, LANES), bf16)
    kt[...] = ka[:, :LANES].T
    product = do_ref[...].astype(f32) * o_ref[...].astype(f32)
    for i in range(2):
        m = half_mask(i)
        qa[i, :, :LANES] = q_ref[...] * (m * bf16(0.125))
        qa[i, :, LANES:] = lanes_with(
            ohq_ref[...].astype(f32), 120, three_terms(-lse_ref[:, i : i + 1])
        )
        da[i, :, :LANES] = do_ref[...] * m
        delta = jnp.sum(product * half_mask(i, f32), axis=1, keepdims=True)
        da[i, :, LANES:] = lanes_with(jnp.zeros((rows, LANES), f32), 0, three_terms(-delta))

    def tile(t, sums):
        at = pl.ds(pl.multiple_of(t * ROW_TILE, ROW_TILE), ROW_TILE)
        dk = jnp.zeros((ROW_TILE, LANES), f32)
        dv = jnp.zeros((ROW_TILE, LANES), f32)
        new = []
        for i in range(2):
            p = jnp.exp(dot(ka[at], qa[i], 1, 1))
            ds = (p * dot(va[at], da[i], 1, 1)).astype(bf16)
            dv = dv + dot(p.astype(bf16), da[i, :, :LANES])
            dk = dk + dot(ds, qa[i, :, :LANES])
            new.append(sums[i] + dot(kt[:, at], ds))
        return tuple(new), dk.astype(bf16), dv.astype(bf16)

    sums = (jnp.zeros((LANES, rows), f32),) * 2
    half = rows // ROW_TILE

    def own(t, sums):
        sums, dk, dv = tile(t, sums)
        at = pl.ds(t * ROW_TILE, ROW_TILE)
        dk_ref[at] = dk
        dv_ref[at] = dv
        return sums

    def other(t, sums):
        sums, dk, dv = tile(t + half, sums)
        at = pl.ds(t * ROW_TILE, ROW_TILE)
        dkp_ref[at] = dk
        dvp_ref[at] = dv
        return sums

    sums = lax.fori_loop(0, half, own, sums)
    sums = lax.fori_loop(0, half, other, sums)
    row = lax.broadcasted_iota(jnp.int32, (LANES, rows), 0)
    dq_ref[...] = (jnp.where(row < HD, sums[0], sums[1]) * 0.125).T.astype(bf16)


def attend_grad(q, k, kp, v, vp, do, o, lse, ohq, ohk):
    rows = q.shape[0]
    pair = pl.BlockSpec((rows, LANES), lambda h: (0, h))
    other = pl.BlockSpec((rows, LANES), lambda h: (0, h + 1 - 2 * lax.rem(h, 2)))
    return pl.pallas_call(
        attend_grad_kernel,
        grid=(D // LANES,),
        in_specs=[pair, pair, other, pair, other, pair, pair, pair]
        + [
            pl.BlockSpec((rows, LANES), lambda h: (0, 0)),
            pl.BlockSpec((2 * rows, LANES), lambda h: (0, 0)),
        ],
        out_specs=[pair, pair, other, pair, other],
        out_shape=[shape((rows, D), bf16)] * 5,
        scratch_shapes=[
            pltpu.VMEM((2 * rows, 2 * LANES), bf16),
            pltpu.VMEM((2 * rows, 2 * LANES), bf16),
            pltpu.VMEM((2, rows, 2 * LANES), bf16),
            pltpu.VMEM((2, rows, 2 * LANES), bf16),
            pltpu.VMEM((LANES, 2 * rows), bf16),
        ],
        compiler_params=params(),
        name="attend_grad",
        cost_estimate=cost(23),
    )(q, k, kp, v, vp, do, o, lse, ohq, ohk)


def proj_grad_kernel(
    dq_ref, dk_ref, dv_ref, dkr_ref, dvr_ref, xs_ref, dr1_ref, w0, w1, w2, w3,
    gk_ref, gs_ref, dx_ref, sums_ref, w_s, dk_s, dv_s,
):
    place_qkv(w_s, (w0, w1, w2, w3))
    zero = jnp.zeros((1, D), f32)

    def tile(t, c):
        at = pl.ds(t * ROW_TILE, ROW_TILE)
        dq = dq_ref[at]
        dk = (dk_ref[at].astype(f32) + dkr_ref[at].astype(f32)).astype(bf16)
        dv = (dv_ref[at].astype(f32) + dvr_ref[at].astype(f32)).astype(bf16)
        dk_s[at] = dk
        dv_s[at] = dv
        dx_ref[at] = (
            dr1_ref[at]
            + dot(dq, w_s[:, :D], 1, 1)
            + dot(dk, w_s[:, D : 2 * D], 1, 1)
            + dot(dv, w_s[:, 2 * D :], 1, 1)
        )
        return (c[0] + col_sum(dq.astype(f32)), c[1] + col_sum(dv.astype(f32)))

    dbq, dbv = lax.fori_loop(0, xs_ref.shape[0] // ROW_TILE, tile, (zero, zero))
    sums_ref[0:1, :] = dbq
    sums_ref[1:2, :] = dbv
    sums_ref[2:8, :] = jnp.zeros((6, D), f32)
    for part, ref in enumerate((dq_ref, dk_s, dv_s)):
        grad = dot(xs_ref[...], ref[...], 0, 0).astype(bf16)
        for r in range(4):
            out = gs_ref if r % 2 else gk_ref
            for row in range(4):
                out[r // 2, row * 3 + part] = grad[row * BLK : (row + 1) * BLK, r * BLK : (r + 1) * BLK]


def proj_grad(dq, dk, dv, dkr, dvr, xs, dr1, wqkv):
    rows = xs.shape[0]
    return pl.pallas_call(
        proj_grad_kernel,
        out_shape=[
            shape((2, 12, BLK, BLK), bf16),
            shape((2, 12, BLK, BLK), bf16),
            shape((rows, D)),
            shape((8, D)),
        ],
        scratch_shapes=[
            pltpu.VMEM((D, 3 * D), bf16),
            pltpu.VMEM((rows, D), bf16),
            pltpu.VMEM((rows, D), bf16),
        ],
        compiler_params=params(),
        name="proj_grad",
        cost_estimate=cost(5),
    )(dq, dk, dv, dkr, dvr, xs, dr1, *wqkv)


def embed_grad_kernel(
    place_ref, series_ref, g_ref, we_ref, s0, q0, b0, s1, q1, b1, in_ref, keep_ref, send_ref, tab
):
    place = place_ref[0]
    g = g_ref[...]
    in_ref[...] = dot_hi(g, we_ref[...], 1, 1)
    tab[:LOOK] = dot_hi(series_ref[...].astype(f32), g, 0, 0)
    tab[LOOK : LOOK + 1] = col_sum(g)
    per_layer = 8 + FF // D
    for layer, (sums, qsums, db1) in enumerate(((s0, q0, b0), (s1, q1, b1))):
        base = LOOK + 1 + layer * per_layer
        for r in range(4):
            h = place ^ r
            lanes = pl.ds(pl.multiple_of(h * BLK, BLK), BLK)
            tab[base : base + 2, lanes] = qsums[0:2, r * BLK : (r + 1) * BLK]
            tab[pl.ds(base + 5 + h, 1), :] = db1[r : r + 1, :]
        tab[base + 2 : base + 5] = sums[0:3]
        tab[base + 5 + FF // D : base + per_layer] = sums[3:6]
    used = LOOK + 1 + LAYERS * per_layer
    tab[used:] = jnp.zeros((BLK - used, D), f32)
    for r in range(4):
        rows = tab[pl.ds(pl.multiple_of((place ^ r) * 32, 32), 32), :]
        out = send_ref if r % 2 else keep_ref
        for c in range(4):
            out[r // 2, c * 32 : (c + 1) * 32] = rows[:, c * BLK : (c + 1) * BLK]


def embed_grad(place, series, g, table, sums):
    rows = series.shape[0]
    spec = pl.BlockSpec(memory_space=pltpu.VMEM)
    return pl.pallas_call(
        embed_grad_kernel,
        in_specs=[pl.BlockSpec(memory_space=pltpu.SMEM)] + [spec] * 9,
        out_shape=[
            shape((rows, LOOK)),
            shape((2, BLK, BLK)),
            shape((2, BLK, BLK)),
        ],
        scratch_shapes=[pltpu.VMEM((BLK, D), f32)],
        compiler_params=params(),
        name="embed_grad",
        cost_estimate=cost(2),
    )(place, series, g, table[:LOOK], *sums)


def vector_kernel(
    place_ref, val_ref, first_ref, second_ref, p0, p1, p2, p3, nv_ref, n1_ref, n2_ref, bias_ref, tab
):
    for r, part in enumerate((p0, p1, p2, p3)):
        rows = pl.ds(pl.multiple_of((place_ref[0] ^ r) * 32, 32), 32)
        for c in range(4):
            tab[rows, c * BLK : (c + 1) * BLK] = part[c * 32 : (c + 1) * 32]
    grad = tab[: val_ref.shape[0]]
    val = val_ref[...]
    first = 0.5 * first_ref[...] + 0.5 * grad
    second = 0.5 * second_ref[...] + 0.5 * grad * grad
    n1_ref[...] = first
    n2_ref[...] = second
    nv_ref[...] = val - rate_vector * (
        first / CORR / (jnp.sqrt(second / CORR) + adam_eps) + weight_decay * val
    )
    per_layer = 8 + FF // D
    for layer in range(LAYERS):
        base = LOOK + 1 + layer * per_layer
        bias_ref[2 * layer : 2 * layer + 1] = tab[base + 2 : base + 3]
        bias_ref[2 * layer + 1 : 2 * layer + 2] = tab[base + 5 + FF // D : base + 6 + FF // D]


def vector_update(place, values, first, second, parts):
    spec = pl.BlockSpec(memory_space=pltpu.VMEM)
    return pl.pallas_call(
        vector_kernel,
        in_specs=[pl.BlockSpec(memory_space=pltpu.SMEM)] + [spec] * 7,
        out_shape=[shape(values.shape)] * 3 + [shape((2 * LAYERS, D))],
        scratch_shapes=[pltpu.VMEM((BLK, D), f32)],
        compiler_params=params(),
        name="vector",
        cost_estimate=cost(2),
    )(place, values, first, second, *parts)


PARTS = ((0, 12), (12, 20), (32, 16))


def natural_kernel(plan, at_ref, *refs):
    count = len(plan)
    slots, outs, held = refs[:count], refs[count:-1], refs[-1]
    for ref, start in zip(slots, plan):
        held[start : start + ref.shape[0]] = ref[...]
    for i, out in enumerate(outs):
        plane, rest = divmod(i, 3 * LAYERS)
        layer, part = divmod(rest, 3)
        first, n = PARTS[part]
        for j in range(n):
            out[j] = held[at_ref[plane * 96 + layer * 48 + first + j]]


def natural_order(at, slots, plan):
    total = sum(s.shape[0] for s in slots)
    spec = pl.BlockSpec(memory_space=pltpu.VMEM)
    return pl.pallas_call(
        functools.partial(natural_kernel, plan),
        in_specs=[pl.BlockSpec(memory_space=pltpu.SMEM)] + [spec] * len(slots),
        out_shape=[
            shape((n, BLK, BLK), bf16)
            for _ in range(at.shape[0] // 96 * LAYERS)
            for _, n in PARTS
        ],
        scratch_shapes=[pltpu.VMEM((total, BLK, BLK), bf16)],
        compiler_params=params(),
        name="natural",
        cost_estimate=cost(4),
    )(at, *slots)


def routed_kernel(at_ref, *refs):
    own, got, out = refs[:6], refs[6:12], refs[12]
    out[...] = jnp.zeros(out.shape, bf16)
    for i in range(6):
        layer, part = divmod(i, 3)
        first, n = PARTS[part]
        for j in range(n):
            place = at_ref[layer * 48 + first + j]
            who = at_ref[96 + layer * 48 + first + j]
            value = own[i][j].astype(f32) + got[i][j].astype(f32)
            out[who, pl.ds(pl.multiple_of(place * BLK, BLK), BLK), :] = value.astype(bf16)


def routed(at, own, got, count, slots_each):
    spec = pl.BlockSpec(memory_space=pltpu.VMEM)
    return pl.pallas_call(
        routed_kernel,
        in_specs=[pl.BlockSpec(memory_space=pltpu.SMEM)] + [spec] * 12,
        out_shape=shape((count, slots_each * BLK, BLK), bf16),
        compiler_params=params(),
        name="routed",
        cost_estimate=cost(4),
    )(at, *own, *got)


def ring_of(count):
    half = count // 2
    return [2 * i for i in range(half)] + [2 * (half - 1 - i) + 1 for i in range(half)]


def ring_shift(value, order, by):
    n = len(order)
    return lax.ppermute(value, "dp", [(order[i], order[(i + by) % n]) for i in range(n)])


def ring_gather(value, order):
    n = len(order)
    half = value.shape[0] // 2
    held = [(value, 0, 0)]
    ahead = behind = value
    for step in range(1, n // 2):
        behind = ring_shift(behind, order, 1)
        ahead = ring_shift(ahead, order, -1)
        held += [(behind, n - step, 0), (ahead, step, 0)]
    held.append((ring_shift(behind[:half], order, 1), n // 2, 0))
    held.append((ring_shift(ahead[half:], order, -1), n // 2, half))
    return held


def ring_reduce(pieces, order, meanwhile):
    n = len(order)
    half = pieces[0].shape[0] // 2
    up = ring_shift(pieces[n // 2][:half], order, 1)
    down = ring_shift(pieces[n // 2][half:], order, -1)
    for step in range(1, n // 2):
        near, far = pieces[n // 2 - step], pieces[n // 2 + step]
        if step == 1:
            up = jnp.concatenate([add_low(up, near[:half]), near[half:]], axis=0)
            down = jnp.concatenate([far[:half], add_low(down, far[half:])], axis=0)
        else:
            up, down = add_low(up, near), add_low(down, far)
        up, down = tied((up, down), meanwhile[step - 1])
        up, down = ring_shift(up, order, 1), ring_shift(down, order, -1)
    return pieces[0], up, down


def dp_sum(value, count, after):
    bit = 1
    while bit < count:
        if 2 * bit >= count:
            value = tied(value, after)
        low = value.astype(bf16)
        there = lax.ppermute(low, "dp", [(i, i ^ bit) for i in range(count)])
        value = low.astype(f32) + there.astype(f32)
        bit *= 2
    return value


def add_low(a, b):
    return (a.astype(f32) + b.astype(f32)).astype(bf16)


def core_swap(value):
    return lax.ppermute(value, "head", [(i, i ^ 1) for i in range(4)])


def far_swap(value):
    return lax.ppermute(value, "head", [(i, i ^ 2) for i in range(4)])


def tied(values, after):
    return lax.optimization_barrier((values, after))[0]


def one_hots(ids):
    lane = jnp.arange(LANES, dtype=jnp.int32)[None, :]
    same = ids[:, None] == lane
    return jnp.where(same, -BIG, 0.0).astype(bf16), jnp.where(same, 0.0, 1.0).astype(bf16)


def relative(row, place):
    pieces = row.reshape(4, -1)
    return jnp.take(pieces, jnp.arange(4) ^ place, axis=0).reshape(1, -1)


def on_device(
    series,
    cotangent,
    window_lengths,
    owner_list,
    master,
    first_moment,
    second_moment,
    left_stats,
    right_stats,
    left_basis,
    right_basis,
    vec_values,
    vec_first,
    vec_second,
):
    place = lax.axis_index("head")
    spot = lax.axis_index("dp")
    dp = lax.axis_size("dp")
    ringed = dp == 8
    rows = series.shape[0]
    own_slots = master.shape[1]
    buckets, win = window_lengths.shape
    bucket_rows = rows * 4 // buckets
    owner_row = owner_list[0]
    who = owner_row // own_slots
    if ringed:
        order = ring_of(dp)
        ring_at = jnp.asarray([order.index(d) for d in range(dp)], jnp.int32)
        who = (ring_at[who] - ring_at[spot]) % dp
    inner = owner_row % own_slots
    gather_at = who * own_slots + inner

    copies = master[0].astype(bf16)
    if ringed:
        held = ring_gather(copies, order)
        slots, plan = [x[0] for x in held], tuple(x[1] * own_slots + x[2] for x in held)
    else:
        slots, plan = [lax.all_gather(copies, "dp", axis=0, tiled=True)], (0,)
    windows = window_ids(window_lengths, bucket_rows)
    ids = windows.reshape(4, rows)
    own_ids = lax.dynamic_index_in_dim(ids, place, 0, False)
    pair_ids = lax.dynamic_index_in_dim(ids, place ^ 1, 0, False)
    ohq, ohk_own = one_hots(own_ids)
    ohk = jnp.concatenate([ohk_own, one_hots(pair_ids)[1]], axis=0)
    valid = (own_ids < win).astype(f32)[:, None]

    x = embed(series, vec_values)
    vectors = []
    for layer in range(LAYERS):
        bq, bv, bo, g1, c1, b1, b2, g2, c2 = depth_vectors(vec_values, layer)
        vec = jnp.stack([bo, g1, c1, b2, g2, c2, g2, c2])
        vectors.append([vec] + [relative(row, place) for row in (bq, bv, b1)])
    grad = cotangent * valid
    slots, (x, vectors, ohq, ohk, valid, gather_at, grad) = lax.optimization_barrier(
        (slots, (x, vectors, ohq, ohk, valid, gather_at, grad))
    )
    mine = natural_order(gather_at, slots, plan)
    moved = []

    def cross(i, after=None):
        own = mine[i] if after is None else tied(mine[i], after)
        moved.append(far_swap(own))
        return moved[-1]

    def four(i, after=None):
        there = moved[i] if after is None else tied(moved[i], after)
        return [mine[i], core_swap(mine[i]), there, core_swap(there)]

    weights = []
    saved = []
    for layer in range(LAYERS):
        vec, bq, bv, b1 = vectors[layer]
        if layer == 0:
            cross(0)
        wqkv = four(3 * layer, x if layer else None)
        x = tied(x, wqkv)
        if layer == 0:
            cross(1, moved[0])
            cross(2, moved[0])
        xs, q, k, v = project(x, bq, bv, wqkv)
        kp, vp = core_swap(k), core_swap(v)
        o, lse = attend(q, k, kp, v, vp, ohq, ohk)
        wmid, wdown = four(3 * layer + 1, o), four(3 * layer + 2, o)
        weights += [wqkv, wmid, wdown]
        if layer + 1 < LAYERS:
            done = moved[-1]
            for i in range(3):
                cross(3 * layer + 3 + i, done if i == 0 else (done, moved[3 * layer + 3]))
        n1, i1, y, hid, slope, n2, i2, x = post(o, x, vec, b1, wmid, wdown)
        saved.append((xs, q, k, v, kp, vp, o, lse, vec, n1, i1, y, hid, slope, n2, i2))
    activations = x * valid

    own_sums = [None] * (3 * LAYERS)
    far_sums = [None] * (3 * LAYERS)
    table_rows = [None] * LAYERS

    waiting = []

    def chip_sum(at, keep, got):
        waiting.append((at, keep, got))
        return add_low(keep[1], got[1])

    def own_chip_sums(after):
        while waiting:
            at, keep, got = waiting.pop()
            keep, got = tied((keep[0], got[0]), after)
            own_sums[at] = add_low(keep, got)

    moving = []
    for layer in reversed(range(LAYERS)):
        xs, q, k, v, kp, vp, o, lse, vec, n1, i1, y, hid, slope, n2, i2 = saved[layer]
        wqkv, wmid, wdown = weights[3 * layer : 3 * layer + 3]
        gk, gs, ok, os, dr1, do, db1, sums = ffn_grad(
            grad, n2, i2, n1, i1, y, hid, slope, o, vec, wmid, wdown
        )
        os, gs, ok, gk, do = tied((os, gs, ok, gk, do), moving)
        own_chip_sums(sums)
        got = [core_swap(os), core_swap(gs)]
        mid = chip_sum(3 * layer + 1, ok, got[0])
        down = chip_sum(3 * layer + 2, gk, got[1])
        far_sums[3 * layer + 1] = far_swap(mid)
        do = tied(do, (mid, down))
        dq, dk, dkp, dv, dvp = attend_grad(q, k, kp, v, vp, do, o, lse, ohq, ohk)
        dkp, dvp = tied((dkp, dvp), far_sums[3 * layer + 1])
        far_sums[3 * layer + 2] = far_swap(tied(down, far_sums[3 * layer + 1]))
        dkr, dvr = core_swap(dkp), core_swap(dvp)
        pk, ps, grad, qsums = proj_grad(dq, dk, dv, dkr, dvr, xs, dr1, wqkv)
        table_rows[layer] = (sums, qsums, db1)
        got = core_swap(ps)
        if layer:
            far = chip_sum(3 * layer, pk, got)
            grad = tied(grad, far)
            far_sums[3 * layer] = far_swap(far)
            moving = far_sums[3 * layer : 3 * layer + 3]
    input_grad, tab_keep, tab_send = embed_grad(
        place.astype(jnp.int32)[None], series, grad, vec_values, table_rows[0] + table_rows[1]
    )
    far_sums[0] = far_swap(chip_sum(0, pk, got))
    own_chip_sums(tab_send)
    tab = dp_sum(tab_keep + core_swap(tab_send), dp, far_sums[0])
    tab_part = tab[0] + far_swap(tab[1])
    tab_there = far_swap(tab_part)
    parts = [tab_part, core_swap(tab_part), tab_there, core_swap(tab_there)]
    vec_new_values, vec_new_first, vec_new_second, branch_bias_grads = vector_update(
        place.astype(jnp.int32)[None], vec_values, vec_first, vec_second, parts
    )
    at = jnp.concatenate([inner, who]).astype(jnp.int32)
    pieces = routed(at, own_sums, far_sums, dp, own_slots)
    if ringed:
        meanwhile = (tab, tab_part, parts)
        terms = ring_reduce([pieces[i] for i in range(dp)], order, meanwhile)
        terms = tied(terms, vec_new_values)
        grads = [t.reshape(own_slots, BLK, BLK) for t in terms]
    else:
        whole = lax.psum_scatter(pieces, "dp", scatter_dimension=0, tiled=True)
        grads = [whole.reshape(own_slots, BLK, BLK)]
    new_master, new_copy, new_first, new_second, new_left, new_right, left_next, right_next = soap(
        grads,
        master[0],
        first_moment[0],
        second_moment[0],
        left_stats[0],
        right_stats[0],
        left_basis[0],
        right_basis[0],
    )
    return (
        activations,
        input_grad,
        new_master[None],
        new_copy[None],
        new_first[None],
        new_second[None],
        new_left[None],
        new_right[None],
        left_next[None],
        right_next[None],
        vec_new_values,
        vec_new_first,
        vec_new_second,
        branch_bias_grads,
    )


def solution(mesh):
    placed = (
        P(("dp", "head"), None),
        P(("dp", "head"), None),
        P("dp", None),
        P("head", None),
        P("head", "dp", None, None),
        P("head", "dp", None, None),
        P("head", "dp", None, None),
        P("head", "dp", None, None),
        P("head", "dp", None, None),
        P("head", "dp", None, None),
        P("head", "dp", None, None),
        P(),
        P(),
        P(),
    )
    return jax.shard_map(
        on_device,
        mesh=mesh,
        in_specs=placed,
        out_specs=(
            P(("dp", "head"), None),
            P(("dp", "head"), None),
            P("head", "dp", None, None),
            P("head", "dp", None, None),
            P("head", "dp", None, None),
            P("head", "dp", None, None),
            P("head", "dp", None, None),
            P("head", "dp", None, None),
            P("head", "dp", None, None),
            P("head", "dp", None, None),
            P(),
            P(),
            P(),
            P(),
        ),
        check_vma=False,
    )
```

```python
import functools

import jax
import jax.numpy as jnp
from jax import lax
from jax.experimental import pallas as pl
from jax.experimental.pallas import tpu as pltpu
from jax.sharding import PartitionSpec as P

D = 512
HEADS = 8
HD = 64
FF = 2048
LOOK = 96
LAYERS = 2
BLK = 128
STEP = 10

f32 = jnp.float32
HI = lax.Precision.HIGHEST
norm_eps = 1e-05
beta_first = 0.5
beta_second = 0.5
beta_stats = 0.5
adam_eps = 1e-08
rate_matrix = 0.02
rate_vector = 0.15
weight_decay = 0.01


def window_ids(lengths, bucket_rows):
    bounds = jnp.cumsum(lengths, axis=1, dtype=jnp.int32)
    places = jnp.arange(bucket_rows, dtype=jnp.int32)
    return jnp.sum(
        (places[None, :, None] >= bounds[:, None, :]).astype(jnp.int32), axis=2, dtype=jnp.int32
    )


def depth_vectors(vec_table, layer_at):
    ff_ratio = FF // D
    base_row = LOOK + 1 + layer_at * (8 + ff_ratio)
    return (
        vec_table[base_row],
        vec_table[base_row + 1],
        vec_table[base_row + 2],
        vec_table[base_row + 3],
        vec_table[base_row + 4],
        vec_table[base_row + 5 : base_row + 5 + ff_ratio].reshape(FF),
        vec_table[base_row + 5 + ff_ratio],
        vec_table[base_row + 6 + ff_ratio],
        vec_table[base_row + 7 + ff_ratio],
    )


def dot_hi(a, b, ca, cb):
    return lax.dot_general(
        a, b, (((ca,), (cb,)), ((), ())), precision=HI, preferred_element_type=f32
    )


def terms(x, count):
    out = []
    for i in range(count):
        part = x.astype(jnp.bfloat16)
        out.append(part)
        if i < count - 1:
            x = x - part.astype(f32)
    return out


def dot_terms(a, b, ca, cb, full=False):
    a = terms(a, 3 if full else 2)
    b = terms(b, 3 if full else 2)
    dims = (((ca,), (cb,)), ((), ()))
    left = jnp.concatenate(a[:2], axis=ca)
    right = jnp.concatenate(
        [jnp.concatenate([b[0], b[1]], axis=cb), jnp.concatenate([b[1], b[0]], axis=cb)], axis=1 - cb
    )
    out = lax.dot_general(left, right, dims, preferred_element_type=f32)
    out = out[:, :BLK] + out[:, BLK:]
    if full:
        out = out + lax.dot_general(
            jnp.concatenate([a[0], a[2]], axis=ca),
            jnp.concatenate([b[2], b[0]], axis=cb),
            dims,
            preferred_element_type=f32,
        )
    return out


PANEL = 32
AHEAD = 2


def recip(x):
    guess = pl.reciprocal(x, approx=True)
    guess = guess * (2.0 - x * guess)
    return guess * (2.0 - x * guess)


def qr_batch(a_ref, count):
    lane = lax.broadcasted_iota(jnp.int32, (1, 1, BLK), 2)
    sub8 = lax.broadcasted_iota(jnp.int32, (1, 8, 1), 1)
    sub = lax.broadcasted_iota(jnp.int32, (1, PANEL, 1), 1)
    for r0 in range(0, BLK, PANEL):
        tiles = [a_ref[:, r0 + 8 * t : r0 + 8 * t + 8, :] for t in range(PANEL // 8)]
        for k0 in range(0, PANEL, AHEAD):
            t0, s0 = divmod(k0, 8)
            cols = [
                [
                    jnp.broadcast_to(tiles[t][:, :, r0 + k : r0 + k + 1], (count, 8, BLK))
                    for k in range(k0, k0 + AHEAD)
                ]
                for t in range(PANEL // 8)
            ]
            for i in range(AHEAD):
                s = s0 + i
                inv = recip(cols[t0][i][:, s : s + 1, :])
                pn = (tiles[t0][:, s : s + 1, :] + (lane == r0 + k0 + i).astype(f32)) * inv
                rest = [cols[t0][j][:, s : s + 1, :] * inv for j in range(i + 1, AHEAD)]
                for t in range(t0, PANEL // 8):
                    c = cols[t][i]
                    if t == t0:
                        if s == 7:
                            continue
                        c = jnp.where(sub8 > s, c, 0.0)
                    tiles[t] = tiles[t] - c * pn
                    for j, m in enumerate(rest):
                        cols[t][i + 1 + j] = cols[t][i + 1 + j] - c * m
        done = jnp.concatenate(tiles, axis=1)
        diag = lane == sub + r0
        pivot = jnp.sum(jnp.where(diag, done, 0.0), axis=2, keepdims=True)
        done = jnp.where(diag, 1.0, jnp.where((lane > sub + r0) & (lane < r0 + PANEL), 0.0, done))
        done = done * lax.rsqrt(pivot)
        a_ref[:, r0 : r0 + PANEL, :] = done
        r1 = r0 + PANEL
        if r1 < BLK:
            lane2 = lax.broadcasted_iota(jnp.int32, (BLK - r1, BLK), 1)
            clear = (lane2 >= r0) & (lane2 < r1)
            z0, z1, z2 = terms(done, 3)
            left = jnp.concatenate([z0, z0, z0, z1, z1, z2], axis=1)
            right = jnp.concatenate([z0, z1, z2, z0, z1, z0], axis=1)
            for b in range(count):
                update = lax.dot_general(
                    left[b], right[b], (((0,), (0,)), ((), ())), preferred_element_type=f32
                )
                a_ref[b, r1:, :] = jnp.where(clear, 0.0, a_ref[b, r1:, :]) - update[r1:]


def soap_kernel(count, *refs):
    for s in range(refs[0].shape[0]):
        soap_slot(s, sum(ref[s].astype(f32) for ref in refs[:count]), *refs[count:])
    soap_finish(*refs[-4:])


def soap_slot(
    s, g, mas_ref, m1_ref, m2_ref, ls_ref, rs_ref, lb_ref, rb_ref,
    nm_ref, nc_ref, n1_ref, n2_ref, nl_ref, nr_ref, ql_ref, qr_ref, mat_ref, a_ref,
):
    group = mas_ref.shape[0]
    lb = lb_ref[s]
    rb = rb_ref[s]
    rot = dot_terms(dot_terms(lb, g, 0, 0), rb, 1, 0)
    n1 = 0.5 * m1_ref[s] + 0.5 * rot
    n2 = 0.5 * m2_ref[s] + 0.5 * rot * rot
    n1_ref[s] = n1
    n2_ref[s] = n2
    corr = 1.0 - 0.5**STEP
    ratio = n1 / corr / (jnp.sqrt(n2 / corr) + adam_eps)
    upd = dot_terms(dot_terms(lb, ratio, 1, 0), rb, 1, 1)
    mas = mas_ref[s]
    nm = mas - rate_matrix * (upd + weight_decay * mas)
    nm_ref[s] = nm
    nc_ref[s] = nm.astype(jnp.bfloat16)
    nl = 0.5 * ls_ref[s] + 0.5 * dot_terms(g, g, 1, 1)
    nr = 0.5 * rs_ref[s] + 0.5 * dot_terms(g, g, 0, 0)
    nl_ref[s] = nl
    nr_ref[s] = nr
    for side, (st, ba) in enumerate(((nl, lb), (nr, rb))):
        m = dot_terms(st, ba, 1, 0, True)
        m = m * lax.rsqrt(jnp.sum(m * m, axis=0, keepdims=True))
        at = 2 * (pl.program_id(0) * group + s) + side
        mat_ref[at] = m
        a_ref[at] = dot_terms(m, m, 0, 0, True)


def soap_finish(ql_ref, qr_ref, mat_ref, a_ref):
    @pl.when(pl.program_id(0) == pl.num_programs(0) - 1)
    def _():
        count = a_ref.shape[0]
        qr_batch(a_ref, count)
        keep = lax.broadcasted_iota(jnp.int32, (BLK, BLK), 1) <= lax.broadcasted_iota(
            jnp.int32, (BLK, BLK), 0
        )
        for j in range(count // 2):
            for side, ref in enumerate((ql_ref, qr_ref)):
                x = jnp.where(keep, a_ref[2 * j + side], 0.0)
                ref[j] = dot_terms(mat_ref[2 * j + side], x, 1, 1, True)


def soap(gs, master, m1, m2, ls, rs, lb, rb):
    n = master.shape[0]
    group = SOAP_GROUP if n % SOAP_GROUP == 0 else n
    one = pl.BlockSpec((group, BLK, BLK), lambda i: (i, 0, 0))
    whole = pl.BlockSpec((n, BLK, BLK), lambda i: (0, 0, 0))
    sh = jax.ShapeDtypeStruct((n, BLK, BLK), f32)
    shb = jax.ShapeDtypeStruct((n, BLK, BLK), jnp.bfloat16)
    return pl.pallas_call(
        functools.partial(soap_kernel, len(gs)),
        grid=(n // group,),
        in_specs=[one] * (len(gs) + 7),
        out_specs=[one] * 6 + [whole] * 2,
        out_shape=[sh, shb, sh, sh, sh, sh, sh, sh],
        scratch_shapes=[pltpu.VMEM((2 * n, BLK, BLK), f32)] * 2,
        compiler_params=pltpu.CompilerParams(vmem_limit_bytes=16 * 2**20),
        cost_estimate=pl.CostEstimate(flops=40 * 10**6, bytes_accessed=0, transcendentals=0),
        name="soap",
    )(*gs, master, m1, m2, ls, rs, lb, rb)


SOAP_GROUP = 2


bf16 = jnp.bfloat16
LANES = 128
ROW_TILE = 512
BIG = 1e30
CORR = 1.0 - 0.5**STEP


def params(mib=48):
    return pltpu.CompilerParams(vmem_limit_bytes=mib * 2**20)


MIB = dict(
    embed=6, project=8, attend=16, post=20, ffn_grad=24, attend_grad=16, proj_grad=12, embed_grad=8, vector=4, natural=6, routed=8,
)


def cost(micros):
    return pl.CostEstimate(flops=int(micros * 1e6), bytes_accessed=0, transcendentals=0)


def shape(dims, kind=f32):
    return jax.ShapeDtypeStruct(dims, kind)


def dot(a, b, ca=1, cb=0):
    return lax.dot_general(a, b, (((ca,), (cb,)), ((), ())), preferred_element_type=f32)


def place_blocks(dst, refs, first, rows, cols, row_step, col_step, col_base=0):
    for r, ref in enumerate(refs):
        for j in range(rows * cols):
            row, col = divmod(j, cols)
            r0 = r * row_step + row * BLK
            c0 = col_base + r * col_step + col * BLK
            dst[r0 : r0 + BLK, c0 : c0 + BLK] = ref[first + j]


def place_qkv(dst, refs):
    for r, ref in enumerate(refs):
        for j in range(12):
            row, col = divmod(j, 3)
            c0 = D + (2 * r + col - 1) * BLK if col else r * BLK
            dst[row * BLK : (row + 1) * BLK, c0 : c0 + BLK] = ref[j]


def layer_norm(resid):
    center = resid - jnp.mean(resid, axis=1, keepdims=True)
    inv = lax.rsqrt(jnp.mean(center * center, axis=1, keepdims=True) + norm_eps)
    return center * inv, inv


def layer_norm_grad(grad, unit, inv, gain):
    dn = grad * gain
    return inv * (
        dn
        - jnp.mean(dn, axis=1, keepdims=True)
        - unit * jnp.mean(dn * unit, axis=1, keepdims=True)
    )


def col_sum(values):
    return jnp.sum(values, axis=0, keepdims=True)


def embed_kernel(series_ref, we_ref, be_ref, x_ref):
    x_ref[...] = dot_hi(series_ref[...].astype(f32), we_ref[...], 1, 0) + be_ref[...]


def embed(series, table):
    rows = series.shape[0]
    return pl.pallas_call(
        embed_kernel, out_shape=shape((rows, D)), compiler_params=params(MIB["embed"]), name="embed"
    )(series, table[:LOOK], table[LOOK : LOOK + 1])


def proj_kernel(x_ref, bq_ref, bv_ref, w0, w1, w2, w3, xs_ref, q_ref, kv_ref, w_s):
    place_qkv(w_s, (w0, w1, w2, w3))
    xs = x_ref[...].astype(bf16)
    xs_ref[...] = xs
    q_ref[...] = (dot(xs, w_s[:, :D]) + bq_ref[...]).astype(bf16)
    kv = dot(xs, w_s[:, D:])
    for r in range(4):
        at = 2 * r * BLK
        kv_ref[:, at : at + BLK] = kv[:, at : at + BLK].astype(bf16)
        value = kv[:, at + BLK : at + 2 * BLK] + bv_ref[:, r * BLK : (r + 1) * BLK]
        kv_ref[:, at + BLK : at + 2 * BLK] = value.astype(bf16)


def project(x, bq, bv, wqkv):
    rows = x.shape[0]
    return pl.pallas_call(
        proj_kernel,
        out_shape=[
            shape((rows, D), bf16),
            shape((rows, D), bf16),
            shape((rows, 2 * D), bf16),
        ],
        scratch_shapes=[pltpu.VMEM((D, 3 * D), bf16)],
        compiler_params=params(MIB["project"]),
        name="project",
        cost_estimate=cost(3),
    )(x, bq, bv, *wqkv)


def half_mask(i, kind=bf16):
    lane = lax.broadcasted_iota(jnp.int32, (1, LANES), 1)
    return ((lane >= HD * i) & (lane < HD * (i + 1))).astype(f32).astype(kind)


def three_terms(col):
    first = col.astype(bf16).astype(f32)
    second = (col - first).astype(bf16).astype(f32)
    return first, second, col - first - second


def lanes_with(base, at, cols):
    lane = lax.broadcasted_iota(jnp.int32, base.shape, 1)
    for i, col in enumerate(cols):
        base = jnp.where(lane == at + i, col, base)
    return base.astype(bf16)


def attend_kernel(q_ref, kv_ref, kvp_ref, ohq_ref, ohk_ref, o_ref, lse_ref, ka, va):
    rows = q_ref.shape[0]
    ka[:rows, :LANES] = kv_ref[:, :LANES]
    ka[rows:, :LANES] = kvp_ref[:, :LANES]
    ka[:, LANES:] = ohk_ref[...]
    lane = lax.broadcasted_iota(jnp.int32, (ROW_TILE, LANES), 1)
    for i in range(2):
        m = half_mask(i)
        va[i, :rows, :LANES] = kv_ref[:, LANES:] * m
        va[i, rows:, :LANES] = kvp_ref[:, LANES:] * m
        va[i, :, LANES:] = jnp.ones((2 * rows, LANES), bf16)

    def tile(t, c):
        at = pl.ds(t * ROW_TILE, ROW_TILE)
        total = jnp.zeros((ROW_TILE, LANES), f32)
        stat = jnp.zeros((ROW_TILE, LANES), f32)
        for i in range(2):
            qa = jnp.concatenate([q_ref[at] * (half_mask(i) * bf16(0.125)), ohq_ref[at]], axis=1)
            s = dot(qa, ka[...], 1, 1)
            high = jnp.max(s, axis=1, keepdims=True)
            e = jnp.exp(s - high).astype(bf16)
            out = dot(e, va[i])
            norm = out[:, LANES:]
            total = total + out[:, :LANES] / norm
            stat = jnp.where(lane == i, high + jnp.log(norm), stat)
        o_ref[at] = total.astype(bf16)
        lse_ref[at] = stat
        return c

    lax.fori_loop(0, rows // ROW_TILE, tile, 0)


def attend(q, kv, kvp, ohq, ohk):
    rows = q.shape[0]
    pair = pl.BlockSpec((rows, LANES), lambda h: (0, h))
    both = pl.BlockSpec((rows, 2 * LANES), lambda h: (0, h))
    other = pl.BlockSpec((rows, 2 * LANES), lambda h: (0, h + 1 - 2 * lax.rem(h, 2)))
    return pl.pallas_call(
        attend_kernel,
        grid=(D // LANES,),
        in_specs=[pair, both, other]
        + [
            pl.BlockSpec((rows, LANES), lambda h: (0, 0)),
            pl.BlockSpec((2 * rows, LANES), lambda h: (0, 0)),
        ],
        out_specs=[pair, pair],
        out_shape=[shape((rows, D), bf16), shape((rows, D))],
        scratch_shapes=[
            pltpu.VMEM((2 * rows, 2 * LANES), bf16),
            pltpu.VMEM((2, 2 * rows, 2 * LANES), bf16),
        ],
        compiler_params=params(MIB["attend"]),
        name="attend",
        cost_estimate=cost(11),
    )(q, kv, kvp, ohq, ohk)


def post_kernel(
    o_ref, x_ref, vec_ref, b1_ref, a0, a1, a2, a3,
    n1_ref, i1_ref, y_ref, hid_ref, slope_ref, n2_ref, i2_ref, x2_ref,
    wo_s, w1_s, w2_s,
):
    place_blocks(wo_s, (a0, a1, a2, a3), 0, 1, 4, BLK, 0)
    place_blocks(w1_s, (a0, a1, a2, a3), 4, 4, 4, 0, D)
    place_blocks(w2_s, (a0, a1, a2, a3), 20, 4, 4, D, 0)

    def tile(t, c):
        at = pl.ds(t * ROW_TILE, ROW_TILE)
        vec = [vec_ref[i : i + 1, :] for i in range(6)]
        unit, inv = layer_norm(x_ref[at] + dot(o_ref[at], wo_s[...]) + vec[0])
        n1_ref[at] = unit
        i1_ref[at] = jnp.broadcast_to(inv, (ROW_TILE, LANES))
        y = unit * vec[1] + vec[2]
        yb = y.astype(bf16)
        y_ref[at] = yb
        pre = dot(yb, w1_s[...]) + b1_ref[...]
        phi = 0.5 * (1.0 + lax.erf(pre * (0.5**0.5)))
        hid = (pre * phi).astype(bf16)
        hid_ref[at] = hid
        slope = phi + pre * (jnp.exp(-0.5 * pre * pre) * 0.3989422804014327)
        slope_ref[at] = slope.astype(bf16)
        fed = dot(hid, w2_s[...])
        unit, inv = layer_norm(y + fed + vec[3])
        n2_ref[at] = unit
        i2_ref[at] = jnp.broadcast_to(inv, (ROW_TILE, LANES))
        x2_ref[at] = unit * vec[4] + vec[5]
        return c

    lax.fori_loop(0, x_ref.shape[0] // ROW_TILE, tile, 0)


def post(o, x, vec, b1, wfeed):
    rows = x.shape[0]
    return pl.pallas_call(
        post_kernel,
        out_shape=[
            shape((rows, D)),
            shape((rows, LANES)),
            shape((rows, D), bf16),
            shape((rows, FF), bf16),
            shape((rows, FF), bf16),
            shape((rows, D)),
            shape((rows, LANES)),
            shape((rows, D)),
        ],
        scratch_shapes=[
            pltpu.VMEM((D, D), bf16),
            pltpu.VMEM((D, FF), bf16),
            pltpu.VMEM((FF, D), bf16),
        ],
        compiler_params=params(MIB["post"]),
        name="post",
        cost_estimate=cost(11),
    )(o, x, vec, b1, *wfeed)


def store_blocks(refs, r, first, rows, cols, value):
    keep_ref, send_ref = refs
    ref = send_ref if r % 2 else keep_ref
    for j in range(rows * cols):
        row, col = divmod(j, cols)
        ref[r // 2, first + j] = value[row * BLK : (row + 1) * BLK, col * BLK : (col + 1) * BLK]


def ffn_grad_kernel(
    e_ref, n2_ref, i2_ref, n1_ref, i1_ref, y_ref, hid_ref, slope_ref, o_ref, vec_ref,
    a0, a1, a2, a3,
    gk_ref, gs_ref, ok_ref, os_ref, dr1_ref, do_ref, db1_ref, sums_ref,
    wo_s, w1_s, w2_s, dr2_s, dfr_s, dpre_s, dar_s,
):
    rows = e_ref.shape[0]
    place_blocks(wo_s, (a0, a1, a2, a3), 0, 1, 4, BLK, 0)
    place_blocks(w1_s, (a0, a1, a2, a3), 4, 4, 4, 0, D)
    place_blocks(w2_s, (a0, a1, a2, a3), 20, 4, 4, D, 0)
    tiles = rows // ROW_TILE
    gain_two = vec_ref[4:5, :]
    gain_one = vec_ref[1:2, :]
    zero = jnp.zeros((1, D), f32)

    def tile_two(t, c):
        at = pl.ds(t * ROW_TILE, ROW_TILE)
        grad = e_ref[at]
        unit = n2_ref[at]
        dr2 = layer_norm_grad(grad, unit, i2_ref[at, 0:1], gain_two)
        dr2_s[at] = dr2
        dfr_s[at] = dr2.astype(bf16)
        return (c[0] + col_sum(dr2), c[1] + col_sum(grad * unit), c[2] + col_sum(grad))

    db2, dg2, dc2 = lax.fori_loop(0, tiles, tile_two, (zero, zero, zero))

    for r in range(FF // D):
        cols = slice(r * D, (r + 1) * D)

        def tile_up(t, c):
            at = pl.ds(t * ROW_TILE, ROW_TILE)
            dh = dot(dfr_s[at], w2_s[cols, :], 1, 1)
            dpre = (dh * slope_ref[at, cols].astype(f32)).astype(bf16)
            dpre_s[at, cols] = dpre
            dr2_s[at] = dr2_s[at] + dot(dpre, w1_s[:, cols], 1, 1)
            return c + col_sum(dpre.astype(f32))

        db1_ref[r : r + 1, :] = lax.fori_loop(0, tiles, tile_up, zero)
        store_blocks((gk_ref, gs_ref), r, 0, 4, 4, dot(hid_ref[:, cols], dfr_s[...], 0, 0).astype(bf16))
        store_blocks((ok_ref, os_ref), r, 4, 4, 4, dot(y_ref[...], dpre_s[:, cols], 0, 0).astype(bf16))

    def tile_one(t, c):
        at = pl.ds(t * ROW_TILE, ROW_TILE)
        grad = dr2_s[at]
        unit = n1_ref[at]
        dr1 = layer_norm_grad(grad, unit, i1_ref[at, 0:1], gain_one)
        dr1_ref[at] = dr1
        dar = dr1.astype(bf16)
        dar_s[at] = dar
        do_ref[at] = dot(dar, wo_s[...], 1, 1).astype(bf16)
        return (c[0] + col_sum(dr1), c[1] + col_sum(grad * unit), c[2] + col_sum(grad))

    dbo, dg1, dc1 = lax.fori_loop(0, tiles, tile_one, (zero, zero, zero))
    dwo = dot(o_ref[...], dar_s[...], 0, 0).astype(bf16)
    for r in range(4):
        store_blocks((ok_ref, os_ref), r, 0, 1, 4, dwo[r * BLK : (r + 1) * BLK])
    for i, value in enumerate((dbo, dg1, dc1, db2, dg2, dc2, zero, zero)):
        sums_ref[i : i + 1, :] = value


def ffn_grad(e, n2, i2, n1, i1, y, hid, slope, o, vec, wfeed):
    rows = e.shape[0]
    return pl.pallas_call(
        ffn_grad_kernel,
        out_shape=[
            shape((2, 16, BLK, BLK), bf16),
            shape((2, 16, BLK, BLK), bf16),
            shape((2, 20, BLK, BLK), bf16),
            shape((2, 20, BLK, BLK), bf16),
            shape((rows, D)),
            shape((rows, D), bf16),
            shape((FF // D, D)),
            shape((8, D)),
        ],
        scratch_shapes=[
            pltpu.VMEM((D, D), bf16),
            pltpu.VMEM((D, FF), bf16),
            pltpu.VMEM((FF, D), bf16),
            pltpu.VMEM((rows, D), f32),
            pltpu.VMEM((rows, D), bf16),
            pltpu.VMEM((rows, FF), bf16),
            pltpu.VMEM((rows, D), bf16),
        ],
        compiler_params=params(MIB["ffn_grad"]),
        name="ffn_grad",
        cost_estimate=cost(16),
    )(e, n2, i2, n1, i1, y, hid, slope, o, vec, *wfeed)


def attend_grad_kernel(
    q_ref, kv_ref, kvp_ref, do_ref, o_ref, lse_ref, ohq_ref, ohk_ref,
    dq_ref, dkv_ref, dkvp_ref,
    ka, va, qa, da, kt,
):
    rows = q_ref.shape[0]
    ka[:rows, :LANES] = kv_ref[:, :LANES]
    ka[rows:, :LANES] = kvp_ref[:, :LANES]
    ka[:, LANES:] = ohk_ref[...]
    va[:rows, :LANES] = kv_ref[:, LANES:]
    va[rows:, :LANES] = kvp_ref[:, LANES:]
    va[:, LANES:] = jnp.ones((2 * rows, LANES), bf16)
    kt[...] = ka[:, :LANES].T
    product = do_ref[...].astype(f32) * o_ref[...].astype(f32)
    for i in range(2):
        m = half_mask(i)
        qa[i, :, :LANES] = q_ref[...] * (m * bf16(0.125))
        qa[i, :, LANES:] = lanes_with(
            ohq_ref[...].astype(f32), 120, three_terms(-lse_ref[:, i : i + 1])
        )
        da[i, :, :LANES] = do_ref[...] * m
        delta = jnp.sum(product * half_mask(i, f32), axis=1, keepdims=True)
        da[i, :, LANES:] = lanes_with(jnp.zeros((rows, LANES), f32), 0, three_terms(-delta))

    def tile(t, sums):
        at = pl.ds(pl.multiple_of(t * ROW_TILE, ROW_TILE), ROW_TILE)
        dk = jnp.zeros((ROW_TILE, LANES), f32)
        dv = jnp.zeros((ROW_TILE, LANES), f32)
        new = []
        for i in range(2):
            p = jnp.exp(dot(ka[at], qa[i], 1, 1))
            ds = (p * dot(va[at], da[i], 1, 1)).astype(bf16)
            dv = dv + dot(p.astype(bf16), da[i, :, :LANES])
            dk = dk + dot(ds, qa[i, :, :LANES])
            new.append(sums[i] + dot(kt[:, at], ds))
        return tuple(new), dk.astype(bf16), dv.astype(bf16)

    sums = (jnp.zeros((LANES, rows), f32),) * 2
    half = rows // ROW_TILE

    def own(t, sums):
        sums, dk, dv = tile(t, sums)
        at = pl.ds(t * ROW_TILE, ROW_TILE)
        dkv_ref[at, :LANES] = dk
        dkv_ref[at, LANES:] = dv
        return sums

    def other(t, sums):
        sums, dk, dv = tile(t + half, sums)
        at = pl.ds(t * ROW_TILE, ROW_TILE)
        dkvp_ref[at, :LANES] = dk
        dkvp_ref[at, LANES:] = dv
        return sums

    sums = lax.fori_loop(0, half, own, sums)
    sums = lax.fori_loop(0, half, other, sums)
    row = lax.broadcasted_iota(jnp.int32, (LANES, rows), 0)
    dq_ref[...] = (jnp.where(row < HD, sums[0], sums[1]) * 0.125).T.astype(bf16)


def attend_grad(q, kv, kvp, do, o, lse, ohq, ohk):
    rows = q.shape[0]
    pair = pl.BlockSpec((rows, LANES), lambda h: (0, h))
    both = pl.BlockSpec((rows, 2 * LANES), lambda h: (0, h))
    other = pl.BlockSpec((rows, 2 * LANES), lambda h: (0, h + 1 - 2 * lax.rem(h, 2)))
    return pl.pallas_call(
        attend_grad_kernel,
        grid=(D // LANES,),
        in_specs=[pair, both, other, pair, pair, pair]
        + [
            pl.BlockSpec((rows, LANES), lambda h: (0, 0)),
            pl.BlockSpec((2 * rows, LANES), lambda h: (0, 0)),
        ],
        out_specs=[pair, both, other],
        out_shape=[shape((rows, D), bf16)] + [shape((rows, 2 * D), bf16)] * 2,
        scratch_shapes=[
            pltpu.VMEM((2 * rows, 2 * LANES), bf16),
            pltpu.VMEM((2 * rows, 2 * LANES), bf16),
            pltpu.VMEM((2, rows, 2 * LANES), bf16),
            pltpu.VMEM((2, rows, 2 * LANES), bf16),
            pltpu.VMEM((LANES, 2 * rows), bf16),
        ],
        compiler_params=params(MIB["attend_grad"]),
        name="attend_grad",
        cost_estimate=cost(23),
    )(q, kv, kvp, do, o, lse, ohq, ohk)


def proj_grad_kernel(
    dq_ref, dkv_ref, dkvr_ref, xs_ref, dr1_ref, w0, w1, w2, w3, gk_ref, gs_ref, dx_ref, sums_ref, w_s
):
    place_qkv(w_s, (w0, w1, w2, w3))
    dq = dq_ref[...]
    dkv = (dkv_ref[...].astype(f32) + dkvr_ref[...].astype(f32)).astype(bf16)
    xs = xs_ref[...]
    sums_ref[0:1, :] = col_sum(dq.astype(f32))
    sums_ref[2:8, :] = jnp.zeros((6, D), f32)
    grads = (dot(xs, dq, 0, 0).astype(bf16), dot(xs, dkv, 0, 0).astype(bf16))
    for r in range(4):
        out = gs_ref if r % 2 else gk_ref
        c0 = (2 * r + 1) * BLK
        sums_ref[1:2, r * BLK : (r + 1) * BLK] = col_sum(dkv[:, c0 : c0 + BLK].astype(f32))
        for row in range(4):
            rows = slice(row * BLK, (row + 1) * BLK)
            out[r // 2, row * 3] = grads[0][rows, r * BLK : (r + 1) * BLK]
            for part in range(2):
                c0 = (2 * r + part) * BLK
                out[r // 2, row * 3 + 1 + part] = grads[1][rows, c0 : c0 + BLK]
    dx_ref[...] = dr1_ref[...] + dot(dq, w_s[:, :D], 1, 1) + dot(dkv, w_s[:, D:], 1, 1)


def proj_grad(dq, dkv, dkvr, xs, dr1, wqkv):
    rows = xs.shape[0]
    return pl.pallas_call(
        proj_grad_kernel,
        out_shape=[
            shape((2, 12, BLK, BLK), bf16),
            shape((2, 12, BLK, BLK), bf16),
            shape((rows, D)),
            shape((8, D)),
        ],
        scratch_shapes=[pltpu.VMEM((D, 3 * D), bf16)],
        compiler_params=params(MIB["proj_grad"]),
        name="proj_grad",
        cost_estimate=cost(5),
    )(dq, dkv, dkvr, xs, dr1, *wqkv)


def embed_grad_kernel(
    place_ref, series_ref, g_ref, we_ref, s0, q0, b0, s1, q1, b1, in_ref, keep_ref, send_ref, tab
):
    place = place_ref[0]
    g = g_ref[...]
    in_ref[...] = dot_hi(g, we_ref[...], 1, 1)
    tab[:LOOK] = dot_hi(series_ref[...].astype(f32), g, 0, 0)
    tab[LOOK : LOOK + 1] = col_sum(g)
    per_layer = 8 + FF // D
    for layer, (sums, qsums, db1) in enumerate(((s0, q0, b0), (s1, q1, b1))):
        base = LOOK + 1 + layer * per_layer
        for r in range(4):
            h = place ^ r
            lanes = pl.ds(pl.multiple_of(h * BLK, BLK), BLK)
            tab[base : base + 2, lanes] = qsums[0:2, r * BLK : (r + 1) * BLK]
            tab[pl.ds(base + 5 + h, 1), :] = db1[r : r + 1, :]
        tab[base + 2 : base + 5] = sums[0:3]
        tab[base + 5 + FF // D : base + per_layer] = sums[3:6]
    used = LOOK + 1 + LAYERS * per_layer
    tab[used:] = jnp.zeros((BLK - used, D), f32)
    for r in range(4):
        rows = tab[pl.ds(pl.multiple_of((place ^ r) * 32, 32), 32), :]
        out = send_ref if r % 2 else keep_ref
        for c in range(4):
            out[r // 2, c * 32 : (c + 1) * 32] = rows[:, c * BLK : (c + 1) * BLK]


def embed_grad(place, series, g, table, sums):
    rows = series.shape[0]
    spec = pl.BlockSpec(memory_space=pltpu.VMEM)
    return pl.pallas_call(
        embed_grad_kernel,
        in_specs=[pl.BlockSpec(memory_space=pltpu.SMEM)] + [spec] * 9,
        out_shape=[
            shape((rows, LOOK)),
            shape((2, BLK, BLK)),
            shape((2, BLK, BLK)),
        ],
        scratch_shapes=[pltpu.VMEM((BLK, D), f32)],
        compiler_params=params(MIB["embed_grad"]),
        name="embed_grad",
        cost_estimate=cost(2),
    )(place, series, g, table[:LOOK], *sums)


def vector_kernel(
    place_ref, val_ref, first_ref, second_ref, p0, p1, p2, p3, nv_ref, n1_ref, n2_ref, bias_ref, tab
):
    for r, part in enumerate((p0, p1, p2, p3)):
        rows = pl.ds(pl.multiple_of((place_ref[0] ^ r) * 32, 32), 32)
        for c in range(4):
            tab[rows, c * BLK : (c + 1) * BLK] = part[c * 32 : (c + 1) * 32]
    grad = tab[: val_ref.shape[0]]
    val = val_ref[...]
    first = 0.5 * first_ref[...] + 0.5 * grad
    second = 0.5 * second_ref[...] + 0.5 * grad * grad
    n1_ref[...] = first
    n2_ref[...] = second
    nv_ref[...] = val - rate_vector * (
        first / CORR / (jnp.sqrt(second / CORR) + adam_eps) + weight_decay * val
    )
    per_layer = 8 + FF // D
    for layer in range(LAYERS):
        base = LOOK + 1 + layer * per_layer
        bias_ref[2 * layer : 2 * layer + 1] = tab[base + 2 : base + 3]
        bias_ref[2 * layer + 1 : 2 * layer + 2] = tab[base + 5 + FF // D : base + 6 + FF // D]


def vector_update(place, values, first, second, parts):
    spec = pl.BlockSpec(memory_space=pltpu.VMEM)
    return pl.pallas_call(
        vector_kernel,
        in_specs=[pl.BlockSpec(memory_space=pltpu.SMEM)] + [spec] * 7,
        out_shape=[shape(values.shape)] * 3 + [shape((2 * LAYERS, D))],
        scratch_shapes=[pltpu.VMEM((BLK, D), f32)],
        compiler_params=params(MIB["vector"]),
        name="vector",
        cost_estimate=cost(2),
    )(place, values, first, second, *parts)


PARTS = ((0, 12), (12, 20), (32, 16))
HELD = ((0, 12), (12, 36))


def natural_kernel(plan, at_ref, *refs):
    count = len(plan)
    slots, outs, held = refs[:count], refs[count:-1], refs[-1]
    for ref, start in zip(slots, plan):
        held[start : start + ref.shape[0]] = ref[...]
    for i, out in enumerate(outs):
        plane, rest = divmod(i, len(HELD) * LAYERS)
        layer, part = divmod(rest, len(HELD))
        first, n = HELD[part]
        for j in range(n):
            out[j] = held[at_ref[plane * 96 + layer * 48 + first + j]]


def natural_order(at, slots, plan):
    total = sum(s.shape[0] for s in slots)
    spec = pl.BlockSpec(memory_space=pltpu.VMEM)
    return pl.pallas_call(
        functools.partial(natural_kernel, plan),
        in_specs=[pl.BlockSpec(memory_space=pltpu.SMEM)] + [spec] * len(slots),
        out_shape=[
            shape((n, BLK, BLK), bf16)
            for _ in range(at.shape[0] // 96 * LAYERS)
            for _, n in HELD
        ],
        scratch_shapes=[pltpu.VMEM((total, BLK, BLK), bf16)],
        compiler_params=params(MIB["natural"]),
        name="natural",
        cost_estimate=cost(4),
    )(at, *slots)


def routed_kernel(at_ref, *refs):
    own, got, out = refs[:6], refs[6:12], refs[12]
    out[...] = jnp.zeros(out.shape, bf16)
    for i in range(6):
        layer, part = divmod(i, 3)
        first, n = PARTS[part]
        for j in range(n):
            place = at_ref[layer * 48 + first + j]
            who = at_ref[96 + layer * 48 + first + j]
            value = own[i][j].astype(f32) + got[i][j].astype(f32)
            out[who, pl.ds(pl.multiple_of(place * BLK, BLK), BLK), :] = value.astype(bf16)


def routed(at, own, got, count, slots_each):
    spec = pl.BlockSpec(memory_space=pltpu.VMEM)
    return pl.pallas_call(
        routed_kernel,
        in_specs=[pl.BlockSpec(memory_space=pltpu.SMEM)] + [spec] * 12,
        out_shape=shape((count, slots_each * BLK, BLK), bf16),
        compiler_params=params(MIB["routed"]),
        name="routed",
        cost_estimate=cost(4),
    )(at, *own, *got)


def ring_of(count):
    half = count // 2
    return [2 * i for i in range(half)] + [2 * (half - 1 - i) + 1 for i in range(half)]


def ring_shift(value, order, by):
    n = len(order)
    return lax.ppermute(value, "dp", [(order[i], order[(i + by) % n]) for i in range(n)])


def ring_gather(value, order):
    n = len(order)
    half = value.shape[0] // 2
    held = [(value, 0, 0)]
    ahead = behind = value
    for step in range(1, n // 2):
        behind = ring_shift(behind, order, 1)
        ahead = ring_shift(ahead, order, -1)
        held += [(behind, n - step, 0), (ahead, step, 0)]
    held.append((ring_shift(behind[:half], order, 1), n // 2, 0))
    held.append((ring_shift(ahead[half:], order, -1), n // 2, half))
    return held


def ring_reduce(pieces, order, meanwhile):
    n = len(order)
    half = pieces[0].shape[0] // 2
    up = ring_shift(pieces[n // 2][:half], order, 1)
    down = ring_shift(pieces[n // 2][half:], order, -1)
    for step in range(1, n // 2):
        near, far = pieces[n // 2 - step], pieces[n // 2 + step]
        if step == 1:
            up = jnp.concatenate([add_low(up, near[:half]), near[half:]], axis=0)
            down = jnp.concatenate([far[:half], add_low(down, far[half:])], axis=0)
        else:
            up, down = add_low(up, near), add_low(down, far)
        up, down = tied((up, down), meanwhile[step - 1])
        up, down = ring_shift(up, order, 1), ring_shift(down, order, -1)
    return pieces[0], up, down


def dp_sum(value, count, after):
    bit = 1
    while bit < count:
        if 2 * bit >= count:
            value = tied(value, after)
        low = value.astype(bf16)
        there = lax.ppermute(low, "dp", [(i, i ^ bit) for i in range(count)])
        value = low.astype(f32) + there.astype(f32)
        bit *= 2
    return value


def add_low(a, b):
    return (a.astype(f32) + b.astype(f32)).astype(bf16)


def core_swap(value):
    return lax.ppermute(value, "head", [(i, i ^ 1) for i in range(4)])


def far_swap(value):
    return lax.ppermute(value, "head", [(i, i ^ 2) for i in range(4)])


def tied(values, after):
    return lax.optimization_barrier((values, after))[0]


def one_hots(ids):
    lane = jnp.arange(LANES, dtype=jnp.int32)[None, :]
    same = ids[:, None] == lane
    return jnp.where(same, -BIG, 0.0).astype(bf16), jnp.where(same, 0.0, 1.0).astype(bf16)


def relative(row, place):
    pieces = row.reshape(4, -1)
    return jnp.take(pieces, jnp.arange(4) ^ place, axis=0).reshape(1, -1)


def on_device(
    series,
    cotangent,
    window_lengths,
    owner_list,
    master,
    first_moment,
    second_moment,
    left_stats,
    right_stats,
    left_basis,
    right_basis,
    vec_values,
    vec_first,
    vec_second,
):
    place = lax.axis_index("head")
    spot = lax.axis_index("dp")
    dp = lax.axis_size("dp")
    ringed = dp == 8
    rows = series.shape[0]
    own_slots = master.shape[1]
    buckets, win = window_lengths.shape
    bucket_rows = rows * 4 // buckets
    owner_row = owner_list[0]
    who = owner_row // own_slots
    if ringed:
        order = ring_of(dp)
        ring_at = jnp.asarray([order.index(d) for d in range(dp)], jnp.int32)
        who = (ring_at[who] - ring_at[spot]) % dp
    inner = owner_row % own_slots
    gather_at = who * own_slots + inner

    copies = master[0].astype(bf16)
    if ringed:
        held = ring_gather(copies, order)
        slots, plan = [x[0] for x in held], tuple(x[1] * own_slots + x[2] for x in held)
    else:
        slots, plan = [lax.all_gather(copies, "dp", axis=0, tiled=True)], (0,)
    windows = window_ids(window_lengths, bucket_rows)
    ids = windows.reshape(4, rows)
    own_ids = lax.dynamic_index_in_dim(ids, place, 0, False)
    pair_ids = lax.dynamic_index_in_dim(ids, place ^ 1, 0, False)
    ohq, ohk_own = one_hots(own_ids)
    ohk = jnp.concatenate([ohk_own, one_hots(pair_ids)[1]], axis=0)
    valid = (own_ids < win).astype(f32)[:, None]

    x = embed(series, vec_values)
    vectors = []
    for layer in range(LAYERS):
        bq, bv, bo, g1, c1, b1, b2, g2, c2 = depth_vectors(vec_values, layer)
        vec = jnp.stack([bo, g1, c1, b2, g2, c2, g2, c2])
        vectors.append([vec] + [relative(row, place) for row in (bq, bv, b1)])
    grad = cotangent * valid
    slots, (x, vectors, ohq, ohk, valid, gather_at, grad) = lax.optimization_barrier(
        (slots, (x, vectors, ohq, ohk, valid, gather_at, grad))
    )
    mine = natural_order(gather_at, slots, plan)
    moved = []

    def cross(i, after=None):
        own = mine[i] if after is None else tied(mine[i], after)
        moved.append(far_swap(own))
        return moved[-1]

    def four(i, after=None):
        there = moved[i] if after is None else tied(moved[i], after)
        return [mine[i], core_swap(mine[i]), there, core_swap(there)]

    weights = []
    saved = []
    for layer in range(LAYERS):
        vec, bq, bv, b1 = vectors[layer]
        if layer == 0:
            cross(0)
        wqkv = four(2 * layer, x if layer else None)
        x = tied(x, wqkv)
        if layer == 0:
            cross(1, moved[0])
        xs, q, kv = project(x, bq, bv, wqkv)
        kvp = core_swap(kv)
        o, lse = attend(q, kv, kvp, ohq, ohk)
        wfeed = four(2 * layer + 1, o)
        weights.append((wqkv, wfeed))
        if layer + 1 < LAYERS:
            done = moved[-1]
            cross(2 * layer + 2, done)
            cross(2 * layer + 3, (done, moved[-1]))
        n1, i1, y, hid, slope, n2, i2, x = post(o, x, vec, b1, wfeed)
        saved.append((xs, q, kv, kvp, o, lse, vec, n1, i1, y, hid, slope, n2, i2))
    activations = x * valid

    own_sums = [None] * (3 * LAYERS)
    far_sums = [None] * (3 * LAYERS)
    table_rows = [None] * LAYERS

    waiting = []

    def chip_sum(at, keep, got):
        waiting.append((at, keep, got))
        return add_low(keep[1], got[1])

    def own_chip_sums(after):
        while waiting:
            at, keep, got = waiting.pop()
            keep, got = tied((keep[0], got[0]), after)
            own_sums[at] = add_low(keep, got)

    moving = []
    for layer in reversed(range(LAYERS)):
        xs, q, kv, kvp, o, lse, vec, n1, i1, y, hid, slope, n2, i2 = saved[layer]
        wqkv, wfeed = weights[layer]
        gk, gs, ok, os, dr1, do, db1, sums = ffn_grad(
            grad, n2, i2, n1, i1, y, hid, slope, o, vec, wfeed
        )
        os, gs, ok, gk, do = tied((os, gs, ok, gk, do), moving)
        own_chip_sums(sums)
        got = [core_swap(os), core_swap(gs)]
        mid = chip_sum(3 * layer + 1, ok, got[0])
        down = chip_sum(3 * layer + 2, gk, got[1])
        far_sums[3 * layer + 1] = far_swap(mid)
        do = tied(do, (mid, down))
        dq, dkv, dkvp = attend_grad(q, kv, kvp, do, o, lse, ohq, ohk)
        dkvp = tied(dkvp, far_sums[3 * layer + 1])
        far_sums[3 * layer + 2] = far_swap(tied(down, far_sums[3 * layer + 1]))
        dkvr = core_swap(dkvp)
        pk, ps, grad, qsums = proj_grad(dq, dkv, dkvr, xs, dr1, wqkv)
        table_rows[layer] = (sums, qsums, db1)
        got = core_swap(ps)
        if layer:
            far = chip_sum(3 * layer, pk, got)
            grad = tied(grad, far)
            far_sums[3 * layer] = far_swap(far)
            moving = far_sums[3 * layer : 3 * layer + 3]
    input_grad, tab_keep, tab_send = embed_grad(
        place.astype(jnp.int32)[None], series, grad, vec_values, table_rows[0] + table_rows[1]
    )
    far_sums[0] = far_swap(chip_sum(0, pk, got))
    own_chip_sums(tab_send)
    tab = dp_sum(tab_keep + core_swap(tab_send), dp, far_sums[0])
    tab_part = tab[0] + far_swap(tab[1])
    tab_there = far_swap(tab_part)
    parts = [tab_part, core_swap(tab_part), tab_there, core_swap(tab_there)]
    vec_new_values, vec_new_first, vec_new_second, branch_bias_grads = vector_update(
        place.astype(jnp.int32)[None], vec_values, vec_first, vec_second, parts
    )
    at = jnp.concatenate([inner, who]).astype(jnp.int32)
    pieces = routed(at, own_sums, far_sums, dp, own_slots)
    if ringed:
        meanwhile = (tab, tab_part, parts)
        terms = ring_reduce([pieces[i] for i in range(dp)], order, meanwhile)
        terms = tied(terms, vec_new_values)
        grads = [t.reshape(own_slots, BLK, BLK) for t in terms]
    else:
        whole = lax.psum_scatter(pieces, "dp", scatter_dimension=0, tiled=True)
        grads = [whole.reshape(own_slots, BLK, BLK)]
    new_master, new_copy, new_first, new_second, new_left, new_right, left_next, right_next = soap(
        grads,
        master[0],
        first_moment[0],
        second_moment[0],
        left_stats[0],
        right_stats[0],
        left_basis[0],
        right_basis[0],
    )
    return (
        activations,
        input_grad,
        new_master[None],
        new_copy[None],
        new_first[None],
        new_second[None],
        new_left[None],
        new_right[None],
        left_next[None],
        right_next[None],
        vec_new_values,
        vec_new_first,
        vec_new_second,
        branch_bias_grads,
    )


def solution(mesh):
    placed = (
        P(("dp", "head"), None),
        P(("dp", "head"), None),
        P("dp", None),
        P("head", None),
        P("head", "dp", None, None),
        P("head", "dp", None, None),
        P("head", "dp", None, None),
        P("head", "dp", None, None),
        P("head", "dp", None, None),
        P("head", "dp", None, None),
        P("head", "dp", None, None),
        P(),
        P(),
        P(),
    )
    return jax.shard_map(
        on_device,
        mesh=mesh,
        in_specs=placed,
        out_specs=(
            P(("dp", "head"), None),
            P(("dp", "head"), None),
            P("head", "dp", None, None),
            P("head", "dp", None, None),
            P("head", "dp", None, None),
            P("head", "dp", None, None),
            P("head", "dp", None, None),
            P("head", "dp", None, None),
            P("head", "dp", None, None),
            P("head", "dp", None, None),
            P(),
            P(),
            P(),
            P(),
        ),
        check_vma=False,
    )
```

```python
import functools

import jax
import jax.numpy as jnp
from jax import lax
from jax.experimental import pallas as pl
from jax.experimental.pallas import tpu as pltpu
from jax.sharding import PartitionSpec as P

D = 512
HEADS = 8
HD = 64
FF = 2048
LOOK = 96
LAYERS = 2
BLK = 128
STEP = 10

f32 = jnp.float32
HI = lax.Precision.HIGHEST
norm_eps = 1e-05
beta_first = 0.5
beta_second = 0.5
beta_stats = 0.5
adam_eps = 1e-08
rate_matrix = 0.02
rate_vector = 0.15
weight_decay = 0.01


def window_ids(lengths, bucket_rows):
    bounds = jnp.cumsum(lengths, axis=1, dtype=jnp.int32)
    places = jnp.arange(bucket_rows, dtype=jnp.int32)
    return jnp.sum(
        (places[None, :, None] >= bounds[:, None, :]).astype(jnp.int32), axis=2, dtype=jnp.int32
    )


def depth_vectors(vec_table, layer_at):
    ff_ratio = FF // D
    base_row = LOOK + 1 + layer_at * (8 + ff_ratio)
    return (
        vec_table[base_row],
        vec_table[base_row + 1],
        vec_table[base_row + 2],
        vec_table[base_row + 3],
        vec_table[base_row + 4],
        vec_table[base_row + 5 : base_row + 5 + ff_ratio].reshape(FF),
        vec_table[base_row + 5 + ff_ratio],
        vec_table[base_row + 6 + ff_ratio],
        vec_table[base_row + 7 + ff_ratio],
    )


def dot_hi(a, b, ca, cb):
    return lax.dot_general(
        a, b, (((ca,), (cb,)), ((), ())), precision=HI, preferred_element_type=f32
    )


def terms(x, count):
    out = []
    for i in range(count):
        part = x.astype(jnp.bfloat16)
        out.append(part)
        if i < count - 1:
            x = x - part.astype(f32)
    return out


def dot_terms(a, b, ca, cb, full=False):
    a = terms(a, 3 if full else 2)
    b = terms(b, 3 if full else 2)
    dims = (((ca,), (cb,)), ((), ()))
    left = jnp.concatenate(a[:2], axis=ca)
    right = jnp.concatenate(
        [jnp.concatenate([b[0], b[1]], axis=cb), jnp.concatenate([b[1], b[0]], axis=cb)], axis=1 - cb
    )
    out = lax.dot_general(left, right, dims, preferred_element_type=f32)
    out = out[:, :BLK] + out[:, BLK:]
    if full:
        out = out + lax.dot_general(
            jnp.concatenate([a[0], a[2]], axis=ca),
            jnp.concatenate([b[2], b[0]], axis=cb),
            dims,
            preferred_element_type=f32,
        )
    return out


PANEL = 32
AHEAD = 2


def recip(x):
    guess = pl.reciprocal(x, approx=True)
    guess = guess * (2.0 - x * guess)
    return guess * (2.0 - x * guess)


def qr_batch(a_ref, count):
    lane = lax.broadcasted_iota(jnp.int32, (1, 1, BLK), 2)
    sub8 = lax.broadcasted_iota(jnp.int32, (1, 8, 1), 1)
    sub = lax.broadcasted_iota(jnp.int32, (1, PANEL, 1), 1)
    for r0 in range(0, BLK, PANEL):
        tiles = [a_ref[:, r0 + 8 * t : r0 + 8 * t + 8, :] for t in range(PANEL // 8)]
        for k0 in range(0, PANEL, AHEAD):
            t0, s0 = divmod(k0, 8)
            cols = [
                [
                    jnp.broadcast_to(tiles[t][:, :, r0 + k : r0 + k + 1], (count, 8, BLK))
                    for k in range(k0, k0 + AHEAD)
                ]
                for t in range(PANEL // 8)
            ]
            for i in range(AHEAD):
                s = s0 + i
                inv = recip(cols[t0][i][:, s : s + 1, :])
                pn = (tiles[t0][:, s : s + 1, :] + (lane == r0 + k0 + i).astype(f32)) * inv
                rest = [cols[t0][j][:, s : s + 1, :] * inv for j in range(i + 1, AHEAD)]
                for t in range(t0, PANEL // 8):
                    c = cols[t][i]
                    if t == t0:
                        if s == 7:
                            continue
                        c = jnp.where(sub8 > s, c, 0.0)
                    tiles[t] = tiles[t] - c * pn
                    for j, m in enumerate(rest):
                        cols[t][i + 1 + j] = cols[t][i + 1 + j] - c * m
        done = jnp.concatenate(tiles, axis=1)
        diag = lane == sub + r0
        pivot = jnp.sum(jnp.where(diag, done, 0.0), axis=2, keepdims=True)
        done = jnp.where(diag, 1.0, jnp.where((lane > sub + r0) & (lane < r0 + PANEL), 0.0, done))
        done = done * lax.rsqrt(pivot)
        a_ref[:, r0 : r0 + PANEL, :] = done
        r1 = r0 + PANEL
        if r1 < BLK:
            lane2 = lax.broadcasted_iota(jnp.int32, (BLK - r1, BLK), 1)
            clear = (lane2 >= r0) & (lane2 < r1)
            z0, z1, z2 = terms(done, 3)
            left = jnp.concatenate([z0, z0, z0, z1, z1, z2], axis=1)
            right = jnp.concatenate([z0, z1, z2, z0, z1, z0], axis=1)
            for b in range(count):
                update = lax.dot_general(
                    left[b], right[b], (((0,), (0,)), ((), ())), preferred_element_type=f32
                )
                a_ref[b, r1:, :] = jnp.where(clear, 0.0, a_ref[b, r1:, :]) - update[r1:]


def soap_kernel(count, *refs):
    for s in range(refs[0].shape[0]):
        soap_slot(s, sum(ref[s].astype(f32) for ref in refs[:count]), *refs[count:])
    soap_finish(*refs[-4:])


def soap_slot(
    s, g, mas_ref, m1_ref, m2_ref, ls_ref, rs_ref, lb_ref, rb_ref,
    nm_ref, nc_ref, n1_ref, n2_ref, nl_ref, nr_ref, ql_ref, qr_ref, mat_ref, a_ref,
):
    group = mas_ref.shape[0]
    lb = lb_ref[s]
    rb = rb_ref[s]
    rot = dot_terms(dot_terms(lb, g, 0, 0), rb, 1, 0)
    n1 = 0.5 * m1_ref[s] + 0.5 * rot
    n2 = 0.5 * m2_ref[s] + 0.5 * rot * rot
    n1_ref[s] = n1
    n2_ref[s] = n2
    corr = 1.0 - 0.5**STEP
    ratio = n1 / corr / (jnp.sqrt(n2 / corr) + adam_eps)
    upd = dot_terms(dot_terms(lb, ratio, 1, 0), rb, 1, 1)
    mas = mas_ref[s]
    nm = mas - rate_matrix * (upd + weight_decay * mas)
    nm_ref[s] = nm
    nc_ref[s] = nm.astype(jnp.bfloat16)
    nl = 0.5 * ls_ref[s] + 0.5 * dot_terms(g, g, 1, 1)
    nr = 0.5 * rs_ref[s] + 0.5 * dot_terms(g, g, 0, 0)
    nl_ref[s] = nl
    nr_ref[s] = nr
    for side, (st, ba) in enumerate(((nl, lb), (nr, rb))):
        m = dot_terms(st, ba, 1, 0, True)
        m = m * lax.rsqrt(jnp.sum(m * m, axis=0, keepdims=True))
        at = 2 * (pl.program_id(0) * group + s) + side
        mat_ref[at] = m
        a_ref[at] = dot_terms(m, m, 0, 0, True)


def soap_finish(ql_ref, qr_ref, mat_ref, a_ref):
    @pl.when(pl.program_id(0) == pl.num_programs(0) - 1)
    def _():
        count = a_ref.shape[0]
        qr_batch(a_ref, count)
        keep = lax.broadcasted_iota(jnp.int32, (BLK, BLK), 1) <= lax.broadcasted_iota(
            jnp.int32, (BLK, BLK), 0
        )
        for j in range(count // 2):
            for side, ref in enumerate((ql_ref, qr_ref)):
                x = jnp.where(keep, a_ref[2 * j + side], 0.0)
                ref[j] = dot_terms(mat_ref[2 * j + side], x, 1, 1, True)


def soap(gs, master, m1, m2, ls, rs, lb, rb):
    n = master.shape[0]
    group = SOAP_GROUP if n % SOAP_GROUP == 0 else n
    one = pl.BlockSpec((group, BLK, BLK), lambda i: (i, 0, 0))
    whole = pl.BlockSpec((n, BLK, BLK), lambda i: (0, 0, 0))
    sh = jax.ShapeDtypeStruct((n, BLK, BLK), f32)
    shb = jax.ShapeDtypeStruct((n, BLK, BLK), jnp.bfloat16)
    return pl.pallas_call(
        functools.partial(soap_kernel, len(gs)),
        grid=(n // group,),
        in_specs=[one] * (len(gs) + 7),
        out_specs=[one] * 6 + [whole] * 2,
        out_shape=[sh, shb, sh, sh, sh, sh, sh, sh],
        scratch_shapes=[pltpu.VMEM((2 * n, BLK, BLK), f32)] * 2,
        compiler_params=pltpu.CompilerParams(vmem_limit_bytes=16 * 2**20),
        cost_estimate=pl.CostEstimate(flops=40 * 10**6, bytes_accessed=0, transcendentals=0),
        name="soap",
    )(*gs, master, m1, m2, ls, rs, lb, rb)


SOAP_GROUP = 2


bf16 = jnp.bfloat16
LANES = 128
TOP = 64
ROW_TILE = 512
BIG = 1e30
CORR = 1.0 - 0.5**STEP


def params(mib=48):
    return pltpu.CompilerParams(vmem_limit_bytes=mib * 2**20)


MIB = dict(
    embed=6, project=8, attend=16, post=20, ffn_grad=24, attend_grad=16, proj_grad=12, embed_grad=8, vector=4, natural=6, routed=8,
)


def cost(micros):
    return pl.CostEstimate(flops=int(micros * 1e6), bytes_accessed=0, transcendentals=0)


def shape(dims, kind=f32):
    return jax.ShapeDtypeStruct(dims, kind)


def dot(a, b, ca=1, cb=0):
    return lax.dot_general(a, b, (((ca,), (cb,)), ((), ())), preferred_element_type=f32)


def planes(refs):
    return (refs[0],), (refs[1],), (refs[2], refs[3]), (refs[4], refs[5])


def place_block(dst, refs, j, r0, c0):
    for ref in refs:
        dst[r0 : r0 + ref.shape[1], c0 : c0 + BLK] = ref[j]
        r0 += ref.shape[1]


def place_blocks(dst, refs, first, rows, cols, row_step, col_step):
    for r, plane in enumerate(planes(refs)):
        for j in range(rows * cols):
            row, col = divmod(j, cols)
            place_block(dst, plane, first + j, r * row_step + row * BLK, r * col_step + col * BLK)


def place_qkv(dst, refs):
    for r, plane in enumerate(planes(refs)):
        for j in range(12):
            row, col = divmod(j, 3)
            c0 = D + (2 * r + col - 1) * BLK if col else r * BLK
            place_block(dst, plane, j, row * BLK, c0)


def layer_norm(resid):
    center = resid - jnp.mean(resid, axis=1, keepdims=True)
    inv = lax.rsqrt(jnp.mean(center * center, axis=1, keepdims=True) + norm_eps)
    return center * inv, inv


def layer_norm_grad(grad, unit, inv, gain):
    dn = grad * gain
    return inv * (
        dn
        - jnp.mean(dn, axis=1, keepdims=True)
        - unit * jnp.mean(dn * unit, axis=1, keepdims=True)
    )


def col_sum(values):
    return jnp.sum(values, axis=0, keepdims=True)


def embed_kernel(series_ref, we_ref, be_ref, x_ref):
    x_ref[...] = dot_hi(series_ref[...].astype(f32), we_ref[...], 1, 0) + be_ref[...]


def embed(series, table):
    rows = series.shape[0]
    return pl.pallas_call(
        embed_kernel, out_shape=shape((rows, D)), compiler_params=params(MIB["embed"]), name="embed"
    )(series, table[:LOOK], table[LOOK : LOOK + 1])


def proj_kernel(x_ref, bq_ref, bv_ref, w0, w1, w2, w3, w4, w5, xs_ref, q_ref, kv_ref, w_s):
    place_qkv(w_s, (w0, w1, w2, w3, w4, w5))
    xs = x_ref[...].astype(bf16)
    xs_ref[...] = xs
    q_ref[...] = (dot(xs, w_s[:, :D]) + bq_ref[...]).astype(bf16)
    kv = dot(xs, w_s[:, D:])
    for r in range(4):
        at = 2 * r * BLK
        kv_ref[:, at : at + BLK] = kv[:, at : at + BLK].astype(bf16)
        value = kv[:, at + BLK : at + 2 * BLK] + bv_ref[:, r * BLK : (r + 1) * BLK]
        kv_ref[:, at + BLK : at + 2 * BLK] = value.astype(bf16)


def project(x, bq, bv, wqkv):
    rows = x.shape[0]
    return pl.pallas_call(
        proj_kernel,
        out_shape=[
            shape((rows, D), bf16),
            shape((rows, D), bf16),
            shape((rows, 2 * D), bf16),
        ],
        scratch_shapes=[pltpu.VMEM((D, 3 * D), bf16)],
        compiler_params=params(MIB["project"]),
        name="project",
        cost_estimate=cost(3),
    )(x, bq, bv, *wqkv)


def half_mask(i, kind=bf16):
    lane = lax.broadcasted_iota(jnp.int32, (1, LANES), 1)
    return ((lane >= HD * i) & (lane < HD * (i + 1))).astype(f32).astype(kind)


def three_terms(col):
    first = col.astype(bf16).astype(f32)
    second = (col - first).astype(bf16).astype(f32)
    return first, second, col - first - second


def lanes_with(base, at, cols):
    lane = lax.broadcasted_iota(jnp.int32, base.shape, 1)
    for i, col in enumerate(cols):
        base = jnp.where(lane == at + i, col, base)
    return base.astype(bf16)


def attend_kernel(q_ref, kv_ref, kvp_ref, ohq_ref, ohk_ref, o_ref, lse_ref, ka, va):
    rows = q_ref.shape[0]
    ka[:rows, :LANES] = kv_ref[:, :LANES]
    ka[rows:, :LANES] = kvp_ref[:, :LANES]
    ka[:, LANES:] = ohk_ref[...]
    lane = lax.broadcasted_iota(jnp.int32, (ROW_TILE, LANES), 1)
    for i in range(2):
        m = half_mask(i)
        va[i, :rows, :LANES] = kv_ref[:, LANES:] * m
        va[i, rows:, :LANES] = kvp_ref[:, LANES:] * m
        va[i, :, LANES:] = jnp.ones((2 * rows, LANES), bf16)

    def tile(t, c):
        at = pl.ds(t * ROW_TILE, ROW_TILE)
        total = jnp.zeros((ROW_TILE, LANES), f32)
        stat = jnp.zeros((ROW_TILE, LANES), f32)
        for i in range(2):
            qa = jnp.concatenate([q_ref[at] * (half_mask(i) * bf16(0.125)), ohq_ref[at]], axis=1)
            s = dot(qa, ka[...], 1, 1)
            high = jnp.max(s, axis=1, keepdims=True)
            e = jnp.exp(s - high).astype(bf16)
            out = dot(e, va[i])
            norm = out[:, LANES:]
            total = total + out[:, :LANES] / norm
            stat = jnp.where(lane == i, high + jnp.log(norm), stat)
        o_ref[at] = total.astype(bf16)
        lse_ref[at] = stat
        return c

    lax.fori_loop(0, rows // ROW_TILE, tile, 0)


def attend(q, kv, kvp, ohq, ohk):
    rows = q.shape[0]
    pair = pl.BlockSpec((rows, LANES), lambda h: (0, h))
    both = pl.BlockSpec((rows, 2 * LANES), lambda h: (0, h))
    other = pl.BlockSpec((rows, 2 * LANES), lambda h: (0, h + 1 - 2 * lax.rem(h, 2)))
    return pl.pallas_call(
        attend_kernel,
        grid=(D // LANES,),
        in_specs=[pair, both, other]
        + [
            pl.BlockSpec((rows, LANES), lambda h: (0, 0)),
            pl.BlockSpec((2 * rows, LANES), lambda h: (0, 0)),
        ],
        out_specs=[pair, pair],
        out_shape=[shape((rows, D), bf16), shape((rows, D))],
        scratch_shapes=[
            pltpu.VMEM((2 * rows, 2 * LANES), bf16),
            pltpu.VMEM((2, 2 * rows, 2 * LANES), bf16),
        ],
        compiler_params=params(MIB["attend"]),
        name="attend",
        cost_estimate=cost(11),
    )(q, kv, kvp, ohq, ohk)


def post_kernel(
    o_ref, x_ref, vec_ref, b1_ref, a0, a1, a2, a3, a4, a5,
    n1_ref, i1_ref, y_ref, hid_ref, slope_ref, n2_ref, i2_ref, x2_ref,
    wo_s, w1_s, w2_s,
):
    place_blocks(wo_s, (a0, a1, a2, a3, a4, a5), 0, 1, 4, BLK, 0)
    place_blocks(w1_s, (a0, a1, a2, a3, a4, a5), 4, 4, 4, 0, D)
    place_blocks(w2_s, (a0, a1, a2, a3, a4, a5), 20, 4, 4, D, 0)

    def tile(t, c):
        at = pl.ds(t * ROW_TILE, ROW_TILE)
        vec = [vec_ref[i : i + 1, :] for i in range(6)]
        unit, inv = layer_norm(x_ref[at] + dot(o_ref[at], wo_s[...]) + vec[0])
        n1_ref[at] = unit
        i1_ref[at] = jnp.broadcast_to(inv, (ROW_TILE, LANES))
        y = unit * vec[1] + vec[2]
        yb = y.astype(bf16)
        y_ref[at] = yb
        pre = dot(yb, w1_s[...]) + b1_ref[...]
        phi = 0.5 * (1.0 + lax.erf(pre * (0.5**0.5)))
        hid = (pre * phi).astype(bf16)
        hid_ref[at] = hid
        slope = phi + pre * (jnp.exp(-0.5 * pre * pre) * 0.3989422804014327)
        slope_ref[at] = slope.astype(bf16)
        fed = dot(hid, w2_s[...])
        unit, inv = layer_norm(y + fed + vec[3])
        n2_ref[at] = unit
        i2_ref[at] = jnp.broadcast_to(inv, (ROW_TILE, LANES))
        x2_ref[at] = unit * vec[4] + vec[5]
        return c

    lax.fori_loop(0, x_ref.shape[0] // ROW_TILE, tile, 0)


def post(o, x, vec, b1, wfeed):
    rows = x.shape[0]
    return pl.pallas_call(
        post_kernel,
        out_shape=[
            shape((rows, D)),
            shape((rows, LANES)),
            shape((rows, D), bf16),
            shape((rows, FF), bf16),
            shape((rows, FF), bf16),
            shape((rows, D)),
            shape((rows, LANES)),
            shape((rows, D)),
        ],
        scratch_shapes=[
            pltpu.VMEM((D, D), bf16),
            pltpu.VMEM((D, FF), bf16),
            pltpu.VMEM((FF, D), bf16),
        ],
        compiler_params=params(MIB["post"]),
        name="post",
        cost_estimate=cost(11),
    )(o, x, vec, b1, *wfeed)


def store_blocks(refs, r, first, rows, cols, value):
    keep_ref, send_ref = refs
    ref = send_ref if r % 2 else keep_ref
    for j in range(rows * cols):
        row, col = divmod(j, cols)
        ref[r // 2, first + j] = value[row * BLK : (row + 1) * BLK, col * BLK : (col + 1) * BLK]


def ffn_grad_kernel(
    e_ref, n2_ref, i2_ref, n1_ref, i1_ref, y_ref, hid_ref, slope_ref, o_ref, vec_ref,
    a0, a1, a2, a3, a4, a5,
    gk_ref, gs_ref, ok_ref, os_ref, dr1_ref, do_ref, db1_ref, sums_ref,
    wo_s, w1_s, w2_s, dr2_s, dfr_s, dpre_s, dar_s,
):
    rows = e_ref.shape[0]
    place_blocks(wo_s, (a0, a1, a2, a3, a4, a5), 0, 1, 4, BLK, 0)
    place_blocks(w1_s, (a0, a1, a2, a3, a4, a5), 4, 4, 4, 0, D)
    place_blocks(w2_s, (a0, a1, a2, a3, a4, a5), 20, 4, 4, D, 0)
    tiles = rows // ROW_TILE
    gain_two = vec_ref[4:5, :]
    gain_one = vec_ref[1:2, :]
    zero = jnp.zeros((1, D), f32)

    def tile_two(t, c):
        at = pl.ds(t * ROW_TILE, ROW_TILE)
        grad = e_ref[at]
        unit = n2_ref[at]
        dr2 = layer_norm_grad(grad, unit, i2_ref[at, 0:1], gain_two)
        dr2_s[at] = dr2
        dfr_s[at] = dr2.astype(bf16)
        return (c[0] + col_sum(dr2), c[1] + col_sum(grad * unit), c[2] + col_sum(grad))

    db2, dg2, dc2 = lax.fori_loop(0, tiles, tile_two, (zero, zero, zero))

    for r in range(FF // D):
        cols = slice(r * D, (r + 1) * D)

        def tile_up(t, c):
            at = pl.ds(t * ROW_TILE, ROW_TILE)
            dh = dot(dfr_s[at], w2_s[cols, :], 1, 1)
            dpre = (dh * slope_ref[at, cols].astype(f32)).astype(bf16)
            dpre_s[at, cols] = dpre
            dr2_s[at] = dr2_s[at] + dot(dpre, w1_s[:, cols], 1, 1)
            return c + col_sum(dpre.astype(f32))

        db1_ref[r : r + 1, :] = lax.fori_loop(0, tiles, tile_up, zero)
        store_blocks((gk_ref, gs_ref), r, 0, 4, 4, dot(hid_ref[:, cols], dfr_s[...], 0, 0).astype(bf16))
        store_blocks((ok_ref, os_ref), r, 4, 4, 4, dot(y_ref[...], dpre_s[:, cols], 0, 0).astype(bf16))

    def tile_one(t, c):
        at = pl.ds(t * ROW_TILE, ROW_TILE)
        grad = dr2_s[at]
        unit = n1_ref[at]
        dr1 = layer_norm_grad(grad, unit, i1_ref[at, 0:1], gain_one)
        dr1_ref[at] = dr1
        dar = dr1.astype(bf16)
        dar_s[at] = dar
        do_ref[at] = dot(dar, wo_s[...], 1, 1).astype(bf16)
        return (c[0] + col_sum(dr1), c[1] + col_sum(grad * unit), c[2] + col_sum(grad))

    dbo, dg1, dc1 = lax.fori_loop(0, tiles, tile_one, (zero, zero, zero))
    dwo = dot(o_ref[...], dar_s[...], 0, 0).astype(bf16)
    for r in range(4):
        store_blocks((ok_ref, os_ref), r, 0, 1, 4, dwo[r * BLK : (r + 1) * BLK])
    for i, value in enumerate((dbo, dg1, dc1, db2, dg2, dc2, zero, zero)):
        sums_ref[i : i + 1, :] = value


def ffn_grad(e, n2, i2, n1, i1, y, hid, slope, o, vec, wfeed):
    rows = e.shape[0]
    return pl.pallas_call(
        ffn_grad_kernel,
        out_shape=[
            shape((2, 16, BLK, BLK), bf16),
            shape((2, 16, BLK, BLK), bf16),
            shape((2, 20, BLK, BLK), bf16),
            shape((2, 20, BLK, BLK), bf16),
            shape((rows, D)),
            shape((rows, D), bf16),
            shape((FF // D, D)),
            shape((8, D)),
        ],
        scratch_shapes=[
            pltpu.VMEM((D, D), bf16),
            pltpu.VMEM((D, FF), bf16),
            pltpu.VMEM((FF, D), bf16),
            pltpu.VMEM((rows, D), f32),
            pltpu.VMEM((rows, D), bf16),
            pltpu.VMEM((rows, FF), bf16),
            pltpu.VMEM((rows, D), bf16),
        ],
        compiler_params=params(MIB["ffn_grad"]),
        name="ffn_grad",
        cost_estimate=cost(16),
    )(e, n2, i2, n1, i1, y, hid, slope, o, vec, *wfeed)


def attend_grad_kernel(
    q_ref, kv_ref, kvp_ref, do_ref, o_ref, lse_ref, ohq_ref, ohk_ref,
    dq_ref, dkv_ref, dkvp_ref,
    ka, va, qa, da, kt,
):
    rows = q_ref.shape[0]
    ka[:rows, :LANES] = kv_ref[:, :LANES]
    ka[rows:, :LANES] = kvp_ref[:, :LANES]
    ka[:, LANES:] = ohk_ref[...]
    va[:rows, :LANES] = kv_ref[:, LANES:]
    va[rows:, :LANES] = kvp_ref[:, LANES:]
    va[:, LANES:] = jnp.ones((2 * rows, LANES), bf16)
    kt[...] = ka[:, :LANES].T
    product = do_ref[...].astype(f32) * o_ref[...].astype(f32)
    for i in range(2):
        m = half_mask(i)
        qa[i, :, :LANES] = q_ref[...] * (m * bf16(0.125))
        qa[i, :, LANES:] = lanes_with(
            ohq_ref[...].astype(f32), 120, three_terms(-lse_ref[:, i : i + 1])
        )
        da[i, :, :LANES] = do_ref[...] * m
        delta = jnp.sum(product * half_mask(i, f32), axis=1, keepdims=True)
        da[i, :, LANES:] = lanes_with(jnp.zeros((rows, LANES), f32), 0, three_terms(-delta))

    def tile(t, sums):
        at = pl.ds(pl.multiple_of(t * ROW_TILE, ROW_TILE), ROW_TILE)
        dk = jnp.zeros((ROW_TILE, LANES), f32)
        dv = jnp.zeros((ROW_TILE, LANES), f32)
        new = []
        for i in range(2):
            p = jnp.exp(dot(ka[at], qa[i], 1, 1))
            ds = (p * dot(va[at], da[i], 1, 1)).astype(bf16)
            dv = dv + dot(p.astype(bf16), da[i, :, :LANES])
            dk = dk + dot(ds, qa[i, :, :LANES])
            new.append(sums[i] + dot(kt[:, at], ds))
        return tuple(new), dk.astype(bf16), dv.astype(bf16)

    sums = (jnp.zeros((LANES, rows), f32),) * 2
    half = rows // ROW_TILE

    def own(t, sums):
        sums, dk, dv = tile(t, sums)
        at = pl.ds(t * ROW_TILE, ROW_TILE)
        dkv_ref[at, :LANES] = dk
        dkv_ref[at, LANES:] = dv
        return sums

    def other(t, sums):
        sums, dk, dv = tile(t + half, sums)
        at = pl.ds(t * ROW_TILE, ROW_TILE)
        dkvp_ref[at, :LANES] = dk
        dkvp_ref[at, LANES:] = dv
        return sums

    sums = lax.fori_loop(0, half, own, sums)
    sums = lax.fori_loop(0, half, other, sums)
    row = lax.broadcasted_iota(jnp.int32, (LANES, rows), 0)
    dq_ref[...] = (jnp.where(row < HD, sums[0], sums[1]) * 0.125).T.astype(bf16)


def attend_grad(q, kv, kvp, do, o, lse, ohq, ohk):
    rows = q.shape[0]
    pair = pl.BlockSpec((rows, LANES), lambda h: (0, h))
    both = pl.BlockSpec((rows, 2 * LANES), lambda h: (0, h))
    other = pl.BlockSpec((rows, 2 * LANES), lambda h: (0, h + 1 - 2 * lax.rem(h, 2)))
    return pl.pallas_call(
        attend_grad_kernel,
        grid=(D // LANES,),
        in_specs=[pair, both, other, pair, pair, pair]
        + [
            pl.BlockSpec((rows, LANES), lambda h: (0, 0)),
            pl.BlockSpec((2 * rows, LANES), lambda h: (0, 0)),
        ],
        out_specs=[pair, both, other],
        out_shape=[shape((rows, D), bf16)] + [shape((rows, 2 * D), bf16)] * 2,
        scratch_shapes=[
            pltpu.VMEM((2 * rows, 2 * LANES), bf16),
            pltpu.VMEM((2 * rows, 2 * LANES), bf16),
            pltpu.VMEM((2, rows, 2 * LANES), bf16),
            pltpu.VMEM((2, rows, 2 * LANES), bf16),
            pltpu.VMEM((LANES, 2 * rows), bf16),
        ],
        compiler_params=params(MIB["attend_grad"]),
        name="attend_grad",
        cost_estimate=cost(23),
    )(q, kv, kvp, do, o, lse, ohq, ohk)


def proj_grad_kernel(
    dq_ref, dkv_ref, dkvr_ref, xs_ref, dr1_ref, w0, w1, w2, w3, w4, w5,
    gk_ref, gs_ref, dx_ref, sums_ref, w_s,
):
    place_qkv(w_s, (w0, w1, w2, w3, w4, w5))
    dq = dq_ref[...]
    dkv = (dkv_ref[...].astype(f32) + dkvr_ref[...].astype(f32)).astype(bf16)
    xs = xs_ref[...]
    sums_ref[0:1, :] = col_sum(dq.astype(f32))
    sums_ref[2:8, :] = jnp.zeros((6, D), f32)
    grads = (dot(xs, dq, 0, 0).astype(bf16), dot(xs, dkv, 0, 0).astype(bf16))
    for r in range(4):
        out = gs_ref if r % 2 else gk_ref
        c0 = (2 * r + 1) * BLK
        sums_ref[1:2, r * BLK : (r + 1) * BLK] = col_sum(dkv[:, c0 : c0 + BLK].astype(f32))
        for row in range(4):
            rows = slice(row * BLK, (row + 1) * BLK)
            out[r // 2, row * 3] = grads[0][rows, r * BLK : (r + 1) * BLK]
            for part in range(2):
                c0 = (2 * r + part) * BLK
                out[r // 2, row * 3 + 1 + part] = grads[1][rows, c0 : c0 + BLK]
    dx_ref[...] = dr1_ref[...] + dot(dq, w_s[:, :D], 1, 1) + dot(dkv, w_s[:, D:], 1, 1)


def proj_grad(dq, dkv, dkvr, xs, dr1, wqkv):
    rows = xs.shape[0]
    return pl.pallas_call(
        proj_grad_kernel,
        out_shape=[
            shape((2, 12, BLK, BLK), bf16),
            shape((2, 12, BLK, BLK), bf16),
            shape((rows, D)),
            shape((8, D)),
        ],
        scratch_shapes=[pltpu.VMEM((D, 3 * D), bf16)],
        compiler_params=params(MIB["proj_grad"]),
        name="proj_grad",
        cost_estimate=cost(5),
    )(dq, dkv, dkvr, xs, dr1, *wqkv)


def embed_grad_kernel(
    place_ref, series_ref, g_ref, we_ref, s0, q0, b0, s1, q1, b1, in_ref, keep_ref, send_ref, tab
):
    place = place_ref[0]
    g = g_ref[...]
    in_ref[...] = dot_hi(g, we_ref[...], 1, 1)
    tab[:LOOK] = dot_hi(series_ref[...].astype(f32), g, 0, 0)
    tab[LOOK : LOOK + 1] = col_sum(g)
    per_layer = 8 + FF // D
    for layer, (sums, qsums, db1) in enumerate(((s0, q0, b0), (s1, q1, b1))):
        base = LOOK + 1 + layer * per_layer
        for r in range(4):
            h = place ^ r
            lanes = pl.ds(pl.multiple_of(h * BLK, BLK), BLK)
            tab[base : base + 2, lanes] = qsums[0:2, r * BLK : (r + 1) * BLK]
            tab[pl.ds(base + 5 + h, 1), :] = db1[r : r + 1, :]
        tab[base + 2 : base + 5] = sums[0:3]
        tab[base + 5 + FF // D : base + per_layer] = sums[3:6]
    used = LOOK + 1 + LAYERS * per_layer
    tab[used:] = jnp.zeros((BLK - used, D), f32)
    for r in range(4):
        rows = tab[pl.ds(pl.multiple_of((place ^ r) * 32, 32), 32), :]
        out = send_ref if r % 2 else keep_ref
        for c in range(4):
            out[r // 2, c * 32 : (c + 1) * 32] = rows[:, c * BLK : (c + 1) * BLK]


def embed_grad(place, series, g, table, sums):
    rows = series.shape[0]
    spec = pl.BlockSpec(memory_space=pltpu.VMEM)
    return pl.pallas_call(
        embed_grad_kernel,
        in_specs=[pl.BlockSpec(memory_space=pltpu.SMEM)] + [spec] * 9,
        out_shape=[
            shape((rows, LOOK)),
            shape((2, BLK, BLK)),
            shape((2, BLK, BLK)),
        ],
        scratch_shapes=[pltpu.VMEM((BLK, D), f32)],
        compiler_params=params(MIB["embed_grad"]),
        name="embed_grad",
        cost_estimate=cost(2),
    )(place, series, g, table[:LOOK], *sums)


def vector_kernel(
    place_ref, val_ref, first_ref, second_ref, p0, p1, p2, p3, nv_ref, n1_ref, n2_ref, bias_ref, tab
):
    for r, part in enumerate((p0, p1, p2, p3)):
        rows = pl.ds(pl.multiple_of((place_ref[0] ^ r) * 32, 32), 32)
        for c in range(4):
            tab[rows, c * BLK : (c + 1) * BLK] = part[c * 32 : (c + 1) * 32]
    grad = tab[: val_ref.shape[0]]
    val = val_ref[...]
    first = 0.5 * first_ref[...] + 0.5 * grad
    second = 0.5 * second_ref[...] + 0.5 * grad * grad
    n1_ref[...] = first
    n2_ref[...] = second
    nv_ref[...] = val - rate_vector * (
        first / CORR / (jnp.sqrt(second / CORR) + adam_eps) + weight_decay * val
    )
    per_layer = 8 + FF // D
    for layer in range(LAYERS):
        base = LOOK + 1 + layer * per_layer
        bias_ref[2 * layer : 2 * layer + 1] = tab[base + 2 : base + 3]
        bias_ref[2 * layer + 1 : 2 * layer + 2] = tab[base + 5 + FF // D : base + 6 + FF // D]


def vector_update(place, values, first, second, parts):
    spec = pl.BlockSpec(memory_space=pltpu.VMEM)
    return pl.pallas_call(
        vector_kernel,
        in_specs=[pl.BlockSpec(memory_space=pltpu.SMEM)] + [spec] * 7,
        out_shape=[shape(values.shape)] * 3 + [shape((2 * LAYERS, D))],
        scratch_shapes=[pltpu.VMEM((BLK, D), f32)],
        compiler_params=params(MIB["vector"]),
        name="vector",
        cost_estimate=cost(2),
    )(place, values, first, second, *parts)


PARTS = ((0, 12), (12, 20), (32, 16))
HELD = ((0, 12), (12, 36))


def natural_kernel(plan, at_ref, *refs):
    count = len(plan)
    slots, outs, held = refs[:count], refs[count:-1], refs[-1]
    for ref, start in zip(slots, plan):
        held[start : start + ref.shape[0]] = ref[...]
    for i in range(len(HELD) * LAYERS):
        layer, part = divmod(i, len(HELD))
        first, n = HELD[part]
        for j in range(n):
            block = held[at_ref[layer * 48 + first + j]]
            outs[i][j] = block
            if len(outs) > len(HELD) * LAYERS:
                outs[len(HELD) * LAYERS + i][j] = block[TOP:]


def natural_order(at, slots, plan, lower):
    total = sum(s.shape[0] for s in slots)
    rows = slots[0].shape[1]
    spec = pl.BlockSpec(memory_space=pltpu.VMEM)
    heights = (rows, BLK - TOP) if lower else (rows,)
    return pl.pallas_call(
        functools.partial(natural_kernel, plan),
        in_specs=[pl.BlockSpec(memory_space=pltpu.SMEM)] + [spec] * len(slots),
        out_shape=[
            shape((n, height, BLK), bf16)
            for height in heights
            for _ in range(LAYERS)
            for _, n in HELD
        ],
        scratch_shapes=[pltpu.VMEM((total, rows, BLK), bf16)],
        compiler_params=params(MIB["natural"]),
        name="natural",
        cost_estimate=cost(3),
    )(at, *slots)


def routed_kernel(at_ref, *refs):
    own, got, out = refs[:6], refs[6:12], refs[12]
    out[...] = jnp.zeros(out.shape, bf16)
    for i in range(6):
        layer, part = divmod(i, 3)
        first, n = PARTS[part]
        for j in range(n):
            place = at_ref[layer * 48 + first + j]
            who = at_ref[96 + layer * 48 + first + j]
            value = own[i][j].astype(f32) + got[i][j].astype(f32)
            out[who, pl.ds(pl.multiple_of(place * BLK, BLK), BLK), :] = value.astype(bf16)


def routed(at, own, got, count, slots_each):
    spec = pl.BlockSpec(memory_space=pltpu.VMEM)
    return pl.pallas_call(
        routed_kernel,
        in_specs=[pl.BlockSpec(memory_space=pltpu.SMEM)] + [spec] * 12,
        out_shape=shape((count, slots_each * BLK, BLK), bf16),
        compiler_params=params(MIB["routed"]),
        name="routed",
        cost_estimate=cost(4),
    )(at, *own, *got)


def ring_of(count):
    half = count // 2
    return [2 * i for i in range(half)] + [2 * (half - 1 - i) + 1 for i in range(half)]


def ring_shift(value, order, by):
    n = len(order)
    return lax.ppermute(value, "dp", [(order[i], order[(i + by) % n]) for i in range(n)])


def ring_gather(value, order):
    n = len(order)
    half = value.shape[0] // 2

    def top(items):
        return [(far_swap(array[:, :TOP]), k, start) for array, k, start in items]

    held = [(value, 0, 0)]
    far = top(held)
    crossing = far
    ahead = behind = value
    for step in range(1, n // 2):
        if step > 1:
            behind, ahead = tied((behind, ahead), [x[0] for x in crossing])
            crossing = top(held[-2:])
            far = far + crossing
        behind = ring_shift(behind, order, 1)
        ahead = ring_shift(ahead, order, -1)
        held += [(behind, n - step, 0), (ahead, step, 0)]
    behind, ahead = tied((behind, ahead), [x[0] for x in crossing])
    far = far + top(held[-2:])
    held.append((ring_shift(behind[:half], order, 1), n // 2, 0))
    held.append((ring_shift(ahead[half:], order, -1), n // 2, half))
    far = far + top(held[-2:])
    return held, far


def ring_reduce(pieces, order, meanwhile):
    n = len(order)
    half = pieces[0].shape[0] // 2
    up = ring_shift(pieces[n // 2][:half], order, 1)
    down = ring_shift(pieces[n // 2][half:], order, -1)
    for step in range(1, n // 2):
        near, far = pieces[n // 2 - step], pieces[n // 2 + step]
        if step == 1:
            up = jnp.concatenate([add_low(up, near[:half]), near[half:]], axis=0)
            down = jnp.concatenate([far[:half], add_low(down, far[half:])], axis=0)
        else:
            up, down = add_low(up, near), add_low(down, far)
        up, down = tied((up, down), meanwhile[step - 1])
        up, down = ring_shift(up, order, 1), ring_shift(down, order, -1)
    return pieces[0], up, down


def dp_sum(value, count, after):
    bit = 1
    while bit < count:
        if 2 * bit >= count:
            value = tied(value, after)
        low = value.astype(bf16)
        there = lax.ppermute(low, "dp", [(i, i ^ bit) for i in range(count)])
        value = low.astype(f32) + there.astype(f32)
        bit *= 2
    return value


def add_low(a, b):
    return (a.astype(f32) + b.astype(f32)).astype(bf16)


def core_swap(value):
    return lax.ppermute(value, "head", [(i, i ^ 1) for i in range(4)])


def far_swap(value):
    return lax.ppermute(value, "head", [(i, i ^ 2) for i in range(4)])


def tied(values, after):
    return lax.optimization_barrier((values, after))[0]


def one_hots(ids):
    lane = jnp.arange(LANES, dtype=jnp.int32)[None, :]
    same = ids[:, None] == lane
    return jnp.where(same, -BIG, 0.0).astype(bf16), jnp.where(same, 0.0, 1.0).astype(bf16)


def relative(row, place):
    pieces = row.reshape(4, -1)
    return jnp.take(pieces, jnp.arange(4) ^ place, axis=0).reshape(1, -1)


def on_device(
    series,
    cotangent,
    window_lengths,
    owner_list,
    master,
    first_moment,
    second_moment,
    left_stats,
    right_stats,
    left_basis,
    right_basis,
    vec_values,
    vec_first,
    vec_second,
):
    place = lax.axis_index("head")
    spot = lax.axis_index("dp")
    dp = lax.axis_size("dp")
    ringed = dp == 8
    rows = series.shape[0]
    own_slots = master.shape[1]
    buckets, win = window_lengths.shape
    bucket_rows = rows * 4 // buckets
    owner_row = owner_list[0]
    who = owner_row // own_slots
    if ringed:
        order = ring_of(dp)
        ring_at = jnp.asarray([order.index(d) for d in range(dp)], jnp.int32)
        who = (ring_at[who] - ring_at[spot]) % dp
    inner = owner_row % own_slots
    gather_at = who * own_slots + inner

    copies = master[0].astype(bf16)
    if ringed:
        held, far = ring_gather(copies, order)
        slots, plan = [x[0] for x in held], tuple(x[1] * own_slots + x[2] for x in held)
        tops, far_plan = [x[0] for x in far], tuple(x[1] * own_slots + x[2] for x in far)
    else:
        slots, plan = [lax.all_gather(copies, "dp", axis=0, tiled=True)], (0,)
        tops, far_plan = [far_swap(slots[0][:, :TOP])], (0,)
    far_at = far_swap(gather_at)
    windows = window_ids(window_lengths, bucket_rows)
    ids = windows.reshape(4, rows)
    own_ids = lax.dynamic_index_in_dim(ids, place, 0, False)
    pair_ids = lax.dynamic_index_in_dim(ids, place ^ 1, 0, False)
    ohq, ohk_own = one_hots(own_ids)
    ohk = jnp.concatenate([ohk_own, one_hots(pair_ids)[1]], axis=0)
    valid = (own_ids < win).astype(f32)[:, None]

    x = embed(series, vec_values)
    vectors = []
    for layer in range(LAYERS):
        bq, bv, bo, g1, c1, b1, b2, g2, c2 = depth_vectors(vec_values, layer)
        vec = jnp.stack([bo, g1, c1, b2, g2, c2, g2, c2])
        vectors.append([vec] + [relative(row, place) for row in (bq, bv, b1)])
    grad = cotangent * valid
    slots, (x, vectors, ohq, ohk, valid, gather_at, far_at, grad) = lax.optimization_barrier(
        (slots, (x, vectors, ohq, ohk, valid, gather_at, far_at, grad))
    )
    mine = natural_order(gather_at, slots, plan, True)
    mine, lower = mine[: len(HELD) * LAYERS], mine[len(HELD) * LAYERS :]
    upper = natural_order(far_at, tops, far_plan, False)
    moved = []

    def cross(i, after=None):
        own = lower[i] if after is None else tied(lower[i], after)
        moved.append(far_swap(own))
        return moved[-1]

    def four(i, after=None):
        there = moved[i] if after is None else tied(moved[i], after)
        return [
            mine[i], core_swap(mine[i]), upper[i], there, core_swap(upper[i]), core_swap(there)
        ]

    weights = []
    saved = []
    for layer in range(LAYERS):
        vec, bq, bv, b1 = vectors[layer]
        if layer == 0:
            cross(0)
        wqkv = four(2 * layer, x if layer else None)
        x = tied(x, wqkv)
        if layer == 0:
            cross(1, moved[0])
        xs, q, kv = project(x, bq, bv, wqkv)
        kvp = core_swap(kv)
        o, lse = attend(q, kv, kvp, ohq, ohk)
        wfeed = four(2 * layer + 1, o)
        weights.append((wqkv, wfeed))
        if layer + 1 < LAYERS:
            done = moved[-1]
            cross(2 * layer + 2, done)
            cross(2 * layer + 3, (done, moved[-1]))
        n1, i1, y, hid, slope, n2, i2, x = post(o, x, vec, b1, wfeed)
        saved.append((xs, q, kv, kvp, o, lse, vec, n1, i1, y, hid, slope, n2, i2))
    activations = x * valid

    own_sums = [None] * (3 * LAYERS)
    far_sums = [None] * (3 * LAYERS)
    table_rows = [None] * LAYERS

    waiting = []

    def chip_sum(at, keep, got):
        waiting.append((at, keep, got))
        return add_low(keep[1], got[1])

    def own_chip_sums(after):
        while waiting:
            at, keep, got = waiting.pop()
            keep, got = tied((keep[0], got[0]), after)
            own_sums[at] = add_low(keep, got)

    moving = []
    for layer in reversed(range(LAYERS)):
        xs, q, kv, kvp, o, lse, vec, n1, i1, y, hid, slope, n2, i2 = saved[layer]
        wqkv, wfeed = weights[layer]
        gk, gs, ok, os, dr1, do, db1, sums = ffn_grad(
            grad, n2, i2, n1, i1, y, hid, slope, o, vec, wfeed
        )
        os, gs, ok, gk, do = tied((os, gs, ok, gk, do), moving)
        own_chip_sums(sums)
        got = [core_swap(os), core_swap(gs)]
        mid = chip_sum(3 * layer + 1, ok, got[0])
        down = chip_sum(3 * layer + 2, gk, got[1])
        far_sums[3 * layer + 1] = far_swap(mid)
        do = tied(do, (mid, down))
        dq, dkv, dkvp = attend_grad(q, kv, kvp, do, o, lse, ohq, ohk)
        dkvp = tied(dkvp, far_sums[3 * layer + 1])
        far_sums[3 * layer + 2] = far_swap(tied(down, far_sums[3 * layer + 1]))
        dkvr = core_swap(dkvp)
        pk, ps, grad, qsums = proj_grad(dq, dkv, dkvr, xs, dr1, wqkv)
        table_rows[layer] = (sums, qsums, db1)
        got = core_swap(ps)
        if layer:
            far = chip_sum(3 * layer, pk, got)
            grad = tied(grad, far)
            far_sums[3 * layer] = far_swap(far)
            moving = far_sums[3 * layer : 3 * layer + 3]
    input_grad, tab_keep, tab_send = embed_grad(
        place.astype(jnp.int32)[None], series, grad, vec_values, table_rows[0] + table_rows[1]
    )
    far_sums[0] = far_swap(chip_sum(0, pk, got))
    own_chip_sums(tab_send)
    tab = dp_sum(tab_keep + core_swap(tab_send), dp, far_sums[0])
    tab_part = tab[0] + far_swap(tab[1])
    tab_there = far_swap(tab_part)
    parts = [tab_part, core_swap(tab_part), tab_there, core_swap(tab_there)]
    vec_new_values, vec_new_first, vec_new_second, branch_bias_grads = vector_update(
        place.astype(jnp.int32)[None], vec_values, vec_first, vec_second, parts
    )
    at = jnp.concatenate([inner, who]).astype(jnp.int32)
    pieces = routed(at, own_sums, far_sums, dp, own_slots)
    if ringed:
        meanwhile = (tab, tab_part, parts)
        terms = ring_reduce([pieces[i] for i in range(dp)], order, meanwhile)
        terms = tied(terms, vec_new_values)
        grads = [t.reshape(own_slots, BLK, BLK) for t in terms]
    else:
        whole = lax.psum_scatter(pieces, "dp", scatter_dimension=0, tiled=True)
        grads = [whole.reshape(own_slots, BLK, BLK)]
    new_master, new_copy, new_first, new_second, new_left, new_right, left_next, right_next = soap(
        grads,
        master[0],
        first_moment[0],
        second_moment[0],
        left_stats[0],
        right_stats[0],
        left_basis[0],
        right_basis[0],
    )
    return (
        activations,
        input_grad,
        new_master[None],
        new_copy[None],
        new_first[None],
        new_second[None],
        new_left[None],
        new_right[None],
        left_next[None],
        right_next[None],
        vec_new_values,
        vec_new_first,
        vec_new_second,
        branch_bias_grads,
    )


def solution(mesh):
    placed = (
        P(("dp", "head"), None),
        P(("dp", "head"), None),
        P("dp", None),
        P("head", None),
        P("head", "dp", None, None),
        P("head", "dp", None, None),
        P("head", "dp", None, None),
        P("head", "dp", None, None),
        P("head", "dp", None, None),
        P("head", "dp", None, None),
        P("head", "dp", None, None),
        P(),
        P(),
        P(),
    )
    return jax.shard_map(
        on_device,
        mesh=mesh,
        in_specs=placed,
        out_specs=(
            P(("dp", "head"), None),
            P(("dp", "head"), None),
            P("head", "dp", None, None),
            P("head", "dp", None, None),
            P("head", "dp", None, None),
            P("head", "dp", None, None),
            P("head", "dp", None, None),
            P("head", "dp", None, None),
            P("head", "dp", None, None),
            P("head", "dp", None, None),
            P(),
            P(),
            P(),
            P(),
        ),
        check_vma=False,
    )
```

```python
import functools

import jax
import jax.numpy as jnp
from jax import lax
from jax.experimental import pallas as pl
from jax.experimental.pallas import tpu as pltpu
from jax.sharding import PartitionSpec as P

D = 512
HEADS = 8
HD = 64
FF = 2048
LOOK = 96
LAYERS = 2
BLK = 128
STEP = 10

f32 = jnp.float32
HI = lax.Precision.HIGHEST
norm_eps = 1e-05
beta_first = 0.5
beta_second = 0.5
beta_stats = 0.5
adam_eps = 1e-08
rate_matrix = 0.02
rate_vector = 0.15
weight_decay = 0.01


def window_ids(lengths, bucket_rows):
    bounds = jnp.cumsum(lengths, axis=1, dtype=jnp.int32)
    places = jnp.arange(bucket_rows, dtype=jnp.int32)
    return jnp.sum(
        (places[None, :, None] >= bounds[:, None, :]).astype(jnp.int32), axis=2, dtype=jnp.int32
    )


def depth_vectors(vec_table, layer_at):
    ff_ratio = FF // D
    base_row = LOOK + 1 + layer_at * (8 + ff_ratio)
    return (
        vec_table[base_row],
        vec_table[base_row + 1],
        vec_table[base_row + 2],
        vec_table[base_row + 3],
        vec_table[base_row + 4],
        vec_table[base_row + 5 : base_row + 5 + ff_ratio].reshape(FF),
        vec_table[base_row + 5 + ff_ratio],
        vec_table[base_row + 6 + ff_ratio],
        vec_table[base_row + 7 + ff_ratio],
    )


def dot_hi(a, b, ca, cb):
    return lax.dot_general(
        a, b, (((ca,), (cb,)), ((), ())), precision=HI, preferred_element_type=f32
    )


def terms(x, count):
    out = []
    for i in range(count):
        part = x.astype(jnp.bfloat16)
        out.append(part)
        if i < count - 1:
            x = x - part.astype(f32)
    return out


def dot_terms(a, b, ca, cb, full=False):
    a = terms(a, 3 if full else 2)
    b = terms(b, 3 if full else 2)
    dims = (((ca,), (cb,)), ((), ()))
    left = jnp.concatenate(a[:2], axis=ca)
    right = jnp.concatenate(
        [jnp.concatenate([b[0], b[1]], axis=cb), jnp.concatenate([b[1], b[0]], axis=cb)], axis=1 - cb
    )
    out = lax.dot_general(left, right, dims, preferred_element_type=f32)
    out = out[:, :BLK] + out[:, BLK:]
    if full:
        out = out + lax.dot_general(
            jnp.concatenate([a[0], a[2]], axis=ca),
            jnp.concatenate([b[2], b[0]], axis=cb),
            dims,
            preferred_element_type=f32,
        )
    return out


PANEL = 32
AHEAD = 2


def recip(x):
    guess = pl.reciprocal(x, approx=True)
    guess = guess * (2.0 - x * guess)
    return guess * (2.0 - x * guess)


def qr_batch(a_ref, count):
    lane = lax.broadcasted_iota(jnp.int32, (1, 1, BLK), 2)
    sub8 = lax.broadcasted_iota(jnp.int32, (1, 8, 1), 1)
    sub = lax.broadcasted_iota(jnp.int32, (1, PANEL, 1), 1)
    for r0 in range(0, BLK, PANEL):
        tiles = [a_ref[:, r0 + 8 * t : r0 + 8 * t + 8, :] for t in range(PANEL // 8)]
        for k0 in range(0, PANEL, AHEAD):
            t0, s0 = divmod(k0, 8)
            cols = [
                [
                    jnp.broadcast_to(tiles[t][:, :, r0 + k : r0 + k + 1], (count, 8, BLK))
                    for k in range(k0, k0 + AHEAD)
                ]
                for t in range(PANEL // 8)
            ]
            for i in range(AHEAD):
                s = s0 + i
                inv = recip(cols[t0][i][:, s : s + 1, :])
                pn = (tiles[t0][:, s : s + 1, :] + (lane == r0 + k0 + i).astype(f32)) * inv
                rest = [cols[t0][j][:, s : s + 1, :] * inv for j in range(i + 1, AHEAD)]
                for t in range(t0, PANEL // 8):
                    c = cols[t][i]
                    if t == t0:
                        if s == 7:
                            continue
                        c = jnp.where(sub8 > s, c, 0.0)
                    tiles[t] = tiles[t] - c * pn
                    for j, m in enumerate(rest):
                        cols[t][i + 1 + j] = cols[t][i + 1 + j] - c * m
        done = jnp.concatenate(tiles, axis=1)
        diag = lane == sub + r0
        pivot = jnp.sum(jnp.where(diag, done, 0.0), axis=2, keepdims=True)
        done = jnp.where(diag, 1.0, jnp.where((lane > sub + r0) & (lane < r0 + PANEL), 0.0, done))
        done = done * lax.rsqrt(pivot)
        a_ref[:, r0 : r0 + PANEL, :] = done
        r1 = r0 + PANEL
        if r1 < BLK:
            lane2 = lax.broadcasted_iota(jnp.int32, (BLK - r1, BLK), 1)
            clear = (lane2 >= r0) & (lane2 < r1)
            z0, z1, z2 = terms(done, 3)
            left = jnp.concatenate([z0, z0, z0, z1, z1, z2], axis=1)
            right = jnp.concatenate([z0, z1, z2, z0, z1, z0], axis=1)
            for b in range(count):
                update = lax.dot_general(
                    left[b], right[b], (((0,), (0,)), ((), ())), preferred_element_type=f32
                )
                a_ref[b, r1:, :] = jnp.where(clear, 0.0, a_ref[b, r1:, :]) - update[r1:]


def soap_kernel(count, *refs):
    for s in range(refs[0].shape[0]):
        soap_slot(s, sum(ref[s].astype(f32) for ref in refs[:count]), *refs[count:])
    soap_finish(*refs[-4:])


def soap_slot(
    s, g, mas_ref, m1_ref, m2_ref, ls_ref, rs_ref, lb_ref, rb_ref,
    nm_ref, nc_ref, n1_ref, n2_ref, nl_ref, nr_ref, ql_ref, qr_ref, mat_ref, a_ref,
):
    group = mas_ref.shape[0]
    lb = lb_ref[s]
    rb = rb_ref[s]
    rot = dot_terms(dot_terms(lb, g, 0, 0), rb, 1, 0)
    n1 = 0.5 * m1_ref[s] + 0.5 * rot
    n2 = 0.5 * m2_ref[s] + 0.5 * rot * rot
    n1_ref[s] = n1
    n2_ref[s] = n2
    corr = 1.0 - 0.5**STEP
    ratio = n1 / corr / (jnp.sqrt(n2 / corr) + adam_eps)
    upd = dot_terms(dot_terms(lb, ratio, 1, 0), rb, 1, 1)
    mas = mas_ref[s]
    nm = mas - rate_matrix * (upd + weight_decay * mas)
    nm_ref[s] = nm
    nc_ref[s] = nm.astype(jnp.bfloat16)
    nl = 0.5 * ls_ref[s] + 0.5 * dot_terms(g, g, 1, 1)
    nr = 0.5 * rs_ref[s] + 0.5 * dot_terms(g, g, 0, 0)
    nl_ref[s] = nl
    nr_ref[s] = nr
    for side, (st, ba) in enumerate(((nl, lb), (nr, rb))):
        m = dot_terms(st, ba, 1, 0, True)
        m = m * lax.rsqrt(jnp.sum(m * m, axis=0, keepdims=True))
        at = 2 * (pl.program_id(0) * group + s) + side
        mat_ref[at] = m
        a_ref[at] = dot_terms(m, m, 0, 0, True)


def soap_finish(ql_ref, qr_ref, mat_ref, a_ref):
    @pl.when(pl.program_id(0) == pl.num_programs(0) - 1)
    def _():
        count = a_ref.shape[0]
        qr_batch(a_ref, count)
        keep = lax.broadcasted_iota(jnp.int32, (BLK, BLK), 1) <= lax.broadcasted_iota(
            jnp.int32, (BLK, BLK), 0
        )
        for j in range(count // 2):
            for side, ref in enumerate((ql_ref, qr_ref)):
                x = jnp.where(keep, a_ref[2 * j + side], 0.0)
                ref[j] = dot_terms(mat_ref[2 * j + side], x, 1, 1, True)


def soap(gs, master, m1, m2, ls, rs, lb, rb):
    n = master.shape[0]
    group = SOAP_GROUP if n % SOAP_GROUP == 0 else n
    one = pl.BlockSpec((group, BLK, BLK), lambda i: (i, 0, 0))
    whole = pl.BlockSpec((n, BLK, BLK), lambda i: (0, 0, 0))
    sh = jax.ShapeDtypeStruct((n, BLK, BLK), f32)
    shb = jax.ShapeDtypeStruct((n, BLK, BLK), jnp.bfloat16)
    return pl.pallas_call(
        functools.partial(soap_kernel, len(gs)),
        grid=(n // group,),
        in_specs=[one] * (len(gs) + 7),
        out_specs=[one] * 6 + [whole] * 2,
        out_shape=[sh, shb, sh, sh, sh, sh, sh, sh],
        scratch_shapes=[pltpu.VMEM((2 * n, BLK, BLK), f32)] * 2,
        compiler_params=pltpu.CompilerParams(vmem_limit_bytes=16 * 2**20),
        cost_estimate=pl.CostEstimate(flops=40 * 10**6, bytes_accessed=0, transcendentals=0),
        name="soap",
    )(*gs, master, m1, m2, ls, rs, lb, rb)


SOAP_GROUP = 2


bf16 = jnp.bfloat16
LANES = 128
TOP = 64
ROW_TILE = 512
BIG = 1e30
CORR = 1.0 - 0.5**STEP


def params(mib=48):
    return pltpu.CompilerParams(vmem_limit_bytes=mib * 2**20)


MIB = dict(
    embed=6, project=8, attend=16, post=20, ffn_grad=24, attend_grad=16, proj_grad=12, embed_grad=8, vector=4, natural=6, routed=8,
)


def cost(micros):
    return pl.CostEstimate(flops=int(micros * 1e6), bytes_accessed=0, transcendentals=0)


def shape(dims, kind=f32):
    return jax.ShapeDtypeStruct(dims, kind)


def dot(a, b, ca=1, cb=0):
    return lax.dot_general(a, b, (((ca,), (cb,)), ((), ())), preferred_element_type=f32)


def planes(refs):
    return (refs[0],), (refs[1],), (refs[2], refs[3]), (refs[4], refs[5])


def place_block(dst, refs, j, r0, c0):
    for ref in refs:
        dst[r0 : r0 + ref.shape[1], c0 : c0 + BLK] = ref[j]
        r0 += ref.shape[1]


def place_blocks(dst, refs, first, rows, cols, row_step, col_step):
    for r, plane in enumerate(planes(refs)):
        for j in range(rows * cols):
            row, col = divmod(j, cols)
            place_block(dst, plane, first + j, r * row_step + row * BLK, r * col_step + col * BLK)


def place_qkv(dst, refs):
    for r, plane in enumerate(planes(refs)):
        for j in range(12):
            row, col = divmod(j, 3)
            c0 = D + (2 * r + col - 1) * BLK if col else r * BLK
            place_block(dst, plane, j, row * BLK, c0)


def layer_norm(resid):
    center = resid - jnp.mean(resid, axis=1, keepdims=True)
    inv = lax.rsqrt(jnp.mean(center * center, axis=1, keepdims=True) + norm_eps)
    return center * inv, inv


def layer_norm_grad(grad, unit, inv, gain):
    dn = grad * gain
    return inv * (
        dn
        - jnp.mean(dn, axis=1, keepdims=True)
        - unit * jnp.mean(dn * unit, axis=1, keepdims=True)
    )


def col_sum(values):
    return jnp.sum(values, axis=0, keepdims=True)


def embed_kernel(series_ref, we_ref, be_ref, x_ref):
    x_ref[...] = dot_hi(series_ref[...].astype(f32), we_ref[...], 1, 0) + be_ref[...]


def embed(series, table):
    rows = series.shape[0]
    return pl.pallas_call(
        embed_kernel, out_shape=shape((rows, D)), compiler_params=params(MIB["embed"]), name="embed"
    )(series, table[:LOOK], table[LOOK : LOOK + 1])


def proj_kernel(x_ref, bq_ref, bv_ref, w0, w1, w2, w3, w4, w5, xs_ref, q_ref, kv_ref, w_s):
    place_qkv(w_s, (w0, w1, w2, w3, w4, w5))
    xs = x_ref[...].astype(bf16)
    xs_ref[...] = xs
    q_ref[...] = (dot(xs, w_s[:, :D]) + bq_ref[...]).astype(bf16)
    kv = dot(xs, w_s[:, D:])
    for r in range(4):
        at = 2 * r * BLK
        kv_ref[:, at : at + BLK] = kv[:, at : at + BLK].astype(bf16)
        value = kv[:, at + BLK : at + 2 * BLK] + bv_ref[:, r * BLK : (r + 1) * BLK]
        kv_ref[:, at + BLK : at + 2 * BLK] = value.astype(bf16)


def project(x, bq, bv, wqkv):
    rows = x.shape[0]
    return pl.pallas_call(
        proj_kernel,
        out_shape=[
            shape((rows, D), bf16),
            shape((rows, D), bf16),
            shape((rows, 2 * D), bf16),
        ],
        scratch_shapes=[pltpu.VMEM((D, 3 * D), bf16)],
        compiler_params=params(MIB["project"]),
        name="project",
        cost_estimate=cost(3),
    )(x, bq, bv, *wqkv)


def half_mask(i, kind=bf16):
    lane = lax.broadcasted_iota(jnp.int32, (1, LANES), 1)
    return ((lane >= HD * i) & (lane < HD * (i + 1))).astype(f32).astype(kind)


def three_terms(col):
    first = col.astype(bf16).astype(f32)
    second = (col - first).astype(bf16).astype(f32)
    return first, second, col - first - second


def lanes_with(base, at, cols):
    lane = lax.broadcasted_iota(jnp.int32, base.shape, 1)
    for i, col in enumerate(cols):
        base = jnp.where(lane == at + i, col, base)
    return base.astype(bf16)


def attend_kernel(q_ref, kv_ref, kvp_ref, ohq_ref, ohk_ref, o_ref, lse_ref, ka, va):
    rows = q_ref.shape[0]
    ka[:rows, :LANES] = kv_ref[:, :LANES]
    ka[rows:, :LANES] = kvp_ref[:, :LANES]
    ka[:, LANES:] = ohk_ref[...]
    lane = lax.broadcasted_iota(jnp.int32, (ROW_TILE, LANES), 1)
    for i in range(2):
        m = half_mask(i)
        va[i, :rows, :LANES] = kv_ref[:, LANES:] * m
        va[i, rows:, :LANES] = kvp_ref[:, LANES:] * m
        va[i, :, LANES:] = jnp.ones((2 * rows, LANES), bf16)

    def tile(t, c):
        at = pl.ds(t * ROW_TILE, ROW_TILE)
        total = jnp.zeros((ROW_TILE, LANES), f32)
        stat = jnp.zeros((ROW_TILE, LANES), f32)
        for i in range(2):
            qa = jnp.concatenate([q_ref[at] * (half_mask(i) * bf16(0.125)), ohq_ref[at]], axis=1)
            s = dot(qa, ka[...], 1, 1)
            high = jnp.max(s, axis=1, keepdims=True)
            e = jnp.exp(s - high).astype(bf16)
            out = dot(e, va[i])
            norm = out[:, LANES:]
            total = total + out[:, :LANES] / norm
            stat = jnp.where(lane == i, high + jnp.log(norm), stat)
        o_ref[at] = total.astype(bf16)
        lse_ref[at] = stat
        return c

    lax.fori_loop(0, rows // ROW_TILE, tile, 0)


def attend(q, kv, kvp, ohq, ohk):
    rows = q.shape[0]
    pair = pl.BlockSpec((rows, LANES), lambda h: (0, h))
    both = pl.BlockSpec((rows, 2 * LANES), lambda h: (0, h))
    other = pl.BlockSpec((rows, 2 * LANES), lambda h: (0, h + 1 - 2 * lax.rem(h, 2)))
    return pl.pallas_call(
        attend_kernel,
        grid=(D // LANES,),
        in_specs=[pair, both, other]
        + [
            pl.BlockSpec((rows, LANES), lambda h: (0, 0)),
            pl.BlockSpec((2 * rows, LANES), lambda h: (0, 0)),
        ],
        out_specs=[pair, pair],
        out_shape=[shape((rows, D), bf16), shape((rows, D))],
        scratch_shapes=[
            pltpu.VMEM((2 * rows, 2 * LANES), bf16),
            pltpu.VMEM((2, 2 * rows, 2 * LANES), bf16),
        ],
        compiler_params=params(MIB["attend"]),
        name="attend",
        cost_estimate=cost(11),
    )(q, kv, kvp, ohq, ohk)


def post_kernel(
    o_ref, x_ref, vec_ref, b1_ref, a0, a1, a2, a3, a4, a5,
    n1_ref, i1_ref, y_ref, hid_ref, slope_ref, n2_ref, i2_ref, x2_ref,
    wo_s, w1_s, w2_s,
):
    place_blocks(wo_s, (a0, a1, a2, a3, a4, a5), 0, 1, 4, BLK, 0)
    place_blocks(w1_s, (a0, a1, a2, a3, a4, a5), 4, 4, 4, 0, D)
    place_blocks(w2_s, (a0, a1, a2, a3, a4, a5), 20, 4, 4, D, 0)

    def tile(t, c):
        at = pl.ds(t * ROW_TILE, ROW_TILE)
        vec = [vec_ref[i : i + 1, :] for i in range(6)]
        unit, inv = layer_norm(x_ref[at] + dot(o_ref[at], wo_s[...]) + vec[0])
        n1_ref[at] = unit
        i1_ref[at] = jnp.broadcast_to(inv, (ROW_TILE, LANES))
        y = unit * vec[1] + vec[2]
        yb = y.astype(bf16)
        y_ref[at] = yb
        pre = dot(yb, w1_s[...]) + b1_ref[...]
        phi = 0.5 * (1.0 + lax.erf(pre * (0.5**0.5)))
        hid = (pre * phi).astype(bf16)
        hid_ref[at] = hid
        slope = phi + pre * (jnp.exp(-0.5 * pre * pre) * 0.3989422804014327)
        slope_ref[at] = slope.astype(bf16)
        fed = dot(hid, w2_s[...])
        unit, inv = layer_norm(y + fed + vec[3])
        n2_ref[at] = unit
        i2_ref[at] = jnp.broadcast_to(inv, (ROW_TILE, LANES))
        x2_ref[at] = unit * vec[4] + vec[5]
        return c

    lax.fori_loop(0, x_ref.shape[0] // ROW_TILE, tile, 0)


def post(o, x, vec, b1, wfeed):
    rows = x.shape[0]
    return pl.pallas_call(
        post_kernel,
        out_shape=[
            shape((rows, D)),
            shape((rows, LANES)),
            shape((rows, D), bf16),
            shape((rows, FF), bf16),
            shape((rows, FF), bf16),
            shape((rows, D)),
            shape((rows, LANES)),
            shape((rows, D)),
        ],
        scratch_shapes=[
            pltpu.VMEM((D, D), bf16),
            pltpu.VMEM((D, FF), bf16),
            pltpu.VMEM((FF, D), bf16),
        ],
        compiler_params=params(MIB["post"]),
        name="post",
        cost_estimate=cost(11),
    )(o, x, vec, b1, *wfeed)


def store_blocks(refs, r, first, rows, cols, value):
    keep_ref, send_ref = refs
    ref = send_ref if r % 2 else keep_ref
    for j in range(rows * cols):
        row, col = divmod(j, cols)
        ref[r // 2, first + j] = value[row * BLK : (row + 1) * BLK, col * BLK : (col + 1) * BLK]


def ffn_grad_kernel(
    e_ref, n2_ref, i2_ref, n1_ref, i1_ref, y_ref, hid_ref, slope_ref, o_ref, vec_ref,
    a0, a1, a2, a3, a4, a5,
    gk_ref, gs_ref, ok_ref, os_ref, dr1_ref, do_ref, db1_ref, sums_ref,
    wo_s, w1_s, w2_s, dr2_s, dfr_s, dpre_s, dar_s,
):
    rows = e_ref.shape[0]
    place_blocks(wo_s, (a0, a1, a2, a3, a4, a5), 0, 1, 4, BLK, 0)
    place_blocks(w1_s, (a0, a1, a2, a3, a4, a5), 4, 4, 4, 0, D)
    place_blocks(w2_s, (a0, a1, a2, a3, a4, a5), 20, 4, 4, D, 0)
    tiles = rows // ROW_TILE
    gain_two = vec_ref[4:5, :]
    gain_one = vec_ref[1:2, :]
    zero = jnp.zeros((1, D), f32)

    def tile_two(t, c):
        at = pl.ds(t * ROW_TILE, ROW_TILE)
        grad = e_ref[at]
        unit = n2_ref[at]
        dr2 = layer_norm_grad(grad, unit, i2_ref[at, 0:1], gain_two)
        dr2_s[at] = dr2
        dfr_s[at] = dr2.astype(bf16)
        return (c[0] + col_sum(dr2), c[1] + col_sum(grad * unit), c[2] + col_sum(grad))

    db2, dg2, dc2 = lax.fori_loop(0, tiles, tile_two, (zero, zero, zero))

    for r in range(FF // D):
        cols = slice(r * D, (r + 1) * D)

        def tile_up(t, c):
            at = pl.ds(t * ROW_TILE, ROW_TILE)
            dh = dot(dfr_s[at], w2_s[cols, :], 1, 1)
            dpre = (dh * slope_ref[at, cols].astype(f32)).astype(bf16)
            dpre_s[at, cols] = dpre
            dr2_s[at] = dr2_s[at] + dot(dpre, w1_s[:, cols], 1, 1)
            return c + col_sum(dpre.astype(f32))

        db1_ref[r : r + 1, :] = lax.fori_loop(0, tiles, tile_up, zero)
        store_blocks((gk_ref, gs_ref), r, 0, 4, 4, dot(hid_ref[:, cols], dfr_s[...], 0, 0).astype(bf16))
        store_blocks((ok_ref, os_ref), r, 4, 4, 4, dot(y_ref[...], dpre_s[:, cols], 0, 0).astype(bf16))

    def tile_one(t, c):
        at = pl.ds(t * ROW_TILE, ROW_TILE)
        grad = dr2_s[at]
        unit = n1_ref[at]
        dr1 = layer_norm_grad(grad, unit, i1_ref[at, 0:1], gain_one)
        dr1_ref[at] = dr1
        dar = dr1.astype(bf16)
        dar_s[at] = dar
        do_ref[at] = dot(dar, wo_s[...], 1, 1).astype(bf16)
        return (c[0] + col_sum(dr1), c[1] + col_sum(grad * unit), c[2] + col_sum(grad))

    dbo, dg1, dc1 = lax.fori_loop(0, tiles, tile_one, (zero, zero, zero))
    dwo = dot(o_ref[...], dar_s[...], 0, 0).astype(bf16)
    for r in range(4):
        store_blocks((ok_ref, os_ref), r, 0, 1, 4, dwo[r * BLK : (r + 1) * BLK])
    for i, value in enumerate((dbo, dg1, dc1, db2, dg2, dc2, zero, zero)):
        sums_ref[i : i + 1, :] = value


def ffn_grad(e, n2, i2, n1, i1, y, hid, slope, o, vec, wfeed):
    rows = e.shape[0]
    return pl.pallas_call(
        ffn_grad_kernel,
        out_shape=[
            shape((2, 16, BLK, BLK), bf16),
            shape((2, 16, BLK, BLK), bf16),
            shape((2, 20, BLK, BLK), bf16),
            shape((2, 20, BLK, BLK), bf16),
            shape((rows, D)),
            shape((rows, D), bf16),
            shape((FF // D, D)),
            shape((8, D)),
        ],
        scratch_shapes=[
            pltpu.VMEM((D, D), bf16),
            pltpu.VMEM((D, FF), bf16),
            pltpu.VMEM((FF, D), bf16),
            pltpu.VMEM((rows, D), f32),
            pltpu.VMEM((rows, D), bf16),
            pltpu.VMEM((rows, FF), bf16),
            pltpu.VMEM((rows, D), bf16),
        ],
        compiler_params=params(MIB["ffn_grad"]),
        name="ffn_grad",
        cost_estimate=cost(16),
    )(e, n2, i2, n1, i1, y, hid, slope, o, vec, *wfeed)


def attend_grad_kernel(
    q_ref, kv_ref, kvp_ref, do_ref, o_ref, lse_ref, ohq_ref, ohk_ref,
    dq_ref, dkv_ref, dkvp_ref,
    ka, va, qa, da, kt,
):
    rows = q_ref.shape[0]
    ka[:rows, :LANES] = kv_ref[:, :LANES]
    ka[rows:, :LANES] = kvp_ref[:, :LANES]
    ka[:, LANES:] = ohk_ref[...]
    va[:rows, :LANES] = kv_ref[:, LANES:]
    va[rows:, :LANES] = kvp_ref[:, LANES:]
    va[:, LANES:] = jnp.ones((2 * rows, LANES), bf16)
    kt[...] = ka[:, :LANES].T
    product = do_ref[...].astype(f32) * o_ref[...].astype(f32)
    for i in range(2):
        m = half_mask(i)
        qa[i, :, :LANES] = q_ref[...] * (m * bf16(0.125))
        qa[i, :, LANES:] = lanes_with(
            ohq_ref[...].astype(f32), 120, three_terms(-lse_ref[:, i : i + 1])
        )
        da[i, :, :LANES] = do_ref[...] * m
        delta = jnp.sum(product * half_mask(i, f32), axis=1, keepdims=True)
        da[i, :, LANES:] = lanes_with(jnp.zeros((rows, LANES), f32), 0, three_terms(-delta))

    def tile(t, sums):
        at = pl.ds(pl.multiple_of(t * ROW_TILE, ROW_TILE), ROW_TILE)
        dk = jnp.zeros((ROW_TILE, LANES), f32)
        dv = jnp.zeros((ROW_TILE, LANES), f32)
        new = []
        for i in range(2):
            p = jnp.exp(dot(ka[at], qa[i], 1, 1))
            ds = (p * dot(va[at], da[i], 1, 1)).astype(bf16)
            dv = dv + dot(p.astype(bf16), da[i, :, :LANES])
            dk = dk + dot(ds, qa[i, :, :LANES])
            new.append(sums[i] + dot(kt[:, at], ds))
        return tuple(new), dk.astype(bf16), dv.astype(bf16)

    sums = (jnp.zeros((LANES, rows), f32),) * 2
    half = rows // ROW_TILE

    def own(t, sums):
        sums, dk, dv = tile(t, sums)
        at = pl.ds(t * ROW_TILE, ROW_TILE)
        dkv_ref[at, :LANES] = dk
        dkv_ref[at, LANES:] = dv
        return sums

    def other(t, sums):
        sums, dk, dv = tile(t + half, sums)
        at = pl.ds(t * ROW_TILE, ROW_TILE)
        dkvp_ref[at, :LANES] = dk
        dkvp_ref[at, LANES:] = dv
        return sums

    sums = lax.fori_loop(0, half, own, sums)
    sums = lax.fori_loop(0, half, other, sums)
    row = lax.broadcasted_iota(jnp.int32, (LANES, rows), 0)
    dq_ref[...] = (jnp.where(row < HD, sums[0], sums[1]) * 0.125).T.astype(bf16)


def attend_grad(q, kv, kvp, do, o, lse, ohq, ohk):
    rows = q.shape[0]
    pair = pl.BlockSpec((rows, LANES), lambda h: (0, h))
    both = pl.BlockSpec((rows, 2 * LANES), lambda h: (0, h))
    other = pl.BlockSpec((rows, 2 * LANES), lambda h: (0, h + 1 - 2 * lax.rem(h, 2)))
    return pl.pallas_call(
        attend_grad_kernel,
        grid=(D // LANES,),
        in_specs=[pair, both, other, pair, pair, pair]
        + [
            pl.BlockSpec((rows, LANES), lambda h: (0, 0)),
            pl.BlockSpec((2 * rows, LANES), lambda h: (0, 0)),
        ],
        out_specs=[pair, both, other],
        out_shape=[shape((rows, D), bf16)] + [shape((rows, 2 * D), bf16)] * 2,
        scratch_shapes=[
            pltpu.VMEM((2 * rows, 2 * LANES), bf16),
            pltpu.VMEM((2 * rows, 2 * LANES), bf16),
            pltpu.VMEM((2, rows, 2 * LANES), bf16),
            pltpu.VMEM((2, rows, 2 * LANES), bf16),
            pltpu.VMEM((LANES, 2 * rows), bf16),
        ],
        compiler_params=params(MIB["attend_grad"]),
        name="attend_grad",
        cost_estimate=cost(23),
    )(q, kv, kvp, do, o, lse, ohq, ohk)


def proj_grad_kernel(
    dq_ref, dkv_ref, dkvr_ref, xs_ref, dr1_ref, w0, w1, w2, w3, w4, w5,
    gk_ref, gs_ref, dx_ref, sums_ref, w_s,
):
    place_qkv(w_s, (w0, w1, w2, w3, w4, w5))
    dq = dq_ref[...]
    dkv = (dkv_ref[...].astype(f32) + dkvr_ref[...].astype(f32)).astype(bf16)
    xs = xs_ref[...]
    sums_ref[0:1, :] = col_sum(dq.astype(f32))
    sums_ref[2:8, :] = jnp.zeros((6, D), f32)
    grads = (dot(xs, dq, 0, 0).astype(bf16), dot(xs, dkv, 0, 0).astype(bf16))
    for r in range(4):
        out = gs_ref if r % 2 else gk_ref
        c0 = (2 * r + 1) * BLK
        sums_ref[1:2, r * BLK : (r + 1) * BLK] = col_sum(dkv[:, c0 : c0 + BLK].astype(f32))
        for row in range(4):
            rows = slice(row * BLK, (row + 1) * BLK)
            out[r // 2, row * 3] = grads[0][rows, r * BLK : (r + 1) * BLK]
            for part in range(2):
                c0 = (2 * r + part) * BLK
                out[r // 2, row * 3 + 1 + part] = grads[1][rows, c0 : c0 + BLK]
    dx_ref[...] = dr1_ref[...] + dot(dq, w_s[:, :D], 1, 1) + dot(dkv, w_s[:, D:], 1, 1)


def proj_grad(dq, dkv, dkvr, xs, dr1, wqkv):
    rows = xs.shape[0]
    return pl.pallas_call(
        proj_grad_kernel,
        out_shape=[
            shape((2, 12, BLK, BLK), bf16),
            shape((2, 12, BLK, BLK), bf16),
            shape((rows, D)),
            shape((8, D)),
        ],
        scratch_shapes=[pltpu.VMEM((D, 3 * D), bf16)],
        compiler_params=params(MIB["proj_grad"]),
        name="proj_grad",
        cost_estimate=cost(5),
    )(dq, dkv, dkvr, xs, dr1, *wqkv)


def embed_grad_kernel(
    place_ref, series_ref, g_ref, we_ref, s0, q0, b0, s1, q1, b1, in_ref, keep_ref, send_ref, tab
):
    place = place_ref[0]
    g = g_ref[...]
    in_ref[...] = dot_hi(g, we_ref[...], 1, 1)
    tab[:LOOK] = dot_hi(series_ref[...].astype(f32), g, 0, 0)
    tab[LOOK : LOOK + 1] = col_sum(g)
    per_layer = 8 + FF // D
    for layer, (sums, qsums, db1) in enumerate(((s0, q0, b0), (s1, q1, b1))):
        base = LOOK + 1 + layer * per_layer
        for r in range(4):
            h = place ^ r
            lanes = pl.ds(pl.multiple_of(h * BLK, BLK), BLK)
            tab[base : base + 2, lanes] = qsums[0:2, r * BLK : (r + 1) * BLK]
            tab[pl.ds(base + 5 + h, 1), :] = db1[r : r + 1, :]
        tab[base + 2 : base + 5] = sums[0:3]
        tab[base + 5 + FF // D : base + per_layer] = sums[3:6]
    used = LOOK + 1 + LAYERS * per_layer
    tab[used:] = jnp.zeros((BLK - used, D), f32)
    for r in range(4):
        rows = tab[pl.ds(pl.multiple_of((place ^ r) * 32, 32), 32), :]
        out = send_ref if r % 2 else keep_ref
        for c in range(4):
            out[r // 2, c * 32 : (c + 1) * 32] = rows[:, c * BLK : (c + 1) * BLK]


def embed_grad(place, series, g, table, sums):
    rows = series.shape[0]
    spec = pl.BlockSpec(memory_space=pltpu.VMEM)
    return pl.pallas_call(
        embed_grad_kernel,
        in_specs=[pl.BlockSpec(memory_space=pltpu.SMEM)] + [spec] * 9,
        out_shape=[
            shape((rows, LOOK)),
            shape((2, BLK, BLK)),
            shape((2, BLK, BLK)),
        ],
        scratch_shapes=[pltpu.VMEM((BLK, D), f32)],
        compiler_params=params(MIB["embed_grad"]),
        name="embed_grad",
        cost_estimate=cost(2),
    )(place, series, g, table[:LOOK], *sums)


def vector_kernel(
    place_ref, val_ref, first_ref, second_ref, p0, p1, p2, p3, nv_ref, n1_ref, n2_ref, bias_ref, tab
):
    for r, part in enumerate((p0, p1, p2, p3)):
        rows = pl.ds(pl.multiple_of((place_ref[0] ^ r) * 32, 32), 32)
        for c in range(4):
            tab[rows, c * BLK : (c + 1) * BLK] = part[c * 32 : (c + 1) * 32]
    grad = tab[: val_ref.shape[0]]
    val = val_ref[...]
    first = 0.5 * first_ref[...] + 0.5 * grad
    second = 0.5 * second_ref[...] + 0.5 * grad * grad
    n1_ref[...] = first
    n2_ref[...] = second
    nv_ref[...] = val - rate_vector * (
        first / CORR / (jnp.sqrt(second / CORR) + adam_eps) + weight_decay * val
    )
    per_layer = 8 + FF // D
    for layer in range(LAYERS):
        base = LOOK + 1 + layer * per_layer
        bias_ref[2 * layer : 2 * layer + 1] = tab[base + 2 : base + 3]
        bias_ref[2 * layer + 1 : 2 * layer + 2] = tab[base + 5 + FF // D : base + 6 + FF // D]


def vector_update(place, values, first, second, parts):
    spec = pl.BlockSpec(memory_space=pltpu.VMEM)
    return pl.pallas_call(
        vector_kernel,
        in_specs=[pl.BlockSpec(memory_space=pltpu.SMEM)] + [spec] * 7,
        out_shape=[shape(values.shape)] * 3 + [shape((2 * LAYERS, D))],
        scratch_shapes=[pltpu.VMEM((BLK, D), f32)],
        compiler_params=params(MIB["vector"]),
        name="vector",
        cost_estimate=cost(2),
    )(place, values, first, second, *parts)


PARTS = ((0, 12), (12, 20), (32, 16))
HELD = ((0, 12), (12, 36))


def natural_kernel(plan, at_ref, *refs):
    count = len(plan)
    slots, outs, held = refs[:count], refs[count:-1], refs[-1]
    for ref, start in zip(slots, plan):
        held[start : start + ref.shape[0]] = ref[...]
    for i in range(len(HELD) * LAYERS):
        layer, part = divmod(i, len(HELD))
        first, n = HELD[part]
        for j in range(n):
            block = held[at_ref[layer * 48 + first + j]]
            outs[i][j] = block
            if len(outs) > len(HELD) * LAYERS:
                outs[len(HELD) * LAYERS + i][j] = block[TOP:]


def natural_order(at, slots, plan, lower):
    total = sum(s.shape[0] for s in slots)
    rows = slots[0].shape[1]
    spec = pl.BlockSpec(memory_space=pltpu.VMEM)
    heights = (rows, BLK - TOP) if lower else (rows,)
    return pl.pallas_call(
        functools.partial(natural_kernel, plan),
        in_specs=[pl.BlockSpec(memory_space=pltpu.SMEM)] + [spec] * len(slots),
        out_shape=[
            shape((n, height, BLK), bf16)
            for height in heights
            for _ in range(LAYERS)
            for _, n in HELD
        ],
        scratch_shapes=[pltpu.VMEM((total, rows, BLK), bf16)],
        compiler_params=params(MIB["natural"]),
        name="natural",
        cost_estimate=cost(3),
    )(at, *slots)


def routed_kernel(at_ref, *refs):
    own, got, out = refs[:6], refs[6:12], refs[12]
    out[...] = jnp.zeros(out.shape, bf16)
    for i in range(6):
        layer, part = divmod(i, 3)
        first, n = PARTS[part]
        for j in range(n):
            place = at_ref[layer * 48 + first + j]
            who = at_ref[96 + layer * 48 + first + j]
            value = own[i][j].astype(f32) + got[i][j].astype(f32)
            out[who, pl.ds(pl.multiple_of(place * BLK, BLK), BLK), :] = value.astype(bf16)


def routed(at, own, got, count, slots_each):
    spec = pl.BlockSpec(memory_space=pltpu.VMEM)
    return pl.pallas_call(
        routed_kernel,
        in_specs=[pl.BlockSpec(memory_space=pltpu.SMEM)] + [spec] * 12,
        out_shape=shape((count, slots_each * BLK, BLK), bf16),
        compiler_params=params(MIB["routed"]),
        name="routed",
        cost_estimate=cost(4),
    )(at, *own, *got)


def ring_of(count):
    half = count // 2
    return [2 * i for i in range(half)] + [2 * (half - 1 - i) + 1 for i in range(half)]


def ring_shift(value, order, by):
    n = len(order)
    return lax.ppermute(value, "dp", [(order[i], order[(i + by) % n]) for i in range(n)])


def ring_gather(value, order):
    n = len(order)
    half = value.shape[0] // 2

    def top(items):
        return [(far_swap(array[:, :TOP]), k, start) for array, k, start in items]

    held = [(value, 0, 0)]
    far = top(held)
    crossing = far
    ahead = behind = value
    for step in range(1, n // 2):
        if step > 2:
            behind, ahead = tied((behind, ahead), [x[0] for x in crossing])
        if step > 1:
            crossing = top(held[-2:]) if step > 2 else crossing + top(held[-2:])
            far = far + crossing[-2:]
        behind = ring_shift(behind, order, 1)
        ahead = ring_shift(ahead, order, -1)
        held += [(behind, n - step, 0), (ahead, step, 0)]
    behind, ahead = tied((behind, ahead), [x[0] for x in crossing])
    far = far + top(held[-2:])
    held.append((ring_shift(behind[:half], order, 1), n // 2, 0))
    held.append((ring_shift(ahead[half:], order, -1), n // 2, half))
    far = far + top(held[-2:])
    return held, far


def ring_reduce(pieces, order, meanwhile):
    n = len(order)
    half = pieces[0].shape[0] // 2
    up = ring_shift(pieces[n // 2][:half], order, 1)
    down = ring_shift(pieces[n // 2][half:], order, -1)
    for step in range(1, n // 2):
        near, far = pieces[n // 2 - step], pieces[n // 2 + step]
        if step == 1:
            up = jnp.concatenate([add_low(up, near[:half]), near[half:]], axis=0)
            down = jnp.concatenate([far[:half], add_low(down, far[half:])], axis=0)
        else:
            up, down = add_low(up, near), add_low(down, far)
        up, down = tied((up, down), meanwhile[step - 1])
        up, down = ring_shift(up, order, 1), ring_shift(down, order, -1)
    return pieces[0], up, down


def dp_sum(value, count, after):
    bit = 1
    while bit < count:
        if 2 * bit >= count:
            value = tied(value, after)
        low = value.astype(bf16)
        there = lax.ppermute(low, "dp", [(i, i ^ bit) for i in range(count)])
        value = low.astype(f32) + there.astype(f32)
        bit *= 2
    return value


def add_low(a, b):
    return (a.astype(f32) + b.astype(f32)).astype(bf16)


def core_swap(value):
    return lax.ppermute(value, "head", [(i, i ^ 1) for i in range(4)])


def far_swap(value):
    return lax.ppermute(value, "head", [(i, i ^ 2) for i in range(4)])


def tied(values, after):
    return lax.optimization_barrier((values, after))[0]


def one_hots(ids):
    lane = jnp.arange(LANES, dtype=jnp.int32)[None, :]
    same = ids[:, None] == lane
    return jnp.where(same, -BIG, 0.0).astype(bf16), jnp.where(same, 0.0, 1.0).astype(bf16)


def relative(row, place):
    pieces = row.reshape(4, -1)
    return jnp.take(pieces, jnp.arange(4) ^ place, axis=0).reshape(1, -1)


def on_device(
    series,
    cotangent,
    window_lengths,
    owner_list,
    master,
    first_moment,
    second_moment,
    left_stats,
    right_stats,
    left_basis,
    right_basis,
    vec_values,
    vec_first,
    vec_second,
):
    place = lax.axis_index("head")
    spot = lax.axis_index("dp")
    dp = lax.axis_size("dp")
    ringed = dp == 8
    rows = series.shape[0]
    own_slots = master.shape[1]
    buckets, win = window_lengths.shape
    bucket_rows = rows * 4 // buckets
    owner_row = owner_list[0]
    who = owner_row // own_slots
    if ringed:
        order = ring_of(dp)
        ring_at = jnp.asarray([order.index(d) for d in range(dp)], jnp.int32)
        who = (ring_at[who] - ring_at[spot]) % dp
    inner = owner_row % own_slots
    gather_at = who * own_slots + inner

    copies = master[0].astype(bf16)
    if ringed:
        held, far = ring_gather(copies, order)
        slots, plan = [x[0] for x in held], tuple(x[1] * own_slots + x[2] for x in held)
        tops, far_plan = [x[0] for x in far], tuple(x[1] * own_slots + x[2] for x in far)
    else:
        slots, plan = [lax.all_gather(copies, "dp", axis=0, tiled=True)], (0,)
        tops, far_plan = [far_swap(slots[0][:, :TOP])], (0,)
    far_at = far_swap(gather_at)
    windows = window_ids(window_lengths, bucket_rows)
    ids = windows.reshape(4, rows)
    own_ids = lax.dynamic_index_in_dim(ids, place, 0, False)
    pair_ids = lax.dynamic_index_in_dim(ids, place ^ 1, 0, False)
    ohq, ohk_own = one_hots(own_ids)
    ohk = jnp.concatenate([ohk_own, one_hots(pair_ids)[1]], axis=0)
    valid = (own_ids < win).astype(f32)[:, None]

    x = embed(series, vec_values)
    vectors = []
    for layer in range(LAYERS):
        bq, bv, bo, g1, c1, b1, b2, g2, c2 = depth_vectors(vec_values, layer)
        vec = jnp.stack([bo, g1, c1, b2, g2, c2, g2, c2])
        vectors.append([vec] + [relative(row, place) for row in (bq, bv, b1)])
    grad = cotangent * valid
    slots, (x, vectors, ohq, ohk, valid, gather_at, far_at, grad) = lax.optimization_barrier(
        (slots, (x, vectors, ohq, ohk, valid, gather_at, far_at, grad))
    )
    mine = natural_order(gather_at, slots, plan, True)
    mine, lower = mine[: len(HELD) * LAYERS], mine[len(HELD) * LAYERS :]
    upper = natural_order(far_at, tops, far_plan, False)
    moved = []

    def cross(i, after=None):
        own = lower[i] if after is None else tied(lower[i], after)
        moved.append(far_swap(own))
        return moved[-1]

    def four(i, after=None):
        there = moved[i] if after is None else tied(moved[i], after)
        return [
            mine[i], core_swap(mine[i]), upper[i], there, core_swap(upper[i]), core_swap(there)
        ]

    weights = []
    saved = []
    for layer in range(LAYERS):
        vec, bq, bv, b1 = vectors[layer]
        if layer == 0:
            cross(0)
        wqkv = four(2 * layer, x if layer else None)
        x = tied(x, wqkv)
        if layer == 0:
            cross(1, moved[0])
        xs, q, kv = project(x, bq, bv, wqkv)
        kvp = core_swap(kv)
        o, lse = attend(q, kv, kvp, ohq, ohk)
        wfeed = four(2 * layer + 1, o)
        weights.append((wqkv, wfeed))
        if layer + 1 < LAYERS:
            done = moved[-1]
            cross(2 * layer + 2, done)
            cross(2 * layer + 3, (done, moved[-1]))
        n1, i1, y, hid, slope, n2, i2, x = post(o, x, vec, b1, wfeed)
        saved.append((xs, q, kv, kvp, o, lse, vec, n1, i1, y, hid, slope, n2, i2))
    activations = x * valid

    own_sums = [None] * (3 * LAYERS)
    far_sums = [None] * (3 * LAYERS)
    table_rows = [None] * LAYERS

    waiting = []

    def chip_sum(at, keep, got):
        waiting.append((at, keep, got))
        return add_low(keep[1], got[1])

    def own_chip_sums(after):
        while waiting:
            at, keep, got = waiting.pop()
            keep, got = tied((keep[0], got[0]), after)
            own_sums[at] = add_low(keep, got)

    moving = []
    for layer in reversed(range(LAYERS)):
        xs, q, kv, kvp, o, lse, vec, n1, i1, y, hid, slope, n2, i2 = saved[layer]
        wqkv, wfeed = weights[layer]
        gk, gs, ok, os, dr1, do, db1, sums = ffn_grad(
            grad, n2, i2, n1, i1, y, hid, slope, o, vec, wfeed
        )
        os, gs, ok, gk, do = tied((os, gs, ok, gk, do), moving)
        own_chip_sums(sums)
        got = [core_swap(os), core_swap(gs)]
        mid = chip_sum(3 * layer + 1, ok, got[0])
        down = chip_sum(3 * layer + 2, gk, got[1])
        far_sums[3 * layer + 1] = far_swap(mid)
        do = tied(do, (mid, down))
        dq, dkv, dkvp = attend_grad(q, kv, kvp, do, o, lse, ohq, ohk)
        dkvp = tied(dkvp, far_sums[3 * layer + 1])
        far_sums[3 * layer + 2] = far_swap(tied(down, far_sums[3 * layer + 1]))
        dkvr = core_swap(dkvp)
        pk, ps, grad, qsums = proj_grad(dq, dkv, dkvr, xs, dr1, wqkv)
        table_rows[layer] = (sums, qsums, db1)
        got = core_swap(ps)
        if layer:
            far = chip_sum(3 * layer, pk, got)
            grad = tied(grad, far)
            far_sums[3 * layer] = far_swap(far)
            moving = far_sums[3 * layer : 3 * layer + 3]
    input_grad, tab_keep, tab_send = embed_grad(
        place.astype(jnp.int32)[None], series, grad, vec_values, table_rows[0] + table_rows[1]
    )
    far_sums[0] = far_swap(chip_sum(0, pk, got))
    own_chip_sums(tab_send)
    tab = dp_sum(tab_keep + core_swap(tab_send), dp, far_sums[0])
    tab_part = tab[0] + far_swap(tab[1])
    tab_there = far_swap(tab_part)
    parts = [tab_part, core_swap(tab_part), tab_there, core_swap(tab_there)]
    vec_new_values, vec_new_first, vec_new_second, branch_bias_grads = vector_update(
        place.astype(jnp.int32)[None], vec_values, vec_first, vec_second, parts
    )
    at = jnp.concatenate([inner, who]).astype(jnp.int32)
    pieces = routed(at, own_sums, far_sums, dp, own_slots)
    if ringed:
        meanwhile = (tab, tab_part, parts)
        terms = ring_reduce([pieces[i] for i in range(dp)], order, meanwhile)
        terms = tied(terms, vec_new_values)
        grads = [t.reshape(own_slots, BLK, BLK) for t in terms]
    else:
        whole = lax.psum_scatter(pieces, "dp", scatter_dimension=0, tiled=True)
        grads = [whole.reshape(own_slots, BLK, BLK)]
    new_master, new_copy, new_first, new_second, new_left, new_right, left_next, right_next = soap(
        grads,
        master[0],
        first_moment[0],
        second_moment[0],
        left_stats[0],
        right_stats[0],
        left_basis[0],
        right_basis[0],
    )
    return (
        activations,
        input_grad,
        new_master[None],
        new_copy[None],
        new_first[None],
        new_second[None],
        new_left[None],
        new_right[None],
        left_next[None],
        right_next[None],
        vec_new_values,
        vec_new_first,
        vec_new_second,
        branch_bias_grads,
    )


def solution(mesh):
    placed = (
        P(("dp", "head"), None),
        P(("dp", "head"), None),
        P("dp", None),
        P("head", None),
        P("head", "dp", None, None),
        P("head", "dp", None, None),
        P("head", "dp", None, None),
        P("head", "dp", None, None),
        P("head", "dp", None, None),
        P("head", "dp", None, None),
        P("head", "dp", None, None),
        P(),
        P(),
        P(),
    )
    return jax.shard_map(
        on_device,
        mesh=mesh,
        in_specs=placed,
        out_specs=(
            P(("dp", "head"), None),
            P(("dp", "head"), None),
            P("head", "dp", None, None),
            P("head", "dp", None, None),
            P("head", "dp", None, None),
            P("head", "dp", None, None),
            P("head", "dp", None, None),
            P("head", "dp", None, None),
            P("head", "dp", None, None),
            P("head", "dp", None, None),
            P(),
            P(),
            P(),
            P(),
        ),
        check_vma=False,
    )
```

```python
import functools

import jax
import jax.numpy as jnp
from jax import lax
from jax.experimental import pallas as pl
from jax.experimental.pallas import tpu as pltpu
from jax.sharding import PartitionSpec as P

D = 512
HEADS = 8
HD = 64
FF = 2048
LOOK = 96
LAYERS = 2
BLK = 128
STEP = 10

f32 = jnp.float32
HI = lax.Precision.HIGHEST
norm_eps = 1e-05
beta_first = 0.5
beta_second = 0.5
beta_stats = 0.5
adam_eps = 1e-08
rate_matrix = 0.02
rate_vector = 0.15
weight_decay = 0.01


def window_ids(lengths, bucket_rows):
    bounds = jnp.cumsum(lengths, axis=1, dtype=jnp.int32)
    places = jnp.arange(bucket_rows, dtype=jnp.int32)
    return jnp.sum(
        (places[None, :, None] >= bounds[:, None, :]).astype(jnp.int32), axis=2, dtype=jnp.int32
    )


def depth_vectors(vec_table, layer_at):
    ff_ratio = FF // D
    base_row = LOOK + 1 + layer_at * (8 + ff_ratio)
    return (
        vec_table[base_row],
        vec_table[base_row + 1],
        vec_table[base_row + 2],
        vec_table[base_row + 3],
        vec_table[base_row + 4],
        vec_table[base_row + 5 : base_row + 5 + ff_ratio].reshape(FF),
        vec_table[base_row + 5 + ff_ratio],
        vec_table[base_row + 6 + ff_ratio],
        vec_table[base_row + 7 + ff_ratio],
    )


def dot_hi(a, b, ca, cb):
    return lax.dot_general(
        a, b, (((ca,), (cb,)), ((), ())), precision=HI, preferred_element_type=f32
    )


def terms(x, count):
    out = []
    for i in range(count):
        part = x.astype(jnp.bfloat16)
        out.append(part)
        if i < count - 1:
            x = x - part.astype(f32)
    return out


def dot_terms(a, b, ca, cb, full=False):
    a = terms(a, 3 if full else 2)
    b = terms(b, 3 if full else 2)
    dims = (((ca,), (cb,)), ((), ()))
    left = jnp.concatenate(a[:2], axis=ca)
    right = jnp.concatenate(
        [jnp.concatenate([b[0], b[1]], axis=cb), jnp.concatenate([b[1], b[0]], axis=cb)], axis=1 - cb
    )
    out = lax.dot_general(left, right, dims, preferred_element_type=f32)
    out = out[:, :BLK] + out[:, BLK:]
    if full:
        out = out + lax.dot_general(
            jnp.concatenate([a[0], a[2]], axis=ca),
            jnp.concatenate([b[2], b[0]], axis=cb),
            dims,
            preferred_element_type=f32,
        )
    return out


PANEL = 32
AHEAD = 2


def recip(x):
    guess = pl.reciprocal(x, approx=True)
    guess = guess * (2.0 - x * guess)
    return guess * (2.0 - x * guess)


def qr_batch(a_ref, count):
    lane = lax.broadcasted_iota(jnp.int32, (1, 1, BLK), 2)
    sub8 = lax.broadcasted_iota(jnp.int32, (1, 8, 1), 1)
    sub = lax.broadcasted_iota(jnp.int32, (1, PANEL, 1), 1)
    for r0 in range(0, BLK, PANEL):
        tiles = [a_ref[:, r0 + 8 * t : r0 + 8 * t + 8, :] for t in range(PANEL // 8)]
        for k0 in range(0, PANEL, AHEAD):
            t0, s0 = divmod(k0, 8)
            cols = [
                [
                    jnp.broadcast_to(tiles[t][:, :, r0 + k : r0 + k + 1], (count, 8, BLK))
                    for k in range(k0, k0 + AHEAD)
                ]
                for t in range(PANEL // 8)
            ]
            for i in range(AHEAD):
                s = s0 + i
                inv = recip(cols[t0][i][:, s : s + 1, :])
                pn = (tiles[t0][:, s : s + 1, :] + (lane == r0 + k0 + i).astype(f32)) * inv
                rest = [cols[t0][j][:, s : s + 1, :] * inv for j in range(i + 1, AHEAD)]
                for t in range(t0, PANEL // 8):
                    c = cols[t][i]
                    if t == t0:
                        if s == 7:
                            continue
                        c = jnp.where(sub8 > s, c, 0.0)
                    tiles[t] = tiles[t] - c * pn
                    for j, m in enumerate(rest):
                        cols[t][i + 1 + j] = cols[t][i + 1 + j] - c * m
        done = jnp.concatenate(tiles, axis=1)
        diag = lane == sub + r0
        pivot = jnp.sum(jnp.where(diag, done, 0.0), axis=2, keepdims=True)
        done = jnp.where(diag, 1.0, jnp.where((lane > sub + r0) & (lane < r0 + PANEL), 0.0, done))
        done = done * lax.rsqrt(pivot)
        a_ref[:, r0 : r0 + PANEL, :] = done
        r1 = r0 + PANEL
        if r1 < BLK:
            lane2 = lax.broadcasted_iota(jnp.int32, (BLK - r1, BLK), 1)
            clear = (lane2 >= r0) & (lane2 < r1)
            z0, z1, z2 = terms(done, 3)
            left = jnp.concatenate([z0, z0, z0, z1, z1, z2], axis=1)
            right = jnp.concatenate([z0, z1, z2, z0, z1, z0], axis=1)
            for b in range(count):
                update = lax.dot_general(
                    left[b], right[b], (((0,), (0,)), ((), ())), preferred_element_type=f32
                )
                a_ref[b, r1:, :] = jnp.where(clear, 0.0, a_ref[b, r1:, :]) - update[r1:]


def soap_kernel(count, *refs):
    for s in range(refs[0].shape[0]):
        soap_slot(s, sum(ref[s].astype(f32) for ref in refs[:count]), *refs[count:])
    soap_finish(*refs[-4:])


def soap_slot(
    s, g, mas_ref, m1_ref, m2_ref, ls_ref, rs_ref, lb_ref, rb_ref,
    nm_ref, nc_ref, n1_ref, n2_ref, nl_ref, nr_ref, ql_ref, qr_ref, mat_ref, a_ref,
):
    group = mas_ref.shape[0]
    lb = lb_ref[s]
    rb = rb_ref[s]
    rot = dot_terms(dot_terms(lb, g, 0, 0), rb, 1, 0)
    n1 = 0.5 * m1_ref[s] + 0.5 * rot
    n2 = 0.5 * m2_ref[s] + 0.5 * rot * rot
    n1_ref[s] = n1
    n2_ref[s] = n2
    corr = 1.0 - 0.5**STEP
    ratio = n1 / corr / (jnp.sqrt(n2 / corr) + adam_eps)
    upd = dot_terms(dot_terms(lb, ratio, 1, 0), rb, 1, 1)
    mas = mas_ref[s]
    nm = mas - rate_matrix * (upd + weight_decay * mas)
    nm_ref[s] = nm
    nc_ref[s] = nm.astype(jnp.bfloat16)
    nl = 0.5 * ls_ref[s] + 0.5 * dot_terms(g, g, 1, 1)
    nr = 0.5 * rs_ref[s] + 0.5 * dot_terms(g, g, 0, 0)
    nl_ref[s] = nl
    nr_ref[s] = nr
    for side, (st, ba) in enumerate(((nl, lb), (nr, rb))):
        m = dot_terms(st, ba, 1, 0, True)
        m = m * lax.rsqrt(jnp.sum(m * m, axis=0, keepdims=True))
        at = 2 * (pl.program_id(0) * group + s) + side
        mat_ref[at] = m
        a_ref[at] = dot_terms(m, m, 0, 0, True)


def soap_finish(ql_ref, qr_ref, mat_ref, a_ref):
    @pl.when(pl.program_id(0) == pl.num_programs(0) - 1)
    def _():
        count = a_ref.shape[0]
        qr_batch(a_ref, count)
        keep = lax.broadcasted_iota(jnp.int32, (BLK, BLK), 1) <= lax.broadcasted_iota(
            jnp.int32, (BLK, BLK), 0
        )
        for j in range(count // 2):
            for side, ref in enumerate((ql_ref, qr_ref)):
                x = jnp.where(keep, a_ref[2 * j + side], 0.0)
                ref[j] = dot_terms(mat_ref[2 * j + side], x, 1, 1, True)


def soap(gs, master, m1, m2, ls, rs, lb, rb):
    n = master.shape[0]
    group = SOAP_GROUP if n % SOAP_GROUP == 0 else n
    one = pl.BlockSpec((group, BLK, BLK), lambda i: (i, 0, 0))
    whole = pl.BlockSpec((n, BLK, BLK), lambda i: (0, 0, 0))
    sh = jax.ShapeDtypeStruct((n, BLK, BLK), f32)
    shb = jax.ShapeDtypeStruct((n, BLK, BLK), jnp.bfloat16)
    return pl.pallas_call(
        functools.partial(soap_kernel, len(gs)),
        grid=(n // group,),
        in_specs=[one] * (len(gs) + 7),
        out_specs=[one] * 6 + [whole] * 2,
        out_shape=[sh, shb, sh, sh, sh, sh, sh, sh],
        scratch_shapes=[pltpu.VMEM((2 * n, BLK, BLK), f32)] * 2,
        compiler_params=pltpu.CompilerParams(vmem_limit_bytes=16 * 2**20),
        cost_estimate=pl.CostEstimate(flops=40 * 10**6, bytes_accessed=0, transcendentals=0),
        name="soap",
    )(*gs, master, m1, m2, ls, rs, lb, rb)


SOAP_GROUP = 2


bf16 = jnp.bfloat16
LANES = 128
TOP = 64
ROW_TILE = 512
BIG = 1e30
CORR = 1.0 - 0.5**STEP


def params(mib=48):
    return pltpu.CompilerParams(vmem_limit_bytes=mib * 2**20)


MIB = dict(
    embed=6, project=8, attend=16, post=20, ffn_grad=24, attend_grad=16, proj_grad=12, embed_grad=8, vector=4, natural=6, routed=8,
)


def cost(micros):
    return pl.CostEstimate(flops=int(micros * 1e6), bytes_accessed=0, transcendentals=0)


def shape(dims, kind=f32):
    return jax.ShapeDtypeStruct(dims, kind)


def dot(a, b, ca=1, cb=0):
    return lax.dot_general(a, b, (((ca,), (cb,)), ((), ())), preferred_element_type=f32)


def planes(refs):
    return (refs[0],), (refs[1],), (refs[2], refs[3]), (refs[4], refs[5])


def place_block(dst, refs, j, r0, c0):
    for ref in refs:
        dst[r0 : r0 + ref.shape[1], c0 : c0 + BLK] = ref[j]
        r0 += ref.shape[1]


def place_blocks(dst, refs, first, rows, cols, row_step, col_step):
    for r, plane in enumerate(planes(refs)):
        for j in range(rows * cols):
            row, col = divmod(j, cols)
            place_block(dst, plane, first + j, r * row_step + row * BLK, r * col_step + col * BLK)


def place_qkv(dst, refs):
    for r, plane in enumerate(planes(refs)):
        for j in range(12):
            row, col = divmod(j, 3)
            c0 = D + (2 * r + col - 1) * BLK if col else r * BLK
            place_block(dst, plane, j, row * BLK, c0)


def layer_norm(resid):
    center = resid - jnp.mean(resid, axis=1, keepdims=True)
    inv = lax.rsqrt(jnp.mean(center * center, axis=1, keepdims=True) + norm_eps)
    return center * inv, inv


def layer_norm_grad(grad, unit, inv, gain):
    dn = grad * gain
    return inv * (
        dn
        - jnp.mean(dn, axis=1, keepdims=True)
        - unit * jnp.mean(dn * unit, axis=1, keepdims=True)
    )


def col_sum(values):
    return jnp.sum(values, axis=0, keepdims=True)


def embed_kernel(series_ref, we_ref, be_ref, x_ref):
    x_ref[...] = dot_hi(series_ref[...].astype(f32), we_ref[...], 1, 0) + be_ref[...]


def embed(series, table):
    rows = series.shape[0]
    return pl.pallas_call(
        embed_kernel, out_shape=shape((rows, D)), compiler_params=params(MIB["embed"]), name="embed"
    )(series, table[:LOOK], table[LOOK : LOOK + 1])


def proj_kernel(x_ref, bq_ref, bv_ref, w0, w1, w2, w3, w4, w5, xs_ref, q_ref, kv_ref, w_s):
    place_qkv(w_s, (w0, w1, w2, w3, w4, w5))
    xs = x_ref[...].astype(bf16)
    xs_ref[...] = xs
    q_ref[...] = (dot(xs, w_s[:, :D]) + bq_ref[...]).astype(bf16)
    kv = dot(xs, w_s[:, D:])
    for r in range(4):
        at = 2 * r * BLK
        kv_ref[:, at : at + BLK] = kv[:, at : at + BLK].astype(bf16)
        value = kv[:, at + BLK : at + 2 * BLK] + bv_ref[:, r * BLK : (r + 1) * BLK]
        kv_ref[:, at + BLK : at + 2 * BLK] = value.astype(bf16)


def project(x, bq, bv, wqkv):
    rows = x.shape[0]
    return pl.pallas_call(
        proj_kernel,
        out_shape=[
            shape((rows, D), bf16),
            shape((rows, D), bf16),
            shape((rows, 2 * D), bf16),
        ],
        scratch_shapes=[pltpu.VMEM((D, 3 * D), bf16)],
        compiler_params=params(MIB["project"]),
        name="project",
        cost_estimate=cost(3),
    )(x, bq, bv, *wqkv)


def half_mask(i, kind=bf16):
    lane = lax.broadcasted_iota(jnp.int32, (1, LANES), 1)
    return ((lane >= HD * i) & (lane < HD * (i + 1))).astype(f32).astype(kind)


def three_terms(col):
    first = col.astype(bf16).astype(f32)
    second = (col - first).astype(bf16).astype(f32)
    return first, second, col - first - second


def lanes_with(base, at, cols):
    lane = lax.broadcasted_iota(jnp.int32, base.shape, 1)
    for i, col in enumerate(cols):
        base = jnp.where(lane == at + i, col, base)
    return base.astype(bf16)


def attend_kernel(q_ref, kv_ref, kvp_ref, ohq_ref, ohk_ref, o_ref, lse_ref, ka, va):
    rows = q_ref.shape[0]
    ka[:rows, :LANES] = kv_ref[:, :LANES]
    ka[rows:, :LANES] = kvp_ref[:, :LANES]
    ka[:, LANES:] = ohk_ref[...]
    lane = lax.broadcasted_iota(jnp.int32, (ROW_TILE, LANES), 1)
    for i in range(2):
        m = half_mask(i)
        va[i, :rows, :LANES] = kv_ref[:, LANES:] * m
        va[i, rows:, :LANES] = kvp_ref[:, LANES:] * m
        va[i, :, LANES:] = jnp.ones((2 * rows, LANES), bf16)

    def tile(t, c):
        at = pl.ds(t * ROW_TILE, ROW_TILE)
        total = jnp.zeros((ROW_TILE, LANES), f32)
        stat = jnp.zeros((ROW_TILE, LANES), f32)
        for i in range(2):
            qa = jnp.concatenate([q_ref[at] * (half_mask(i) * bf16(0.125)), ohq_ref[at]], axis=1)
            s = dot(qa, ka[...], 1, 1)
            high = jnp.max(s, axis=1, keepdims=True)
            e = jnp.exp(s - high).astype(bf16)
            out = dot(e, va[i])
            norm = out[:, LANES:]
            total = total + out[:, :LANES] / norm
            stat = jnp.where(lane == i, high + jnp.log(norm), stat)
        o_ref[at] = total.astype(bf16)
        lse_ref[at] = stat
        return c

    lax.fori_loop(0, rows // ROW_TILE, tile, 0)


def attend(q, kv, kvp, ohq, ohk):
    rows = q.shape[0]
    pair = pl.BlockSpec((rows, LANES), lambda h: (0, h))
    both = pl.BlockSpec((rows, 2 * LANES), lambda h: (0, h))
    other = pl.BlockSpec((rows, 2 * LANES), lambda h: (0, h + 1 - 2 * lax.rem(h, 2)))
    return pl.pallas_call(
        attend_kernel,
        grid=(D // LANES,),
        in_specs=[pair, both, other]
        + [
            pl.BlockSpec((rows, LANES), lambda h: (0, 0)),
            pl.BlockSpec((2 * rows, LANES), lambda h: (0, 0)),
        ],
        out_specs=[pair, pair],
        out_shape=[shape((rows, D), bf16), shape((rows, D))],
        scratch_shapes=[
            pltpu.VMEM((2 * rows, 2 * LANES), bf16),
            pltpu.VMEM((2, 2 * rows, 2 * LANES), bf16),
        ],
        compiler_params=params(MIB["attend"]),
        name="attend",
        cost_estimate=cost(11),
    )(q, kv, kvp, ohq, ohk)


def post_kernel(
    o_ref, x_ref, vec_ref, b1_ref, a0, a1, a2, a3, a4, a5,
    n1_ref, i1_ref, y_ref, hid_ref, slope_ref, n2_ref, i2_ref, x2_ref,
    wo_s, w1_s, w2_s,
):
    place_blocks(wo_s, (a0, a1, a2, a3, a4, a5), 0, 1, 4, BLK, 0)
    place_blocks(w1_s, (a0, a1, a2, a3, a4, a5), 4, 4, 4, 0, D)
    place_blocks(w2_s, (a0, a1, a2, a3, a4, a5), 20, 4, 4, D, 0)

    def tile(t, c):
        at = pl.ds(t * ROW_TILE, ROW_TILE)
        vec = [vec_ref[i : i + 1, :] for i in range(6)]
        unit, inv = layer_norm(x_ref[at] + dot(o_ref[at], wo_s[...]) + vec[0])
        n1_ref[at] = unit
        i1_ref[at] = jnp.broadcast_to(inv, (ROW_TILE, LANES))
        y = unit * vec[1] + vec[2]
        yb = y.astype(bf16)
        y_ref[at] = yb
        pre = dot(yb, w1_s[...]) + b1_ref[...]
        phi = 0.5 * (1.0 + lax.erf(pre * (0.5**0.5)))
        hid = (pre * phi).astype(bf16)
        hid_ref[at] = hid
        slope = phi + pre * (jnp.exp(-0.5 * pre * pre) * 0.3989422804014327)
        slope_ref[at] = slope.astype(bf16)
        fed = dot(hid, w2_s[...])
        unit, inv = layer_norm(y + fed + vec[3])
        n2_ref[at] = unit
        i2_ref[at] = jnp.broadcast_to(inv, (ROW_TILE, LANES))
        x2_ref[at] = unit * vec[4] + vec[5]
        return c

    lax.fori_loop(0, x_ref.shape[0] // ROW_TILE, tile, 0)


def post(o, x, vec, b1, wfeed):
    rows = x.shape[0]
    return pl.pallas_call(
        post_kernel,
        out_shape=[
            shape((rows, D)),
            shape((rows, LANES)),
            shape((rows, D), bf16),
            shape((rows, FF), bf16),
            shape((rows, FF), bf16),
            shape((rows, D)),
            shape((rows, LANES)),
            shape((rows, D)),
        ],
        scratch_shapes=[
            pltpu.VMEM((D, D), bf16),
            pltpu.VMEM((D, FF), bf16),
            pltpu.VMEM((FF, D), bf16),
        ],
        compiler_params=params(MIB["post"]),
        name="post",
        cost_estimate=cost(11),
    )(o, x, vec, b1, *wfeed)


def store_blocks(refs, r, first, rows, cols, value):
    keep_ref, send_ref = refs
    ref = send_ref if r % 2 else keep_ref
    for j in range(rows * cols):
        row, col = divmod(j, cols)
        ref[r // 2, first + j] = value[row * BLK : (row + 1) * BLK, col * BLK : (col + 1) * BLK]


def ffn_grad_kernel(
    e_ref, n2_ref, i2_ref, n1_ref, i1_ref, y_ref, hid_ref, slope_ref, o_ref, vec_ref,
    a0, a1, a2, a3, a4, a5,
    gk_ref, gs_ref, ok_ref, os_ref, dr1_ref, do_ref, db1_ref, sums_ref,
    wo_s, w1_s, w2_s, dr2_s, dfr_s, dpre_s, dar_s,
):
    rows = e_ref.shape[0]
    place_blocks(wo_s, (a0, a1, a2, a3, a4, a5), 0, 1, 4, BLK, 0)
    place_blocks(w1_s, (a0, a1, a2, a3, a4, a5), 4, 4, 4, 0, D)
    place_blocks(w2_s, (a0, a1, a2, a3, a4, a5), 20, 4, 4, D, 0)
    tiles = rows // ROW_TILE
    gain_two = vec_ref[4:5, :]
    gain_one = vec_ref[1:2, :]
    zero = jnp.zeros((1, D), f32)

    def tile_two(t, c):
        at = pl.ds(t * ROW_TILE, ROW_TILE)
        grad = e_ref[at]
        unit = n2_ref[at]
        dr2 = layer_norm_grad(grad, unit, i2_ref[at, 0:1], gain_two)
        dr2_s[at] = dr2
        dfr_s[at] = dr2.astype(bf16)
        return (c[0] + col_sum(dr2), c[1] + col_sum(grad * unit), c[2] + col_sum(grad))

    db2, dg2, dc2 = lax.fori_loop(0, tiles, tile_two, (zero, zero, zero))

    for r in range(FF // D):
        cols = slice(r * D, (r + 1) * D)

        def tile_up(t, c):
            at = pl.ds(t * ROW_TILE, ROW_TILE)
            dh = dot(dfr_s[at], w2_s[cols, :], 1, 1)
            dpre = (dh * slope_ref[at, cols].astype(f32)).astype(bf16)
            dpre_s[at, cols] = dpre
            dr2_s[at] = dr2_s[at] + dot(dpre, w1_s[:, cols], 1, 1)
            return c + col_sum(dpre.astype(f32))

        db1_ref[r : r + 1, :] = lax.fori_loop(0, tiles, tile_up, zero)
        store_blocks((gk_ref, gs_ref), r, 0, 4, 4, dot(hid_ref[:, cols], dfr_s[...], 0, 0).astype(bf16))
        store_blocks((ok_ref, os_ref), r, 4, 4, 4, dot(y_ref[...], dpre_s[:, cols], 0, 0).astype(bf16))

    def tile_one(t, c):
        at = pl.ds(t * ROW_TILE, ROW_TILE)
        grad = dr2_s[at]
        unit = n1_ref[at]
        dr1 = layer_norm_grad(grad, unit, i1_ref[at, 0:1], gain_one)
        dr1_ref[at] = dr1
        dar = dr1.astype(bf16)
        dar_s[at] = dar
        do_ref[at] = dot(dar, wo_s[...], 1, 1).astype(bf16)
        return (c[0] + col_sum(dr1), c[1] + col_sum(grad * unit), c[2] + col_sum(grad))

    dbo, dg1, dc1 = lax.fori_loop(0, tiles, tile_one, (zero, zero, zero))
    dwo = dot(o_ref[...], dar_s[...], 0, 0).astype(bf16)
    for r in range(4):
        store_blocks((ok_ref, os_ref), r, 0, 1, 4, dwo[r * BLK : (r + 1) * BLK])
    for i, value in enumerate((dbo, dg1, dc1, db2, dg2, dc2, zero, zero)):
        sums_ref[i : i + 1, :] = value


def ffn_grad(e, n2, i2, n1, i1, y, hid, slope, o, vec, wfeed):
    rows = e.shape[0]
    return pl.pallas_call(
        ffn_grad_kernel,
        out_shape=[
            shape((2, 16, BLK, BLK), bf16),
            shape((2, 16, BLK, BLK), bf16),
            shape((2, 20, BLK, BLK), bf16),
            shape((2, 20, BLK, BLK), bf16),
            shape((rows, D)),
            shape((rows, D), bf16),
            shape((FF // D, D)),
            shape((8, D)),
        ],
        scratch_shapes=[
            pltpu.VMEM((D, D), bf16),
            pltpu.VMEM((D, FF), bf16),
            pltpu.VMEM((FF, D), bf16),
            pltpu.VMEM((rows, D), f32),
            pltpu.VMEM((rows, D), bf16),
            pltpu.VMEM((rows, FF), bf16),
            pltpu.VMEM((rows, D), bf16),
        ],
        compiler_params=params(MIB["ffn_grad"]),
        name="ffn_grad",
        cost_estimate=cost(16),
    )(e, n2, i2, n1, i1, y, hid, slope, o, vec, *wfeed)


def attend_grad_kernel(
    q_ref, kv_ref, kvp_ref, do_ref, o_ref, lse_ref, ohq_ref, ohk_ref,
    dq_ref, dkv_ref, dkvp_ref,
    ka, va, qa, da, kt,
):
    rows = q_ref.shape[0]
    ka[:rows, :LANES] = kv_ref[:, :LANES]
    ka[rows:, :LANES] = kvp_ref[:, :LANES]
    ka[:, LANES:] = ohk_ref[...]
    va[:rows, :LANES] = kv_ref[:, LANES:]
    va[rows:, :LANES] = kvp_ref[:, LANES:]
    va[:, LANES:] = jnp.ones((2 * rows, LANES), bf16)
    kt[...] = ka[:, :LANES].T
    product = do_ref[...].astype(f32) * o_ref[...].astype(f32)
    for i in range(2):
        m = half_mask(i)
        qa[i, :, :LANES] = q_ref[...] * (m * bf16(0.125))
        qa[i, :, LANES:] = lanes_with(
            ohq_ref[...].astype(f32), 120, three_terms(-lse_ref[:, i : i + 1])
        )
        da[i, :, :LANES] = do_ref[...] * m
        delta = jnp.sum(product * half_mask(i, f32), axis=1, keepdims=True)
        da[i, :, LANES:] = lanes_with(jnp.zeros((rows, LANES), f32), 0, three_terms(-delta))

    def tile(t, sums):
        at = pl.ds(pl.multiple_of(t * ROW_TILE, ROW_TILE), ROW_TILE)
        dk = jnp.zeros((ROW_TILE, LANES), f32)
        dv = jnp.zeros((ROW_TILE, LANES), f32)
        new = []
        for i in range(2):
            p = jnp.exp(dot(ka[at], qa[i], 1, 1))
            ds = (p * dot(va[at], da[i], 1, 1)).astype(bf16)
            dv = dv + dot(p.astype(bf16), da[i, :, :LANES])
            dk = dk + dot(ds, qa[i, :, :LANES])
            new.append(sums[i] + dot(kt[:, at], ds))
        return tuple(new), dk.astype(bf16), dv.astype(bf16)

    sums = (jnp.zeros((LANES, rows), f32),) * 2
    half = rows // ROW_TILE

    def own(t, sums):
        sums, dk, dv = tile(t, sums)
        at = pl.ds(t * ROW_TILE, ROW_TILE)
        dkv_ref[at, :LANES] = dk
        dkv_ref[at, LANES:] = dv
        return sums

    def other(t, sums):
        sums, dk, dv = tile(t + half, sums)
        at = pl.ds(t * ROW_TILE, ROW_TILE)
        dkvp_ref[at, :LANES] = dk
        dkvp_ref[at, LANES:] = dv
        return sums

    sums = lax.fori_loop(0, half, own, sums)
    sums = lax.fori_loop(0, half, other, sums)
    row = lax.broadcasted_iota(jnp.int32, (LANES, rows), 0)
    dq_ref[...] = (jnp.where(row < HD, sums[0], sums[1]) * 0.125).T.astype(bf16)


def attend_grad(q, kv, kvp, do, o, lse, ohq, ohk):
    rows = q.shape[0]
    pair = pl.BlockSpec((rows, LANES), lambda h: (0, h))
    both = pl.BlockSpec((rows, 2 * LANES), lambda h: (0, h))
    other = pl.BlockSpec((rows, 2 * LANES), lambda h: (0, h + 1 - 2 * lax.rem(h, 2)))
    return pl.pallas_call(
        attend_grad_kernel,
        grid=(D // LANES,),
        in_specs=[pair, both, other, pair, pair, pair]
        + [
            pl.BlockSpec((rows, LANES), lambda h: (0, 0)),
            pl.BlockSpec((2 * rows, LANES), lambda h: (0, 0)),
        ],
        out_specs=[pair, both, other],
        out_shape=[shape((rows, D), bf16)] + [shape((rows, 2 * D), bf16)] * 2,
        scratch_shapes=[
            pltpu.VMEM((2 * rows, 2 * LANES), bf16),
            pltpu.VMEM((2 * rows, 2 * LANES), bf16),
            pltpu.VMEM((2, rows, 2 * LANES), bf16),
            pltpu.VMEM((2, rows, 2 * LANES), bf16),
            pltpu.VMEM((LANES, 2 * rows), bf16),
        ],
        compiler_params=params(MIB["attend_grad"]),
        name="attend_grad",
        cost_estimate=cost(23),
    )(q, kv, kvp, do, o, lse, ohq, ohk)


def proj_grad_kernel(
    dq_ref, dkv_ref, dkvr_ref, xs_ref, dr1_ref, w0, w1, w2, w3, w4, w5,
    gk_ref, gs_ref, dx_ref, sums_ref, w_s,
):
    place_qkv(w_s, (w0, w1, w2, w3, w4, w5))
    dq = dq_ref[...]
    dkv = (dkv_ref[...].astype(f32) + dkvr_ref[...].astype(f32)).astype(bf16)
    xs = xs_ref[...]
    sums_ref[0:1, :] = col_sum(dq.astype(f32))
    sums_ref[2:8, :] = jnp.zeros((6, D), f32)
    grads = (dot(xs, dq, 0, 0).astype(bf16), dot(xs, dkv, 0, 0).astype(bf16))
    for r in range(4):
        out = gs_ref if r % 2 else gk_ref
        c0 = (2 * r + 1) * BLK
        sums_ref[1:2, r * BLK : (r + 1) * BLK] = col_sum(dkv[:, c0 : c0 + BLK].astype(f32))
        for row in range(4):
            rows = slice(row * BLK, (row + 1) * BLK)
            out[r // 2, row * 3] = grads[0][rows, r * BLK : (r + 1) * BLK]
            for part in range(2):
                c0 = (2 * r + part) * BLK
                out[r // 2, row * 3 + 1 + part] = grads[1][rows, c0 : c0 + BLK]
    dx_ref[...] = dr1_ref[...] + dot(dq, w_s[:, :D], 1, 1) + dot(dkv, w_s[:, D:], 1, 1)


def proj_grad(dq, dkv, dkvr, xs, dr1, wqkv):
    rows = xs.shape[0]
    return pl.pallas_call(
        proj_grad_kernel,
        out_shape=[
            shape((2, 12, BLK, BLK), bf16),
            shape((2, 12, BLK, BLK), bf16),
            shape((rows, D)),
            shape((8, D)),
        ],
        scratch_shapes=[pltpu.VMEM((D, 3 * D), bf16)],
        compiler_params=params(MIB["proj_grad"]),
        name="proj_grad",
        cost_estimate=cost(5),
    )(dq, dkv, dkvr, xs, dr1, *wqkv)


def embed_grad_kernel(
    place_ref, series_ref, g_ref, we_ref, s0, q0, b0, s1, q1, b1, in_ref, keep_ref, send_ref, tab
):
    place = place_ref[0]
    g = g_ref[...]
    in_ref[...] = dot_hi(g, we_ref[...], 1, 1)
    tab[:LOOK] = dot_hi(series_ref[...].astype(f32), g, 0, 0)
    tab[LOOK : LOOK + 1] = col_sum(g)
    per_layer = 8 + FF // D
    for layer, (sums, qsums, db1) in enumerate(((s0, q0, b0), (s1, q1, b1))):
        base = LOOK + 1 + layer * per_layer
        for r in range(4):
            h = place ^ r
            lanes = pl.ds(pl.multiple_of(h * BLK, BLK), BLK)
            tab[base : base + 2, lanes] = qsums[0:2, r * BLK : (r + 1) * BLK]
            tab[pl.ds(base + 5 + h, 1), :] = db1[r : r + 1, :]
        tab[base + 2 : base + 5] = sums[0:3]
        tab[base + 5 + FF // D : base + per_layer] = sums[3:6]
    used = LOOK + 1 + LAYERS * per_layer
    tab[used:] = jnp.zeros((BLK - used, D), f32)
    for r in range(4):
        rows = tab[pl.ds(pl.multiple_of((place ^ r) * 32, 32), 32), :]
        out = send_ref if r % 2 else keep_ref
        for c in range(4):
            out[r // 2, c * 32 : (c + 1) * 32] = rows[:, c * BLK : (c + 1) * BLK]


def embed_grad(place, series, g, table, sums):
    rows = series.shape[0]
    spec = pl.BlockSpec(memory_space=pltpu.VMEM)
    return pl.pallas_call(
        embed_grad_kernel,
        in_specs=[pl.BlockSpec(memory_space=pltpu.SMEM)] + [spec] * 9,
        out_shape=[
            shape((rows, LOOK)),
            shape((2, BLK, BLK)),
            shape((2, BLK, BLK)),
        ],
        scratch_shapes=[pltpu.VMEM((BLK, D), f32)],
        compiler_params=params(MIB["embed_grad"]),
        name="embed_grad",
        cost_estimate=cost(2),
    )(place, series, g, table[:LOOK], *sums)


def vector_kernel(
    place_ref, val_ref, first_ref, second_ref, p0, p1, p2, p3, nv_ref, n1_ref, n2_ref, bias_ref, tab
):
    for r, part in enumerate((p0, p1, p2, p3)):
        rows = pl.ds(pl.multiple_of((place_ref[0] ^ r) * 32, 32), 32)
        for c in range(4):
            tab[rows, c * BLK : (c + 1) * BLK] = part[c * 32 : (c + 1) * 32]
    grad = tab[: val_ref.shape[0]]
    val = val_ref[...]
    first = 0.5 * first_ref[...] + 0.5 * grad
    second = 0.5 * second_ref[...] + 0.5 * grad * grad
    n1_ref[...] = first
    n2_ref[...] = second
    nv_ref[...] = val - rate_vector * (
        first / CORR / (jnp.sqrt(second / CORR) + adam_eps) + weight_decay * val
    )
    per_layer = 8 + FF // D
    for layer in range(LAYERS):
        base = LOOK + 1 + layer * per_layer
        bias_ref[2 * layer : 2 * layer + 1] = tab[base + 2 : base + 3]
        bias_ref[2 * layer + 1 : 2 * layer + 2] = tab[base + 5 + FF // D : base + 6 + FF // D]


def vector_update(place, values, first, second, parts):
    spec = pl.BlockSpec(memory_space=pltpu.VMEM)
    return pl.pallas_call(
        vector_kernel,
        in_specs=[pl.BlockSpec(memory_space=pltpu.SMEM)] + [spec] * 7,
        out_shape=[shape(values.shape)] * 3 + [shape((2 * LAYERS, D))],
        scratch_shapes=[pltpu.VMEM((BLK, D), f32)],
        compiler_params=params(MIB["vector"]),
        name="vector",
        cost_estimate=cost(2),
    )(place, values, first, second, *parts)


PARTS = ((0, 12), (12, 20), (32, 16))
HELD = ((0, 12), (12, 36))


def natural_kernel(plan, at_ref, *refs):
    count = len(plan)
    slots, outs, held = refs[:count], refs[count:-1], refs[-1]
    for ref, start in zip(slots, plan):
        held[start : start + ref.shape[0]] = ref[...]
    for i in range(len(HELD) * LAYERS):
        layer, part = divmod(i, len(HELD))
        first, n = HELD[part]
        for j in range(n):
            block = held[at_ref[layer * 48 + first + j]]
            outs[i][j] = block
            if len(outs) > len(HELD) * LAYERS:
                outs[len(HELD) * LAYERS + i][j] = block[TOP:]


def natural_order(at, slots, plan, lower):
    total = sum(s.shape[0] for s in slots)
    rows = slots[0].shape[1]
    spec = pl.BlockSpec(memory_space=pltpu.VMEM)
    heights = (rows, BLK - TOP) if lower else (rows,)
    return pl.pallas_call(
        functools.partial(natural_kernel, plan),
        in_specs=[pl.BlockSpec(memory_space=pltpu.SMEM)] + [spec] * len(slots),
        out_shape=[
            shape((n, height, BLK), bf16)
            for height in heights
            for _ in range(LAYERS)
            for _, n in HELD
        ],
        scratch_shapes=[pltpu.VMEM((total, rows, BLK), bf16)],
        compiler_params=params(MIB["natural"]),
        name="natural",
        cost_estimate=cost(3),
    )(at, *slots)


def routed_kernel(at_ref, *refs):
    own, got, out = refs[:6], refs[6:12], refs[12]
    out[...] = jnp.zeros(out.shape, bf16)
    for i in range(6):
        layer, part = divmod(i, 3)
        first, n = PARTS[part]
        for j in range(n):
            place = at_ref[layer * 48 + first + j]
            who = at_ref[96 + layer * 48 + first + j]
            value = own[i][j].astype(f32) + got[i][j].astype(f32)
            out[who, pl.ds(pl.multiple_of(place * BLK, BLK), BLK), :] = value.astype(bf16)


def routed(at, own, got, count, slots_each):
    spec = pl.BlockSpec(memory_space=pltpu.VMEM)
    return pl.pallas_call(
        routed_kernel,
        in_specs=[pl.BlockSpec(memory_space=pltpu.SMEM)] + [spec] * 12,
        out_shape=shape((count, slots_each * BLK, BLK), bf16),
        compiler_params=params(MIB["routed"]),
        name="routed",
        cost_estimate=cost(4),
    )(at, *own, *got)


def ring_of(count):
    half = count // 2
    return [2 * i for i in range(half)] + [2 * (half - 1 - i) + 1 for i in range(half)]


def ring_shift(value, order, by):
    n = len(order)
    return lax.ppermute(value, "dp", [(order[i], order[(i + by) % n]) for i in range(n)])


def ring_gather(value, order):
    n = len(order)
    half = value.shape[0] // 2

    def top(items):
        return [(far_swap(array[:, :TOP]), k, start) for array, k, start in items]

    held = [(value, 0, 0)]
    far = top(held)
    crossing = far
    ahead = behind = value
    for step in range(1, n // 2):
        if step > 2:
            behind, ahead = tied((behind, ahead), [x[0] for x in crossing])
        if step > 1:
            crossing = top(held[-2:]) if step > 2 else crossing + top(held[-2:])
            far = far + crossing[-2:]
        behind = ring_shift(behind, order, 1)
        ahead = ring_shift(ahead, order, -1)
        held += [(behind, n - step, 0), (ahead, step, 0)]
    behind, ahead = tied((behind, ahead), [x[0] for x in crossing])
    far = far + top(held[-2:])
    held.append((ring_shift(behind[:half], order, 1), n // 2, 0))
    held.append((ring_shift(ahead[half:], order, -1), n // 2, half))
    far = far + top(held[-2:])
    return held, far


def ring_reduce(pieces, order, meanwhile):
    n = len(order)
    half = pieces[0].shape[0] // 2
    up = ring_shift(pieces[n // 2][:half], order, 1)
    down = ring_shift(pieces[n // 2][half:], order, -1)
    for step in range(1, n // 2):
        near, far = pieces[n // 2 - step], pieces[n // 2 + step]
        if step == 1:
            up = jnp.concatenate([add_low(up, near[:half]), near[half:]], axis=0)
            down = jnp.concatenate([far[:half], add_low(down, far[half:])], axis=0)
        else:
            up, down = add_low(up, near), add_low(down, far)
        up, down = tied((up, down), meanwhile[step - 1])
        up, down = ring_shift(up, order, 1), ring_shift(down, order, -1)
    return pieces[0], up, down


def dp_sum(value, count, after):
    bit = 1
    while bit < count:
        if 2 * bit >= count:
            value = tied(value, after)
        low = value.astype(bf16)
        there = lax.ppermute(low, "dp", [(i, i ^ bit) for i in range(count)])
        value = low.astype(f32) + there.astype(f32)
        bit *= 2
    return value


def add_low(a, b):
    return (a.astype(f32) + b.astype(f32)).astype(bf16)


def core_swap(value):
    return lax.ppermute(value, "head", [(i, i ^ 1) for i in range(4)])


def far_swap(value):
    return lax.ppermute(value, "head", [(i, i ^ 2) for i in range(4)])


def tied(values, after):
    return lax.optimization_barrier((values, after))[0]


def one_hots(ids):
    lane = jnp.arange(LANES, dtype=jnp.int32)[None, :]
    same = ids[:, None] == lane
    return jnp.where(same, -BIG, 0.0).astype(bf16), jnp.where(same, 0.0, 1.0).astype(bf16)


def relative(row, place):
    pieces = row.reshape(4, -1)
    return jnp.take(pieces, jnp.arange(4) ^ place, axis=0).reshape(1, -1)


def on_device(
    series,
    cotangent,
    window_lengths,
    owner_list,
    master,
    first_moment,
    second_moment,
    left_stats,
    right_stats,
    left_basis,
    right_basis,
    vec_values,
    vec_first,
    vec_second,
):
    place = lax.axis_index("head")
    spot = lax.axis_index("dp")
    dp = lax.axis_size("dp")
    ringed = dp == 8
    rows = series.shape[0]
    own_slots = master.shape[1]
    buckets, win = window_lengths.shape
    bucket_rows = rows * 4 // buckets
    owner_row = owner_list[0]
    who = owner_row // own_slots
    if ringed:
        order = ring_of(dp)
        ring_at = jnp.asarray([order.index(d) for d in range(dp)], jnp.int32)
        who = (ring_at[who] - ring_at[spot]) % dp
    inner = owner_row % own_slots
    gather_at = who * own_slots + inner

    copies = master[0].astype(bf16)
    if ringed:
        held, far = ring_gather(copies, order)
        slots, plan = [x[0] for x in held], tuple(x[1] * own_slots + x[2] for x in held)
        tops, far_plan = [x[0] for x in far], tuple(x[1] * own_slots + x[2] for x in far)
    else:
        slots, plan = [lax.all_gather(copies, "dp", axis=0, tiled=True)], (0,)
        tops, far_plan = [far_swap(slots[0][:, :TOP])], (0,)
    far_at = far_swap(gather_at)
    windows = window_ids(window_lengths, bucket_rows)
    ids = windows.reshape(4, rows)
    own_ids = lax.dynamic_index_in_dim(ids, place, 0, False)
    pair_ids = lax.dynamic_index_in_dim(ids, place ^ 1, 0, False)
    ohq, ohk_own = one_hots(own_ids)
    ohk = jnp.concatenate([ohk_own, one_hots(pair_ids)[1]], axis=0)
    valid = (own_ids < win).astype(f32)[:, None]

    x = embed(series, vec_values)
    vectors = []
    for layer in range(LAYERS):
        bq, bv, bo, g1, c1, b1, b2, g2, c2 = depth_vectors(vec_values, layer)
        vec = jnp.stack([bo, g1, c1, b2, g2, c2, g2, c2])
        vectors.append([vec] + [relative(row, place) for row in (bq, bv, b1)])
    grad = cotangent * valid
    slots, (x, vectors, ohq, ohk, valid, gather_at, far_at, grad) = lax.optimization_barrier(
        (slots, (x, vectors, ohq, ohk, valid, gather_at, far_at, grad))
    )
    mine = natural_order(gather_at, slots, plan, True)
    mine, lower = mine[: len(HELD) * LAYERS], mine[len(HELD) * LAYERS :]
    upper = natural_order(far_at, tops, far_plan, False)
    moved = []

    def cross(i, after=None):
        own = lower[i] if after is None else tied(lower[i], after)
        moved.append(far_swap(own))
        return moved[-1]

    def four(i, after=None):
        there = moved[i] if after is None else tied(moved[i], after)
        return [
            mine[i], core_swap(mine[i]), upper[i], there, core_swap(upper[i]), core_swap(there)
        ]

    weights = []
    saved = []
    for layer in range(LAYERS):
        vec, bq, bv, b1 = vectors[layer]
        if layer == 0:
            cross(0)
        wqkv = four(2 * layer, x if layer else None)
        x = tied(x, wqkv)
        if layer == 0:
            cross(1, moved[0])
        xs, q, kv = project(x, bq, bv, wqkv)
        kvp = core_swap(kv)
        o, lse = attend(q, kv, kvp, ohq, ohk)
        wfeed = four(2 * layer + 1, o)
        weights.append((wqkv, wfeed))
        if layer + 1 < LAYERS:
            done = moved[-1]
            cross(2 * layer + 2, done)
            cross(2 * layer + 3, (done, moved[-1]))
        n1, i1, y, hid, slope, n2, i2, x = post(o, x, vec, b1, wfeed)
        saved.append((xs, q, kv, kvp, o, lse, vec, n1, i1, y, hid, slope, n2, i2))
    activations = x * valid

    own_sums = [None] * (3 * LAYERS)
    far_sums = [None] * (3 * LAYERS)
    table_rows = [None] * LAYERS

    waiting = []

    def chip_sum(at, keep, got):
        waiting.append((at, keep, got))
        return add_low(keep[1], got[1])

    def own_chip_sums(after):
        while waiting:
            at, keep, got = waiting.pop()
            keep, got = tied((keep[0], got[0]), after)
            own_sums[at] = add_low(keep, got)

    moving = []
    for layer in reversed(range(LAYERS)):
        xs, q, kv, kvp, o, lse, vec, n1, i1, y, hid, slope, n2, i2 = saved[layer]
        wqkv, wfeed = weights[layer]
        gk, gs, ok, os, dr1, do, db1, sums = ffn_grad(
            grad, n2, i2, n1, i1, y, hid, slope, o, vec, wfeed
        )
        os, gs, ok, gk, do = tied((os, gs, ok, gk, do), moving)
        own_chip_sums(sums)
        got = [core_swap(os), core_swap(gs)]
        mid = chip_sum(3 * layer + 1, ok, got[0])
        down = chip_sum(3 * layer + 2, gk, got[1])
        far_sums[3 * layer + 1] = far_swap(mid)
        do = tied(do, (mid, down))
        dq, dkv, dkvp = attend_grad(q, kv, kvp, do, o, lse, ohq, ohk)
        dkvp = tied(dkvp, far_sums[3 * layer + 1])
        far_sums[3 * layer + 2] = far_swap(tied(down, far_sums[3 * layer + 1]))
        if layer == 0:
            far_sums[late[0]] = far_swap(tied(late[1], far_sums[1]))
        dkvr = core_swap(dkvp)
        pk, ps, grad, qsums = proj_grad(dq, dkv, dkvr, xs, dr1, wqkv)
        table_rows[layer] = (sums, qsums, db1)
        got = core_swap(ps)
        if layer:
            far = chip_sum(3 * layer, pk, got)
            grad = tied(grad, far)
            late = (3 * layer, far)
            moving = [far_sums[3 * layer + 2]]
    input_grad, tab_keep, tab_send = embed_grad(
        place.astype(jnp.int32)[None], series, grad, vec_values, table_rows[0] + table_rows[1]
    )
    far_sums[0] = far_swap(chip_sum(0, pk, got))
    own_chip_sums(tab_send)
    tab = dp_sum(tab_keep + core_swap(tab_send), dp, far_sums[0])
    tab_part = tab[0] + far_swap(tab[1])
    tab_there = far_swap(tab_part)
    parts = [tab_part, core_swap(tab_part), tab_there, core_swap(tab_there)]
    vec_new_values, vec_new_first, vec_new_second, branch_bias_grads = vector_update(
        place.astype(jnp.int32)[None], vec_values, vec_first, vec_second, parts
    )
    at = jnp.concatenate([inner, who]).astype(jnp.int32)
    pieces = routed(at, own_sums, far_sums, dp, own_slots)
    if ringed:
        meanwhile = (tab, tab_part, parts)
        terms = ring_reduce([pieces[i] for i in range(dp)], order, meanwhile)
        terms = tied(terms, vec_new_values)
        grads = [t.reshape(own_slots, BLK, BLK) for t in terms]
    else:
        whole = lax.psum_scatter(pieces, "dp", scatter_dimension=0, tiled=True)
        grads = [whole.reshape(own_slots, BLK, BLK)]
    new_master, new_copy, new_first, new_second, new_left, new_right, left_next, right_next = soap(
        grads,
        master[0],
        first_moment[0],
        second_moment[0],
        left_stats[0],
        right_stats[0],
        left_basis[0],
        right_basis[0],
    )
    return (
        activations,
        input_grad,
        new_master[None],
        new_copy[None],
        new_first[None],
        new_second[None],
        new_left[None],
        new_right[None],
        left_next[None],
        right_next[None],
        vec_new_values,
        vec_new_first,
        vec_new_second,
        branch_bias_grads,
    )


def solution(mesh):
    placed = (
        P(("dp", "head"), None),
        P(("dp", "head"), None),
        P("dp", None),
        P("head", None),
        P("head", "dp", None, None),
        P("head", "dp", None, None),
        P("head", "dp", None, None),
        P("head", "dp", None, None),
        P("head", "dp", None, None),
        P("head", "dp", None, None),
        P("head", "dp", None, None),
        P(),
        P(),
        P(),
    )
    return jax.shard_map(
        on_device,
        mesh=mesh,
        in_specs=placed,
        out_specs=(
            P(("dp", "head"), None),
            P(("dp", "head"), None),
            P("head", "dp", None, None),
            P("head", "dp", None, None),
            P("head", "dp", None, None),
            P("head", "dp", None, None),
            P("head", "dp", None, None),
            P("head", "dp", None, None),
            P("head", "dp", None, None),
            P("head", "dp", None, None),
            P(),
            P(),
            P(),
            P(),
        ),
        check_vma=False,
    )
```

```python
import functools

import jax
import jax.numpy as jnp
from jax import lax
from jax.experimental import pallas as pl
from jax.experimental.pallas import tpu as pltpu
from jax.sharding import PartitionSpec as P

D = 512
HEADS = 8
HD = 64
FF = 2048
LOOK = 96
LAYERS = 2
BLK = 128
STEP = 10

f32 = jnp.float32
HI = lax.Precision.HIGHEST
norm_eps = 1e-05
beta_first = 0.5
beta_second = 0.5
beta_stats = 0.5
adam_eps = 1e-08
rate_matrix = 0.02
rate_vector = 0.15
weight_decay = 0.01


def window_ids(lengths, bucket_rows):
    bounds = jnp.cumsum(lengths, axis=1, dtype=jnp.int32)
    places = jnp.arange(bucket_rows, dtype=jnp.int32)
    return jnp.sum(
        (places[None, :, None] >= bounds[:, None, :]).astype(jnp.int32), axis=2, dtype=jnp.int32
    )


def depth_vectors(vec_table, layer_at):
    ff_ratio = FF // D
    base_row = LOOK + 1 + layer_at * (8 + ff_ratio)
    return (
        vec_table[base_row],
        vec_table[base_row + 1],
        vec_table[base_row + 2],
        vec_table[base_row + 3],
        vec_table[base_row + 4],
        vec_table[base_row + 5 : base_row + 5 + ff_ratio].reshape(FF),
        vec_table[base_row + 5 + ff_ratio],
        vec_table[base_row + 6 + ff_ratio],
        vec_table[base_row + 7 + ff_ratio],
    )


def dot_hi(a, b, ca, cb):
    return lax.dot_general(
        a, b, (((ca,), (cb,)), ((), ())), precision=HI, preferred_element_type=f32
    )


def terms(x, count):
    out = []
    for i in range(count):
        part = x.astype(jnp.bfloat16)
        out.append(part)
        if i < count - 1:
            x = x - part.astype(f32)
    return out


def dot_terms(a, b, ca, cb, full=False):
    a = terms(a, 3 if full else 2)
    b = terms(b, 3 if full else 2)
    dims = (((ca,), (cb,)), ((), ()))
    left = jnp.concatenate(a[:2], axis=ca)
    right = jnp.concatenate(
        [jnp.concatenate([b[0], b[1]], axis=cb), jnp.concatenate([b[1], b[0]], axis=cb)], axis=1 - cb
    )
    out = lax.dot_general(left, right, dims, preferred_element_type=f32)
    out = out[:, :BLK] + out[:, BLK:]
    if full:
        out = out + lax.dot_general(
            jnp.concatenate([a[0], a[2]], axis=ca),
            jnp.concatenate([b[2], b[0]], axis=cb),
            dims,
            preferred_element_type=f32,
        )
    return out


PANEL = 32
AHEAD = 2


def recip(x):
    guess = pl.reciprocal(x, approx=True)
    guess = guess * (2.0 - x * guess)
    return guess * (2.0 - x * guess)


def qr_batch(a_ref, count):
    lane = lax.broadcasted_iota(jnp.int32, (1, 1, BLK), 2)
    sub8 = lax.broadcasted_iota(jnp.int32, (1, 8, 1), 1)
    sub = lax.broadcasted_iota(jnp.int32, (1, PANEL, 1), 1)
    for r0 in range(0, BLK, PANEL):
        tiles = [a_ref[:, r0 + 8 * t : r0 + 8 * t + 8, :] for t in range(PANEL // 8)]
        for k0 in range(0, PANEL, AHEAD):
            t0, s0 = divmod(k0, 8)
            cols = [
                [
                    jnp.broadcast_to(tiles[t][:, :, r0 + k : r0 + k + 1], (count, 8, BLK))
                    for k in range(k0, k0 + AHEAD)
                ]
                for t in range(PANEL // 8)
            ]
            for i in range(AHEAD):
                s = s0 + i
                inv = recip(cols[t0][i][:, s : s + 1, :])
                pn = (tiles[t0][:, s : s + 1, :] + (lane == r0 + k0 + i).astype(f32)) * inv
                rest = [cols[t0][j][:, s : s + 1, :] * inv for j in range(i + 1, AHEAD)]
                for t in range(t0, PANEL // 8):
                    c = cols[t][i]
                    if t == t0:
                        if s == 7:
                            continue
                        c = jnp.where(sub8 > s, c, 0.0)
                    tiles[t] = tiles[t] - c * pn
                    for j, m in enumerate(rest):
                        cols[t][i + 1 + j] = cols[t][i + 1 + j] - c * m
        done = jnp.concatenate(tiles, axis=1)
        diag = lane == sub + r0
        pivot = jnp.sum(jnp.where(diag, done, 0.0), axis=2, keepdims=True)
        done = jnp.where(diag, 1.0, jnp.where((lane > sub + r0) & (lane < r0 + PANEL), 0.0, done))
        done = done * lax.rsqrt(pivot)
        a_ref[:, r0 : r0 + PANEL, :] = done
        r1 = r0 + PANEL
        if r1 < BLK:
            lane2 = lax.broadcasted_iota(jnp.int32, (BLK - r1, BLK), 1)
            clear = (lane2 >= r0) & (lane2 < r1)
            z0, z1, z2 = terms(done, 3)
            left = jnp.concatenate([z0, z0, z0, z1, z1, z2], axis=1)
            right = jnp.concatenate([z0, z1, z2, z0, z1, z0], axis=1)
            for b in range(count):
                update = lax.dot_general(
                    left[b], right[b], (((0,), (0,)), ((), ())), preferred_element_type=f32
                )
                a_ref[b, r1:, :] = jnp.where(clear, 0.0, a_ref[b, r1:, :]) - update[r1:]


def soap_kernel(count, *refs):
    for s in range(refs[0].shape[0]):
        soap_slot(s, sum(ref[s].astype(f32) for ref in refs[:count]), *refs[count:])
    soap_finish(*refs[-4:])


def soap_slot(
    s, g, mas_ref, m1_ref, m2_ref, ls_ref, rs_ref, lb_ref, rb_ref,
    nm_ref, nc_ref, n1_ref, n2_ref, nl_ref, nr_ref, ql_ref, qr_ref, mat_ref, a_ref,
):
    group = mas_ref.shape[0]
    lb = lb_ref[s]
    rb = rb_ref[s]
    rot = dot_terms(dot_terms(lb, g, 0, 0), rb, 1, 0)
    n1 = 0.5 * m1_ref[s] + 0.5 * rot
    n2 = 0.5 * m2_ref[s] + 0.5 * rot * rot
    n1_ref[s] = n1
    n2_ref[s] = n2
    corr = 1.0 - 0.5**STEP
    ratio = n1 / corr / (jnp.sqrt(n2 / corr) + adam_eps)
    upd = dot_terms(dot_terms(lb, ratio, 1, 0), rb, 1, 1)
    mas = mas_ref[s]
    nm = mas - rate_matrix * (upd + weight_decay * mas)
    nm_ref[s] = nm
    nc_ref[s] = nm.astype(jnp.bfloat16)
    nl = 0.5 * ls_ref[s] + 0.5 * dot_terms(g, g, 1, 1)
    nr = 0.5 * rs_ref[s] + 0.5 * dot_terms(g, g, 0, 0)
    nl_ref[s] = nl
    nr_ref[s] = nr
    for side, (st, ba) in enumerate(((nl, lb), (nr, rb))):
        m = dot_terms(st, ba, 1, 0, True)
        m = m * lax.rsqrt(jnp.sum(m * m, axis=0, keepdims=True))
        at = 2 * (pl.program_id(0) * group + s) + side
        mat_ref[at] = m
        a_ref[at] = dot_terms(m, m, 0, 0, True)


def soap_finish(ql_ref, qr_ref, mat_ref, a_ref):
    @pl.when(pl.program_id(0) == pl.num_programs(0) - 1)
    def _():
        count = a_ref.shape[0]
        qr_batch(a_ref, count)
        keep = lax.broadcasted_iota(jnp.int32, (BLK, BLK), 1) <= lax.broadcasted_iota(
            jnp.int32, (BLK, BLK), 0
        )
        for j in range(count // 2):
            for side, ref in enumerate((ql_ref, qr_ref)):
                x = jnp.where(keep, a_ref[2 * j + side], 0.0)
                ref[j] = dot_terms(mat_ref[2 * j + side], x, 1, 1, True)


def soap(gs, master, m1, m2, ls, rs, lb, rb):
    n = master.shape[0]
    group = SOAP_GROUP if n % SOAP_GROUP == 0 else n
    one = pl.BlockSpec((group, BLK, BLK), lambda i: (i, 0, 0))
    whole = pl.BlockSpec((n, BLK, BLK), lambda i: (0, 0, 0))
    sh = jax.ShapeDtypeStruct((n, BLK, BLK), f32)
    shb = jax.ShapeDtypeStruct((n, BLK, BLK), jnp.bfloat16)
    return pl.pallas_call(
        functools.partial(soap_kernel, len(gs)),
        grid=(n // group,),
        in_specs=[one] * (len(gs) + 7),
        out_specs=[one] * 6 + [whole] * 2,
        out_shape=[sh, shb, sh, sh, sh, sh, sh, sh],
        scratch_shapes=[pltpu.VMEM((2 * n, BLK, BLK), f32)] * 2,
        compiler_params=pltpu.CompilerParams(vmem_limit_bytes=16 * 2**20),
        cost_estimate=pl.CostEstimate(flops=40 * 10**6, bytes_accessed=0, transcendentals=0),
        name="soap",
    )(*gs, master, m1, m2, ls, rs, lb, rb)


SOAP_GROUP = 4


bf16 = jnp.bfloat16
LANES = 128
TOP = 64
ROW_TILE = 512
BIG = 1e30
CORR = 1.0 - 0.5**STEP


def params(mib=48):
    return pltpu.CompilerParams(vmem_limit_bytes=mib * 2**20)


MIB = dict(
    embed=6, project=8, attend=16, post=20, ffn_grad=24, attend_grad=16, proj_grad=12, embed_grad=8, vector=4, natural=6, routed=8,
)


def cost(micros):
    return pl.CostEstimate(flops=int(micros * 1e6), bytes_accessed=0, transcendentals=0)


def shape(dims, kind=f32):
    return jax.ShapeDtypeStruct(dims, kind)


def dot(a, b, ca=1, cb=0):
    return lax.dot_general(a, b, (((ca,), (cb,)), ((), ())), preferred_element_type=f32)


def planes(refs):
    return (refs[0],), (refs[1],), (refs[2], refs[3]), (refs[4], refs[5])


def place_block(dst, refs, j, r0, c0):
    for ref in refs:
        dst[r0 : r0 + ref.shape[1], c0 : c0 + BLK] = ref[j]
        r0 += ref.shape[1]


def place_blocks(dst, refs, first, rows, cols, row_step, col_step):
    for r, plane in enumerate(planes(refs)):
        for j in range(rows * cols):
            row, col = divmod(j, cols)
            place_block(dst, plane, first + j, r * row_step + row * BLK, r * col_step + col * BLK)


def place_qkv(dst, refs):
    for r, plane in enumerate(planes(refs)):
        for j in range(12):
            row, col = divmod(j, 3)
            c0 = D + (2 * r + col - 1) * BLK if col else r * BLK
            place_block(dst, plane, j, row * BLK, c0)


def layer_norm(resid):
    center = resid - jnp.mean(resid, axis=1, keepdims=True)
    inv = lax.rsqrt(jnp.mean(center * center, axis=1, keepdims=True) + norm_eps)
    return center * inv, inv


def layer_norm_grad(grad, unit, inv, gain):
    dn = grad * gain
    return inv * (
        dn
        - jnp.mean(dn, axis=1, keepdims=True)
        - unit * jnp.mean(dn * unit, axis=1, keepdims=True)
    )


def col_sum(values):
    return jnp.sum(values, axis=0, keepdims=True)


def embed_kernel(series_ref, we_ref, be_ref, x_ref):
    x_ref[...] = dot_hi(series_ref[...].astype(f32), we_ref[...], 1, 0) + be_ref[...]


def embed(series, table):
    rows = series.shape[0]
    return pl.pallas_call(
        embed_kernel, out_shape=shape((rows, D)), compiler_params=params(MIB["embed"]), name="embed"
    )(series, table[:LOOK], table[LOOK : LOOK + 1])


def proj_kernel(x_ref, bq_ref, bv_ref, w0, w1, w2, w3, w4, w5, xs_ref, q_ref, kv_ref, w_s):
    place_qkv(w_s, (w0, w1, w2, w3, w4, w5))
    xs = x_ref[...].astype(bf16)
    xs_ref[...] = xs
    q_ref[...] = (dot(xs, w_s[:, :D]) + bq_ref[...]).astype(bf16)
    kv = dot(xs, w_s[:, D:])
    for r in range(4):
        at = 2 * r * BLK
        kv_ref[:, at : at + BLK] = kv[:, at : at + BLK].astype(bf16)
        value = kv[:, at + BLK : at + 2 * BLK] + bv_ref[:, r * BLK : (r + 1) * BLK]
        kv_ref[:, at + BLK : at + 2 * BLK] = value.astype(bf16)


def project(x, bq, bv, wqkv):
    rows = x.shape[0]
    return pl.pallas_call(
        proj_kernel,
        out_shape=[
            shape((rows, D), bf16),
            shape((rows, D), bf16),
            shape((rows, 2 * D), bf16),
        ],
        scratch_shapes=[pltpu.VMEM((D, 3 * D), bf16)],
        compiler_params=params(MIB["project"]),
        name="project",
        cost_estimate=cost(3),
    )(x, bq, bv, *wqkv)


def half_mask(i, kind=bf16):
    lane = lax.broadcasted_iota(jnp.int32, (1, LANES), 1)
    return ((lane >= HD * i) & (lane < HD * (i + 1))).astype(f32).astype(kind)


def three_terms(col):
    first = col.astype(bf16).astype(f32)
    second = (col - first).astype(bf16).astype(f32)
    return first, second, col - first - second


def lanes_with(base, at, cols):
    lane = lax.broadcasted_iota(jnp.int32, base.shape, 1)
    for i, col in enumerate(cols):
        base = jnp.where(lane == at + i, col, base)
    return base.astype(bf16)


def attend_kernel(q_ref, kv_ref, kvp_ref, ohq_ref, ohk_ref, o_ref, lse_ref, ka, va):
    rows = q_ref.shape[0]
    ka[:rows, :LANES] = kv_ref[:, :LANES]
    ka[rows:, :LANES] = kvp_ref[:, :LANES]
    ka[:, LANES:] = ohk_ref[...]
    lane = lax.broadcasted_iota(jnp.int32, (ROW_TILE, LANES), 1)
    for i in range(2):
        m = half_mask(i)
        va[i, :rows, :LANES] = kv_ref[:, LANES:] * m
        va[i, rows:, :LANES] = kvp_ref[:, LANES:] * m
        va[i, :, LANES:] = jnp.ones((2 * rows, LANES), bf16)

    def tile(t, c):
        at = pl.ds(t * ROW_TILE, ROW_TILE)
        total = jnp.zeros((ROW_TILE, LANES), f32)
        stat = jnp.zeros((ROW_TILE, LANES), f32)
        for i in range(2):
            qa = jnp.concatenate([q_ref[at] * (half_mask(i) * bf16(0.125)), ohq_ref[at]], axis=1)
            s = dot(qa, ka[...], 1, 1)
            high = jnp.max(s, axis=1, keepdims=True)
            e = jnp.exp(s - high).astype(bf16)
            out = dot(e, va[i])
            norm = out[:, LANES:]
            total = total + out[:, :LANES] / norm
            stat = jnp.where(lane == i, high + jnp.log(norm), stat)
        o_ref[at] = total.astype(bf16)
        lse_ref[at] = stat
        return c

    lax.fori_loop(0, rows // ROW_TILE, tile, 0)


def attend(q, kv, kvp, ohq, ohk):
    rows = q.shape[0]
    pair = pl.BlockSpec((rows, LANES), lambda h: (0, h))
    both = pl.BlockSpec((rows, 2 * LANES), lambda h: (0, h))
    other = pl.BlockSpec((rows, 2 * LANES), lambda h: (0, h + 1 - 2 * lax.rem(h, 2)))
    return pl.pallas_call(
        attend_kernel,
        grid=(D // LANES,),
        in_specs=[pair, both, other]
        + [
            pl.BlockSpec((rows, LANES), lambda h: (0, 0)),
            pl.BlockSpec((2 * rows, LANES), lambda h: (0, 0)),
        ],
        out_specs=[pair, pair],
        out_shape=[shape((rows, D), bf16), shape((rows, D))],
        scratch_shapes=[
            pltpu.VMEM((2 * rows, 2 * LANES), bf16),
            pltpu.VMEM((2, 2 * rows, 2 * LANES), bf16),
        ],
        compiler_params=params(MIB["attend"]),
        name="attend",
        cost_estimate=cost(11),
    )(q, kv, kvp, ohq, ohk)


def post_kernel(
    o_ref, x_ref, vec_ref, b1_ref, a0, a1, a2, a3, a4, a5,
    n1_ref, i1_ref, y_ref, hid_ref, slope_ref, n2_ref, i2_ref, x2_ref,
    wo_s, w1_s, w2_s,
):
    place_blocks(wo_s, (a0, a1, a2, a3, a4, a5), 0, 1, 4, BLK, 0)
    place_blocks(w1_s, (a0, a1, a2, a3, a4, a5), 4, 4, 4, 0, D)
    place_blocks(w2_s, (a0, a1, a2, a3, a4, a5), 20, 4, 4, D, 0)

    def tile(t, c):
        at = pl.ds(t * ROW_TILE, ROW_TILE)
        vec = [vec_ref[i : i + 1, :] for i in range(6)]
        unit, inv = layer_norm(x_ref[at] + dot(o_ref[at], wo_s[...]) + vec[0])
        n1_ref[at] = unit
        i1_ref[at] = jnp.broadcast_to(inv, (ROW_TILE, LANES))
        y = unit * vec[1] + vec[2]
        yb = y.astype(bf16)
        y_ref[at] = yb
        pre = dot(yb, w1_s[...]) + b1_ref[...]
        phi = 0.5 * (1.0 + lax.erf(pre * (0.5**0.5)))
        hid = (pre * phi).astype(bf16)
        hid_ref[at] = hid
        slope = phi + pre * (jnp.exp(-0.5 * pre * pre) * 0.3989422804014327)
        slope_ref[at] = slope.astype(bf16)
        fed = dot(hid, w2_s[...])
        unit, inv = layer_norm(y + fed + vec[3])
        n2_ref[at] = unit
        i2_ref[at] = jnp.broadcast_to(inv, (ROW_TILE, LANES))
        x2_ref[at] = unit * vec[4] + vec[5]
        return c

    lax.fori_loop(0, x_ref.shape[0] // ROW_TILE, tile, 0)


def post(o, x, vec, b1, wfeed):
    rows = x.shape[0]
    return pl.pallas_call(
        post_kernel,
        out_shape=[
            shape((rows, D)),
            shape((rows, LANES)),
            shape((rows, D), bf16),
            shape((rows, FF), bf16),
            shape((rows, FF), bf16),
            shape((rows, D)),
            shape((rows, LANES)),
            shape((rows, D)),
        ],
        scratch_shapes=[
            pltpu.VMEM((D, D), bf16),
            pltpu.VMEM((D, FF), bf16),
            pltpu.VMEM((FF, D), bf16),
        ],
        compiler_params=params(MIB["post"]),
        name="post",
        cost_estimate=cost(11),
    )(o, x, vec, b1, *wfeed)


def store_blocks(refs, r, first, rows, cols, value):
    keep_ref, send_ref = refs
    ref = send_ref if r % 2 else keep_ref
    for j in range(rows * cols):
        row, col = divmod(j, cols)
        ref[r // 2, first + j] = value[row * BLK : (row + 1) * BLK, col * BLK : (col + 1) * BLK]


def ffn_grad_kernel(
    e_ref, n2_ref, i2_ref, n1_ref, i1_ref, y_ref, hid_ref, slope_ref, o_ref, vec_ref,
    a0, a1, a2, a3, a4, a5,
    gk_ref, gs_ref, ok_ref, os_ref, dr1_ref, do_ref, db1_ref, sums_ref,
    wo_s, w1_s, w2_s, dr2_s, dfr_s, dpre_s, dar_s,
):
    rows = e_ref.shape[0]
    place_blocks(wo_s, (a0, a1, a2, a3, a4, a5), 0, 1, 4, BLK, 0)
    place_blocks(w1_s, (a0, a1, a2, a3, a4, a5), 4, 4, 4, 0, D)
    place_blocks(w2_s, (a0, a1, a2, a3, a4, a5), 20, 4, 4, D, 0)
    tiles = rows // ROW_TILE
    gain_two = vec_ref[4:5, :]
    gain_one = vec_ref[1:2, :]
    zero = jnp.zeros((1, D), f32)

    def tile_two(t, c):
        at = pl.ds(t * ROW_TILE, ROW_TILE)
        grad = e_ref[at]
        unit = n2_ref[at]
        dr2 = layer_norm_grad(grad, unit, i2_ref[at, 0:1], gain_two)
        dr2_s[at] = dr2
        dfr_s[at] = dr2.astype(bf16)
        return (c[0] + col_sum(dr2), c[1] + col_sum(grad * unit), c[2] + col_sum(grad))

    db2, dg2, dc2 = lax.fori_loop(0, tiles, tile_two, (zero, zero, zero))

    for r in range(FF // D):
        cols = slice(r * D, (r + 1) * D)

        def tile_up(t, c):
            at = pl.ds(t * ROW_TILE, ROW_TILE)
            dh = dot(dfr_s[at], w2_s[cols, :], 1, 1)
            dpre = (dh * slope_ref[at, cols].astype(f32)).astype(bf16)
            dpre_s[at, cols] = dpre
            dr2_s[at] = dr2_s[at] + dot(dpre, w1_s[:, cols], 1, 1)
            return c + col_sum(dpre.astype(f32))

        db1_ref[r : r + 1, :] = lax.fori_loop(0, tiles, tile_up, zero)
        store_blocks((gk_ref, gs_ref), r, 0, 4, 4, dot(hid_ref[:, cols], dfr_s[...], 0, 0).astype(bf16))
        store_blocks((ok_ref, os_ref), r, 4, 4, 4, dot(y_ref[...], dpre_s[:, cols], 0, 0).astype(bf16))

    def tile_one(t, c):
        at = pl.ds(t * ROW_TILE, ROW_TILE)
        grad = dr2_s[at]
        unit = n1_ref[at]
        dr1 = layer_norm_grad(grad, unit, i1_ref[at, 0:1], gain_one)
        dr1_ref[at] = dr1
        dar = dr1.astype(bf16)
        dar_s[at] = dar
        do_ref[at] = dot(dar, wo_s[...], 1, 1).astype(bf16)
        return (c[0] + col_sum(dr1), c[1] + col_sum(grad * unit), c[2] + col_sum(grad))

    dbo, dg1, dc1 = lax.fori_loop(0, tiles, tile_one, (zero, zero, zero))
    dwo = dot(o_ref[...], dar_s[...], 0, 0).astype(bf16)
    for r in range(4):
        store_blocks((ok_ref, os_ref), r, 0, 1, 4, dwo[r * BLK : (r + 1) * BLK])
    for i, value in enumerate((dbo, dg1, dc1, db2, dg2, dc2, zero, zero)):
        sums_ref[i : i + 1, :] = value


def ffn_grad(e, n2, i2, n1, i1, y, hid, slope, o, vec, wfeed):
    rows = e.shape[0]
    return pl.pallas_call(
        ffn_grad_kernel,
        out_shape=[
            shape((2, 16, BLK, BLK), bf16),
            shape((2, 16, BLK, BLK), bf16),
            shape((2, 20, BLK, BLK), bf16),
            shape((2, 20, BLK, BLK), bf16),
            shape((rows, D)),
            shape((rows, D), bf16),
            shape((FF // D, D)),
            shape((8, D)),
        ],
        scratch_shapes=[
            pltpu.VMEM((D, D), bf16),
            pltpu.VMEM((D, FF), bf16),
            pltpu.VMEM((FF, D), bf16),
            pltpu.VMEM((rows, D), f32),
            pltpu.VMEM((rows, D), bf16),
            pltpu.VMEM((rows, FF), bf16),
            pltpu.VMEM((rows, D), bf16),
        ],
        compiler_params=params(MIB["ffn_grad"]),
        name="ffn_grad",
        cost_estimate=cost(16),
    )(e, n2, i2, n1, i1, y, hid, slope, o, vec, *wfeed)


def attend_grad_kernel(
    q_ref, kv_ref, kvp_ref, do_ref, o_ref, lse_ref, ohq_ref, ohk_ref,
    dq_ref, dkv_ref, dkvp_ref,
    ka, va, qa, da, kt,
):
    rows = q_ref.shape[0]
    ka[:rows, :LANES] = kv_ref[:, :LANES]
    ka[rows:, :LANES] = kvp_ref[:, :LANES]
    ka[:, LANES:] = ohk_ref[...]
    va[:rows, :LANES] = kv_ref[:, LANES:]
    va[rows:, :LANES] = kvp_ref[:, LANES:]
    va[:, LANES:] = jnp.ones((2 * rows, LANES), bf16)
    kt[...] = ka[:, :LANES].T
    product = do_ref[...].astype(f32) * o_ref[...].astype(f32)
    for i in range(2):
        m = half_mask(i)
        qa[i, :, :LANES] = q_ref[...] * (m * bf16(0.125))
        qa[i, :, LANES:] = lanes_with(
            ohq_ref[...].astype(f32), 120, three_terms(-lse_ref[:, i : i + 1])
        )
        da[i, :, :LANES] = do_ref[...] * m
        delta = jnp.sum(product * half_mask(i, f32), axis=1, keepdims=True)
        da[i, :, LANES:] = lanes_with(jnp.zeros((rows, LANES), f32), 0, three_terms(-delta))

    def tile(t, sums):
        at = pl.ds(pl.multiple_of(t * ROW_TILE, ROW_TILE), ROW_TILE)
        dk = jnp.zeros((ROW_TILE, LANES), f32)
        dv = jnp.zeros((ROW_TILE, LANES), f32)
        new = []
        for i in range(2):
            p = jnp.exp(dot(ka[at], qa[i], 1, 1))
            ds = (p * dot(va[at], da[i], 1, 1)).astype(bf16)
            dv = dv + dot(p.astype(bf16), da[i, :, :LANES])
            dk = dk + dot(ds, qa[i, :, :LANES])
            new.append(sums[i] + dot(kt[:, at], ds))
        return tuple(new), dk.astype(bf16), dv.astype(bf16)

    sums = (jnp.zeros((LANES, rows), f32),) * 2
    half = rows // ROW_TILE

    def own(t, sums):
        sums, dk, dv = tile(t, sums)
        at = pl.ds(t * ROW_TILE, ROW_TILE)
        dkv_ref[at, :LANES] = dk
        dkv_ref[at, LANES:] = dv
        return sums

    def other(t, sums):
        sums, dk, dv = tile(t + half, sums)
        at = pl.ds(t * ROW_TILE, ROW_TILE)
        dkvp_ref[at, :LANES] = dk
        dkvp_ref[at, LANES:] = dv
        return sums

    sums = lax.fori_loop(0, half, own, sums)
    sums = lax.fori_loop(0, half, other, sums)
    row = lax.broadcasted_iota(jnp.int32, (LANES, rows), 0)
    dq_ref[...] = (jnp.where(row < HD, sums[0], sums[1]) * 0.125).T.astype(bf16)


def attend_grad(q, kv, kvp, do, o, lse, ohq, ohk):
    rows = q.shape[0]
    pair = pl.BlockSpec((rows, LANES), lambda h: (0, h))
    both = pl.BlockSpec((rows, 2 * LANES), lambda h: (0, h))
    other = pl.BlockSpec((rows, 2 * LANES), lambda h: (0, h + 1 - 2 * lax.rem(h, 2)))
    return pl.pallas_call(
        attend_grad_kernel,
        grid=(D // LANES,),
        in_specs=[pair, both, other, pair, pair, pair]
        + [
            pl.BlockSpec((rows, LANES), lambda h: (0, 0)),
            pl.BlockSpec((2 * rows, LANES), lambda h: (0, 0)),
        ],
        out_specs=[pair, both, other],
        out_shape=[shape((rows, D), bf16)] + [shape((rows, 2 * D), bf16)] * 2,
        scratch_shapes=[
            pltpu.VMEM((2 * rows, 2 * LANES), bf16),
            pltpu.VMEM((2 * rows, 2 * LANES), bf16),
            pltpu.VMEM((2, rows, 2 * LANES), bf16),
            pltpu.VMEM((2, rows, 2 * LANES), bf16),
            pltpu.VMEM((LANES, 2 * rows), bf16),
        ],
        compiler_params=params(MIB["attend_grad"]),
        name="attend_grad",
        cost_estimate=cost(23),
    )(q, kv, kvp, do, o, lse, ohq, ohk)


def proj_grad_kernel(
    dq_ref, dkv_ref, dkvr_ref, xs_ref, dr1_ref, w0, w1, w2, w3, w4, w5,
    gk_ref, gs_ref, dx_ref, sums_ref, w_s,
):
    place_qkv(w_s, (w0, w1, w2, w3, w4, w5))
    dq = dq_ref[...]
    dkv = (dkv_ref[...].astype(f32) + dkvr_ref[...].astype(f32)).astype(bf16)
    xs = xs_ref[...]
    sums_ref[0:1, :] = col_sum(dq.astype(f32))
    sums_ref[2:8, :] = jnp.zeros((6, D), f32)
    grads = (dot(xs, dq, 0, 0).astype(bf16), dot(xs, dkv, 0, 0).astype(bf16))
    for r in range(4):
        out = gs_ref if r % 2 else gk_ref
        c0 = (2 * r + 1) * BLK
        sums_ref[1:2, r * BLK : (r + 1) * BLK] = col_sum(dkv[:, c0 : c0 + BLK].astype(f32))
        for row in range(4):
            rows = slice(row * BLK, (row + 1) * BLK)
            out[r // 2, row * 3] = grads[0][rows, r * BLK : (r + 1) * BLK]
            for part in range(2):
                c0 = (2 * r + part) * BLK
                out[r // 2, row * 3 + 1 + part] = grads[1][rows, c0 : c0 + BLK]
    dx_ref[...] = dr1_ref[...] + dot(dq, w_s[:, :D], 1, 1) + dot(dkv, w_s[:, D:], 1, 1)


def proj_grad(dq, dkv, dkvr, xs, dr1, wqkv):
    rows = xs.shape[0]
    return pl.pallas_call(
        proj_grad_kernel,
        out_shape=[
            shape((2, 12, BLK, BLK), bf16),
            shape((2, 12, BLK, BLK), bf16),
            shape((rows, D)),
            shape((8, D)),
        ],
        scratch_shapes=[pltpu.VMEM((D, 3 * D), bf16)],
        compiler_params=params(MIB["proj_grad"]),
        name="proj_grad",
        cost_estimate=cost(5),
    )(dq, dkv, dkvr, xs, dr1, *wqkv)


def embed_grad_kernel(
    place_ref, series_ref, g_ref, we_ref, s0, q0, b0, s1, q1, b1, in_ref, keep_ref, send_ref, tab
):
    place = place_ref[0]
    g = g_ref[...]
    in_ref[...] = dot_hi(g, we_ref[...], 1, 1)
    tab[:LOOK] = dot_hi(series_ref[...].astype(f32), g, 0, 0)
    tab[LOOK : LOOK + 1] = col_sum(g)
    per_layer = 8 + FF // D
    for layer, (sums, qsums, db1) in enumerate(((s0, q0, b0), (s1, q1, b1))):
        base = LOOK + 1 + layer * per_layer
        for r in range(4):
            h = place ^ r
            lanes = pl.ds(pl.multiple_of(h * BLK, BLK), BLK)
            tab[base : base + 2, lanes] = qsums[0:2, r * BLK : (r + 1) * BLK]
            tab[pl.ds(base + 5 + h, 1), :] = db1[r : r + 1, :]
        tab[base + 2 : base + 5] = sums[0:3]
        tab[base + 5 + FF // D : base + per_layer] = sums[3:6]
    used = LOOK + 1 + LAYERS * per_layer
    tab[used:] = jnp.zeros((BLK - used, D), f32)
    for r in range(4):
        rows = tab[pl.ds(pl.multiple_of((place ^ r) * 32, 32), 32), :]
        out = send_ref if r % 2 else keep_ref
        for c in range(4):
            out[r // 2, c * 32 : (c + 1) * 32] = rows[:, c * BLK : (c + 1) * BLK]


def embed_grad(place, series, g, table, sums):
    rows = series.shape[0]
    spec = pl.BlockSpec(memory_space=pltpu.VMEM)
    return pl.pallas_call(
        embed_grad_kernel,
        in_specs=[pl.BlockSpec(memory_space=pltpu.SMEM)] + [spec] * 9,
        out_shape=[
            shape((rows, LOOK)),
            shape((2, BLK, BLK)),
            shape((2, BLK, BLK)),
        ],
        scratch_shapes=[pltpu.VMEM((BLK, D), f32)],
        compiler_params=params(MIB["embed_grad"]),
        name="embed_grad",
        cost_estimate=cost(2),
    )(place, series, g, table[:LOOK], *sums)


def vector_kernel(
    place_ref, val_ref, first_ref, second_ref, p0, p1, p2, p3, nv_ref, n1_ref, n2_ref, bias_ref, tab
):
    for r, part in enumerate((p0, p1, p2, p3)):
        rows = pl.ds(pl.multiple_of((place_ref[0] ^ r) * 32, 32), 32)
        for c in range(4):
            tab[rows, c * BLK : (c + 1) * BLK] = part[c * 32 : (c + 1) * 32]
    grad = tab[: val_ref.shape[0]]
    val = val_ref[...]
    first = 0.5 * first_ref[...] + 0.5 * grad
    second = 0.5 * second_ref[...] + 0.5 * grad * grad
    n1_ref[...] = first
    n2_ref[...] = second
    nv_ref[...] = val - rate_vector * (
        first / CORR / (jnp.sqrt(second / CORR) + adam_eps) + weight_decay * val
    )
    per_layer = 8 + FF // D
    for layer in range(LAYERS):
        base = LOOK + 1 + layer * per_layer
        bias_ref[2 * layer : 2 * layer + 1] = tab[base + 2 : base + 3]
        bias_ref[2 * layer + 1 : 2 * layer + 2] = tab[base + 5 + FF // D : base + 6 + FF // D]


def vector_update(place, values, first, second, parts):
    spec = pl.BlockSpec(memory_space=pltpu.VMEM)
    return pl.pallas_call(
        vector_kernel,
        in_specs=[pl.BlockSpec(memory_space=pltpu.SMEM)] + [spec] * 7,
        out_shape=[shape(values.shape)] * 3 + [shape((2 * LAYERS, D))],
        scratch_shapes=[pltpu.VMEM((BLK, D), f32)],
        compiler_params=params(MIB["vector"]),
        name="vector",
        cost_estimate=cost(2),
    )(place, values, first, second, *parts)


PARTS = ((0, 12), (12, 20), (32, 16))
HELD = ((0, 12), (12, 36))


def natural_kernel(plan, at_ref, *refs):
    count = len(plan)
    slots, outs, held = refs[:count], refs[count:-1], refs[-1]
    for ref, start in zip(slots, plan):
        held[start : start + ref.shape[0]] = ref[...]
    for i in range(len(HELD) * LAYERS):
        layer, part = divmod(i, len(HELD))
        first, n = HELD[part]
        for j in range(n):
            block = held[at_ref[layer * 48 + first + j]]
            outs[i][j] = block
            if len(outs) > len(HELD) * LAYERS:
                outs[len(HELD) * LAYERS + i][j] = block[TOP:]


def natural_order(at, slots, plan, lower):
    total = sum(s.shape[0] for s in slots)
    rows = slots[0].shape[1]
    spec = pl.BlockSpec(memory_space=pltpu.VMEM)
    heights = (rows, BLK - TOP) if lower else (rows,)
    return pl.pallas_call(
        functools.partial(natural_kernel, plan),
        in_specs=[pl.BlockSpec(memory_space=pltpu.SMEM)] + [spec] * len(slots),
        out_shape=[
            shape((n, height, BLK), bf16)
            for height in heights
            for _ in range(LAYERS)
            for _, n in HELD
        ],
        scratch_shapes=[pltpu.VMEM((total, rows, BLK), bf16)],
        compiler_params=params(MIB["natural"]),
        name="natural",
        cost_estimate=cost(3),
    )(at, *slots)


def routed_kernel(at_ref, *refs):
    own, got, out = refs[:6], refs[6:12], refs[12]
    out[...] = jnp.zeros(out.shape, bf16)
    for i in range(6):
        layer, part = divmod(i, 3)
        first, n = PARTS[part]
        for j in range(n):
            place = at_ref[layer * 48 + first + j]
            who = at_ref[96 + layer * 48 + first + j]
            value = own[i][j].astype(f32) + got[i][j].astype(f32)
            out[who, pl.ds(pl.multiple_of(place * BLK, BLK), BLK), :] = value.astype(bf16)


def routed(at, own, got, count, slots_each):
    spec = pl.BlockSpec(memory_space=pltpu.VMEM)
    return pl.pallas_call(
        routed_kernel,
        in_specs=[pl.BlockSpec(memory_space=pltpu.SMEM)] + [spec] * 12,
        out_shape=shape((count, slots_each * BLK, BLK), bf16),
        compiler_params=params(MIB["routed"]),
        name="routed",
        cost_estimate=cost(4),
    )(at, *own, *got)


def ring_of(count):
    half = count // 2
    return [2 * i for i in range(half)] + [2 * (half - 1 - i) + 1 for i in range(half)]


def ring_shift(value, order, by):
    n = len(order)
    return lax.ppermute(value, "dp", [(order[i], order[(i + by) % n]) for i in range(n)])


def ring_gather(value, order):
    n = len(order)
    half = value.shape[0] // 2

    def top(items):
        return [(far_swap(array[:, :TOP]), k, start) for array, k, start in items]

    held = [(value, 0, 0)]
    far = top(held)
    crossing = far
    ahead = behind = value
    for step in range(1, n // 2):
        if step > 2:
            behind, ahead = tied((behind, ahead), [x[0] for x in crossing])
        if step > 1:
            crossing = top(held[-2:]) if step > 2 else crossing + top(held[-2:])
            far = far + crossing[-2:]
        behind = ring_shift(behind, order, 1)
        ahead = ring_shift(ahead, order, -1)
        held += [(behind, n - step, 0), (ahead, step, 0)]
    behind, ahead = tied((behind, ahead), [x[0] for x in crossing])
    far = far + top(held[-2:])
    held.append((ring_shift(behind[:half], order, 1), n // 2, 0))
    held.append((ring_shift(ahead[half:], order, -1), n // 2, half))
    far = far + top(held[-2:])
    return held, far


def ring_reduce(pieces, order, meanwhile):
    n = len(order)
    half = pieces[0].shape[0] // 2
    up = ring_shift(pieces[n // 2][:half], order, 1)
    down = ring_shift(pieces[n // 2][half:], order, -1)
    for step in range(1, n // 2):
        near, far = pieces[n // 2 - step], pieces[n // 2 + step]
        if step == 1:
            up = jnp.concatenate([add_low(up, near[:half]), near[half:]], axis=0)
            down = jnp.concatenate([far[:half], add_low(down, far[half:])], axis=0)
        else:
            up, down = add_low(up, near), add_low(down, far)
        up, down = tied((up, down), meanwhile[step - 1])
        up, down = ring_shift(up, order, 1), ring_shift(down, order, -1)
    return pieces[0], up, down


def dp_sum(value, count, after):
    bit = 1
    while bit < count:
        if 2 * bit >= count:
            value = tied(value, after)
        low = value.astype(bf16)
        there = lax.ppermute(low, "dp", [(i, i ^ bit) for i in range(count)])
        value = low.astype(f32) + there.astype(f32)
        bit *= 2
    return value


def add_low(a, b):
    return (a.astype(f32) + b.astype(f32)).astype(bf16)


def core_swap(value):
    return lax.ppermute(value, "head", [(i, i ^ 1) for i in range(4)])


def far_swap(value):
    return lax.ppermute(value, "head", [(i, i ^ 2) for i in range(4)])


def tied(values, after):
    return lax.optimization_barrier((values, after))[0]


def one_hots(ids):
    lane = jnp.arange(LANES, dtype=jnp.int32)[None, :]
    same = ids[:, None] == lane
    return jnp.where(same, -BIG, 0.0).astype(bf16), jnp.where(same, 0.0, 1.0).astype(bf16)


def relative(row, place):
    pieces = row.reshape(4, -1)
    return jnp.take(pieces, jnp.arange(4) ^ place, axis=0).reshape(1, -1)


def on_device(
    series,
    cotangent,
    window_lengths,
    owner_list,
    master,
    first_moment,
    second_moment,
    left_stats,
    right_stats,
    left_basis,
    right_basis,
    vec_values,
    vec_first,
    vec_second,
):
    place = lax.axis_index("head")
    spot = lax.axis_index("dp")
    dp = lax.axis_size("dp")
    ringed = dp == 8
    rows = series.shape[0]
    own_slots = master.shape[1]
    buckets, win = window_lengths.shape
    bucket_rows = rows * 4 // buckets
    owner_row = owner_list[0]
    who = owner_row // own_slots
    if ringed:
        order = ring_of(dp)
        ring_at = jnp.asarray([order.index(d) for d in range(dp)], jnp.int32)
        who = (ring_at[who] - ring_at[spot]) % dp
    inner = owner_row % own_slots
    gather_at = who * own_slots + inner

    copies = master[0].astype(bf16)
    if ringed:
        held, far = ring_gather(copies, order)
        slots, plan = [x[0] for x in held], tuple(x[1] * own_slots + x[2] for x in held)
        tops, far_plan = [x[0] for x in far], tuple(x[1] * own_slots + x[2] for x in far)
    else:
        slots, plan = [lax.all_gather(copies, "dp", axis=0, tiled=True)], (0,)
        tops, far_plan = [far_swap(slots[0][:, :TOP])], (0,)
    far_at = far_swap(gather_at)
    windows = window_ids(window_lengths, bucket_rows)
    ids = windows.reshape(4, rows)
    own_ids = lax.dynamic_index_in_dim(ids, place, 0, False)
    pair_ids = lax.dynamic_index_in_dim(ids, place ^ 1, 0, False)
    ohq, ohk_own = one_hots(own_ids)
    ohk = jnp.concatenate([ohk_own, one_hots(pair_ids)[1]], axis=0)
    valid = (own_ids < win).astype(f32)[:, None]

    x = embed(series, vec_values)
    vectors = []
    for layer in range(LAYERS):
        bq, bv, bo, g1, c1, b1, b2, g2, c2 = depth_vectors(vec_values, layer)
        vec = jnp.stack([bo, g1, c1, b2, g2, c2, g2, c2])
        vectors.append([vec] + [relative(row, place) for row in (bq, bv, b1)])
    grad = cotangent * valid
    slots, (x, vectors, ohq, ohk, valid, gather_at, far_at, grad) = lax.optimization_barrier(
        (slots, (x, vectors, ohq, ohk, valid, gather_at, far_at, grad))
    )
    mine = natural_order(gather_at, slots, plan, True)
    mine, lower = mine[: len(HELD) * LAYERS], mine[len(HELD) * LAYERS :]
    upper = natural_order(far_at, tops, far_plan, False)
    moved = []

    def cross(i, after=None):
        own = lower[i] if after is None else tied(lower[i], after)
        moved.append(far_swap(own))
        return moved[-1]

    def four(i, after=None):
        there = moved[i] if after is None else tied(moved[i], after)
        return [
            mine[i], core_swap(mine[i]), upper[i], there, core_swap(upper[i]), core_swap(there)
        ]

    weights = []
    saved = []
    for layer in range(LAYERS):
        vec, bq, bv, b1 = vectors[layer]
        if layer == 0:
            cross(0)
        wqkv = four(2 * layer, x if layer else None)
        x = tied(x, wqkv)
        if layer == 0:
            cross(1, moved[0])
        xs, q, kv = project(x, bq, bv, wqkv)
        kvp = core_swap(kv)
        o, lse = attend(q, kv, kvp, ohq, ohk)
        wfeed = four(2 * layer + 1, o)
        weights.append((wqkv, wfeed))
        if layer + 1 < LAYERS:
            done = moved[-1]
            cross(2 * layer + 2, done)
            cross(2 * layer + 3, (done, moved[-1]))
        n1, i1, y, hid, slope, n2, i2, x = post(o, x, vec, b1, wfeed)
        saved.append((xs, q, kv, kvp, o, lse, vec, n1, i1, y, hid, slope, n2, i2))
    activations = x * valid

    own_sums = [None] * (3 * LAYERS)
    far_sums = [None] * (3 * LAYERS)
    table_rows = [None] * LAYERS

    waiting = []

    def chip_sum(at, keep, got):
        waiting.append((at, keep, got))
        return add_low(keep[1], got[1])

    def own_chip_sums(after):
        while waiting:
            at, keep, got = waiting.pop()
            keep, got = tied((keep[0], got[0]), after)
            own_sums[at] = add_low(keep, got)

    moving = []
    for layer in reversed(range(LAYERS)):
        xs, q, kv, kvp, o, lse, vec, n1, i1, y, hid, slope, n2, i2 = saved[layer]
        wqkv, wfeed = weights[layer]
        gk, gs, ok, os, dr1, do, db1, sums = ffn_grad(
            grad, n2, i2, n1, i1, y, hid, slope, o, vec, wfeed
        )
        os, gs, ok, gk, do = tied((os, gs, ok, gk, do), moving)
        own_chip_sums(sums)
        got = [core_swap(os), core_swap(gs)]
        mid = chip_sum(3 * layer + 1, ok, got[0])
        down = chip_sum(3 * layer + 2, gk, got[1])
        far_sums[3 * layer + 1] = far_swap(mid)
        do = tied(do, (mid, down))
        dq, dkv, dkvp = attend_grad(q, kv, kvp, do, o, lse, ohq, ohk)
        dkvp = tied(dkvp, far_sums[3 * layer + 1])
        far_sums[3 * layer + 2] = far_swap(tied(down, far_sums[3 * layer + 1]))
        if layer == 0:
            far_sums[late[0]] = far_swap(tied(late[1], far_sums[1]))
        dkvr = core_swap(dkvp)
        pk, ps, grad, qsums = proj_grad(dq, dkv, dkvr, xs, dr1, wqkv)
        table_rows[layer] = (sums, qsums, db1)
        got = core_swap(ps)
        if layer:
            far = chip_sum(3 * layer, pk, got)
            grad = tied(grad, far)
            late = (3 * layer, far)
            moving = [far_sums[3 * layer + 2]]
    input_grad, tab_keep, tab_send = embed_grad(
        place.astype(jnp.int32)[None], series, grad, vec_values, table_rows[0] + table_rows[1]
    )
    far_sums[0] = far_swap(chip_sum(0, pk, got))
    own_chip_sums(tab_send)
    tab = dp_sum(tab_keep + core_swap(tab_send), dp, far_sums[0])
    tab_part = tab[0] + far_swap(tab[1])
    tab_there = far_swap(tab_part)
    parts = [tab_part, core_swap(tab_part), tab_there, core_swap(tab_there)]
    vec_new_values, vec_new_first, vec_new_second, branch_bias_grads = vector_update(
        place.astype(jnp.int32)[None], vec_values, vec_first, vec_second, parts
    )
    at = jnp.concatenate([inner, who]).astype(jnp.int32)
    pieces = routed(at, own_sums, far_sums, dp, own_slots)
    if ringed:
        meanwhile = (tab, tab_part, parts)
        terms = ring_reduce([pieces[i] for i in range(dp)], order, meanwhile)
        terms = tied(terms, vec_new_values)
        grads = [t.reshape(own_slots, BLK, BLK) for t in terms]
    else:
        whole = lax.psum_scatter(pieces, "dp", scatter_dimension=0, tiled=True)
        grads = [whole.reshape(own_slots, BLK, BLK)]
    new_master, new_copy, new_first, new_second, new_left, new_right, left_next, right_next = soap(
        grads,
        master[0],
        first_moment[0],
        second_moment[0],
        left_stats[0],
        right_stats[0],
        left_basis[0],
        right_basis[0],
    )
    return (
        activations,
        input_grad,
        new_master[None],
        new_copy[None],
        new_first[None],
        new_second[None],
        new_left[None],
        new_right[None],
        left_next[None],
        right_next[None],
        vec_new_values,
        vec_new_first,
        vec_new_second,
        branch_bias_grads,
    )


def solution(mesh):
    placed = (
        P(("dp", "head"), None),
        P(("dp", "head"), None),
        P("dp", None),
        P("head", None),
        P("head", "dp", None, None),
        P("head", "dp", None, None),
        P("head", "dp", None, None),
        P("head", "dp", None, None),
        P("head", "dp", None, None),
        P("head", "dp", None, None),
        P("head", "dp", None, None),
        P(),
        P(),
        P(),
    )
    return jax.shard_map(
        on_device,
        mesh=mesh,
        in_specs=placed,
        out_specs=(
            P(("dp", "head"), None),
            P(("dp", "head"), None),
            P("head", "dp", None, None),
            P("head", "dp", None, None),
            P("head", "dp", None, None),
            P("head", "dp", None, None),
            P("head", "dp", None, None),
            P("head", "dp", None, None),
            P("head", "dp", None, None),
            P("head", "dp", None, None),
            P(),
            P(),
            P(),
            P(),
        ),
        check_vma=False,
    )
```
